32 devices in a mesh: groups: 2 (over y), frame: 4 (over x, core), row: 4 (over z).
Axes of the slice: x: 2, y: 2, z: 4, core: 2. Of those that a mesh axis runs over, the one named last changes fastest.
Arguments:
- observed: float32 [16, 128, 2048], P('frame', ('groups', 'row')), parts along dimension 1, may hold values from 0.5 to 8
- kernels: float32 [8, 5], replicated, may hold values from 0.05 to 1
- band_kernel: int32 [16], P('groups'), parts along dimension 0, may hold values from 0 to 7
- masks: int32 [256, 128, 16], P(None, ('groups', 'row'), 'frame'), parts along dimension 1, may hold values from 0 to 1, as said below
Outputs:
- spikes: bfloat16 [16, 128, 2048], P(None, ('groups', 'row'), 'frame'), parts along dimension 1
- traces: float32 [512, 16], P(('groups', 'frame', 'row')), parts along dimension 0
The draws below stay inside these ranges and needn't reach their ends.
There are 2 independent parts, one for each index of `groups`. The reference program is written for one: setup_inputs(seed, part) draws one part's arguments, and reference() takes and returns one part's arrays. A program takes and returns all parts, laid end to end along the dimension named above; an argument that names none is the same for every part. Nothing has to cross between parts.
Inputs may be any that keep to these rules, and one draw needn't show every extreme that they name: `masks`: each component covers the tile at its centre and a random half of the tiles within 8 rows and one tile column of that centre, so it covers at least one tile.
All inputs are finite; a program needn't handle non-finite values.
Results may differ from the reference program's by a relative error of at most 0.0062.
Values may be sent and summed in bfloat16 or wider, within the bound.
No kernel may reach another device: no remote copies, remote signals or barrier semaphores. Data moves between devices by JAX's collectives and lax.ppermute only.
A program may use at most 64 MiB of HBM per device.

```python
import math
import jax
import jax.numpy as jnp
from jax import lax

W = 2048
K = 256
TILE = 128
TAPS = 5
NK = 8
BAND = 8
REACH = 8
ITERS = 3
F = 16
H = 64
NT = 16


def draw_masks(key, part):
    key_row, key_col, key_coin = jax.random.split(key, 3)
    centre_row = jax.random.randint(key_row, (K,), 0, H)
    centre_col = jax.random.randint(key_col, (K,), 0, NT)
    coin_flips = jax.random.randint(key_coin, (K, H, NT), 0, 2)
    row_ids = jnp.arange(H)[None, :, None]
    col_ids = jnp.arange(NT)[None, None, :]
    row_gap = jnp.abs(row_ids - centre_row[:, None, None])
    col_gap = jnp.abs(col_ids - centre_col[:, None, None])
    nearby = (row_gap <= REACH) & (col_gap <= 1) & (coin_flips == 1)
    centre = (row_gap == 0) & (col_gap == 0)
    return jnp.where(nearby | centre, 1, 0).astype(jnp.int32)


def plant(array, key, smallest, top_value):
    place = [jax.random.randint(jax.random.fold_in(key, axis), (), 0, length) for axis, length in enumerate(array.shape)]
    longest = array.shape.index(max(array.shape))
    neighbour = place[:longest] + [(place[longest] + 1) % array.shape[longest]] + place[longest + 1:]
    return array.at[tuple(place)].set(smallest).at[tuple(neighbour)].set(top_value)


def levels(rng, shape, shards, low, high):
    loudness, own = 1.0, jax.random.fold_in(rng, 6)
    for dim, shards_of in shards:
        steps = jnp.exp(jax.random.uniform(jax.random.fold_in(own, dim), (shards_of,), jnp.float32, low / len(shards), high / len(shards)))
        loudness = loudness * jnp.repeat(steps, shape[dim] // shards_of).reshape([-1 if axis == dim else 1 for axis in range(len(shape))])
    return loudness


def setup_inputs(seed: int = 0, part: int = 0) -> dict:
    streams_of = jax.random.split(jax.random.key(seed), 5)
    part_splits = jax.random.split(jax.random.fold_in(streams_of[4], part), 5)
    return {
        "observed": jnp.clip(jnp.exp(math.log(8.0) - 2.7725887 * jax.random.uniform(part_splits[0], (F, H, W), jnp.float32) ** levels(part_splits[0], (F, H, W), ((0, 4), (1, 4)), -0.2, 0.2)), 0.5, 8.0),
        "kernels": jnp.clip(jnp.exp(jax.random.uniform(streams_of[1], (NK, TAPS), jnp.float32, math.log(0.05), math.log(1.0))), 0.05, 1.0),
        "band_kernel": plant(jax.random.randint(part_splits[2], (H // BAND,), 0, NK), jax.random.fold_in(part_splits[2], 1), 0, NK - 1).astype(jnp.int32),
        "masks": draw_masks(jax.random.fold_in(jax.random.fold_in(streams_of[4], part), 71), part),
    }


SMOOTHING = 1024.0
DECAY_RATE = 0.9

def table_rows(kernels, band_kernel):
    tap_table = kernels / jnp.sum(kernels, axis=1, keepdims=True)
    row_bands = jnp.arange(H) // BAND
    return tap_table[band_kernel[row_bands]]

def restore_image(image, row_taps):
    padded_taps = jnp.pad(row_taps, ((2, 2), (0, 0)))
    current = image
    for iteration in range(ITERS):
        padded = jnp.pad(current, ((2, 2), (0, 0)))
        blurred = row_taps[:, 0:1] * padded[0:H]
        for offset in range(1, 5):
            blurred = blurred + row_taps[:, offset:offset + 1] * padded[offset:offset + H]
        quotient = image / blurred
        padded_quotient = jnp.pad(quotient, ((2, 2), (0, 0)))
        back = padded_taps[4:4 + H, 0:1] * padded_quotient[4:4 + H]
        for offset in range(1, 5):
            start = 4 - offset
            back = back + padded_taps[start:start + H, offset:offset + 1] * padded_quotient[start:start + H]
        current = current * back
    return current.astype(jnp.bfloat16)

def smooth_series(series):
    values = series.astype(jnp.float32)
    frame_total = values.shape[0]
    frame_ids = jnp.arange(frame_total)
    at_ends = (frame_ids == 0) | (frame_ids == frame_total - 1)
    middle = (1.0 + SMOOTHING * jnp.where(at_ends, 1.0, 2.0)).astype(jnp.float32)
    sub_diag = jnp.where(frame_ids == 0, 0.0, -SMOOTHING).astype(jnp.float32)
    super_diag = jnp.where(frame_ids == frame_total - 1, 0.0, -SMOOTHING).astype(jnp.float32)
    baseline = lax.linalg.tridiagonal_solve(sub_diag, middle, super_diag, values)
    detrended = values - baseline
    earlier = jnp.concatenate([jnp.zeros((1, values.shape[1]), jnp.float32), detrended[:-1]], axis=0)
    return (detrended - DECAY_RATE * earlier).astype(jnp.bfloat16)

def reference(observed, kernels, band_kernel, masks):
    row_taps = table_rows(kernels, band_kernel)
    estimate = lax.map(lambda image: restore_image(image, row_taps), observed)
    by_rows = jnp.transpose(estimate, (1, 0, 2))
    spikes = jnp.transpose(lax.map(smooth_series, by_rows), (1, 0, 2))
    tile_sums = jnp.sum(spikes.astype(jnp.float32).reshape(F, H, NT, TILE), axis=3)
    weights = masks.astype(jnp.float32)
    trace_sums = jnp.einsum('khc,fhc->kf', weights, tile_sums, precision=lax.Precision.HIGHEST)
    counts = jnp.sum(weights, axis=(1, 2))
    traces = trace_sums / (TILE * counts[:, None])
    return (spikes, traces)
```

```python
import functools

import jax
import jax.numpy as jnp
from jax import lax
from jax.experimental import pallas as pl
from jax.experimental.pallas import tpu as pltpu
from jax.sharding import PartitionSpec as P

TILE = 128
BAND = 8
ITERS = 3
TAPS = 5


SMOOTHING = 1024.0
DECAY_RATE = 0.9


def padded_2(cells, sides, width):
    for axis, dim in sides:
        count = lax.axis_size(axis)
        ends = count - 1
        head = lax.slice_in_dim(cells, 0, width, axis=dim)
        tail = lax.slice_in_dim(cells, cells.shape[dim] - width, cells.shape[dim], axis=dim)
        cells = jnp.concatenate(
            [
                lax.ppermute(tail, axis, [(i, (i + 1) % count) for i in range(ends)]),
                cells,
                lax.ppermute(head, axis, [((i + 1) % count, i) for i in range(ends)]),
            ],
            axis=dim,
        )
    return cells


def tap_rows(tap_table, band_kernel, first_row, row_count, height):
    row_ids = jnp.clip(first_row + jnp.arange(row_count), 0, height - 1)
    row_bands = row_ids // BAND
    band_slots = jnp.arange(band_kernel.shape[0])
    kernel_ids = jnp.sum(
        jnp.where(row_bands[:, None] == band_slots[None, :], band_kernel[None, :], 0), axis=1
    )
    kernel_slots = jnp.arange(tap_table.shape[0])
    picked = jnp.where(
        kernel_ids[:, None, None] == kernel_slots[None, :, None], tap_table[None, :, :], 0.0
    )
    return jnp.sum(picked, axis=1)


def blur_rows(padded, row_taps, row_count):
    summed = row_taps[:, 0][None, :, None] * padded[:, 0:row_count]
    for offset in range(1, 5):
        summed = (
            summed + row_taps[:, offset][None, :, None] * padded[:, offset : offset + row_count]
        )
    return summed


def back_rows(padded_quotient, outer_taps, row_count):
    summed = outer_taps[4 : 4 + row_count, 0][None, :, None] * padded_quotient[:, 4 : 4 + row_count]
    for offset in range(1, 5):
        start = 4 - offset
        summed = (
            summed
            + outer_taps[start : start + row_count, offset][None, :, None]
            * padded_quotient[:, start : start + row_count]
        )
    return summed


def temporal(series_block):
    frame_total, item_count, columns = series_block.shape
    values = series_block.astype(jnp.float32).reshape(frame_total, item_count * columns)
    frame_ids = jnp.arange(frame_total)
    at_ends = (frame_ids == 0) | (frame_ids == frame_total - 1)
    middle = (1.0 + SMOOTHING * jnp.where(at_ends, 1.0, 2.0)).astype(jnp.float32)
    sub_diag = jnp.where(frame_ids == 0, 0.0, -SMOOTHING).astype(jnp.float32)
    super_diag = jnp.where(frame_ids == frame_total - 1, 0.0, -SMOOTHING).astype(jnp.float32)
    baseline = lax.linalg.tridiagonal_solve(sub_diag, middle, super_diag, values)
    detrended = values - baseline
    earlier = jnp.concatenate(
        [jnp.zeros((1, values.shape[1]), jnp.float32), detrended[:-1]], axis=0
    )
    result = (detrended - DECAY_RATE * earlier).astype(jnp.bfloat16)
    return result.reshape(frame_total, item_count, columns)


def local(observed, kernels, band_kernel, masks):
    frames_dev, rows_dev, row_pixels = observed.shape
    height = rows_dev * lax.axis_size("row")
    tap_table = kernels / jnp.sum(kernels, axis=1, keepdims=True)
    first_row = lax.axis_index("row") * rows_dev
    own_taps = tap_rows(tap_table, band_kernel, first_row, rows_dev, height)
    outer_taps = tap_rows(tap_table, band_kernel, first_row - 2, rows_dev + 4, height)
    current = observed
    for iteration in range(ITERS):
        padded = padded_2(current, (("row", 1),), 2)
        blurred = blur_rows(padded, own_taps, rows_dev)
        quotient = observed / blurred
        padded_quotient = padded_2(quotient, (("row", 1),), 2)
        current = current * back_rows(padded_quotient, outer_taps, rows_dev)
    estimate = current.astype(jnp.bfloat16)
    spikes = temporal(lax.all_to_all(estimate, "frame", split_axis=2, concat_axis=0, tiled=True))
    frames_all, _, columns = spikes.shape
    tile_count = columns // TILE
    tile_sums = jnp.sum(
        spikes.reshape(frames_all, rows_dev * tile_count, TILE).astype(jnp.float32), axis=2
    )
    weights = masks.astype(jnp.float32).reshape(masks.shape[0], rows_dev * tile_count)
    local_sums = lax.dot_general(
        weights, tile_sums, (((1,), (1,)), ((), ())), precision=lax.Precision.HIGHEST
    )
    counts = jnp.sum(weights, axis=1)
    trace_sums, totals = (
        lax.psum_scatter(local_sums, ("frame", "row"), scatter_dimension=0, tiled=True),
        lax.psum_scatter(counts, ("frame", "row"), scatter_dimension=0, tiled=True),
    )
    traces = trace_sums / (TILE * totals[:, None])
    return (spikes, traces)


def roll_rows(cells, shift):
    rows = cells.shape[0]
    return cells if shift % rows == 0 else pltpu.roll(cells, shift % rows, 0)


def restore_kernel(
    band_ref, kernels_ref, observed_ref, masks_ref, out_ref, tap_ref, sums_ref, *, devices, rows_dev, tiles_dev
):
    n_frame, n_row = devices
    height, _ = observed_ref.shape
    positions = rows_dev * tiles_dev
    row_ids = lax.broadcasted_iota(jnp.int32, (BAND, TILE), 0)
    for band in range(height // BAND):
        kernel = band_ref[band]
        raw = [kernels_ref[kernel, tap] for tap in range(TAPS)]
        total = raw[0]
        for tap in range(1, TAPS):
            total = total + raw[tap]
        for tap in range(TAPS):
            weight = jnp.full((BAND, TILE), raw[tap], jnp.float32) / jnp.full((BAND, TILE), total, jnp.float32)
            target = row_ids + (band * BAND + tap - TAPS // 2)
            weight = jnp.where((target >= 0) & (target < height), weight, 0.0)
            tap_ref[tap, band * BAND : (band + 1) * BAND, :] = weight
    flat = jnp.concatenate([masks_ref[row].astype(jnp.float32) for row in range(rows_dev)], axis=0)
    both = jnp.concatenate([flat, flat], axis=0).T.astype(jnp.bfloat16)
    share = both.shape[0] // (n_frame * n_row)
    est_rows = rows_dev * tiles_dev
    for place in range(n_frame * n_row):
        out_ref[place, est_rows + rows_dev : est_rows + rows_dev + share, :] = both[place * share : (place + 1) * share]
    lanes = lax.broadcasted_iota(jnp.int32, (rows_dev, TILE), 1)
    own_rows = lax.broadcasted_iota(jnp.int32, (rows_dev, TILE), 0)
    ones = jnp.ones((TILE, TILE), jnp.bfloat16)

    def column_block(block, carry):
        gathered = [jnp.zeros((1, TILE), jnp.float32) for _ in range(n_row)]
        for tile in range(tiles_dev):
            start = pl.multiple_of((block * tiles_dev + tile) * TILE, TILE)
            image = observed_ref[:, pl.ds(start, TILE)].astype(jnp.float32)
            current = image
            for _ in range(ITERS):
                blurred = tap_ref[2] * current
                for tap in (0, 1, 3, 4):
                    blurred = blurred + tap_ref[tap] * roll_rows(current, 2 - tap)
                quotient = image / blurred
                back = tap_ref[2] * quotient
                for tap in (0, 1, 3, 4):
                    back = back + roll_rows(tap_ref[tap] * quotient, tap - 2)
                current = current * back
            estimate = current.astype(jnp.bfloat16)
            for row in range(n_row):
                out_ref[block * n_row + row, tile * rows_dev : (tile + 1) * rows_dev, :] = estimate[
                    row * rows_dev : (row + 1) * rows_dev
                ]
            tile_sums = jnp.dot(estimate, ones, preferred_element_type=jnp.float32)
            here = lanes % positions == own_rows * tiles_dev + tile
            for row in range(n_row):
                part = jnp.where(here, tile_sums[row * rows_dev : (row + 1) * rows_dev], 0.0)
                gathered[row] = gathered[row] + jnp.sum(part, axis=0, keepdims=True)
        for row in range(n_row):
            sums_ref[pl.ds(block * n_row + row, 1), :] = gathered[row]
        return carry

    lax.fori_loop(0, n_frame, column_block, 0)
    sums = sums_ref[...]
    high = sums.astype(jnp.bfloat16).astype(jnp.float32)
    split = jnp.where(lax.broadcasted_iota(jnp.int32, sums.shape, 1) < positions, high, sums - high)
    split = split.astype(jnp.bfloat16)
    for place in range(n_frame * n_row):
        out_ref[place, est_rows : est_rows + rows_dev, :] = split


def deconvolved(series, factors):
    total = len(series)
    forward = [series[0] * factors[0]]
    for step in range(1, total):
        forward.append((series[step] + SMOOTHING * forward[step - 1]) * factors[step])
    baseline = [None] * total
    baseline[total - 1] = forward[total - 1]
    for step in range(total - 2, -1, -1):
        baseline[step] = forward[step] + (SMOOTHING * factors[step]) * baseline[step + 1]
    result, earlier = [], None
    for step in range(total):
        detrended = series[step] - baseline[step]
        result.append(detrended if earlier is None else detrended - DECAY_RATE * earlier)
        earlier = detrended
    return result


def solve_factors(total):
    factors = []
    for step in range(total):
        middle = 1.0 + SMOOTHING * (1.0 if step in (0, total - 1) else 2.0)
        if step:
            middle -= SMOOTHING * SMOOTHING * factors[-1]
        factors.append(1.0 / middle)
    return factors


def temporal_kernel(in_ref, spikes_ref, traces_ref, sums_ref, *, rows_dev, tiles_dev, share):
    frames = in_ref.shape[0]
    factors = solve_factors(frames)
    for tile in range(tiles_dev):
        series = [in_ref[t, tile * rows_dev : (tile + 1) * rows_dev, :].astype(jnp.float32) for t in range(frames)]
        for t, spikes in enumerate(deconvolved(series, factors)):
            spikes_ref[t, :, tile * TILE : (tile + 1) * TILE] = spikes.astype(spikes_ref.dtype)
    first = rows_dev * tiles_dev
    series = [in_ref[t, first : first + frames, :].astype(jnp.float32) for t in range(frames)]
    for t, sums in enumerate(deconvolved(series, factors)):
        sums_ref[t * frames : (t + 1) * frames, :] = sums
    first += frames
    weights = jnp.concatenate([in_ref[j, first : first + share, :].astype(jnp.float32) for j in range(frames)], axis=1)
    sums = jnp.concatenate([sums_ref[pl.ds(j, frames, stride=frames), :] for j in range(frames)], axis=1)
    trace_sums = lax.dot_general(
        weights, sums, (((1,), (1,)), ((), ())), precision=lax.Precision.HIGHEST, preferred_element_type=jnp.float32
    )
    counts = 0.5 * jnp.sum(weights, axis=1, keepdims=True)
    traces_ref[...] = trace_sums / (TILE * counts)


def by_frame(observed, kernels, band_kernel, masks):
    n_frame, n_row = lax.axis_size("frame"), lax.axis_size("row")
    places = n_frame * n_row
    components, rows_dev, tiles_dev = masks.shape
    height, width = rows_dev * n_row, observed.shape[2]
    share = components // places
    block_rows = rows_dev * tiles_dev + places + share
    sent = lax.all_to_all(observed.astype(jnp.float16), "row", split_axis=0, concat_axis=0, tiled=True)
    image = sent.astype(jnp.float32).reshape(height, width)
    blocks = pl.pallas_call(
        functools.partial(restore_kernel, devices=(n_frame, n_row), rows_dev=rows_dev, tiles_dev=tiles_dev),
        out_shape=jax.ShapeDtypeStruct((places, block_rows, TILE), jnp.bfloat16),
        in_specs=[pl.BlockSpec(memory_space=pltpu.SMEM)] * 2 + [pl.BlockSpec(memory_space=pltpu.VMEM)] * 2,
        out_specs=pl.BlockSpec(memory_space=pltpu.VMEM),
        scratch_shapes=[pltpu.VMEM((TAPS, height, TILE), jnp.float32), pltpu.VMEM((places, TILE), jnp.float32)],
        compiler_params=pltpu.CompilerParams(vmem_limit_bytes=16 << 20),
        name="restore",
    )(band_kernel, kernels, image, masks.transpose(1, 2, 0))
    series = lax.all_to_all(blocks, ("frame", "row"), split_axis=0, concat_axis=0, tiled=True)
    spikes, traces = pl.pallas_call(
        functools.partial(temporal_kernel, rows_dev=rows_dev, tiles_dev=tiles_dev, share=share),
        out_shape=(
            jax.ShapeDtypeStruct((places, rows_dev, tiles_dev * TILE), jnp.bfloat16),
            jax.ShapeDtypeStruct((share, places), jnp.float32),
        ),
        in_specs=[pl.BlockSpec(memory_space=pltpu.VMEM)],
        out_specs=(pl.BlockSpec(memory_space=pltpu.VMEM),) * 2,
        scratch_shapes=[pltpu.VMEM((places * places, TILE), jnp.float32)],
        compiler_params=pltpu.CompilerParams(vmem_limit_bytes=16 << 20),
        name="temporal",
    )(series)
    return (spikes, traces)


def fits(mesh, observed, masks):
    frames_dev = observed.shape[0] // mesh.shape["frame"]
    rows_dev = masks.shape[1] // (mesh.shape["groups"] * mesh.shape["row"])
    tiles_dev = masks.shape[2] // mesh.shape["frame"]
    places = mesh.shape["frame"] * mesh.shape["row"]
    return (
        frames_dev == mesh.shape["row"]
        and 2 * rows_dev * tiles_dev == TILE
        and rows_dev == 16
        and places == 16
        and masks.shape[0] // places == 16
    )


def solution(mesh):
    in_specs = (
        P("frame", ("groups", "row"), None),
        P(),
        P("groups"),
        P(None, ("groups", "row"), "frame"),
    )
    out_specs = (P(None, ("groups", "row"), "frame"), P(("groups", "frame", "row"), None))

    def whole(observed, kernels, band_kernel, masks):
        body = by_frame if fits(mesh, observed, masks) else local
        mapped = jax.shard_map(body, mesh=mesh, in_specs=in_specs, out_specs=out_specs, check_vma=False)
        return mapped(observed, kernels, band_kernel, masks)

    return whole
```

```python
import functools

import jax
import jax.numpy as jnp
from jax import lax
from jax.experimental import pallas as pl
from jax.experimental.pallas import tpu as pltpu
from jax.sharding import PartitionSpec as P

TILE = 128
BAND = 8
ITERS = 3
TAPS = 5


SMOOTHING = 1024.0
DECAY_RATE = 0.9


def padded_2(cells, sides, width):
    for axis, dim in sides:
        count = lax.axis_size(axis)
        ends = count - 1
        head = lax.slice_in_dim(cells, 0, width, axis=dim)
        tail = lax.slice_in_dim(cells, cells.shape[dim] - width, cells.shape[dim], axis=dim)
        cells = jnp.concatenate(
            [
                lax.ppermute(tail, axis, [(i, (i + 1) % count) for i in range(ends)]),
                cells,
                lax.ppermute(head, axis, [((i + 1) % count, i) for i in range(ends)]),
            ],
            axis=dim,
        )
    return cells


def tap_rows(tap_table, band_kernel, first_row, row_count, height):
    row_ids = jnp.clip(first_row + jnp.arange(row_count), 0, height - 1)
    row_bands = row_ids // BAND
    band_slots = jnp.arange(band_kernel.shape[0])
    kernel_ids = jnp.sum(
        jnp.where(row_bands[:, None] == band_slots[None, :], band_kernel[None, :], 0), axis=1
    )
    kernel_slots = jnp.arange(tap_table.shape[0])
    picked = jnp.where(
        kernel_ids[:, None, None] == kernel_slots[None, :, None], tap_table[None, :, :], 0.0
    )
    return jnp.sum(picked, axis=1)


def blur_rows(padded, row_taps, row_count):
    summed = row_taps[:, 0][None, :, None] * padded[:, 0:row_count]
    for offset in range(1, 5):
        summed = (
            summed + row_taps[:, offset][None, :, None] * padded[:, offset : offset + row_count]
        )
    return summed


def back_rows(padded_quotient, outer_taps, row_count):
    summed = outer_taps[4 : 4 + row_count, 0][None, :, None] * padded_quotient[:, 4 : 4 + row_count]
    for offset in range(1, 5):
        start = 4 - offset
        summed = (
            summed
            + outer_taps[start : start + row_count, offset][None, :, None]
            * padded_quotient[:, start : start + row_count]
        )
    return summed


def temporal(series_block):
    frame_total, item_count, columns = series_block.shape
    values = series_block.astype(jnp.float32).reshape(frame_total, item_count * columns)
    frame_ids = jnp.arange(frame_total)
    at_ends = (frame_ids == 0) | (frame_ids == frame_total - 1)
    middle = (1.0 + SMOOTHING * jnp.where(at_ends, 1.0, 2.0)).astype(jnp.float32)
    sub_diag = jnp.where(frame_ids == 0, 0.0, -SMOOTHING).astype(jnp.float32)
    super_diag = jnp.where(frame_ids == frame_total - 1, 0.0, -SMOOTHING).astype(jnp.float32)
    baseline = lax.linalg.tridiagonal_solve(sub_diag, middle, super_diag, values)
    detrended = values - baseline
    earlier = jnp.concatenate(
        [jnp.zeros((1, values.shape[1]), jnp.float32), detrended[:-1]], axis=0
    )
    result = (detrended - DECAY_RATE * earlier).astype(jnp.bfloat16)
    return result.reshape(frame_total, item_count, columns)


def local(observed, kernels, band_kernel, masks):
    frames_dev, rows_dev, row_pixels = observed.shape
    height = rows_dev * lax.axis_size("row")
    tap_table = kernels / jnp.sum(kernels, axis=1, keepdims=True)
    first_row = lax.axis_index("row") * rows_dev
    own_taps = tap_rows(tap_table, band_kernel, first_row, rows_dev, height)
    outer_taps = tap_rows(tap_table, band_kernel, first_row - 2, rows_dev + 4, height)
    current = observed
    for iteration in range(ITERS):
        padded = padded_2(current, (("row", 1),), 2)
        blurred = blur_rows(padded, own_taps, rows_dev)
        quotient = observed / blurred
        padded_quotient = padded_2(quotient, (("row", 1),), 2)
        current = current * back_rows(padded_quotient, outer_taps, rows_dev)
    estimate = current.astype(jnp.bfloat16)
    spikes = temporal(lax.all_to_all(estimate, "frame", split_axis=2, concat_axis=0, tiled=True))
    frames_all, _, columns = spikes.shape
    tile_count = columns // TILE
    tile_sums = jnp.sum(
        spikes.reshape(frames_all, rows_dev * tile_count, TILE).astype(jnp.float32), axis=2
    )
    weights = masks.astype(jnp.float32).reshape(masks.shape[0], rows_dev * tile_count)
    local_sums = lax.dot_general(
        weights, tile_sums, (((1,), (1,)), ((), ())), precision=lax.Precision.HIGHEST
    )
    counts = jnp.sum(weights, axis=1)
    trace_sums, totals = (
        lax.psum_scatter(local_sums, ("frame", "row"), scatter_dimension=0, tiled=True),
        lax.psum_scatter(counts, ("frame", "row"), scatter_dimension=0, tiled=True),
    )
    traces = trace_sums / (TILE * totals[:, None])
    return (spikes, traces)


def roll_rows(cells, shift):
    rows = cells.shape[0]
    return cells if shift % rows == 0 else pltpu.roll(cells, shift % rows, 0)


def restore_kernel(
    place_ref, band_ref, kernels_ref, *refs, devices, rows_dev, tiles_dev
):
    n_frame, n_row = devices
    pieces, (masks_ref, out_ref, observed_ref, tap_ref, sums_ref) = refs[:n_row], refs[n_row:]
    for step, piece in enumerate(pieces):
        start = pl.multiple_of((place_ref[0] ^ step) * rows_dev, rows_dev)
        observed_ref[pl.ds(start, rows_dev), :] = piece[...]
    height, _ = observed_ref.shape
    positions = rows_dev * tiles_dev
    row_ids = lax.broadcasted_iota(jnp.int32, (BAND, TILE), 0)
    for band in range(height // BAND):
        kernel = band_ref[band]
        raw = [kernels_ref[kernel, tap] for tap in range(TAPS)]
        total = raw[0]
        for tap in range(1, TAPS):
            total = total + raw[tap]
        for tap in range(TAPS):
            weight = jnp.full((BAND, TILE), raw[tap], jnp.float32) / jnp.full((BAND, TILE), total, jnp.float32)
            target = row_ids + (band * BAND + tap - TAPS // 2)
            weight = jnp.where((target >= 0) & (target < height), weight, 0.0)
            tap_ref[tap, band * BAND : (band + 1) * BAND, :] = weight
    flat = jnp.concatenate([masks_ref[row].astype(jnp.float32) for row in range(rows_dev)], axis=0)
    both = jnp.concatenate([flat, flat], axis=0).T.astype(jnp.bfloat16)
    share = both.shape[0] // (n_frame * n_row)
    est_rows = rows_dev * tiles_dev
    for place in range(n_frame * n_row):
        out_ref[place, est_rows + rows_dev : est_rows + rows_dev + share, :] = both[place * share : (place + 1) * share]
    lanes = lax.broadcasted_iota(jnp.int32, (rows_dev, TILE), 1)
    own_rows = lax.broadcasted_iota(jnp.int32, (rows_dev, TILE), 0)
    ones = jnp.ones((TILE, TILE), jnp.bfloat16)

    def column_block(block, carry):
        gathered = [jnp.zeros((1, TILE), jnp.float32) for _ in range(n_row)]
        for tile in range(tiles_dev):
            start = pl.multiple_of((block * tiles_dev + tile) * TILE, TILE)
            image = observed_ref[:, pl.ds(start, TILE)].astype(jnp.float32)
            current = image
            for _ in range(ITERS):
                blurred = tap_ref[2] * current
                for tap in (0, 1, 3, 4):
                    blurred = blurred + tap_ref[tap] * roll_rows(current, 2 - tap)
                quotient = image / blurred
                back = tap_ref[2] * quotient
                for tap in (0, 1, 3, 4):
                    back = back + roll_rows(tap_ref[tap] * quotient, tap - 2)
                current = current * back
            estimate = current.astype(jnp.bfloat16)
            for row in range(n_row):
                out_ref[block * n_row + row, tile * rows_dev : (tile + 1) * rows_dev, :] = estimate[
                    row * rows_dev : (row + 1) * rows_dev
                ]
            tile_sums = jnp.dot(estimate, ones, preferred_element_type=jnp.float32)
            here = lanes % positions == own_rows * tiles_dev + tile
            for row in range(n_row):
                part = jnp.where(here, tile_sums[row * rows_dev : (row + 1) * rows_dev], 0.0)
                gathered[row] = gathered[row] + jnp.sum(part, axis=0, keepdims=True)
        for row in range(n_row):
            sums_ref[pl.ds(block * n_row + row, 1), :] = gathered[row]
        return carry

    lax.fori_loop(0, n_frame, column_block, 0)
    sums = sums_ref[...]
    high = sums.astype(jnp.bfloat16).astype(jnp.float32)
    split = jnp.where(lax.broadcasted_iota(jnp.int32, sums.shape, 1) < positions, high, sums - high)
    split = split.astype(jnp.bfloat16)
    for place in range(n_frame * n_row):
        out_ref[place, est_rows : est_rows + rows_dev, :] = split


def deconvolved(series, factors):
    total = len(series)
    forward = [series[0] * factors[0]]
    for step in range(1, total):
        forward.append((series[step] + SMOOTHING * forward[step - 1]) * factors[step])
    baseline = [None] * total
    baseline[total - 1] = forward[total - 1]
    for step in range(total - 2, -1, -1):
        baseline[step] = forward[step] + (SMOOTHING * factors[step]) * baseline[step + 1]
    result, earlier = [], None
    for step in range(total):
        detrended = series[step] - baseline[step]
        result.append(detrended if earlier is None else detrended - DECAY_RATE * earlier)
        earlier = detrended
    return result


def solve_factors(total):
    factors = []
    for step in range(total):
        middle = 1.0 + SMOOTHING * (1.0 if step in (0, total - 1) else 2.0)
        if step:
            middle -= SMOOTHING * SMOOTHING * factors[-1]
        factors.append(1.0 / middle)
    return factors


def temporal_kernel(in_ref, spikes_ref, traces_ref, sums_ref, *, rows_dev, tiles_dev, share):
    frames = in_ref.shape[0]
    factors = solve_factors(frames)
    for tile in range(tiles_dev):
        series = [in_ref[t, tile * rows_dev : (tile + 1) * rows_dev, :].astype(jnp.float32) for t in range(frames)]
        for t, spikes in enumerate(deconvolved(series, factors)):
            spikes_ref[t, :, tile * TILE : (tile + 1) * TILE] = spikes.astype(spikes_ref.dtype)
    first = rows_dev * tiles_dev
    series = [in_ref[t, first : first + frames, :].astype(jnp.float32) for t in range(frames)]
    for t, sums in enumerate(deconvolved(series, factors)):
        sums_ref[t * frames : (t + 1) * frames, :] = sums
    first += frames
    weights = jnp.concatenate([in_ref[j, first : first + share, :].astype(jnp.float32) for j in range(frames)], axis=1)
    sums = jnp.concatenate([sums_ref[pl.ds(j, frames, stride=frames), :] for j in range(frames)], axis=1)
    trace_sums = lax.dot_general(
        weights, sums, (((1,), (1,)), ((), ())), precision=lax.Precision.HIGHEST, preferred_element_type=jnp.float32
    )
    counts = 0.5 * jnp.sum(weights, axis=1, keepdims=True)
    traces_ref[...] = trace_sums / (TILE * counts)


def swapped(parts, axis):
    count, place = lax.axis_size(axis), lax.axis_index(axis)
    arrived = [lax.dynamic_index_in_dim(parts, place, 0, keepdims=False, allow_negative_indices=False)]
    for step in range(1, count):
        part = lax.dynamic_index_in_dim(parts, place ^ step, 0, keepdims=False, allow_negative_indices=False)
        arrived.append(lax.ppermute(part, axis, [(i, i ^ step) for i in range(count)]))
    return arrived


def by_frame(observed, kernels, band_kernel, masks):
    n_frame, n_row = lax.axis_size("frame"), lax.axis_size("row")
    places = n_frame * n_row
    components, rows_dev, tiles_dev = masks.shape
    height, width = rows_dev * n_row, observed.shape[2]
    share = components // places
    block_rows = rows_dev * tiles_dev + places + share
    place = lax.axis_index("row")
    pieces = swapped(observed.astype(jnp.float16), "row")
    pieces = [piece.astype(jnp.float32) for piece in pieces]
    blocks = pl.pallas_call(
        functools.partial(restore_kernel, devices=(n_frame, n_row), rows_dev=rows_dev, tiles_dev=tiles_dev),
        out_shape=jax.ShapeDtypeStruct((places, block_rows, TILE), jnp.bfloat16),
        in_specs=[pl.BlockSpec(memory_space=pltpu.SMEM)] * 3 + [pl.BlockSpec(memory_space=pltpu.VMEM)] * (n_row + 1),
        out_specs=pl.BlockSpec(memory_space=pltpu.VMEM),
        scratch_shapes=[
            pltpu.VMEM((height, width), jnp.float32),
            pltpu.VMEM((TAPS, height, TILE), jnp.float32),
            pltpu.VMEM((places, TILE), jnp.float32),
        ],
        compiler_params=pltpu.CompilerParams(vmem_limit_bytes=16 << 20),
        name="restore",
    )(place.reshape(1), band_kernel, kernels, *pieces, masks.transpose(1, 2, 0))
    series = lax.all_to_all(blocks, ("frame", "row"), split_axis=0, concat_axis=0, tiled=True)
    spikes, traces = pl.pallas_call(
        functools.partial(temporal_kernel, rows_dev=rows_dev, tiles_dev=tiles_dev, share=share),
        out_shape=(
            jax.ShapeDtypeStruct((places, rows_dev, tiles_dev * TILE), jnp.bfloat16),
            jax.ShapeDtypeStruct((share, places), jnp.float32),
        ),
        in_specs=[pl.BlockSpec(memory_space=pltpu.VMEM)],
        out_specs=(pl.BlockSpec(memory_space=pltpu.VMEM),) * 2,
        scratch_shapes=[pltpu.VMEM((places * places, TILE), jnp.float32)],
        compiler_params=pltpu.CompilerParams(vmem_limit_bytes=16 << 20),
        name="temporal",
    )(series)
    return (spikes, traces)


def fits(mesh, observed, masks):
    frames_dev = observed.shape[0] // mesh.shape["frame"]
    rows_dev = masks.shape[1] // (mesh.shape["groups"] * mesh.shape["row"])
    tiles_dev = masks.shape[2] // mesh.shape["frame"]
    places = mesh.shape["frame"] * mesh.shape["row"]
    return (
        frames_dev == mesh.shape["row"] == 4
        and 2 * rows_dev * tiles_dev == TILE
        and rows_dev == 16
        and places == 16
        and masks.shape[0] // places == 16
    )


def solution(mesh):
    in_specs = (
        P("frame", ("groups", "row"), None),
        P(),
        P("groups"),
        P(None, ("groups", "row"), "frame"),
    )
    out_specs = (P(None, ("groups", "row"), "frame"), P(("groups", "frame", "row"), None))

    def whole(observed, kernels, band_kernel, masks):
        body = by_frame if fits(mesh, observed, masks) else local
        mapped = jax.shard_map(body, mesh=mesh, in_specs=in_specs, out_specs=out_specs, check_vma=False)
        return mapped(observed, kernels, band_kernel, masks)

    return whole
```

```python
import functools

import jax
import jax.numpy as jnp
from jax import lax
from jax.experimental import pallas as pl
from jax.experimental.pallas import tpu as pltpu
from jax.sharding import PartitionSpec as P

TILE = 128
BAND = 8
ITERS = 3
TAPS = 5


SMOOTHING = 1024.0
DECAY_RATE = 0.9


def padded_2(cells, sides, width):
    for axis, dim in sides:
        count = lax.axis_size(axis)
        ends = count - 1
        head = lax.slice_in_dim(cells, 0, width, axis=dim)
        tail = lax.slice_in_dim(cells, cells.shape[dim] - width, cells.shape[dim], axis=dim)
        cells = jnp.concatenate(
            [
                lax.ppermute(tail, axis, [(i, (i + 1) % count) for i in range(ends)]),
                cells,
                lax.ppermute(head, axis, [((i + 1) % count, i) for i in range(ends)]),
            ],
            axis=dim,
        )
    return cells


def tap_rows(tap_table, band_kernel, first_row, row_count, height):
    row_ids = jnp.clip(first_row + jnp.arange(row_count), 0, height - 1)
    row_bands = row_ids // BAND
    band_slots = jnp.arange(band_kernel.shape[0])
    kernel_ids = jnp.sum(
        jnp.where(row_bands[:, None] == band_slots[None, :], band_kernel[None, :], 0), axis=1
    )
    kernel_slots = jnp.arange(tap_table.shape[0])
    picked = jnp.where(
        kernel_ids[:, None, None] == kernel_slots[None, :, None], tap_table[None, :, :], 0.0
    )
    return jnp.sum(picked, axis=1)


def blur_rows(padded, row_taps, row_count):
    summed = row_taps[:, 0][None, :, None] * padded[:, 0:row_count]
    for offset in range(1, 5):
        summed = (
            summed + row_taps[:, offset][None, :, None] * padded[:, offset : offset + row_count]
        )
    return summed


def back_rows(padded_quotient, outer_taps, row_count):
    summed = outer_taps[4 : 4 + row_count, 0][None, :, None] * padded_quotient[:, 4 : 4 + row_count]
    for offset in range(1, 5):
        start = 4 - offset
        summed = (
            summed
            + outer_taps[start : start + row_count, offset][None, :, None]
            * padded_quotient[:, start : start + row_count]
        )
    return summed


def temporal(series_block):
    frame_total, item_count, columns = series_block.shape
    values = series_block.astype(jnp.float32).reshape(frame_total, item_count * columns)
    frame_ids = jnp.arange(frame_total)
    at_ends = (frame_ids == 0) | (frame_ids == frame_total - 1)
    middle = (1.0 + SMOOTHING * jnp.where(at_ends, 1.0, 2.0)).astype(jnp.float32)
    sub_diag = jnp.where(frame_ids == 0, 0.0, -SMOOTHING).astype(jnp.float32)
    super_diag = jnp.where(frame_ids == frame_total - 1, 0.0, -SMOOTHING).astype(jnp.float32)
    baseline = lax.linalg.tridiagonal_solve(sub_diag, middle, super_diag, values)
    detrended = values - baseline
    earlier = jnp.concatenate(
        [jnp.zeros((1, values.shape[1]), jnp.float32), detrended[:-1]], axis=0
    )
    result = (detrended - DECAY_RATE * earlier).astype(jnp.bfloat16)
    return result.reshape(frame_total, item_count, columns)


def local(observed, kernels, band_kernel, masks):
    frames_dev, rows_dev, row_pixels = observed.shape
    height = rows_dev * lax.axis_size("row")
    tap_table = kernels / jnp.sum(kernels, axis=1, keepdims=True)
    first_row = lax.axis_index("row") * rows_dev
    own_taps = tap_rows(tap_table, band_kernel, first_row, rows_dev, height)
    outer_taps = tap_rows(tap_table, band_kernel, first_row - 2, rows_dev + 4, height)
    current = observed
    for iteration in range(ITERS):
        padded = padded_2(current, (("row", 1),), 2)
        blurred = blur_rows(padded, own_taps, rows_dev)
        quotient = observed / blurred
        padded_quotient = padded_2(quotient, (("row", 1),), 2)
        current = current * back_rows(padded_quotient, outer_taps, rows_dev)
    estimate = current.astype(jnp.bfloat16)
    spikes = temporal(lax.all_to_all(estimate, "frame", split_axis=2, concat_axis=0, tiled=True))
    frames_all, _, columns = spikes.shape
    tile_count = columns // TILE
    tile_sums = jnp.sum(
        spikes.reshape(frames_all, rows_dev * tile_count, TILE).astype(jnp.float32), axis=2
    )
    weights = masks.astype(jnp.float32).reshape(masks.shape[0], rows_dev * tile_count)
    local_sums = lax.dot_general(
        weights, tile_sums, (((1,), (1,)), ((), ())), precision=lax.Precision.HIGHEST
    )
    counts = jnp.sum(weights, axis=1)
    trace_sums, totals = (
        lax.psum_scatter(local_sums, ("frame", "row"), scatter_dimension=0, tiled=True),
        lax.psum_scatter(counts, ("frame", "row"), scatter_dimension=0, tiled=True),
    )
    traces = trace_sums / (TILE * totals[:, None])
    return (spikes, traces)


def roll_rows(cells, shift):
    rows = cells.shape[0]
    return cells if shift % rows == 0 else pltpu.roll(cells, shift % rows, 0)


def restore_kernel(
    place_ref, band_ref, kernels_ref, *refs, devices, rows_dev, tiles_dev
):
    n_frame, n_row = devices
    pieces, (masks_ref, out_ref, observed_ref, tap_ref, sums_ref) = refs[:n_row], refs[n_row:]
    for step, piece in enumerate(pieces):
        start = pl.multiple_of((place_ref[1] ^ step) * rows_dev, rows_dev)
        observed_ref[pl.ds(start, rows_dev), :] = piece[...]
    height, _ = observed_ref.shape
    positions = rows_dev * tiles_dev
    row_ids = lax.broadcasted_iota(jnp.int32, (BAND, TILE), 0)
    for band in range(height // BAND):
        kernel = band_ref[band]
        raw = [kernels_ref[kernel, tap] for tap in range(TAPS)]
        total = raw[0]
        for tap in range(1, TAPS):
            total = total + raw[tap]
        for tap in range(TAPS):
            weight = jnp.full((BAND, TILE), raw[tap], jnp.float32) / jnp.full((BAND, TILE), total, jnp.float32)
            target = row_ids + (band * BAND + tap - TAPS // 2)
            weight = jnp.where((target >= 0) & (target < height), weight, 0.0)
            tap_ref[tap, band * BAND : (band + 1) * BAND, :] = weight
    flat = jnp.concatenate([masks_ref[row].astype(jnp.float32) for row in range(rows_dev)], axis=0)
    both = jnp.concatenate([flat, flat], axis=0).T
    share = both.shape[0] // (n_frame * n_row)
    left = lax.broadcasted_iota(jnp.int32, (share, TILE), 1) < positions
    sums_row = n_frame * positions
    masks_row = sums_row + n_frame * n_row
    for row in range(n_row):
        for pair in range(n_frame // 2):
            first = (2 * pair * n_row + row) * share
            second = first + n_row * share
            halves = jnp.where(left, both[first : first + share], both[second : second + share])
            start = masks_row + pair * share
            out_ref[row, start : start + share, :] = halves.astype(jnp.bfloat16)
    lanes = lax.broadcasted_iota(jnp.int32, (rows_dev, TILE), 1)
    own_rows = lax.broadcasted_iota(jnp.int32, (rows_dev, TILE), 0)
    ones = jnp.ones((TILE, TILE), jnp.bfloat16)

    def column_block(block, carry):
        gathered = [jnp.zeros((1, TILE), jnp.float32) for _ in range(n_row)]
        for tile in range(tiles_dev):
            start = pl.multiple_of((block * tiles_dev + tile) * TILE, TILE)
            image = observed_ref[:, pl.ds(start, TILE)].astype(jnp.float32)
            current = image
            for _ in range(ITERS):
                blurred = tap_ref[2] * current
                for tap in (0, 1, 3, 4):
                    blurred = blurred + tap_ref[tap] * roll_rows(current, 2 - tap)
                quotient = image / blurred
                back = tap_ref[2] * quotient
                for tap in (0, 1, 3, 4):
                    back = back + roll_rows(tap_ref[tap] * quotient, tap - 2)
                current = current * back
            estimate = current.astype(jnp.bfloat16)
            for row in range(n_row):
                start = pl.multiple_of(block * positions + tile * rows_dev, rows_dev)
                out_ref[row, pl.ds(start, rows_dev), :] = estimate[row * rows_dev : (row + 1) * rows_dev]
            tile_sums = jnp.dot(estimate, ones, preferred_element_type=jnp.float32)
            here = lanes % positions == own_rows * tiles_dev + tile
            for row in range(n_row):
                part = jnp.where(here, tile_sums[row * rows_dev : (row + 1) * rows_dev], 0.0)
                gathered[row] = gathered[row] + jnp.sum(part, axis=0, keepdims=True)
        for row in range(n_row):
            sums_ref[pl.ds(block * n_row + row, 1), :] = gathered[row]
        return carry

    lax.fori_loop(0, n_frame, column_block, 0)
    sums = sums_ref[...]
    high = sums.astype(jnp.bfloat16).astype(jnp.float32)
    split = jnp.where(lax.broadcasted_iota(jnp.int32, sums.shape, 1) < positions, high, sums - high)
    split = split.astype(jnp.bfloat16)
    for row in range(n_row):
        out_ref[row, sums_row:masks_row, :] = split


def regroup_kernel(*refs, positions, places, share):
    pieces, out_ref = refs[:-1], refs[-1]
    n_frame = out_ref.shape[0]
    sums_row = n_frame * positions
    masks_row = sums_row + places
    for block in range(n_frame):
        for step, piece in enumerate(pieces):
            out_ref[block, step, :positions, :] = piece[block * positions : (block + 1) * positions, :]
            out_ref[block, step, positions : positions + places, :] = piece[sums_row:masks_row, :]
            start = masks_row + block // 2 * share
            out_ref[block, step, positions + places :, :] = piece[start : start + share, :]


def deconvolved(series, factors):
    total = len(series)
    forward = [series[0] * factors[0]]
    for step in range(1, total):
        forward.append((series[step] + SMOOTHING * forward[step - 1]) * factors[step])
    baseline = [None] * total
    baseline[total - 1] = forward[total - 1]
    for step in range(total - 2, -1, -1):
        baseline[step] = forward[step] + (SMOOTHING * factors[step]) * baseline[step + 1]
    result, earlier = [], None
    for step in range(total):
        detrended = series[step] - baseline[step]
        result.append(detrended if earlier is None else detrended - DECAY_RATE * earlier)
        earlier = detrended
    return result


def solve_factors(total):
    factors = []
    for step in range(total):
        middle = 1.0 + SMOOTHING * (1.0 if step in (0, total - 1) else 2.0)
        if step:
            middle -= SMOOTHING * SMOOTHING * factors[-1]
        factors.append(1.0 / middle)
    return factors


def temporal_kernel(place_ref, *refs, devices, rows_dev, tiles_dev, share):
    n_frame, n_row = devices
    pieces, (spikes_ref, traces_ref, in_ref, sums_ref) = refs[:n_frame], refs[n_frame:]
    for step, piece in enumerate(pieces):
        for inner in range(n_row):
            in_ref[(place_ref[0] ^ step) * n_row + (place_ref[1] ^ inner)] = piece[inner]
    frames = in_ref.shape[0]
    factors = solve_factors(frames)
    for tile in range(tiles_dev):
        series = [in_ref[t, tile * rows_dev : (tile + 1) * rows_dev, :].astype(jnp.float32) for t in range(frames)]
        for t, spikes in enumerate(deconvolved(series, factors)):
            spikes_ref[t, :, tile * TILE : (tile + 1) * TILE] = spikes.astype(spikes_ref.dtype)
    first = rows_dev * tiles_dev
    series = [in_ref[t, first : first + frames, :].astype(jnp.float32) for t in range(frames)]
    for t, sums in enumerate(deconvolved(series, factors)):
        sums_ref[t * frames : (t + 1) * frames, :] = sums + pltpu.roll(sums, TILE // 2, 1)
    first += frames
    weights = jnp.concatenate([in_ref[j, first : first + share, :].astype(jnp.float32) for j in range(frames)], axis=1)
    halves = lax.broadcasted_iota(jnp.int32, weights.shape, 1) // (TILE // 2)
    weights = jnp.where(halves % 2 == place_ref[0] % 2, weights, 0.0)
    sums = jnp.concatenate([sums_ref[pl.ds(j, frames, stride=frames), :] for j in range(frames)], axis=1)
    trace_sums = lax.dot_general(
        weights, sums, (((1,), (1,)), ((), ())), precision=lax.Precision.HIGHEST, preferred_element_type=jnp.float32
    )
    counts = jnp.sum(weights, axis=1, keepdims=True)
    traces_ref[...] = trace_sums / (TILE * counts)


def swapped(parts, axis):
    count, place = lax.axis_size(axis), lax.axis_index(axis)
    arrived = [lax.dynamic_index_in_dim(parts, place, 0, keepdims=False, allow_negative_indices=False)]
    for step in range(1, count):
        part = lax.dynamic_index_in_dim(parts, place ^ step, 0, keepdims=False, allow_negative_indices=False)
        arrived.append(lax.ppermute(part, axis, [(i, i ^ step) for i in range(count)]))
    return arrived


def by_frame(observed, kernels, band_kernel, masks):
    devices = n_frame, n_row = lax.axis_size("frame"), lax.axis_size("row")
    places = n_frame * n_row
    components, rows_dev, tiles_dev = masks.shape
    height, width = rows_dev * n_row, observed.shape[2]
    share = components // places
    positions = rows_dev * tiles_dev
    place = jnp.stack([lax.axis_index("frame"), lax.axis_index("row")])
    smem, vmem = pl.BlockSpec(memory_space=pltpu.SMEM), pl.BlockSpec(memory_space=pltpu.VMEM)
    params = pltpu.CompilerParams(vmem_limit_bytes=16 << 20)
    pieces = [piece.astype(jnp.float32) for piece in swapped(observed.astype(jnp.float16), "row")]
    block_rows = n_frame * positions + places + n_frame // 2 * share
    blocks = pl.pallas_call(
        functools.partial(restore_kernel, devices=devices, rows_dev=rows_dev, tiles_dev=tiles_dev),
        out_shape=jax.ShapeDtypeStruct((n_row, block_rows, TILE), jnp.bfloat16),
        in_specs=[smem] * 3 + [vmem] * (n_row + 1),
        out_specs=vmem,
        scratch_shapes=[
            pltpu.VMEM((height, width), jnp.float32),
            pltpu.VMEM((TAPS, height, TILE), jnp.float32),
            pltpu.VMEM((places, TILE), jnp.float32),
        ],
        compiler_params=params,
        name="restore",
    )(place, band_kernel, kernels, *pieces, masks.transpose(1, 2, 0))
    blocks = pl.pallas_call(
        functools.partial(regroup_kernel, positions=positions, places=places, share=share),
        out_shape=jax.ShapeDtypeStruct((n_frame, n_row, positions + places + share, TILE), jnp.bfloat16),
        in_specs=[vmem] * n_row,
        out_specs=vmem,
        compiler_params=params,
        name="regroup",
    )(*swapped(blocks, "row"))
    spikes, traces = pl.pallas_call(
        functools.partial(temporal_kernel, devices=devices, rows_dev=rows_dev, tiles_dev=tiles_dev, share=share),
        out_shape=(
            jax.ShapeDtypeStruct((places, rows_dev, tiles_dev * TILE), jnp.bfloat16),
            jax.ShapeDtypeStruct((share, places), jnp.float32),
        ),
        in_specs=[smem] + [vmem] * n_frame,
        out_specs=(vmem, vmem),
        scratch_shapes=[
            pltpu.VMEM((places, positions + places + share, TILE), jnp.bfloat16),
            pltpu.VMEM((places * places, TILE), jnp.float32),
        ],
        compiler_params=params,
        name="temporal",
    )(place, *swapped(blocks, "frame"))
    return (spikes, traces)


def fits(mesh, observed, masks):
    frames_dev = observed.shape[0] // mesh.shape["frame"]
    rows_dev = masks.shape[1] // (mesh.shape["groups"] * mesh.shape["row"])
    tiles_dev = masks.shape[2] // mesh.shape["frame"]
    places = mesh.shape["frame"] * mesh.shape["row"]
    return (
        frames_dev == mesh.shape["row"] == 4
        and mesh.shape["frame"] == 4
        and 2 * rows_dev * tiles_dev == TILE
        and rows_dev == 16
        and places == 16
        and masks.shape[0] // places == 16
    )


def solution(mesh):
    in_specs = (
        P("frame", ("groups", "row"), None),
        P(),
        P("groups"),
        P(None, ("groups", "row"), "frame"),
    )
    out_specs = (P(None, ("groups", "row"), "frame"), P(("groups", "frame", "row"), None))

    def whole(observed, kernels, band_kernel, masks):
        body = by_frame if fits(mesh, observed, masks) else local
        mapped = jax.shard_map(body, mesh=mesh, in_specs=in_specs, out_specs=out_specs, check_vma=False)
        return mapped(observed, kernels, band_kernel, masks)

    return whole
```

```python
import functools

import jax
import jax.numpy as jnp
from jax import lax
from jax.experimental import pallas as pl
from jax.experimental.pallas import tpu as pltpu
from jax.sharding import PartitionSpec as P

TILE = 128
BAND = 8
ITERS = 3
TAPS = 5
NEAR, FAR = 8, 4
MARGIN = 2 * BAND
STEPS = (((0, 48), (8, 40)), ((8, 40), (8, 40)), ((8, 40), (16, 32)))


SMOOTHING = 1024.0
DECAY_RATE = 0.9


def padded_2(cells, sides, width):
    for axis, dim in sides:
        count = lax.axis_size(axis)
        ends = count - 1
        head = lax.slice_in_dim(cells, 0, width, axis=dim)
        tail = lax.slice_in_dim(cells, cells.shape[dim] - width, cells.shape[dim], axis=dim)
        cells = jnp.concatenate(
            [
                lax.ppermute(tail, axis, [(i, (i + 1) % count) for i in range(ends)]),
                cells,
                lax.ppermute(head, axis, [((i + 1) % count, i) for i in range(ends)]),
            ],
            axis=dim,
        )
    return cells


def tap_rows(tap_table, band_kernel, first_row, row_count, height):
    row_ids = jnp.clip(first_row + jnp.arange(row_count), 0, height - 1)
    row_bands = row_ids // BAND
    band_slots = jnp.arange(band_kernel.shape[0])
    kernel_ids = jnp.sum(
        jnp.where(row_bands[:, None] == band_slots[None, :], band_kernel[None, :], 0), axis=1
    )
    kernel_slots = jnp.arange(tap_table.shape[0])
    picked = jnp.where(
        kernel_ids[:, None, None] == kernel_slots[None, :, None], tap_table[None, :, :], 0.0
    )
    return jnp.sum(picked, axis=1)


def blur_rows(padded, row_taps, row_count):
    summed = row_taps[:, 0][None, :, None] * padded[:, 0:row_count]
    for offset in range(1, 5):
        summed = (
            summed + row_taps[:, offset][None, :, None] * padded[:, offset : offset + row_count]
        )
    return summed


def back_rows(padded_quotient, outer_taps, row_count):
    summed = outer_taps[4 : 4 + row_count, 0][None, :, None] * padded_quotient[:, 4 : 4 + row_count]
    for offset in range(1, 5):
        start = 4 - offset
        summed = (
            summed
            + outer_taps[start : start + row_count, offset][None, :, None]
            * padded_quotient[:, start : start + row_count]
        )
    return summed


def temporal(series_block):
    frame_total, item_count, columns = series_block.shape
    values = series_block.astype(jnp.float32).reshape(frame_total, item_count * columns)
    frame_ids = jnp.arange(frame_total)
    at_ends = (frame_ids == 0) | (frame_ids == frame_total - 1)
    middle = (1.0 + SMOOTHING * jnp.where(at_ends, 1.0, 2.0)).astype(jnp.float32)
    sub_diag = jnp.where(frame_ids == 0, 0.0, -SMOOTHING).astype(jnp.float32)
    super_diag = jnp.where(frame_ids == frame_total - 1, 0.0, -SMOOTHING).astype(jnp.float32)
    baseline = lax.linalg.tridiagonal_solve(sub_diag, middle, super_diag, values)
    detrended = values - baseline
    earlier = jnp.concatenate(
        [jnp.zeros((1, values.shape[1]), jnp.float32), detrended[:-1]], axis=0
    )
    result = (detrended - DECAY_RATE * earlier).astype(jnp.bfloat16)
    return result.reshape(frame_total, item_count, columns)


def local(observed, kernels, band_kernel, masks):
    frames_dev, rows_dev, row_pixels = observed.shape
    height = rows_dev * lax.axis_size("row")
    tap_table = kernels / jnp.sum(kernels, axis=1, keepdims=True)
    first_row = lax.axis_index("row") * rows_dev
    own_taps = tap_rows(tap_table, band_kernel, first_row, rows_dev, height)
    outer_taps = tap_rows(tap_table, band_kernel, first_row - 2, rows_dev + 4, height)
    current = observed
    for iteration in range(ITERS):
        padded = padded_2(current, (("row", 1),), 2)
        blurred = blur_rows(padded, own_taps, rows_dev)
        quotient = observed / blurred
        padded_quotient = padded_2(quotient, (("row", 1),), 2)
        current = current * back_rows(padded_quotient, outer_taps, rows_dev)
    estimate = current.astype(jnp.bfloat16)
    spikes = temporal(lax.all_to_all(estimate, "frame", split_axis=2, concat_axis=0, tiled=True))
    frames_all, _, columns = spikes.shape
    tile_count = columns // TILE
    tile_sums = jnp.sum(
        spikes.reshape(frames_all, rows_dev * tile_count, TILE).astype(jnp.float32), axis=2
    )
    weights = masks.astype(jnp.float32).reshape(masks.shape[0], rows_dev * tile_count)
    local_sums = lax.dot_general(
        weights, tile_sums, (((1,), (1,)), ((), ())), precision=lax.Precision.HIGHEST
    )
    counts = jnp.sum(weights, axis=1)
    trace_sums, totals = (
        lax.psum_scatter(local_sums, ("frame", "row"), scatter_dimension=0, tiled=True),
        lax.psum_scatter(counts, ("frame", "row"), scatter_dimension=0, tiled=True),
    )
    traces = trace_sums / (TILE * totals[:, None])
    return (spikes, traces)


def to_half(cells):
    return cells.astype(jnp.float16)


def halo_kernel(observed_ref, first_ref, second_ref, own_ref):
    even = lax.axis_index("row") % 2 == 0
    frames = observed_ref.shape[0]
    own_ref[...] = observed_ref[...]
    for frame in range(frames):
        image = observed_ref[frame]
        near, far = slice(frame * NEAR, (frame + 1) * NEAR), slice(frames * NEAR + frame * FAR, frames * NEAR + (frame + 1) * FAR)
        low, high = image[-NEAR:], image[:NEAR]
        first_ref[near, :] = jnp.where(even, low, high)
        second_ref[near, :] = jnp.where(even, high, low)
        low, high = image[-NEAR - FAR : -NEAR], image[NEAR : NEAR + FAR]
        first_ref[far, :] = jnp.where(even, low, high)
        second_ref[far, :] = jnp.where(even, high, low)


def tables_kernel(band_ref, kernels_ref, masks_ref, taps_ref, back_ref, guard_ref, feet_ref, pad_ref, *, height):
    rows_dev = masks_ref.shape[0]
    span = rows_dev + 2 * MARGIN
    first_row = lax.axis_index("row") * rows_dev - MARGIN
    row_ids = lax.broadcasted_iota(jnp.int32, (BAND, TILE), 0)
    pad_ref[...] = jnp.zeros_like(pad_ref)
    for band in range(span // BAND):
        row = first_row + band * BAND
        inside = (row >= 0) & (row < height)
        kernel = band_ref[jnp.clip(row, 0, height - 1) // BAND]
        raw = [kernels_ref[kernel, tap] for tap in range(TAPS)]
        total = raw[0]
        for tap in range(1, TAPS):
            total = total + raw[tap]
        total = jnp.full((BAND, TILE), total, jnp.float32)
        start = band * BAND
        guard_ref[start : start + BAND, :] = jnp.where(inside, 0.0, jnp.ones((BAND, TILE), jnp.float32))
        for tap in range(TAPS):
            weight = jnp.full((BAND, TILE), raw[tap], jnp.float32) / total
            target = row_ids + (row + tap - TAPS // 2)
            weight = jnp.where(inside & (target >= 0) & (target < height), weight, 0.0)
            taps_ref[tap, start : start + BAND, :] = weight
            pad_ref[tap, BAND + start : 2 * BAND + start, :] = weight
    for tap in range(TAPS):
        start = BAND + TAPS // 2 - tap
        back_ref[tap] = pad_ref[tap, start : start + span, :]
    flat = jnp.concatenate([masks_ref[row].astype(jnp.float32) for row in range(rows_dev)], axis=0)
    positions = flat.shape[0]
    both = jnp.concatenate([flat, flat], axis=0).T
    half = feet_ref.shape[1]
    left = lax.broadcasted_iota(jnp.int32, (half, TILE), 1) < positions
    for block in range(feet_ref.shape[0]):
        start = 2 * block * half
        halves = jnp.where(left, both[start : start + half], both[start + half : start + 2 * half])
        feet_ref[block] = halves.astype(jnp.bfloat16)


def restore_kernel(taps_ref, back_ref, guard_ref, feet_ref, own_ref, first_ref, second_ref, out_ref):
    n_frame = out_ref.shape[0]
    frames, rows_dev, width = own_ref.shape
    tiles_dev = width // (n_frame * TILE)
    positions = rows_dev * tiles_dev
    span = rows_dev + 2 * MARGIN
    even = lax.axis_index("row") % 2 == 0

    def between(cells, middle, start, stop):
        pieces = [cells[:start]] if start else []
        pieces.append(middle)
        return jnp.concatenate(pieces + ([cells[stop:]] if stop < span else []), axis=0)

    def blur(cells, start, stop):
        total = guard_ref[start:stop, :] + taps_ref[2, start:stop, :] * cells[start:stop]
        for tap in (0, 1, 3, 4):
            total = total + taps_ref[tap, start:stop, :] * pltpu.roll(cells, (2 - tap) % span, 0)[start:stop]
        return total

    def spread(cells, start, stop):
        total = back_ref[2, start:stop, :] * cells[start:stop]
        for tap in (0, 1, 3, 4):
            total = total + back_ref[tap, start:stop, :] * pltpu.roll(cells, (tap - 2) % span, 0)[start:stop]
        return total

    def column_block(block, carry):
        for tile in range(tiles_dev):
            columns = pl.ds(pl.multiple_of((block * tiles_dev + tile) * TILE, TILE), TILE)
            for frame in range(frames):
                near, far = frame * NEAR, frames * NEAR + frame * FAR
                nears = first_ref[near : near + NEAR, columns], second_ref[near : near + NEAR, columns]
                fars = first_ref[far : far + FAR, columns], second_ref[far : far + FAR, columns]
                blank = jnp.zeros((MARGIN - NEAR - FAR, TILE), jnp.float32)
                image = jnp.concatenate(
                    [
                        blank,
                        jnp.where(even, fars[1], fars[0]),
                        jnp.where(even, nears[1], nears[0]),
                        own_ref[frame, :, columns],
                        jnp.where(even, nears[0], nears[1]),
                        jnp.where(even, fars[0], fars[1]),
                        blank,
                    ],
                    axis=0,
                )
                current = image
                for (low, high), (back_low, back_high) in STEPS:
                    quotient = image[low:high] / blur(current, low, high)
                    quotient = between(image, quotient, low, high)
                    updated = current[back_low:back_high] * spread(quotient, back_low, back_high)
                    current = between(image, updated, back_low, back_high)
                estimate = current[MARGIN : MARGIN + rows_dev].astype(jnp.bfloat16)
                start = frame * positions + tile * rows_dev
                out_ref[block, start : start + rows_dev, :] = estimate
        return carry

    lax.fori_loop(0, n_frame, column_block, 0)
    ones_row = lax.broadcasted_iota(jnp.int32, (TILE, TILE), 1) % tiles_dev
    gathered = jnp.zeros((frames * n_frame * rows_dev, TILE), jnp.float32)
    for tile in range(tiles_dev):
        pieces = []
        for frame in range(frames):
            start = frame * positions + tile * rows_dev
            pieces += [out_ref[block, start : start + rows_dev, :] for block in range(n_frame)]
        picked = jnp.where(ones_row == tile, 1.0, 0.0).astype(jnp.bfloat16)
        gathered = gathered + jnp.dot(jnp.concatenate(pieces, axis=0), picked, preferred_element_type=jnp.float32)
    lanes = lax.broadcasted_iota(jnp.int32, (rows_dev, TILE), 1)
    here = lanes % positions // tiles_dev == lax.broadcasted_iota(jnp.int32, (rows_dev, TILE), 0)
    sums = []
    for place in range(frames * n_frame):
        part = jnp.where(here, gathered[place * rows_dev : (place + 1) * rows_dev], 0.0)
        sums.append(jnp.sum(part, axis=0, keepdims=True))
    sums = jnp.concatenate(sums, axis=0)
    high = sums.astype(jnp.bfloat16).astype(jnp.float32)
    split = jnp.where(lax.broadcasted_iota(jnp.int32, sums.shape, 1) < positions, high, sums - high).astype(jnp.bfloat16)
    start = frames * positions
    for block in range(n_frame):
        out_ref[block, start : start + frames * n_frame, :] = split
        out_ref[block, start + frames * n_frame :, :] = feet_ref[block]


def deconvolved(series):
    total = len(series)
    factors = []
    for step in range(total):
        middle = 1.0 + SMOOTHING * (1.0 if step in (0, total - 1) else 2.0)
        if step:
            middle -= SMOOTHING * SMOOTHING * factors[-1]
        factors.append(1.0 / middle)
    forward = [series[0] * factors[0]]
    for step in range(1, total):
        forward.append((series[step] + SMOOTHING * forward[step - 1]) * factors[step])
    baseline = [None] * total
    baseline[total - 1] = forward[total - 1]
    for step in range(total - 2, -1, -1):
        baseline[step] = forward[step] + (SMOOTHING * factors[step]) * baseline[step + 1]
    result, earlier = [], None
    for step in range(total):
        detrended = series[step] - baseline[step]
        result.append(detrended if earlier is None else detrended - DECAY_RATE * earlier)
        earlier = detrended
    return result


def partial_kernel(*refs, frames, positions):
    pieces, (out_ref, sums_ref, feet_ref) = refs[:-3], refs[-3:]
    n_frame = len(pieces)
    place = lax.axis_index("frame")
    start = frames * positions
    rows = frames * n_frame
    half = feet_ref.shape[1]
    for step, piece in enumerate(pieces):
        sums_ref[pl.ds(pl.multiple_of((place ^ step) * rows, rows), rows), :] = piece[start : start + rows, :].astype(jnp.float32)
        feet_ref[place ^ step] = piece[start + rows :, :].astype(jnp.float32)
    series = [sums_ref[t * n_frame : (t + 1) * n_frame, :] for t in range(rows)]
    for t, sums in enumerate(deconvolved(series)):
        sums_ref[t * n_frame : (t + 1) * n_frame, :] = sums + pltpu.roll(sums, TILE // 2, 1)
    left = lax.broadcasted_iota(jnp.int32, (half, TILE), 1) < positions
    weights, sums = [], []
    extra = jnp.where(lax.broadcasted_iota(jnp.int32, (8, TILE), 0) == 0, 1.0, 0.0)
    for block in range(n_frame):
        feet = feet_ref[block]
        weights.append(jnp.concatenate([jnp.where(left, feet, 0.0), jnp.where(left, 0.0, feet)], axis=0))
        sums.append(jnp.concatenate([sums_ref[pl.ds(block, rows, stride=n_frame), :], extra], axis=0))
    totals = lax.dot_general(
        jnp.concatenate(weights, axis=1),
        jnp.concatenate(sums, axis=1),
        (((1,), (1,)), ((), ())),
        precision=lax.Precision.HIGHEST,
        preferred_element_type=jnp.float32,
    )
    share = out_ref.shape[1]
    out_ref[...] = jnp.zeros_like(out_ref)
    for row in range(out_ref.shape[0]):
        out_ref[row, :, : rows + 8] = totals[row * share : (row + 1) * share]


def temporal_kernel(*refs, frames):
    pieces, (spikes_ref, in_ref) = refs[:-2], refs[-2:]
    place = lax.axis_index("frame")
    for step, piece in enumerate(pieces):
        in_ref[place ^ step] = piece[: in_ref.shape[1], :]
    total, rows_dev, columns = spikes_ref.shape
    positions = in_ref.shape[1] // frames
    for tile in range(columns // TILE):
        series = []
        for t in range(total):
            start = t % frames * positions + tile * rows_dev
            series.append(in_ref[t // frames, start : start + rows_dev, :].astype(jnp.float32))
        for t, spikes in enumerate(deconvolved(series)):
            spikes_ref[t, :, tile * TILE : (tile + 1) * TILE] = spikes.astype(spikes_ref.dtype)


def means_kernel(*refs):
    pieces, traces_ref = refs[:-1], refs[-1]
    frames = traces_ref.shape[1]
    total = pieces[0][...]
    for piece in pieces[1:]:
        total = total + piece[...]
    traces_ref[...] = total[:, :frames] / (TILE * total[:, frames : frames + 1])


def swapped(parts, axis):
    count, place = lax.axis_size(axis), lax.axis_index(axis)
    arrived = [lax.dynamic_index_in_dim(parts, place, 0, keepdims=False, allow_negative_indices=False)]
    for step in range(1, count):
        part = lax.dynamic_index_in_dim(parts, place ^ step, 0, keepdims=False, allow_negative_indices=False)
        arrived.append(lax.ppermute(part, axis, [(i, i ^ step) for i in range(count)]))
    return arrived


def by_halo(observed, kernels, band_kernel, masks):
    n_frame, n_row = lax.axis_size("frame"), lax.axis_size("row")
    frames, rows_dev, width = observed.shape
    components, _, tiles_dev = masks.shape
    positions = rows_dev * tiles_dev
    share = components // (n_frame * n_row)
    span = rows_dev + 2 * MARGIN
    smem, vmem = pl.BlockSpec(memory_space=pltpu.SMEM), pl.BlockSpec(memory_space=pltpu.VMEM)

    def call(kernel, name, in_specs, out_shape, scratch=(), cost=1000000):
        many = isinstance(out_shape, tuple)
        return pl.pallas_call(
            kernel,
            name=name,
            out_shape=out_shape,
            in_specs=in_specs,
            out_specs=(vmem,) * len(out_shape) if many else vmem,
            scratch_shapes=scratch,
            compiler_params=pltpu.CompilerParams(vmem_limit_bytes=16 << 20),
            cost_estimate=pl.CostEstimate(flops=cost, bytes_accessed=cost, transcendentals=0),
        )

    def array(*shape, dtype=jnp.float32):
        return jax.ShapeDtypeStruct(shape, dtype)

    packed = array(frames * (NEAR + FAR), width)
    first, second, own = call(halo_kernel, "halo", [vmem], (packed, packed, array(*observed.shape)))(observed)
    pairs = [(i, i + 1) for i in range(0, n_row - 1, 2)], [(i, i + 1) for i in range(1, n_row - 1, 2)]
    first, second = (
        lax.ppermute(to_half(sent), "row", pair + [(j, i) for i, j in pair]).astype(jnp.float32)
        for sent, pair in zip((first, second), pairs)
    )
    taps, back, guard, feet = call(
        functools.partial(tables_kernel, height=rows_dev * n_row),
        "tables",
        [smem, smem, vmem],
        (
            array(TAPS, span, TILE),
            array(TAPS, span, TILE),
            array(span, TILE),
            array(n_frame, n_row * share // 2, TILE, dtype=jnp.bfloat16),
        ),
        [pltpu.VMEM((TAPS, span + 2 * BAND, TILE), jnp.float32)],
    )(band_kernel, kernels, masks.transpose(1, 2, 0))
    block_rows = frames * positions + frames * n_frame + n_row * share // 2
    blocks = call(restore_kernel, "restore", [vmem] * 7, array(n_frame, block_rows, TILE, dtype=jnp.bfloat16))(
        taps, back, guard, feet, own, first, second
    )
    pieces = swapped(blocks, "frame")
    partial = call(
        functools.partial(partial_kernel, frames=frames, positions=positions),
        "partial",
        [vmem] * n_frame,
        array(n_row, share, TILE),
        [
            pltpu.VMEM((n_frame * frames * n_frame, TILE), jnp.float32),
            pltpu.VMEM((n_frame, n_row * share // 2, TILE), jnp.float32),
        ],
    )(*pieces)
    shares = swapped(partial, "row")
    spikes = call(
        functools.partial(temporal_kernel, frames=frames),
        "temporal",
        [vmem] * n_frame,
        array(n_frame * frames, rows_dev, tiles_dev * TILE, dtype=jnp.bfloat16),
        [pltpu.VMEM((n_frame, frames * positions, TILE), jnp.bfloat16)],
    )(*pieces)
    traces = call(means_kernel, "means", [vmem] * n_row, array(share, n_frame * frames))(*shares)
    return (spikes, traces)


def fits(mesh, observed, masks):
    frames_dev = observed.shape[0] // mesh.shape["frame"]
    rows_dev = masks.shape[1] // (mesh.shape["groups"] * mesh.shape["row"])
    tiles_dev = masks.shape[2] // mesh.shape["frame"]
    places = mesh.shape["frame"] * mesh.shape["row"]
    return (
        frames_dev == mesh.shape["frame"] == mesh.shape["row"] == 4
        and 2 * rows_dev * tiles_dev == TILE
        and rows_dev == 16
        and masks.shape[0] // places == 16
    )


def solution(mesh):
    in_specs = (
        P("frame", ("groups", "row"), None),
        P(),
        P("groups"),
        P(None, ("groups", "row"), "frame"),
    )
    out_specs = (P(None, ("groups", "row"), "frame"), P(("groups", "frame", "row"), None))

    def whole(observed, kernels, band_kernel, masks):
        body = by_halo if fits(mesh, observed, masks) else local
        mapped = jax.shard_map(body, mesh=mesh, in_specs=in_specs, out_specs=out_specs, check_vma=False)
        return mapped(observed, kernels, band_kernel, masks)

    return whole
```

```python
import functools

import jax
import jax.numpy as jnp
from jax import lax
from jax.experimental import pallas as pl
from jax.experimental.pallas import tpu as pltpu
from jax.sharding import PartitionSpec as P

TILE = 128
BAND = 8
ITERS = 3
TAPS = 5
NEAR, FAR = 8, 4
MARGIN = 2 * BAND
PAD = BAND
STEPS = (((6, 46), (8, 40)), ((10, 42), (12, 36)), ((14, 38), (16, 32)))
SIDES = (0, 1, 3, 4)
HALVES = 2
TOGETHER = 2


SMOOTHING = 1024.0
DECAY_RATE = 0.9


def padded_2(cells, sides, width):
    for axis, dim in sides:
        count = lax.axis_size(axis)
        ends = count - 1
        head = lax.slice_in_dim(cells, 0, width, axis=dim)
        tail = lax.slice_in_dim(cells, cells.shape[dim] - width, cells.shape[dim], axis=dim)
        cells = jnp.concatenate(
            [
                lax.ppermute(tail, axis, [(i, (i + 1) % count) for i in range(ends)]),
                cells,
                lax.ppermute(head, axis, [((i + 1) % count, i) for i in range(ends)]),
            ],
            axis=dim,
        )
    return cells


def tap_rows(tap_table, band_kernel, first_row, row_count, height):
    row_ids = jnp.clip(first_row + jnp.arange(row_count), 0, height - 1)
    row_bands = row_ids // BAND
    band_slots = jnp.arange(band_kernel.shape[0])
    kernel_ids = jnp.sum(
        jnp.where(row_bands[:, None] == band_slots[None, :], band_kernel[None, :], 0), axis=1
    )
    kernel_slots = jnp.arange(tap_table.shape[0])
    picked = jnp.where(
        kernel_ids[:, None, None] == kernel_slots[None, :, None], tap_table[None, :, :], 0.0
    )
    return jnp.sum(picked, axis=1)


def blur_rows(padded, row_taps, row_count):
    summed = row_taps[:, 0][None, :, None] * padded[:, 0:row_count]
    for offset in range(1, 5):
        summed = (
            summed + row_taps[:, offset][None, :, None] * padded[:, offset : offset + row_count]
        )
    return summed


def back_rows(padded_quotient, outer_taps, row_count):
    summed = outer_taps[4 : 4 + row_count, 0][None, :, None] * padded_quotient[:, 4 : 4 + row_count]
    for offset in range(1, 5):
        start = 4 - offset
        summed = (
            summed
            + outer_taps[start : start + row_count, offset][None, :, None]
            * padded_quotient[:, start : start + row_count]
        )
    return summed


def temporal(series_block):
    frame_total, item_count, columns = series_block.shape
    values = series_block.astype(jnp.float32).reshape(frame_total, item_count * columns)
    frame_ids = jnp.arange(frame_total)
    at_ends = (frame_ids == 0) | (frame_ids == frame_total - 1)
    middle = (1.0 + SMOOTHING * jnp.where(at_ends, 1.0, 2.0)).astype(jnp.float32)
    sub_diag = jnp.where(frame_ids == 0, 0.0, -SMOOTHING).astype(jnp.float32)
    super_diag = jnp.where(frame_ids == frame_total - 1, 0.0, -SMOOTHING).astype(jnp.float32)
    baseline = lax.linalg.tridiagonal_solve(sub_diag, middle, super_diag, values)
    detrended = values - baseline
    earlier = jnp.concatenate(
        [jnp.zeros((1, values.shape[1]), jnp.float32), detrended[:-1]], axis=0
    )
    result = (detrended - DECAY_RATE * earlier).astype(jnp.bfloat16)
    return result.reshape(frame_total, item_count, columns)


def local(observed, kernels, band_kernel, masks):
    frames_dev, rows_dev, row_pixels = observed.shape
    height = rows_dev * lax.axis_size("row")
    tap_table = kernels / jnp.sum(kernels, axis=1, keepdims=True)
    first_row = lax.axis_index("row") * rows_dev
    own_taps = tap_rows(tap_table, band_kernel, first_row, rows_dev, height)
    outer_taps = tap_rows(tap_table, band_kernel, first_row - 2, rows_dev + 4, height)
    current = observed
    for iteration in range(ITERS):
        padded = padded_2(current, (("row", 1),), 2)
        blurred = blur_rows(padded, own_taps, rows_dev)
        quotient = observed / blurred
        padded_quotient = padded_2(quotient, (("row", 1),), 2)
        current = current * back_rows(padded_quotient, outer_taps, rows_dev)
    estimate = current.astype(jnp.bfloat16)
    spikes = temporal(lax.all_to_all(estimate, "frame", split_axis=2, concat_axis=0, tiled=True))
    frames_all, _, columns = spikes.shape
    tile_count = columns // TILE
    tile_sums = jnp.sum(
        spikes.reshape(frames_all, rows_dev * tile_count, TILE).astype(jnp.float32), axis=2
    )
    weights = masks.astype(jnp.float32).reshape(masks.shape[0], rows_dev * tile_count)
    local_sums = lax.dot_general(
        weights, tile_sums, (((1,), (1,)), ((), ())), precision=lax.Precision.HIGHEST
    )
    counts = jnp.sum(weights, axis=1)
    trace_sums, totals = (
        lax.psum_scatter(local_sums, ("frame", "row"), scatter_dimension=0, tiled=True),
        lax.psum_scatter(counts, ("frame", "row"), scatter_dimension=0, tiled=True),
    )
    traces = trace_sums / (TILE * totals[:, None])
    return (spikes, traces)


def halo_kernel(observed_ref, *refs):
    sent, (own_ref, arrived) = refs[:-2], refs[-2:]
    even = lax.axis_index("row") % 2 == 0
    copies = [
        pltpu.make_async_copy(observed_ref.at[frame], own_ref.at[frame], arrived.at[frame])
        for frame in range(own_ref.shape[0])
    ]
    for copy in copies:
        copy.start()
    frames = len(copies) // HALVES
    for frame, copy in enumerate(copies):
        first_ref, second_ref = sent[2 * (frame // frames) : 2 * (frame // frames) + 2]
        copy.wait()
        near = frame % frames * NEAR
        far = frames * NEAR + frame % frames * FAR
        low, high = own_ref[frame, -NEAR:, :], own_ref[frame, :NEAR, :]
        first_ref[near : near + NEAR, :] = jnp.where(even, low, high)
        second_ref[near : near + NEAR, :] = jnp.where(even, high, low)
        low, high = own_ref[frame, -NEAR - FAR : -NEAR, :], own_ref[frame, NEAR : NEAR + FAR, :]
        first_ref[far : far + FAR, :] = jnp.where(even, low, high)
        second_ref[far : far + FAR, :] = jnp.where(even, high, low)


def tables_kernel(band_ref, kernels_ref, masks_ref, taps_ref, back_ref, feet_ref, pad_ref, *, height):
    rows_dev = masks_ref.shape[0]
    span = rows_dev + 2 * MARGIN
    first_row = lax.axis_index("row") * rows_dev - MARGIN
    row_ids = lax.broadcasted_iota(jnp.int32, (BAND, TILE), 0)
    pad_ref[...] = jnp.zeros_like(pad_ref)
    for band in range(span // BAND):
        row = first_row + band * BAND
        inside = (row >= 0) & (row < height)
        kernel = band_ref[jnp.clip(row, 0, height - 1) // BAND]
        centre = jnp.full((BAND, TILE), kernels_ref[kernel, TAPS // 2], jnp.float32)
        start = band * BAND
        for slot, tap in enumerate(SIDES):
            weight = jnp.full((BAND, TILE), kernels_ref[kernel, tap], jnp.float32) / centre
            target = row_ids + (row + tap - TAPS // 2)
            weight = jnp.where(inside & (target >= 0) & (target < height), weight, 0.0)
            taps_ref[slot, start : start + BAND, :] = weight
            pad_ref[slot, BAND + start : 2 * BAND + start, :] = weight
    for slot, tap in enumerate(SIDES):
        start = BAND + TAPS // 2 - tap
        back_ref[slot] = pad_ref[slot, start : start + span, :]
    flat = jnp.concatenate([masks_ref[row].astype(jnp.float32) for row in range(rows_dev)], axis=0)
    positions = flat.shape[0]
    both = jnp.concatenate([flat, flat], axis=0).T
    half = feet_ref.shape[1]
    left = lax.broadcasted_iota(jnp.int32, (half, TILE), 1) < positions
    for block in range(feet_ref.shape[0]):
        start = 2 * block * half
        halves = jnp.where(left, both[start : start + half], both[start + half : start + 2 * half])
        feet_ref[block] = halves.astype(jnp.bfloat16)


def restore_half(taps_ref, back_ref, own_ref, inner_ref, outer_ref, out_ref, image_ref, current_ref, quotient_ref, half):
    n_frame = out_ref.shape[0]
    _, rows_dev, width = own_ref.shape
    frames = own_ref.shape[0] // HALVES
    tiles_dev = width // (n_frame * TILE)
    positions = rows_dev * tiles_dev
    units = [(frame, tile) for frame in range(frames) for tile in range(TOGETHER)]
    for ref in (image_ref, current_ref, quotient_ref):
        ref[...] = jnp.ones_like(ref)
    row = lax.axis_index("row")
    even = row % 2 == 0
    fill = jnp.where((row == 0) | (row == lax.axis_size("row") - 1), 1.0, 0.0)

    def columns_step(step, carry):
        for unit, (frame, tile) in enumerate(units):
            columns = pl.ds(pl.multiple_of((step * TOGETHER + tile) * TILE, TILE), TILE)
            near, far = frame * NEAR, frames * NEAR + frame * FAR
            start, stop = PAD + MARGIN, PAD + MARGIN + rows_dev
            inner, outer = inner_ref[near : near + NEAR, columns], outer_ref[near : near + NEAR, columns] + fill
            image_ref[unit, start - NEAR : start, :] = jnp.where(even, outer, inner)
            image_ref[unit, stop : stop + NEAR, :] = jnp.where(even, inner, outer)
            inner, outer = inner_ref[far : far + FAR, columns], outer_ref[far : far + FAR, columns] + fill
            image_ref[unit, start - NEAR - FAR : start - NEAR, :] = jnp.where(even, outer, inner)
            image_ref[unit, stop + NEAR : stop + NEAR + FAR, :] = jnp.where(even, inner, outer)
            image_ref[unit, start:stop, :] = own_ref[half * frames + frame, :, columns]
        source_ref = image_ref
        for (low, high), (back_low, back_high) in STEPS:
            for row in range(low, high, BAND):
                weights = [taps_ref[slot, row : row + BAND, :] for slot in range(len(SIDES))]
                for unit in range(len(units)):
                    rows = slice(PAD + row, PAD + row + BAND)
                    blurred = source_ref[unit, rows, :]
                    for weight, tap in zip(weights, SIDES):
                        start = PAD + row + tap - TAPS // 2
                        blurred = blurred + weight * source_ref[unit, start : start + BAND, :]
                    quotient_ref[unit, rows, :] = image_ref[unit, rows, :] / blurred
            for row in range(back_low, back_high, BAND):
                weights = [back_ref[slot, row : row + BAND, :] for slot in range(len(SIDES))]
                for unit in range(len(units)):
                    rows = slice(PAD + row, PAD + row + BAND)
                    spread = quotient_ref[unit, rows, :]
                    for weight, tap in zip(weights, SIDES):
                        start = PAD + row - tap + TAPS // 2
                        spread = spread + weight * quotient_ref[unit, start : start + BAND, :]
                    current_ref[unit, rows, :] = source_ref[unit, rows, :] * spread
            source_ref = current_ref
        steps = tiles_dev // TOGETHER
        first = pl.multiple_of(lax.rem(step, steps) * (TOGETHER * rows_dev), TOGETHER * rows_dev)
        for unit, (frame, tile) in enumerate(units):
            estimate = current_ref[unit, PAD + MARGIN : PAD + MARGIN + rows_dev, :].astype(jnp.bfloat16)
            start = first + ((half * frames + frame) * positions + tile * rows_dev)
            out_ref[step // steps, pl.ds(pl.multiple_of(start, rows_dev), rows_dev), :] = estimate
        return carry

    lax.fori_loop(0, n_frame * tiles_dev // TOGETHER, columns_step, 0)
    lane_tiles = lax.broadcasted_iota(jnp.int32, (TILE, TILE), 1) % tiles_dev
    gathered = jnp.zeros((frames * n_frame * rows_dev, TILE), jnp.float32)
    for tile in range(tiles_dev):
        pieces = []
        for frame in range(frames):
            start = (half * frames + frame) * positions + tile * rows_dev
            pieces += [out_ref[block, start : start + rows_dev, :] for block in range(n_frame)]
        picked = jnp.where(lane_tiles == tile, 1.0, 0.0).astype(jnp.bfloat16)
        gathered = gathered + jnp.dot(jnp.concatenate(pieces, axis=0), picked, preferred_element_type=jnp.float32)
    lanes = lax.broadcasted_iota(jnp.int32, (rows_dev, TILE), 1)
    here = lanes % positions // tiles_dev == lax.broadcasted_iota(jnp.int32, (rows_dev, TILE), 0)
    sums = []
    for place in range(frames * n_frame):
        part = jnp.where(here, gathered[place * rows_dev : (place + 1) * rows_dev], 0.0)
        sums.append(jnp.sum(part, axis=0, keepdims=True))
    return jnp.concatenate(sums, axis=0)


def first_kernel(taps_ref, back_ref, own_ref, inner_ref, outer_ref, out_ref, sums_ref, *scratch):
    sums_ref[...] = restore_half(taps_ref, back_ref, own_ref, inner_ref, outer_ref, out_ref, *scratch, 0)


def second_kernel(
    taps_ref, back_ref, own_ref, inner_ref, outer_ref, feet_ref, estimate_ref, sums_ref, out_ref, *scratch
):
    sums = restore_half(taps_ref, back_ref, own_ref, inner_ref, outer_ref, out_ref, *scratch, 1)
    sums = jnp.concatenate([sums_ref[...], sums], axis=0)
    n_frame, done, _ = estimate_ref.shape
    positions = done * HALVES // own_ref.shape[0]
    high = sums.astype(jnp.bfloat16).astype(jnp.float32)
    split = jnp.where(lax.broadcasted_iota(jnp.int32, sums.shape, 1) < positions, high, sums - high).astype(jnp.bfloat16)
    start = HALVES * done
    for block in range(n_frame):
        out_ref[block, :done, :] = estimate_ref[block]
        out_ref[block, start : start + split.shape[0], :] = split
        out_ref[block, start + split.shape[0] :, :] = feet_ref[block]


def deconvolved(series):
    total = len(series)
    factors = []
    for step in range(total):
        middle = 1.0 + SMOOTHING * (1.0 if step in (0, total - 1) else 2.0)
        if step:
            middle -= SMOOTHING * SMOOTHING * factors[-1]
        factors.append(1.0 / middle)
    forward = [series[0] * factors[0]]
    for step in range(1, total):
        forward.append((series[step] + SMOOTHING * forward[step - 1]) * factors[step])
    baseline = [None] * total
    baseline[total - 1] = forward[total - 1]
    for step in range(total - 2, -1, -1):
        baseline[step] = forward[step] + (SMOOTHING * factors[step]) * baseline[step + 1]
    result, earlier = [], None
    for step in range(total):
        detrended = series[step] - baseline[step]
        result.append(detrended if earlier is None else detrended - DECAY_RATE * earlier)
        earlier = detrended
    return result


def partial_kernel(*refs, frames, positions):
    pieces, (out_ref, sums_ref, feet_ref) = refs[:-3], refs[-3:]
    n_frame = len(pieces)
    place = lax.axis_index("frame")
    start = frames * positions
    rows = frames * n_frame
    half = feet_ref.shape[1]
    for step, piece in enumerate(pieces):
        sums_ref[pl.ds(pl.multiple_of((place ^ step) * rows, rows), rows), :] = piece[start : start + rows, :].astype(jnp.float32)
        feet_ref[place ^ step] = piece[start + rows :, :].astype(jnp.float32)
    series = [sums_ref[t * n_frame : (t + 1) * n_frame, :] for t in range(rows)]
    for t, sums in enumerate(deconvolved(series)):
        sums_ref[t * n_frame : (t + 1) * n_frame, :] = sums + pltpu.roll(sums, TILE // 2, 1)
    left = lax.broadcasted_iota(jnp.int32, (half, TILE), 1) < positions
    weights, sums = [], []
    extra = jnp.where(lax.broadcasted_iota(jnp.int32, (8, TILE), 0) == 0, 1.0, 0.0)
    for block in range(n_frame):
        feet = feet_ref[block]
        weights.append(jnp.concatenate([jnp.where(left, feet, 0.0), jnp.where(left, 0.0, feet)], axis=0))
        sums.append(jnp.concatenate([sums_ref[pl.ds(block, rows, stride=n_frame), :], extra], axis=0))
    totals = lax.dot_general(
        jnp.concatenate(weights, axis=1),
        jnp.concatenate(sums, axis=1),
        (((1,), (1,)), ((), ())),
        precision=lax.Precision.HIGHEST,
        preferred_element_type=jnp.float32,
    )
    share = out_ref.shape[1]
    out_ref[...] = jnp.zeros_like(out_ref)
    for row in range(out_ref.shape[0]):
        out_ref[row, :, : rows + 8] = totals[row * share : (row + 1) * share]


def temporal_kernel(*refs, frames):
    pieces, (spikes_ref, in_ref) = refs[:-2], refs[-2:]
    place = lax.axis_index("frame")
    for step, piece in enumerate(pieces):
        in_ref[place ^ step] = piece[: in_ref.shape[1], :]
    total, rows_dev, columns = spikes_ref.shape
    positions = in_ref.shape[1] // frames
    for tile in range(columns // TILE):
        series = []
        for t in range(total):
            start = t % frames * positions + tile * rows_dev
            series.append(in_ref[t // frames, start : start + rows_dev, :].astype(jnp.float32))
        for t, spikes in enumerate(deconvolved(series)):
            spikes_ref[t, :, tile * TILE : (tile + 1) * TILE] = spikes.astype(spikes_ref.dtype)


def means_kernel(*refs):
    pieces, traces_ref = refs[:-1], refs[-1]
    frames = traces_ref.shape[1]
    total = pieces[0][...]
    for piece in pieces[1:]:
        total = total + piece[...]
    traces_ref[...] = total[:, :frames] / (TILE * total[:, frames : frames + 1])


def swapped(parts, axis):
    count, place = lax.axis_size(axis), lax.axis_index(axis)
    arrived = [lax.dynamic_index_in_dim(parts, place, 0, keepdims=False, allow_negative_indices=False)]
    for step in range(1, count):
        part = lax.dynamic_index_in_dim(parts, place ^ step, 0, keepdims=False, allow_negative_indices=False)
        arrived.append(lax.ppermute(part, axis, [(i, i ^ step) for i in range(count)]))
    return arrived


def by_halo(observed, kernels, band_kernel, masks):
    n_frame, n_row = lax.axis_size("frame"), lax.axis_size("row")
    frames, rows_dev, width = observed.shape
    components, _, tiles_dev = masks.shape
    positions = rows_dev * tiles_dev
    share = components // (n_frame * n_row)
    span = rows_dev + 2 * MARGIN
    smem, vmem = pl.BlockSpec(memory_space=pltpu.SMEM), pl.BlockSpec(memory_space=pltpu.VMEM)

    def call(kernel, name, in_specs, out_shape, scratch=(), cost=1000000):
        many = isinstance(out_shape, tuple)
        return pl.pallas_call(
            kernel,
            name=name,
            out_shape=out_shape,
            in_specs=in_specs,
            out_specs=(vmem,) * len(out_shape) if many else vmem,
            scratch_shapes=scratch,
            compiler_params=pltpu.CompilerParams(vmem_limit_bytes=16 << 20),
            cost_estimate=pl.CostEstimate(flops=cost, bytes_accessed=cost, transcendentals=0),
        )

    def array(*shape, dtype=jnp.float32):
        return jax.ShapeDtypeStruct(shape, dtype)

    half = frames // HALVES
    packed = array(half * (NEAR + FAR), width)
    *sent, own = call(
        halo_kernel,
        "halo",
        [pl.BlockSpec(memory_space=pltpu.HBM)],
        (packed,) * (2 * HALVES) + (array(*observed.shape),),
        [pltpu.SemaphoreType.DMA((frames,))],
    )(observed)
    pairs = [(i, i + 1) for i in range(0, n_row - 1, 2)], [(i, i + 1) for i in range(1, n_row - 1, 2)]
    pairs = [pair + [(j, i) for i, j in pair] for pair in pairs]
    arrived = [lax.ppermute(rows.astype(jnp.float16), "row", pairs[i % 2]) for i, rows in enumerate(sent)]
    taps, back, feet = call(
        functools.partial(tables_kernel, height=rows_dev * n_row),
        "tables",
        [smem, smem, vmem],
        (
            array(len(SIDES), span, TILE),
            array(len(SIDES), span, TILE),
            array(n_frame, n_row * share // 2, TILE, dtype=jnp.bfloat16),
        ),
        [pltpu.VMEM((len(SIDES), span + 2 * BAND, TILE), jnp.float32)],
    )(band_kernel, kernels, masks.transpose(1, 2, 0))
    arrived = [rows.astype(jnp.float32) for rows in arrived]
    buffers = [pltpu.VMEM((half * TOGETHER, span + 2 * PAD, TILE), jnp.float32)] * 3
    estimate, sums = call(
        first_kernel,
        "restore1",
        [vmem] * 5,
        (array(n_frame, half * positions, TILE, dtype=jnp.bfloat16), array(half * n_frame, TILE)),
        buffers,
        cost=6000000,
    )(taps, back, own, *arrived[:2])
    block_rows = frames * positions + frames * n_frame + n_row * share // 2
    blocks = call(
        second_kernel, "restore2", [vmem] * 8, array(n_frame, block_rows, TILE, dtype=jnp.bfloat16), buffers, cost=6000000
    )(taps, back, own, *arrived[2:], feet, estimate, sums)
    pieces = swapped(blocks, "frame")
    partial = call(
        functools.partial(partial_kernel, frames=frames, positions=positions),
        "partial",
        [vmem] * n_frame,
        array(n_row, share, TILE),
        [
            pltpu.VMEM((n_frame * frames * n_frame, TILE), jnp.float32),
            pltpu.VMEM((n_frame, n_row * share // 2, TILE), jnp.float32),
        ],
    )(*pieces)
    shares = swapped(partial, "row")
    spikes = call(
        functools.partial(temporal_kernel, frames=frames),
        "temporal",
        [vmem] * n_frame,
        array(n_frame * frames, rows_dev, tiles_dev * TILE, dtype=jnp.bfloat16),
        [pltpu.VMEM((n_frame, frames * positions, TILE), jnp.bfloat16)],
    )(*pieces)
    traces = call(means_kernel, "means", [vmem] * n_row, array(share, n_frame * frames))(*shares)
    return (spikes, traces)


def fits(mesh, observed, masks):
    frames_dev = observed.shape[0] // mesh.shape["frame"]
    rows_dev = masks.shape[1] // (mesh.shape["groups"] * mesh.shape["row"])
    tiles_dev = masks.shape[2] // mesh.shape["frame"]
    places = mesh.shape["frame"] * mesh.shape["row"]
    return (
        frames_dev == mesh.shape["frame"] == mesh.shape["row"] == 4
        and 2 * rows_dev * tiles_dev == TILE
        and rows_dev == 16
        and masks.shape[0] // places == 16
    )


def solution(mesh):
    in_specs = (
        P("frame", ("groups", "row"), None),
        P(),
        P("groups"),
        P(None, ("groups", "row"), "frame"),
    )
    out_specs = (P(None, ("groups", "row"), "frame"), P(("groups", "frame", "row"), None))

    def whole(observed, kernels, band_kernel, masks):
        body = by_halo if fits(mesh, observed, masks) else local
        mapped = jax.shard_map(body, mesh=mesh, in_specs=in_specs, out_specs=out_specs, check_vma=False)
        return mapped(observed, kernels, band_kernel, masks)

    return whole
```

```python
import functools

import jax
import jax.numpy as jnp
from jax import lax
from jax.experimental import pallas as pl
from jax.experimental.pallas import tpu as pltpu
from jax.sharding import PartitionSpec as P

TILE = 128
BAND = 8
ITERS = 3
TAPS = 5
NEAR, FAR = 8, 4
MARGIN = 2 * BAND
PAD = BAND
STEPS = (((6, 46), (8, 40)), ((10, 42), (12, 36)), ((14, 38), (16, 32)))
SIDES = (0, 1, 3, 4)


SMOOTHING = 1024.0
DECAY_RATE = 0.9


def padded_2(cells, sides, width):
    for axis, dim in sides:
        count = lax.axis_size(axis)
        ends = count - 1
        head = lax.slice_in_dim(cells, 0, width, axis=dim)
        tail = lax.slice_in_dim(cells, cells.shape[dim] - width, cells.shape[dim], axis=dim)
        cells = jnp.concatenate(
            [
                lax.ppermute(tail, axis, [(i, (i + 1) % count) for i in range(ends)]),
                cells,
                lax.ppermute(head, axis, [((i + 1) % count, i) for i in range(ends)]),
            ],
            axis=dim,
        )
    return cells


def tap_rows(tap_table, band_kernel, first_row, row_count, height):
    row_ids = jnp.clip(first_row + jnp.arange(row_count), 0, height - 1)
    row_bands = row_ids // BAND
    band_slots = jnp.arange(band_kernel.shape[0])
    kernel_ids = jnp.sum(
        jnp.where(row_bands[:, None] == band_slots[None, :], band_kernel[None, :], 0), axis=1
    )
    kernel_slots = jnp.arange(tap_table.shape[0])
    picked = jnp.where(
        kernel_ids[:, None, None] == kernel_slots[None, :, None], tap_table[None, :, :], 0.0
    )
    return jnp.sum(picked, axis=1)


def blur_rows(padded, row_taps, row_count):
    summed = row_taps[:, 0][None, :, None] * padded[:, 0:row_count]
    for offset in range(1, 5):
        summed = (
            summed + row_taps[:, offset][None, :, None] * padded[:, offset : offset + row_count]
        )
    return summed


def back_rows(padded_quotient, outer_taps, row_count):
    summed = outer_taps[4 : 4 + row_count, 0][None, :, None] * padded_quotient[:, 4 : 4 + row_count]
    for offset in range(1, 5):
        start = 4 - offset
        summed = (
            summed
            + outer_taps[start : start + row_count, offset][None, :, None]
            * padded_quotient[:, start : start + row_count]
        )
    return summed


def temporal(series_block):
    frame_total, item_count, columns = series_block.shape
    values = series_block.astype(jnp.float32).reshape(frame_total, item_count * columns)
    frame_ids = jnp.arange(frame_total)
    at_ends = (frame_ids == 0) | (frame_ids == frame_total - 1)
    middle = (1.0 + SMOOTHING * jnp.where(at_ends, 1.0, 2.0)).astype(jnp.float32)
    sub_diag = jnp.where(frame_ids == 0, 0.0, -SMOOTHING).astype(jnp.float32)
    super_diag = jnp.where(frame_ids == frame_total - 1, 0.0, -SMOOTHING).astype(jnp.float32)
    baseline = lax.linalg.tridiagonal_solve(sub_diag, middle, super_diag, values)
    detrended = values - baseline
    earlier = jnp.concatenate(
        [jnp.zeros((1, values.shape[1]), jnp.float32), detrended[:-1]], axis=0
    )
    result = (detrended - DECAY_RATE * earlier).astype(jnp.bfloat16)
    return result.reshape(frame_total, item_count, columns)


def local(observed, kernels, band_kernel, masks):
    frames_dev, rows_dev, row_pixels = observed.shape
    height = rows_dev * lax.axis_size("row")
    tap_table = kernels / jnp.sum(kernels, axis=1, keepdims=True)
    first_row = lax.axis_index("row") * rows_dev
    own_taps = tap_rows(tap_table, band_kernel, first_row, rows_dev, height)
    outer_taps = tap_rows(tap_table, band_kernel, first_row - 2, rows_dev + 4, height)
    current = observed
    for iteration in range(ITERS):
        padded = padded_2(current, (("row", 1),), 2)
        blurred = blur_rows(padded, own_taps, rows_dev)
        quotient = observed / blurred
        padded_quotient = padded_2(quotient, (("row", 1),), 2)
        current = current * back_rows(padded_quotient, outer_taps, rows_dev)
    estimate = current.astype(jnp.bfloat16)
    spikes = temporal(lax.all_to_all(estimate, "frame", split_axis=2, concat_axis=0, tiled=True))
    frames_all, _, columns = spikes.shape
    tile_count = columns // TILE
    tile_sums = jnp.sum(
        spikes.reshape(frames_all, rows_dev * tile_count, TILE).astype(jnp.float32), axis=2
    )
    weights = masks.astype(jnp.float32).reshape(masks.shape[0], rows_dev * tile_count)
    local_sums = lax.dot_general(
        weights, tile_sums, (((1,), (1,)), ((), ())), precision=lax.Precision.HIGHEST
    )
    counts = jnp.sum(weights, axis=1)
    trace_sums, totals = (
        lax.psum_scatter(local_sums, ("frame", "row"), scatter_dimension=0, tiled=True),
        lax.psum_scatter(counts, ("frame", "row"), scatter_dimension=0, tiled=True),
    )
    traces = trace_sums / (TILE * totals[:, None])
    return (spikes, traces)


def low_first():
    return (lax.axis_index("row") + lax.axis_index("frame")) % 2 == 0


def halo_kernel(observed_ref, first_ref, second_ref, own_ref):
    low = low_first()
    frames = observed_ref.shape[0]
    own_ref[...] = observed_ref[...]
    for frame in range(frames):
        near = frame * NEAR
        far = frames * NEAR + frame * FAR
        bottom, top = observed_ref[frame, -NEAR:, :], observed_ref[frame, :NEAR, :]
        first_ref[near : near + NEAR, :] = jnp.where(low, bottom, top)
        second_ref[near : near + NEAR, :] = jnp.where(low, top, bottom)
        bottom, top = observed_ref[frame, -NEAR - FAR : -NEAR, :], observed_ref[frame, NEAR : NEAR + FAR, :]
        first_ref[far : far + FAR, :] = jnp.where(low, bottom, top)
        second_ref[far : far + FAR, :] = jnp.where(low, top, bottom)


def tables_kernel(band_ref, kernels_ref, masks_ref, taps_ref, back_ref, feet_ref, pad_ref, *, height):
    rows_dev = masks_ref.shape[0]
    span = rows_dev + 2 * MARGIN
    first_row = lax.axis_index("row") * rows_dev - MARGIN
    row_ids = lax.broadcasted_iota(jnp.int32, (BAND, TILE), 0)
    pad_ref[...] = jnp.zeros_like(pad_ref)
    for band in range(span // BAND):
        row = first_row + band * BAND
        inside = (row >= 0) & (row < height)
        kernel = band_ref[jnp.clip(row, 0, height - 1) // BAND]
        centre = jnp.full((BAND, TILE), kernels_ref[kernel, TAPS // 2], jnp.float32)
        start = band * BAND
        for slot, tap in enumerate(SIDES):
            weight = jnp.full((BAND, TILE), kernels_ref[kernel, tap], jnp.float32) / centre
            target = row_ids + (row + tap - TAPS // 2)
            weight = jnp.where(inside & (target >= 0) & (target < height), weight, 0.0)
            taps_ref[slot, start : start + BAND, :] = weight
            pad_ref[slot, BAND + start : 2 * BAND + start, :] = weight
    for slot, tap in enumerate(SIDES):
        start = BAND + TAPS // 2 - tap
        back_ref[slot] = pad_ref[slot, start : start + span, :]
    flat = jnp.concatenate([masks_ref[row].astype(jnp.float32) for row in range(rows_dev)], axis=0)
    positions = flat.shape[0]
    both = jnp.concatenate([flat, flat], axis=0).T
    half = feet_ref.shape[1]
    left = lax.broadcasted_iota(jnp.int32, (half, TILE), 1) < positions
    for block in range(feet_ref.shape[0]):
        start = 2 * block * half
        halves = jnp.where(left, both[start : start + half], both[start + half : start + 2 * half])
        feet_ref[block] = halves.astype(jnp.bfloat16)


def restore_kernel(
    taps_ref, back_ref, feet_ref, own_ref, first_ref, second_ref, out_ref, side_ref, image_ref, current_ref, quotient_ref
):
    n_frame = out_ref.shape[0]
    frames, rows_dev, width = own_ref.shape
    tiles_dev = width // (n_frame * TILE)
    positions = rows_dev * tiles_dev
    for ref in (image_ref, current_ref, quotient_ref):
        ref[...] = jnp.ones_like(ref)
    low = low_first()
    row = lax.axis_index("row")
    above = jnp.where(row == 0, 1.0, 0.0)
    below = jnp.where(row == lax.axis_size("row") - 1, 1.0, 0.0)

    def columns_step(step, carry):
        columns = pl.ds(pl.multiple_of(step * TILE, TILE), TILE)
        for frame in range(frames):
            near, far = frame * NEAR, frames * NEAR + frame * FAR
            start, stop = PAD + MARGIN, PAD + MARGIN + rows_dev
            first, second = first_ref[near : near + NEAR, columns], second_ref[near : near + NEAR, columns]
            image_ref[frame, start - NEAR : start, :] = jnp.where(low, second, first) + above
            image_ref[frame, stop : stop + NEAR, :] = jnp.where(low, first, second) + below
            first, second = first_ref[far : far + FAR, columns], second_ref[far : far + FAR, columns]
            image_ref[frame, start - NEAR - FAR : start - NEAR, :] = jnp.where(low, second, first) + above
            image_ref[frame, stop + NEAR : stop + NEAR + FAR, :] = jnp.where(low, first, second) + below
            image_ref[frame, start:stop, :] = own_ref[frame, :, columns]
        source_ref = image_ref
        for (first, last), (back_first, back_last) in STEPS:
            for row in range(first, last, BAND):
                weights = [taps_ref[slot, row : row + BAND, :] for slot in range(len(SIDES))]
                for frame in range(frames):
                    rows = slice(PAD + row, PAD + row + BAND)
                    blurred = source_ref[frame, rows, :]
                    for weight, tap in zip(weights, SIDES):
                        start = PAD + row + tap - TAPS // 2
                        blurred = blurred + weight * source_ref[frame, start : start + BAND, :]
                    quotient_ref[frame, rows, :] = image_ref[frame, rows, :] / blurred
            for row in range(back_first, back_last, BAND):
                weights = [back_ref[slot, row : row + BAND, :] for slot in range(len(SIDES))]
                for frame in range(frames):
                    rows = slice(PAD + row, PAD + row + BAND)
                    spread = quotient_ref[frame, rows, :]
                    for weight, tap in zip(weights, SIDES):
                        start = PAD + row - tap + TAPS // 2
                        spread = spread + weight * quotient_ref[frame, start : start + BAND, :]
                    current_ref[frame, rows, :] = source_ref[frame, rows, :] * spread
            source_ref = current_ref
        first = pl.multiple_of(lax.rem(step, tiles_dev) * rows_dev, rows_dev)
        for frame in range(frames):
            estimate = current_ref[frame, PAD + MARGIN : PAD + MARGIN + rows_dev, :].astype(jnp.bfloat16)
            start = pl.multiple_of(first + frame * positions, rows_dev)
            out_ref[step // tiles_dev, pl.ds(start, rows_dev), :] = estimate
        return carry

    lax.fori_loop(0, n_frame * tiles_dev, columns_step, 0)
    lane_tiles = lax.broadcasted_iota(jnp.int32, (TILE, TILE), 1) % tiles_dev
    gathered = jnp.zeros((frames * n_frame * rows_dev, TILE), jnp.float32)
    for tile in range(tiles_dev):
        pieces = []
        for frame in range(frames):
            start = frame * positions + tile * rows_dev
            pieces += [out_ref[block, start : start + rows_dev, :] for block in range(n_frame)]
        picked = jnp.where(lane_tiles == tile, 1.0, 0.0).astype(jnp.bfloat16)
        gathered = gathered + jnp.dot(jnp.concatenate(pieces, axis=0), picked, preferred_element_type=jnp.float32)
    lanes = lax.broadcasted_iota(jnp.int32, (rows_dev, TILE), 1)
    here = lanes % positions // tiles_dev == lax.broadcasted_iota(jnp.int32, (rows_dev, TILE), 0)
    sums = []
    for place in range(frames * n_frame):
        part = jnp.where(here, gathered[place * rows_dev : (place + 1) * rows_dev], 0.0)
        sums.append(jnp.sum(part, axis=0, keepdims=True))
    sums = jnp.concatenate(sums, axis=0)
    high = sums.astype(jnp.bfloat16).astype(jnp.float32)
    split = jnp.where(lax.broadcasted_iota(jnp.int32, sums.shape, 1) < positions, high, sums - high).astype(jnp.bfloat16)
    for block in range(n_frame):
        side_ref[block, : split.shape[0], :] = split
        side_ref[block, split.shape[0] :, :] = feet_ref[block]


def deconvolved(series):
    total = len(series)
    factors = []
    for step in range(total):
        middle = 1.0 + SMOOTHING * (1.0 if step in (0, total - 1) else 2.0)
        if step:
            middle -= SMOOTHING * SMOOTHING * factors[-1]
        factors.append(1.0 / middle)
    forward = [series[0] * factors[0]]
    for step in range(1, total):
        forward.append((series[step] + SMOOTHING * forward[step - 1]) * factors[step])
    baseline = [None] * total
    baseline[total - 1] = forward[total - 1]
    for step in range(total - 2, -1, -1):
        baseline[step] = forward[step] + (SMOOTHING * factors[step]) * baseline[step + 1]
    result, earlier = [], None
    for step in range(total):
        detrended = series[step] - baseline[step]
        result.append(detrended if earlier is None else detrended - DECAY_RATE * earlier)
        earlier = detrended
    return result


def partial_kernel(*refs, positions):
    pieces, (out_ref, sums_ref, feet_ref) = refs[:-3], refs[-3:]
    n_frame = len(pieces)
    place = lax.axis_index("frame")
    rows = sums_ref.shape[0] // n_frame
    half = feet_ref.shape[1]
    for step, piece in enumerate(pieces):
        sums_ref[pl.ds(pl.multiple_of((place ^ step) * rows, rows), rows), :] = piece[:rows, :].astype(jnp.float32)
        feet_ref[place ^ step] = piece[rows:, :].astype(jnp.float32)
    series = [sums_ref[t * n_frame : (t + 1) * n_frame, :] for t in range(rows)]
    for t, sums in enumerate(deconvolved(series)):
        sums_ref[t * n_frame : (t + 1) * n_frame, :] = sums + pltpu.roll(sums, TILE // 2, 1)
    left = lax.broadcasted_iota(jnp.int32, (half, TILE), 1) < positions
    weights, sums = [], []
    extra = jnp.where(lax.broadcasted_iota(jnp.int32, (8, TILE), 0) == 0, 1.0, 0.0)
    for block in range(n_frame):
        feet = feet_ref[block]
        weights.append(jnp.concatenate([jnp.where(left, feet, 0.0), jnp.where(left, 0.0, feet)], axis=0))
        sums.append(jnp.concatenate([sums_ref[pl.ds(block, rows, stride=n_frame), :], extra], axis=0))
    totals = lax.dot_general(
        jnp.concatenate(weights, axis=1),
        jnp.concatenate(sums, axis=1),
        (((1,), (1,)), ((), ())),
        precision=lax.Precision.HIGHEST,
        preferred_element_type=jnp.float32,
    )
    share = out_ref.shape[1]
    out_ref[...] = jnp.zeros_like(out_ref)
    for row in range(out_ref.shape[0]):
        out_ref[row, :, : rows + 8] = totals[row * share : (row + 1) * share]


def temporal_kernel(*refs, frames):
    pieces, (spikes_ref, in_ref) = refs[:-2], refs[-2:]
    place = lax.axis_index("frame")
    for step, piece in enumerate(pieces):
        in_ref[place ^ step] = piece[...]
    total, rows_dev, columns = spikes_ref.shape
    positions = in_ref.shape[1] // frames
    for tile in range(columns // TILE):
        series = []
        for t in range(total):
            start = t % frames * positions + tile * rows_dev
            series.append(in_ref[t // frames, start : start + rows_dev, :].astype(jnp.float32))
        for t, spikes in enumerate(deconvolved(series)):
            spikes_ref[t, :, tile * TILE : (tile + 1) * TILE] = spikes.astype(spikes_ref.dtype)


def means_kernel(*refs):
    pieces, traces_ref = refs[:-1], refs[-1]
    frames = traces_ref.shape[1]
    total = pieces[0][...]
    for piece in pieces[1:]:
        total = total + piece[...]
    traces_ref[...] = total[:, :frames] / (TILE * total[:, frames : frames + 1])


def swapped(parts, axis):
    count, place = lax.axis_size(axis), lax.axis_index(axis)
    arrived = [lax.dynamic_index_in_dim(parts, place, 0, keepdims=False, allow_negative_indices=False)]
    for step in range(1, count):
        part = lax.dynamic_index_in_dim(parts, place ^ step, 0, keepdims=False, allow_negative_indices=False)
        arrived.append(lax.ppermute(part, axis, [(i, i ^ step) for i in range(count)]))
    return arrived


def by_halo(observed, kernels, band_kernel, masks):
    n_frame, n_row = lax.axis_size("frame"), lax.axis_size("row")
    frames, rows_dev, width = observed.shape
    components, _, tiles_dev = masks.shape
    positions = rows_dev * tiles_dev
    share = components // (n_frame * n_row)
    span = rows_dev + 2 * MARGIN
    smem, vmem = pl.BlockSpec(memory_space=pltpu.SMEM), pl.BlockSpec(memory_space=pltpu.VMEM)

    def call(kernel, name, in_specs, out_shape, scratch=(), cost=1000000):
        many = isinstance(out_shape, tuple)
        return pl.pallas_call(
            kernel,
            name=name,
            out_shape=out_shape,
            in_specs=in_specs,
            out_specs=(vmem,) * len(out_shape) if many else vmem,
            scratch_shapes=scratch,
            compiler_params=pltpu.CompilerParams(vmem_limit_bytes=16 << 20),
            cost_estimate=pl.CostEstimate(flops=cost, bytes_accessed=cost, transcendentals=0),
        )

    def array(*shape, dtype=jnp.float32):
        return jax.ShapeDtypeStruct(shape, dtype)

    packed = array(frames * (NEAR + FAR), width)
    *sent, own = call(halo_kernel, "halo", [vmem], (packed, packed, array(*observed.shape)))(observed)
    pairs = [[(i, i + 1) for i in range(first, n_row - 1, 2)] for first in (0, 1)]
    swaps = [
        [(f * n_row + i, f * n_row + j) for f in range(n_frame) for pair in pairs[(f + turn) % 2] for i, j in (pair, pair[::-1])]
        for turn in range(2)
    ]
    arrived = [
        lax.ppermute(rows.astype(jnp.float16), ("frame", "row"), swap).astype(jnp.float32)
        for rows, swap in zip(sent, swaps)
    ]
    taps, back, feet = call(
        functools.partial(tables_kernel, height=rows_dev * n_row),
        "tables",
        [smem, smem, vmem],
        (
            array(len(SIDES), span, TILE),
            array(len(SIDES), span, TILE),
            array(n_frame, n_row * share // 2, TILE, dtype=jnp.bfloat16),
        ),
        [pltpu.VMEM((len(SIDES), span + 2 * PAD, TILE), jnp.float32)],
    )(band_kernel, kernels, masks.transpose(1, 2, 0))
    side_rows = frames * n_frame + n_row * share // 2
    blocks, sides = call(
        restore_kernel,
        "restore",
        [vmem] * 6,
        (
            array(n_frame, frames * positions, TILE, dtype=jnp.bfloat16),
            array(n_frame, side_rows, TILE, dtype=jnp.bfloat16),
        ),
        [pltpu.VMEM((frames, span + 2 * PAD, TILE), jnp.float32)] * 3,
    )(taps, back, feet, own, *arrived)
    sides = swapped(sides, "frame")
    pieces = swapped(blocks, "frame")
    partial = call(
        functools.partial(partial_kernel, positions=positions),
        "partial",
        [vmem] * n_frame,
        array(n_row, share, TILE),
        [
            pltpu.VMEM((n_frame * frames * n_frame, TILE), jnp.float32),
            pltpu.VMEM((n_frame, n_row * share // 2, TILE), jnp.float32),
        ],
    )(*sides)
    shares = swapped(partial, "row")
    spikes = call(
        functools.partial(temporal_kernel, frames=frames),
        "temporal",
        [vmem] * n_frame,
        array(n_frame * frames, rows_dev, tiles_dev * TILE, dtype=jnp.bfloat16),
        [pltpu.VMEM((n_frame, frames * positions, TILE), jnp.bfloat16)],
    )(*pieces)
    spikes, *shares = lax.optimization_barrier((spikes, *shares))
    traces = call(means_kernel, "means", [vmem] * n_row, array(share, n_frame * frames))(*shares)
    return (spikes, traces)


def fits(mesh, observed, masks):
    frames_dev = observed.shape[0] // mesh.shape["frame"]
    rows_dev = masks.shape[1] // (mesh.shape["groups"] * mesh.shape["row"])
    tiles_dev = masks.shape[2] // mesh.shape["frame"]
    places = mesh.shape["frame"] * mesh.shape["row"]
    return (
        frames_dev == mesh.shape["frame"] == mesh.shape["row"] == 4
        and 2 * rows_dev * tiles_dev == TILE
        and rows_dev == 16
        and masks.shape[0] // places == 16
    )


def solution(mesh):
    in_specs = (
        P("frame", ("groups", "row"), None),
        P(),
        P("groups"),
        P(None, ("groups", "row"), "frame"),
    )
    out_specs = (P(None, ("groups", "row"), "frame"), P(("groups", "frame", "row"), None))

    def whole(observed, kernels, band_kernel, masks):
        body = by_halo if fits(mesh, observed, masks) else local
        mapped = jax.shard_map(body, mesh=mesh, in_specs=in_specs, out_specs=out_specs, check_vma=False)
        return mapped(observed, kernels, band_kernel, masks)

    return whole
```

```python
import functools

import jax
import jax.numpy as jnp
from jax import lax
from jax.experimental import pallas as pl
from jax.experimental.pallas import tpu as pltpu
from jax.sharding import PartitionSpec as P

TILE = 128
BAND = 8
ITERS = 3
TAPS = 5
NEAR, FAR = 8, 4
MARGIN = 2 * BAND
PAD = BAND
STEPS = (((6, 46), (8, 40)), ((10, 42), (12, 36)), ((14, 38), (16, 32)))
SIDES = (0, 1, 3, 4)
HALVES = 2
TOGETHER = 2


SMOOTHING = 1024.0
DECAY_RATE = 0.9


def padded_2(cells, sides, width):
    for axis, dim in sides:
        count = lax.axis_size(axis)
        ends = count - 1
        head = lax.slice_in_dim(cells, 0, width, axis=dim)
        tail = lax.slice_in_dim(cells, cells.shape[dim] - width, cells.shape[dim], axis=dim)
        cells = jnp.concatenate(
            [
                lax.ppermute(tail, axis, [(i, (i + 1) % count) for i in range(ends)]),
                cells,
                lax.ppermute(head, axis, [((i + 1) % count, i) for i in range(ends)]),
            ],
            axis=dim,
        )
    return cells


def tap_rows(tap_table, band_kernel, first_row, row_count, height):
    row_ids = jnp.clip(first_row + jnp.arange(row_count), 0, height - 1)
    row_bands = row_ids // BAND
    band_slots = jnp.arange(band_kernel.shape[0])
    kernel_ids = jnp.sum(
        jnp.where(row_bands[:, None] == band_slots[None, :], band_kernel[None, :], 0), axis=1
    )
    kernel_slots = jnp.arange(tap_table.shape[0])
    picked = jnp.where(
        kernel_ids[:, None, None] == kernel_slots[None, :, None], tap_table[None, :, :], 0.0
    )
    return jnp.sum(picked, axis=1)


def blur_rows(padded, row_taps, row_count):
    summed = row_taps[:, 0][None, :, None] * padded[:, 0:row_count]
    for offset in range(1, 5):
        summed = (
            summed + row_taps[:, offset][None, :, None] * padded[:, offset : offset + row_count]
        )
    return summed


def back_rows(padded_quotient, outer_taps, row_count):
    summed = outer_taps[4 : 4 + row_count, 0][None, :, None] * padded_quotient[:, 4 : 4 + row_count]
    for offset in range(1, 5):
        start = 4 - offset
        summed = (
            summed
            + outer_taps[start : start + row_count, offset][None, :, None]
            * padded_quotient[:, start : start + row_count]
        )
    return summed


def temporal(series_block):
    frame_total, item_count, columns = series_block.shape
    values = series_block.astype(jnp.float32).reshape(frame_total, item_count * columns)
    frame_ids = jnp.arange(frame_total)
    at_ends = (frame_ids == 0) | (frame_ids == frame_total - 1)
    middle = (1.0 + SMOOTHING * jnp.where(at_ends, 1.0, 2.0)).astype(jnp.float32)
    sub_diag = jnp.where(frame_ids == 0, 0.0, -SMOOTHING).astype(jnp.float32)
    super_diag = jnp.where(frame_ids == frame_total - 1, 0.0, -SMOOTHING).astype(jnp.float32)
    baseline = lax.linalg.tridiagonal_solve(sub_diag, middle, super_diag, values)
    detrended = values - baseline
    earlier = jnp.concatenate(
        [jnp.zeros((1, values.shape[1]), jnp.float32), detrended[:-1]], axis=0
    )
    result = (detrended - DECAY_RATE * earlier).astype(jnp.bfloat16)
    return result.reshape(frame_total, item_count, columns)


def local(observed, kernels, band_kernel, masks):
    frames_dev, rows_dev, row_pixels = observed.shape
    height = rows_dev * lax.axis_size("row")
    tap_table = kernels / jnp.sum(kernels, axis=1, keepdims=True)
    first_row = lax.axis_index("row") * rows_dev
    own_taps = tap_rows(tap_table, band_kernel, first_row, rows_dev, height)
    outer_taps = tap_rows(tap_table, band_kernel, first_row - 2, rows_dev + 4, height)
    current = observed
    for iteration in range(ITERS):
        padded = padded_2(current, (("row", 1),), 2)
        blurred = blur_rows(padded, own_taps, rows_dev)
        quotient = observed / blurred
        padded_quotient = padded_2(quotient, (("row", 1),), 2)
        current = current * back_rows(padded_quotient, outer_taps, rows_dev)
    estimate = current.astype(jnp.bfloat16)
    spikes = temporal(lax.all_to_all(estimate, "frame", split_axis=2, concat_axis=0, tiled=True))
    frames_all, _, columns = spikes.shape
    tile_count = columns // TILE
    tile_sums = jnp.sum(
        spikes.reshape(frames_all, rows_dev * tile_count, TILE).astype(jnp.float32), axis=2
    )
    weights = masks.astype(jnp.float32).reshape(masks.shape[0], rows_dev * tile_count)
    local_sums = lax.dot_general(
        weights, tile_sums, (((1,), (1,)), ((), ())), precision=lax.Precision.HIGHEST
    )
    counts = jnp.sum(weights, axis=1)
    trace_sums, totals = (
        lax.psum_scatter(local_sums, ("frame", "row"), scatter_dimension=0, tiled=True),
        lax.psum_scatter(counts, ("frame", "row"), scatter_dimension=0, tiled=True),
    )
    traces = trace_sums / (TILE * totals[:, None])
    return (spikes, traces)


def halo_kernel(observed_ref, *refs):
    sent, own_ref = refs[:-1], refs[-1]
    even = lax.axis_index("row") % 2 == 0
    frames = observed_ref.shape[0] // HALVES
    own_ref[...] = observed_ref[...]
    for frame in range(observed_ref.shape[0]):
        inner_ref, outer_ref = sent[2 * (frame // frames) : 2 * (frame // frames) + 2]
        near = frame % frames * NEAR
        far = frames * NEAR + frame % frames * FAR
        bottom, top = observed_ref[frame, -NEAR:, :], observed_ref[frame, :NEAR, :]
        inner_ref[near : near + NEAR, :] = jnp.where(even, bottom, top)
        outer_ref[near : near + NEAR, :] = jnp.where(even, top, bottom)
        bottom, top = observed_ref[frame, -NEAR - FAR : -NEAR, :], observed_ref[frame, NEAR : NEAR + FAR, :]
        inner_ref[far : far + FAR, :] = jnp.where(even, bottom, top)
        outer_ref[far : far + FAR, :] = jnp.where(even, top, bottom)


def tables_kernel(band_ref, kernels_ref, masks_ref, taps_ref, back_ref, feet_ref, pad_ref, *, height):
    rows_dev = masks_ref.shape[0]
    span = rows_dev + 2 * MARGIN
    first_row = lax.axis_index("row") * rows_dev - MARGIN
    row_ids = lax.broadcasted_iota(jnp.int32, (BAND, TILE), 0)
    pad_ref[...] = jnp.zeros_like(pad_ref)
    for band in range(span // BAND):
        row = first_row + band * BAND
        inside = (row >= 0) & (row < height)
        kernel = band_ref[jnp.clip(row, 0, height - 1) // BAND]
        centre = jnp.full((BAND, TILE), kernels_ref[kernel, TAPS // 2], jnp.float32)
        start = band * BAND
        for slot, tap in enumerate(SIDES):
            weight = jnp.full((BAND, TILE), kernels_ref[kernel, tap], jnp.float32) / centre
            target = row_ids + (row + tap - TAPS // 2)
            weight = jnp.where(inside & (target >= 0) & (target < height), weight, 0.0)
            taps_ref[slot, start : start + BAND, :] = weight
            pad_ref[slot, BAND + start : 2 * BAND + start, :] = weight
    for slot, tap in enumerate(SIDES):
        start = BAND + TAPS // 2 - tap
        back_ref[slot] = pad_ref[slot, start : start + span, :]
    flat = jnp.concatenate([masks_ref[row].astype(jnp.float32) for row in range(rows_dev)], axis=0)
    positions = flat.shape[0]
    both = jnp.concatenate([flat, flat], axis=0).T
    half = feet_ref.shape[1]
    left = lax.broadcasted_iota(jnp.int32, (half, TILE), 1) < positions
    for block in range(feet_ref.shape[0]):
        start = 2 * block * half
        halves = jnp.where(left, both[start : start + half], both[start + half : start + 2 * half])
        feet_ref[block] = halves.astype(jnp.bfloat16)


def restore_half(taps_ref, back_ref, own_ref, inner_ref, outer_ref, out_ref, image_ref, current_ref, quotient_ref, half):
    n_frame = out_ref.shape[0]
    _, rows_dev, width = own_ref.shape
    frames = own_ref.shape[0] // HALVES
    tiles_dev = width // (n_frame * TILE)
    positions = rows_dev * tiles_dev
    units = [(frame, tile) for frame in range(frames) for tile in range(TOGETHER)]
    for ref in (image_ref, current_ref, quotient_ref):
        ref[...] = jnp.ones_like(ref)
    row = lax.axis_index("row")
    even = row % 2 == 0
    fill = jnp.where((row == 0) | (row == lax.axis_size("row") - 1), 1.0, 0.0)

    def columns_step(step, carry):
        for unit, (frame, tile) in enumerate(units):
            columns = pl.ds(pl.multiple_of((step * TOGETHER + tile) * TILE, TILE), TILE)
            near, far = frame * NEAR, frames * NEAR + frame * FAR
            start, stop = PAD + MARGIN, PAD + MARGIN + rows_dev
            inner, outer = inner_ref[near : near + NEAR, columns], outer_ref[near : near + NEAR, columns] + fill
            image_ref[unit, start - NEAR : start, :] = jnp.where(even, outer, inner)
            image_ref[unit, stop : stop + NEAR, :] = jnp.where(even, inner, outer)
            inner, outer = inner_ref[far : far + FAR, columns], outer_ref[far : far + FAR, columns] + fill
            image_ref[unit, start - NEAR - FAR : start - NEAR, :] = jnp.where(even, outer, inner)
            image_ref[unit, stop + NEAR : stop + NEAR + FAR, :] = jnp.where(even, inner, outer)
            image_ref[unit, start:stop, :] = own_ref[half * frames + frame, :, columns]
        source_ref = image_ref
        for (low, high), (back_low, back_high) in STEPS:
            for row in range(low, high, BAND):
                weights = [taps_ref[slot, row : row + BAND, :] for slot in range(len(SIDES))]
                for unit in range(len(units)):
                    rows = slice(PAD + row, PAD + row + BAND)
                    blurred = source_ref[unit, rows, :]
                    for weight, tap in zip(weights, SIDES):
                        start = PAD + row + tap - TAPS // 2
                        blurred = blurred + weight * source_ref[unit, start : start + BAND, :]
                    quotient_ref[unit, rows, :] = image_ref[unit, rows, :] / blurred
            for row in range(back_low, back_high, BAND):
                weights = [back_ref[slot, row : row + BAND, :] for slot in range(len(SIDES))]
                for unit in range(len(units)):
                    rows = slice(PAD + row, PAD + row + BAND)
                    spread = quotient_ref[unit, rows, :]
                    for weight, tap in zip(weights, SIDES):
                        start = PAD + row - tap + TAPS // 2
                        spread = spread + weight * quotient_ref[unit, start : start + BAND, :]
                    current_ref[unit, rows, :] = source_ref[unit, rows, :] * spread
            source_ref = current_ref
        steps = tiles_dev // TOGETHER
        first = pl.multiple_of(lax.rem(step, steps) * (TOGETHER * rows_dev), TOGETHER * rows_dev)
        for unit, (frame, tile) in enumerate(units):
            estimate = current_ref[unit, PAD + MARGIN : PAD + MARGIN + rows_dev, :].astype(jnp.bfloat16)
            start = first + ((half * frames + frame) * positions + tile * rows_dev)
            out_ref[step // steps, pl.ds(pl.multiple_of(start, rows_dev), rows_dev), :] = estimate
        return carry

    lax.fori_loop(0, n_frame * tiles_dev // TOGETHER, columns_step, 0)
    lane_tiles = lax.broadcasted_iota(jnp.int32, (TILE, TILE), 1) % tiles_dev
    gathered = jnp.zeros((frames * n_frame * rows_dev, TILE), jnp.float32)
    for tile in range(tiles_dev):
        pieces = []
        for frame in range(frames):
            start = (half * frames + frame) * positions + tile * rows_dev
            pieces += [out_ref[block, start : start + rows_dev, :] for block in range(n_frame)]
        picked = jnp.where(lane_tiles == tile, 1.0, 0.0).astype(jnp.bfloat16)
        gathered = gathered + jnp.dot(jnp.concatenate(pieces, axis=0), picked, preferred_element_type=jnp.float32)
    lanes = lax.broadcasted_iota(jnp.int32, (rows_dev, TILE), 1)
    here = lanes % positions // tiles_dev == lax.broadcasted_iota(jnp.int32, (rows_dev, TILE), 0)
    sums = []
    for place in range(frames * n_frame):
        part = jnp.where(here, gathered[place * rows_dev : (place + 1) * rows_dev], 0.0)
        sums.append(jnp.sum(part, axis=0, keepdims=True))
    return jnp.concatenate(sums, axis=0)


def first_kernel(taps_ref, back_ref, own_ref, inner_ref, outer_ref, out_ref, sums_ref, *scratch):
    sums_ref[...] = restore_half(taps_ref, back_ref, own_ref, inner_ref, outer_ref, out_ref, *scratch, 0)


def second_kernel(
    taps_ref, back_ref, own_ref, inner_ref, outer_ref, feet_ref, estimate_ref, sums_ref, out_ref, side_ref, *scratch
):
    sums = restore_half(taps_ref, back_ref, own_ref, inner_ref, outer_ref, out_ref, *scratch, 1)
    sums = jnp.concatenate([sums_ref[...], sums], axis=0)
    n_frame, done, _ = estimate_ref.shape
    positions = done * HALVES // own_ref.shape[0]
    high = sums.astype(jnp.bfloat16).astype(jnp.float32)
    split = jnp.where(lax.broadcasted_iota(jnp.int32, sums.shape, 1) < positions, high, sums - high).astype(jnp.bfloat16)
    for block in range(n_frame):
        out_ref[block, :done, :] = estimate_ref[block]
        side_ref[block, : split.shape[0], :] = split
        side_ref[block, split.shape[0] :, :] = feet_ref[block]


def deconvolved(series):
    total = len(series)
    factors = []
    for step in range(total):
        middle = 1.0 + SMOOTHING * (1.0 if step in (0, total - 1) else 2.0)
        if step:
            middle -= SMOOTHING * SMOOTHING * factors[-1]
        factors.append(1.0 / middle)
    forward = [series[0] * factors[0]]
    for step in range(1, total):
        forward.append((series[step] + SMOOTHING * forward[step - 1]) * factors[step])
    baseline = [None] * total
    baseline[total - 1] = forward[total - 1]
    for step in range(total - 2, -1, -1):
        baseline[step] = forward[step] + (SMOOTHING * factors[step]) * baseline[step + 1]
    result, earlier = [], None
    for step in range(total):
        detrended = series[step] - baseline[step]
        result.append(detrended if earlier is None else detrended - DECAY_RATE * earlier)
        earlier = detrended
    return result


def partial_kernel(*refs, positions):
    pieces, (out_ref, sums_ref, feet_ref) = refs[:-3], refs[-3:]
    n_frame = len(pieces)
    place = lax.axis_index("frame")
    rows = sums_ref.shape[0] // n_frame
    half = feet_ref.shape[1]
    for step, piece in enumerate(pieces):
        sums_ref[pl.ds(pl.multiple_of((place ^ step) * rows, rows), rows), :] = piece[:rows, :].astype(jnp.float32)
        feet_ref[place ^ step] = piece[rows:, :].astype(jnp.float32)
    series = [sums_ref[t * n_frame : (t + 1) * n_frame, :] for t in range(rows)]
    for t, sums in enumerate(deconvolved(series)):
        sums_ref[t * n_frame : (t + 1) * n_frame, :] = sums + pltpu.roll(sums, TILE // 2, 1)
    left = lax.broadcasted_iota(jnp.int32, (half, TILE), 1) < positions
    weights, sums = [], []
    extra = jnp.where(lax.broadcasted_iota(jnp.int32, (8, TILE), 0) == 0, 1.0, 0.0)
    for block in range(n_frame):
        feet = feet_ref[block]
        weights.append(jnp.concatenate([jnp.where(left, feet, 0.0), jnp.where(left, 0.0, feet)], axis=0))
        sums.append(jnp.concatenate([sums_ref[pl.ds(block, rows, stride=n_frame), :], extra], axis=0))
    totals = lax.dot_general(
        jnp.concatenate(weights, axis=1),
        jnp.concatenate(sums, axis=1),
        (((1,), (1,)), ((), ())),
        precision=lax.Precision.HIGHEST,
        preferred_element_type=jnp.float32,
    )
    share = out_ref.shape[1]
    out_ref[...] = jnp.zeros_like(out_ref)
    for row in range(out_ref.shape[0]):
        out_ref[row, :, : rows + 8] = totals[row * share : (row + 1) * share]


def temporal_kernel(*refs, frames):
    pieces, (spikes_ref, in_ref) = refs[:-2], refs[-2:]
    place = lax.axis_index("frame")
    for step, piece in enumerate(pieces):
        in_ref[place ^ step] = piece[...]
    total, rows_dev, columns = spikes_ref.shape
    positions = in_ref.shape[1] // frames
    for tile in range(columns // TILE):
        series = []
        for t in range(total):
            start = t % frames * positions + tile * rows_dev
            series.append(in_ref[t // frames, start : start + rows_dev, :].astype(jnp.float32))
        for t, spikes in enumerate(deconvolved(series)):
            spikes_ref[t, :, tile * TILE : (tile + 1) * TILE] = spikes.astype(spikes_ref.dtype)


def means_kernel(*refs):
    pieces, traces_ref = refs[:-1], refs[-1]
    frames = traces_ref.shape[1]
    total = pieces[0][...]
    for piece in pieces[1:]:
        total = total + piece[...]
    traces_ref[...] = total[:, :frames] / (TILE * total[:, frames : frames + 1])


def swapped(parts, axis):
    count, place = lax.axis_size(axis), lax.axis_index(axis)
    arrived = [lax.dynamic_index_in_dim(parts, place, 0, keepdims=False, allow_negative_indices=False)]
    for step in range(1, count):
        part = lax.dynamic_index_in_dim(parts, place ^ step, 0, keepdims=False, allow_negative_indices=False)
        arrived.append(lax.ppermute(part, axis, [(i, i ^ step) for i in range(count)]))
    return arrived


def in_turn(*arrays):
    done = []
    for array in arrays:
        done = list(lax.optimization_barrier((*done, array)))
    return done


def by_halo(observed, kernels, band_kernel, masks):
    n_frame, n_row = lax.axis_size("frame"), lax.axis_size("row")
    frames, rows_dev, width = observed.shape
    components, _, tiles_dev = masks.shape
    positions = rows_dev * tiles_dev
    share = components // (n_frame * n_row)
    span = rows_dev + 2 * MARGIN
    smem, vmem = pl.BlockSpec(memory_space=pltpu.SMEM), pl.BlockSpec(memory_space=pltpu.VMEM)

    def call(kernel, name, in_specs, out_shape, scratch=(), cost=1000):
        many = isinstance(out_shape, tuple)
        return pl.pallas_call(
            kernel,
            name=name,
            out_shape=out_shape,
            in_specs=in_specs,
            out_specs=(vmem,) * len(out_shape) if many else vmem,
            scratch_shapes=scratch,
            compiler_params=pltpu.CompilerParams(vmem_limit_bytes=16 << 20),
            cost_estimate=pl.CostEstimate(flops=cost, bytes_accessed=cost, transcendentals=0),
        )

    def array(*shape, dtype=jnp.float32):
        return jax.ShapeDtypeStruct(shape, dtype)

    half = frames // HALVES
    packed = array(half * (NEAR + FAR), width)
    *sent, own = call(halo_kernel, "halo", [vmem], (packed,) * (2 * HALVES) + (array(*observed.shape),))(observed)
    swaps = [
        [pair for i in range(first, n_row - 1, 2) for pair in ((i, i + 1), (i + 1, i))] for first in (0, 1)
    ]

    def swap(inner, outer):
        inner, outer = inner.astype(jnp.float16), outer.astype(jnp.float16)
        return inner, lax.ppermute(outer, "row", swaps[1]), lax.ppermute(inner, "row", swaps[0])

    last, *arrived1 = swap(*sent[:2])
    outer1, inner1 = in_turn(*arrived1)
    band_kernel, last = lax.optimization_barrier((band_kernel, last))
    taps, back, feet = call(
        functools.partial(tables_kernel, height=rows_dev * n_row),
        "tables",
        [smem, smem, vmem],
        (
            array(len(SIDES), span, TILE),
            array(len(SIDES), span, TILE),
            array(n_frame, n_row * share // 2, TILE, dtype=jnp.bfloat16),
        ),
        [pltpu.VMEM((len(SIDES), span + 2 * PAD, TILE), jnp.float32)],
    )(band_kernel, kernels, masks.transpose(1, 2, 0))
    *sent, taps = lax.optimization_barrier((*sent[2:], taps))
    _, *arrived2 = swap(*sent)
    buffers = [pltpu.VMEM((half * TOGETHER, span + 2 * PAD, TILE), jnp.float32)] * 3
    estimate, sums = call(
        first_kernel,
        "restore1",
        [vmem] * 5,
        (array(n_frame, half * positions, TILE, dtype=jnp.bfloat16), array(half * n_frame, TILE)),
        buffers,
    )(taps, back, own, inner1.astype(jnp.float32), outer1.astype(jnp.float32))
    estimate, outer2, inner2 = in_turn(estimate, *arrived2)
    side_rows = frames * n_frame + n_row * share // 2
    blocks, sides = call(
        second_kernel,
        "restore2",
        [vmem] * 8,
        (
            array(n_frame, frames * positions, TILE, dtype=jnp.bfloat16),
            array(n_frame, side_rows, TILE, dtype=jnp.bfloat16),
        ),
        buffers,
    )(taps, back, own, inner2.astype(jnp.float32), outer2.astype(jnp.float32), feet, estimate, sums)
    sides = swapped(sides, "frame")
    pieces = swapped(blocks, "frame")
    partial = call(
        functools.partial(partial_kernel, positions=positions),
        "partial",
        [vmem] * n_frame,
        array(n_row, share, TILE),
        [
            pltpu.VMEM((n_frame * frames * n_frame, TILE), jnp.float32),
            pltpu.VMEM((n_frame, n_row * share // 2, TILE), jnp.float32),
        ],
    )(*sides)
    shares = swapped(partial, "row")
    spikes = call(
        functools.partial(temporal_kernel, frames=frames),
        "temporal",
        [vmem] * n_frame,
        array(n_frame * frames, rows_dev, tiles_dev * TILE, dtype=jnp.bfloat16),
        [pltpu.VMEM((n_frame, frames * positions, TILE), jnp.bfloat16)],
    )(*pieces)
    spikes, *shares = in_turn(spikes, *shares[::-1])
    traces = call(means_kernel, "means", [vmem] * n_row, array(share, n_frame * frames))(*shares)
    return (spikes, traces)


def fits(mesh, observed, masks):
    frames_dev = observed.shape[0] // mesh.shape["frame"]
    rows_dev = masks.shape[1] // (mesh.shape["groups"] * mesh.shape["row"])
    tiles_dev = masks.shape[2] // mesh.shape["frame"]
    places = mesh.shape["frame"] * mesh.shape["row"]
    return (
        frames_dev == mesh.shape["frame"] == mesh.shape["row"] == 4
        and 2 * rows_dev * tiles_dev == TILE
        and rows_dev == 16
        and masks.shape[0] // places == 16
    )


def solution(mesh):
    in_specs = (
        P("frame", ("groups", "row"), None),
        P(),
        P("groups"),
        P(None, ("groups", "row"), "frame"),
    )
    out_specs = (P(None, ("groups", "row"), "frame"), P(("groups", "frame", "row"), None))

    def whole(observed, kernels, band_kernel, masks):
        body = by_halo if fits(mesh, observed, masks) else local
        mapped = jax.shard_map(body, mesh=mesh, in_specs=in_specs, out_specs=out_specs, check_vma=False)
        return mapped(observed, kernels, band_kernel, masks)

    return whole
```

```python
import functools

import jax
import jax.numpy as jnp
from jax import lax
from jax.experimental import pallas as pl
from jax.experimental.pallas import tpu as pltpu
from jax.sharding import PartitionSpec as P

TILE = 128
BAND = 8
ITERS = 3
TAPS = 5
NEAR, FAR = 8, 4
MARGIN = 2 * BAND
PAD = BAND
STEPS = (((6, 46), (8, 40)), ((10, 42), (12, 36)), ((14, 38), (16, 32)))
SIDES = (0, 1, 3, 4)
HALVES = 2
TOGETHER = 2


SMOOTHING = 1024.0
DECAY_RATE = 0.9


def padded_2(cells, sides, width):
    for axis, dim in sides:
        count = lax.axis_size(axis)
        ends = count - 1
        head = lax.slice_in_dim(cells, 0, width, axis=dim)
        tail = lax.slice_in_dim(cells, cells.shape[dim] - width, cells.shape[dim], axis=dim)
        cells = jnp.concatenate(
            [
                lax.ppermute(tail, axis, [(i, (i + 1) % count) for i in range(ends)]),
                cells,
                lax.ppermute(head, axis, [((i + 1) % count, i) for i in range(ends)]),
            ],
            axis=dim,
        )
    return cells


def tap_rows(tap_table, band_kernel, first_row, row_count, height):
    row_ids = jnp.clip(first_row + jnp.arange(row_count), 0, height - 1)
    row_bands = row_ids // BAND
    band_slots = jnp.arange(band_kernel.shape[0])
    kernel_ids = jnp.sum(
        jnp.where(row_bands[:, None] == band_slots[None, :], band_kernel[None, :], 0), axis=1
    )
    kernel_slots = jnp.arange(tap_table.shape[0])
    picked = jnp.where(
        kernel_ids[:, None, None] == kernel_slots[None, :, None], tap_table[None, :, :], 0.0
    )
    return jnp.sum(picked, axis=1)


def blur_rows(padded, row_taps, row_count):
    summed = row_taps[:, 0][None, :, None] * padded[:, 0:row_count]
    for offset in range(1, 5):
        summed = (
            summed + row_taps[:, offset][None, :, None] * padded[:, offset : offset + row_count]
        )
    return summed


def back_rows(padded_quotient, outer_taps, row_count):
    summed = outer_taps[4 : 4 + row_count, 0][None, :, None] * padded_quotient[:, 4 : 4 + row_count]
    for offset in range(1, 5):
        start = 4 - offset
        summed = (
            summed
            + outer_taps[start : start + row_count, offset][None, :, None]
            * padded_quotient[:, start : start + row_count]
        )
    return summed


def temporal(series_block):
    frame_total, item_count, columns = series_block.shape
    values = series_block.astype(jnp.float32).reshape(frame_total, item_count * columns)
    frame_ids = jnp.arange(frame_total)
    at_ends = (frame_ids == 0) | (frame_ids == frame_total - 1)
    middle = (1.0 + SMOOTHING * jnp.where(at_ends, 1.0, 2.0)).astype(jnp.float32)
    sub_diag = jnp.where(frame_ids == 0, 0.0, -SMOOTHING).astype(jnp.float32)
    super_diag = jnp.where(frame_ids == frame_total - 1, 0.0, -SMOOTHING).astype(jnp.float32)
    baseline = lax.linalg.tridiagonal_solve(sub_diag, middle, super_diag, values)
    detrended = values - baseline
    earlier = jnp.concatenate(
        [jnp.zeros((1, values.shape[1]), jnp.float32), detrended[:-1]], axis=0
    )
    result = (detrended - DECAY_RATE * earlier).astype(jnp.bfloat16)
    return result.reshape(frame_total, item_count, columns)


def local(observed, kernels, band_kernel, masks):
    frames_dev, rows_dev, row_pixels = observed.shape
    height = rows_dev * lax.axis_size("row")
    tap_table = kernels / jnp.sum(kernels, axis=1, keepdims=True)
    first_row = lax.axis_index("row") * rows_dev
    own_taps = tap_rows(tap_table, band_kernel, first_row, rows_dev, height)
    outer_taps = tap_rows(tap_table, band_kernel, first_row - 2, rows_dev + 4, height)
    current = observed
    for iteration in range(ITERS):
        padded = padded_2(current, (("row", 1),), 2)
        blurred = blur_rows(padded, own_taps, rows_dev)
        quotient = observed / blurred
        padded_quotient = padded_2(quotient, (("row", 1),), 2)
        current = current * back_rows(padded_quotient, outer_taps, rows_dev)
    estimate = current.astype(jnp.bfloat16)
    spikes = temporal(lax.all_to_all(estimate, "frame", split_axis=2, concat_axis=0, tiled=True))
    frames_all, _, columns = spikes.shape
    tile_count = columns // TILE
    tile_sums = jnp.sum(
        spikes.reshape(frames_all, rows_dev * tile_count, TILE).astype(jnp.float32), axis=2
    )
    weights = masks.astype(jnp.float32).reshape(masks.shape[0], rows_dev * tile_count)
    local_sums = lax.dot_general(
        weights, tile_sums, (((1,), (1,)), ((), ())), precision=lax.Precision.HIGHEST
    )
    counts = jnp.sum(weights, axis=1)
    trace_sums, totals = (
        lax.psum_scatter(local_sums, ("frame", "row"), scatter_dimension=0, tiled=True),
        lax.psum_scatter(counts, ("frame", "row"), scatter_dimension=0, tiled=True),
    )
    traces = trace_sums / (TILE * totals[:, None])
    return (spikes, traces)


def halo_kernel(observed_ref, *refs):
    sent, own_ref = refs[:-1], refs[-1]
    even = lax.axis_index("row") % 2 == 0
    frames = observed_ref.shape[0] // HALVES
    own_ref[...] = observed_ref[...]
    for frame in range(observed_ref.shape[0]):
        inner_ref, outer_ref = sent[2 * (frame // frames) : 2 * (frame // frames) + 2]
        near = frame % frames * NEAR
        far = frames * NEAR + frame % frames * FAR
        bottom, top = observed_ref[frame, -NEAR:, :], observed_ref[frame, :NEAR, :]
        inner_ref[near : near + NEAR, :] = jnp.where(even, bottom, top)
        outer_ref[near : near + NEAR, :] = jnp.where(even, top, bottom)
        bottom, top = observed_ref[frame, -NEAR - FAR : -NEAR, :], observed_ref[frame, NEAR : NEAR + FAR, :]
        inner_ref[far : far + FAR, :] = jnp.where(even, bottom, top)
        outer_ref[far : far + FAR, :] = jnp.where(even, top, bottom)


def taps_kernel(band_ref, kernels_ref, taps_ref, back_ref, pad_ref, *, height, rows_dev):
    span = rows_dev + 2 * MARGIN
    first_row = lax.axis_index("row") * rows_dev - MARGIN
    row_ids = lax.broadcasted_iota(jnp.int32, (BAND, TILE), 0)
    pad_ref[...] = jnp.zeros_like(pad_ref)
    for band in range(span // BAND):
        row = first_row + band * BAND
        inside = (row >= 0) & (row < height)
        kernel = band_ref[jnp.clip(row, 0, height - 1) // BAND]
        centre = jnp.full((BAND, TILE), kernels_ref[kernel, TAPS // 2], jnp.float32)
        start = band * BAND
        for slot, tap in enumerate(SIDES):
            weight = jnp.full((BAND, TILE), kernels_ref[kernel, tap], jnp.float32) / centre
            target = row_ids + (row + tap - TAPS // 2)
            weight = jnp.where(inside & (target >= 0) & (target < height), weight, 0.0)
            taps_ref[slot, start : start + BAND, :] = weight
            pad_ref[slot, BAND + start : 2 * BAND + start, :] = weight
    for slot, tap in enumerate(SIDES):
        start = BAND + TAPS // 2 - tap
        back_ref[slot] = pad_ref[slot, start : start + span, :]


def feet_kernel(masks_ref, feet_ref):
    rows_dev = masks_ref.shape[0]
    flat = jnp.concatenate([masks_ref[row].astype(jnp.float32) for row in range(rows_dev)], axis=0)
    positions = flat.shape[0]
    both = jnp.concatenate([flat, flat], axis=0).T
    half = feet_ref.shape[1]
    left = lax.broadcasted_iota(jnp.int32, (half, TILE), 1) < positions
    for block in range(feet_ref.shape[0]):
        start = 2 * block * half
        halves = jnp.where(left, both[start : start + half], both[start + half : start + 2 * half])
        feet_ref[block] = halves.astype(jnp.bfloat16)


def restore_half(taps_ref, back_ref, own_ref, inner_ref, outer_ref, out_ref, image_ref, current_ref, quotient_ref, half):
    n_frame = out_ref.shape[0]
    _, rows_dev, width = own_ref.shape
    frames = own_ref.shape[0] // HALVES
    tiles_dev = width // (n_frame * TILE)
    positions = rows_dev * tiles_dev
    units = [(frame, tile) for frame in range(frames) for tile in range(TOGETHER)]
    for ref in (image_ref, current_ref, quotient_ref):
        ref[...] = jnp.ones_like(ref)
    row = lax.axis_index("row")
    even = row % 2 == 0
    fill = jnp.where((row == 0) | (row == lax.axis_size("row") - 1), 1.0, 0.0)

    def columns_step(step, carry):
        for unit, (frame, tile) in enumerate(units):
            columns = pl.ds(pl.multiple_of((step * TOGETHER + tile) * TILE, TILE), TILE)
            near, far = frame * NEAR, frames * NEAR + frame * FAR
            start, stop = PAD + MARGIN, PAD + MARGIN + rows_dev
            inner, outer = inner_ref[near : near + NEAR, columns], outer_ref[near : near + NEAR, columns] + fill
            image_ref[unit, start - NEAR : start, :] = jnp.where(even, outer, inner)
            image_ref[unit, stop : stop + NEAR, :] = jnp.where(even, inner, outer)
            inner, outer = inner_ref[far : far + FAR, columns], outer_ref[far : far + FAR, columns] + fill
            image_ref[unit, start - NEAR - FAR : start - NEAR, :] = jnp.where(even, outer, inner)
            image_ref[unit, stop + NEAR : stop + NEAR + FAR, :] = jnp.where(even, inner, outer)
            image_ref[unit, start:stop, :] = own_ref[half * frames + frame, :, columns]
        source_ref = image_ref
        for (low, high), (back_low, back_high) in STEPS:
            for row in range(low, high, BAND):
                weights = [taps_ref[slot, row : row + BAND, :] for slot in range(len(SIDES))]
                for unit in range(len(units)):
                    rows = slice(PAD + row, PAD + row + BAND)
                    blurred = source_ref[unit, rows, :]
                    for weight, tap in zip(weights, SIDES):
                        start = PAD + row + tap - TAPS // 2
                        blurred = blurred + weight * source_ref[unit, start : start + BAND, :]
                    quotient_ref[unit, rows, :] = image_ref[unit, rows, :] / blurred
            for row in range(back_low, back_high, BAND):
                weights = [back_ref[slot, row : row + BAND, :] for slot in range(len(SIDES))]
                for unit in range(len(units)):
                    rows = slice(PAD + row, PAD + row + BAND)
                    spread = quotient_ref[unit, rows, :]
                    for weight, tap in zip(weights, SIDES):
                        start = PAD + row - tap + TAPS // 2
                        spread = spread + weight * quotient_ref[unit, start : start + BAND, :]
                    current_ref[unit, rows, :] = source_ref[unit, rows, :] * spread
            source_ref = current_ref
        steps = tiles_dev // TOGETHER
        first = pl.multiple_of(lax.rem(step, steps) * (TOGETHER * rows_dev), TOGETHER * rows_dev)
        for unit, (frame, tile) in enumerate(units):
            estimate = current_ref[unit, PAD + MARGIN : PAD + MARGIN + rows_dev, :].astype(jnp.bfloat16)
            start = first + ((half * frames + frame) * positions + tile * rows_dev)
            out_ref[step // steps, pl.ds(pl.multiple_of(start, rows_dev), rows_dev), :] = estimate
        return carry

    lax.fori_loop(0, n_frame * tiles_dev // TOGETHER, columns_step, 0)
    lane_tiles = lax.broadcasted_iota(jnp.int32, (TILE, TILE), 1) % tiles_dev
    gathered = jnp.zeros((frames * n_frame * rows_dev, TILE), jnp.float32)
    for tile in range(tiles_dev):
        pieces = []
        for frame in range(frames):
            start = (half * frames + frame) * positions + tile * rows_dev
            pieces += [out_ref[block, start : start + rows_dev, :] for block in range(n_frame)]
        picked = jnp.where(lane_tiles == tile, 1.0, 0.0).astype(jnp.bfloat16)
        gathered = gathered + jnp.dot(jnp.concatenate(pieces, axis=0), picked, preferred_element_type=jnp.float32)
    lanes = lax.broadcasted_iota(jnp.int32, (rows_dev, TILE), 1)
    here = lanes % positions // tiles_dev == lax.broadcasted_iota(jnp.int32, (rows_dev, TILE), 0)
    sums = []
    for place in range(frames * n_frame):
        part = jnp.where(here, gathered[place * rows_dev : (place + 1) * rows_dev], 0.0)
        sums.append(jnp.sum(part, axis=0, keepdims=True))
    return jnp.concatenate(sums, axis=0)


def first_kernel(taps_ref, back_ref, own_ref, inner_ref, outer_ref, out_ref, sums_ref, *scratch):
    sums_ref[...] = restore_half(taps_ref, back_ref, own_ref, inner_ref, outer_ref, out_ref, *scratch, 0)


def second_kernel(
    taps_ref, back_ref, own_ref, inner_ref, outer_ref, feet_ref, estimate_ref, sums_ref, out_ref, side_ref, *scratch
):
    sums = restore_half(taps_ref, back_ref, own_ref, inner_ref, outer_ref, out_ref, *scratch, 1)
    sums = jnp.concatenate([sums_ref[...], sums], axis=0)
    n_frame, done, _ = estimate_ref.shape
    positions = done * HALVES // own_ref.shape[0]
    high = sums.astype(jnp.bfloat16).astype(jnp.float32)
    split = jnp.where(lax.broadcasted_iota(jnp.int32, sums.shape, 1) < positions, high, sums - high).astype(jnp.bfloat16)
    for block in range(n_frame):
        out_ref[block, :done, :] = estimate_ref[block]
        side_ref[block, : split.shape[0], :] = split
        side_ref[block, split.shape[0] :, :] = feet_ref[block]


def deconvolved(series):
    total = len(series)
    factors = []
    for step in range(total):
        middle = 1.0 + SMOOTHING * (1.0 if step in (0, total - 1) else 2.0)
        if step:
            middle -= SMOOTHING * SMOOTHING * factors[-1]
        factors.append(1.0 / middle)
    forward = [series[0] * factors[0]]
    for step in range(1, total):
        forward.append((series[step] + SMOOTHING * forward[step - 1]) * factors[step])
    baseline = [None] * total
    baseline[total - 1] = forward[total - 1]
    for step in range(total - 2, -1, -1):
        baseline[step] = forward[step] + (SMOOTHING * factors[step]) * baseline[step + 1]
    result, earlier = [], None
    for step in range(total):
        detrended = series[step] - baseline[step]
        result.append(detrended if earlier is None else detrended - DECAY_RATE * earlier)
        earlier = detrended
    return result


def partial_kernel(*refs, positions):
    pieces, (out_ref, sums_ref, feet_ref) = refs[:-3], refs[-3:]
    n_frame = len(pieces)
    place = lax.axis_index("frame")
    rows = sums_ref.shape[0] // n_frame
    half = feet_ref.shape[1]
    for step, piece in enumerate(pieces):
        sums_ref[pl.ds(pl.multiple_of((place ^ step) * rows, rows), rows), :] = piece[:rows, :].astype(jnp.float32)
        feet_ref[place ^ step] = piece[rows:, :].astype(jnp.float32)
    series = [sums_ref[t * n_frame : (t + 1) * n_frame, :] for t in range(rows)]
    for t, sums in enumerate(deconvolved(series)):
        sums_ref[t * n_frame : (t + 1) * n_frame, :] = sums + pltpu.roll(sums, TILE // 2, 1)
    left = lax.broadcasted_iota(jnp.int32, (half, TILE), 1) < positions
    weights, sums = [], []
    extra = jnp.where(lax.broadcasted_iota(jnp.int32, (8, TILE), 0) == 0, 1.0, 0.0)
    for block in range(n_frame):
        feet = feet_ref[block]
        weights.append(jnp.concatenate([jnp.where(left, feet, 0.0), jnp.where(left, 0.0, feet)], axis=0))
        sums.append(jnp.concatenate([sums_ref[pl.ds(block, rows, stride=n_frame), :], extra], axis=0))
    totals = lax.dot_general(
        jnp.concatenate(weights, axis=1),
        jnp.concatenate(sums, axis=1),
        (((1,), (1,)), ((), ())),
        precision=lax.Precision.HIGHEST,
        preferred_element_type=jnp.float32,
    )
    share = out_ref.shape[1]
    out_ref[...] = jnp.zeros_like(out_ref)
    for row in range(out_ref.shape[0]):
        out_ref[row, :, : rows + 8] = totals[row * share : (row + 1) * share]


def temporal_kernel(*refs, frames):
    pieces, (spikes_ref, in_ref) = refs[:-2], refs[-2:]
    place = lax.axis_index("frame")
    for step, piece in enumerate(pieces):
        in_ref[place ^ step] = piece[...]
    total, rows_dev, columns = spikes_ref.shape
    positions = in_ref.shape[1] // frames
    for tile in range(columns // TILE):
        series = []
        for t in range(total):
            start = t % frames * positions + tile * rows_dev
            series.append(in_ref[t // frames, start : start + rows_dev, :].astype(jnp.float32))
        for t, spikes in enumerate(deconvolved(series)):
            spikes_ref[t, :, tile * TILE : (tile + 1) * TILE] = spikes.astype(spikes_ref.dtype)


def means_kernel(*refs):
    pieces, traces_ref = refs[:-1], refs[-1]
    frames = traces_ref.shape[1]
    total = pieces[0][...]
    for piece in pieces[1:]:
        total = total + piece[...]
    traces_ref[...] = total[:, :frames] / (TILE * total[:, frames : frames + 1])


def swapped(parts, axis):
    count, place = lax.axis_size(axis), lax.axis_index(axis)
    arrived = [lax.dynamic_index_in_dim(parts, place, 0, keepdims=False, allow_negative_indices=False)]
    for step in range(1, count):
        part = lax.dynamic_index_in_dim(parts, place ^ step, 0, keepdims=False, allow_negative_indices=False)
        arrived.append(lax.ppermute(part, axis, [(i, i ^ step) for i in range(count)]))
    return arrived


def in_turn(*arrays):
    done = []
    for array in arrays:
        done = list(lax.optimization_barrier((*done, array)))
    return done


def by_halo(observed, kernels, band_kernel, masks):
    n_frame, n_row = lax.axis_size("frame"), lax.axis_size("row")
    frames, rows_dev, width = observed.shape
    components, _, tiles_dev = masks.shape
    positions = rows_dev * tiles_dev
    share = components // (n_frame * n_row)
    span = rows_dev + 2 * MARGIN
    smem, vmem = pl.BlockSpec(memory_space=pltpu.SMEM), pl.BlockSpec(memory_space=pltpu.VMEM)

    def call(kernel, name, in_specs, out_shape, scratch=(), cost=1000):
        many = isinstance(out_shape, tuple)
        return pl.pallas_call(
            kernel,
            name=name,
            out_shape=out_shape,
            in_specs=in_specs,
            out_specs=(vmem,) * len(out_shape) if many else vmem,
            scratch_shapes=scratch,
            compiler_params=pltpu.CompilerParams(vmem_limit_bytes=16 << 20),
            cost_estimate=pl.CostEstimate(flops=cost, bytes_accessed=cost, transcendentals=0),
        )

    def array(*shape, dtype=jnp.float32):
        return jax.ShapeDtypeStruct(shape, dtype)

    half = frames // HALVES
    packed = array(half * (NEAR + FAR), width)
    taps, back = call(
        functools.partial(taps_kernel, height=rows_dev * n_row, rows_dev=rows_dev),
        "taps",
        [smem, smem],
        (array(len(SIDES), span, TILE),) * 2,
        [pltpu.VMEM((len(SIDES), span + 2 * PAD, TILE), jnp.float32)],
    )(band_kernel, kernels)
    *sent, own = call(halo_kernel, "halo", [vmem], (packed,) * (2 * HALVES) + (array(*observed.shape),))(observed)
    swaps = [
        [pair for i in range(first, n_row - 1, 2) for pair in ((i, i + 1), (i + 1, i))] for first in (0, 1)
    ]
    taps, *sent = lax.optimization_barrier((taps, *sent))
    sent = [rows.astype(jnp.float16) for rows in sent]
    inner1, outer1, inner2, outer2 = (lax.ppermute(rows, "row", swaps[i % 2]) for i, rows in enumerate(sent))
    buffers = [pltpu.VMEM((half * TOGETHER, span + 2 * PAD, TILE), jnp.float32)] * 3
    estimate, sums = call(
        first_kernel,
        "restore1",
        [vmem] * 5,
        (array(n_frame, half * positions, TILE, dtype=jnp.bfloat16), array(half * n_frame, TILE)),
        buffers,
    )(taps, back, own, inner1.astype(jnp.float32), outer1.astype(jnp.float32))
    estimate, masks = in_turn(estimate, masks.transpose(1, 2, 0))
    feet = call(feet_kernel, "feet", [vmem], array(n_frame, n_row * share // 2, TILE, dtype=jnp.bfloat16))(masks)
    feet, outer2, inner2 = in_turn(feet, outer2, inner2)
    side_rows = frames * n_frame + n_row * share // 2
    blocks, sides = call(
        second_kernel,
        "restore2",
        [vmem] * 8,
        (
            array(n_frame, frames * positions, TILE, dtype=jnp.bfloat16),
            array(n_frame, side_rows, TILE, dtype=jnp.bfloat16),
        ),
        buffers,
    )(taps, back, own, inner2.astype(jnp.float32), outer2.astype(jnp.float32), feet, estimate, sums)
    sides = swapped(sides, "frame")
    pieces = swapped(blocks, "frame")
    partial = call(
        functools.partial(partial_kernel, positions=positions),
        "partial",
        [vmem] * n_frame,
        array(n_row, share, TILE),
        [
            pltpu.VMEM((n_frame * frames * n_frame, TILE), jnp.float32),
            pltpu.VMEM((n_frame, n_row * share // 2, TILE), jnp.float32),
        ],
    )(*sides)
    shares = swapped(partial, "row")
    spikes = call(
        functools.partial(temporal_kernel, frames=frames),
        "temporal",
        [vmem] * n_frame,
        array(n_frame * frames, rows_dev, tiles_dev * TILE, dtype=jnp.bfloat16),
        [pltpu.VMEM((n_frame, frames * positions, TILE), jnp.bfloat16)],
    )(*pieces)
    spikes, *shares = in_turn(spikes, *shares[::-1])
    traces = call(means_kernel, "means", [vmem] * n_row, array(share, n_frame * frames))(*shares)
    return (spikes, traces)


def fits(mesh, observed, masks):
    frames_dev = observed.shape[0] // mesh.shape["frame"]
    rows_dev = masks.shape[1] // (mesh.shape["groups"] * mesh.shape["row"])
    tiles_dev = masks.shape[2] // mesh.shape["frame"]
    places = mesh.shape["frame"] * mesh.shape["row"]
    return (
        frames_dev == mesh.shape["frame"] == mesh.shape["row"] == 4
        and 2 * rows_dev * tiles_dev == TILE
        and rows_dev == 16
        and masks.shape[0] // places == 16
    )


def solution(mesh):
    in_specs = (
        P("frame", ("groups", "row"), None),
        P(),
        P("groups"),
        P(None, ("groups", "row"), "frame"),
    )
    out_specs = (P(None, ("groups", "row"), "frame"), P(("groups", "frame", "row"), None))

    def whole(observed, kernels, band_kernel, masks):
        body = by_halo if fits(mesh, observed, masks) else local
        mapped = jax.shard_map(body, mesh=mesh, in_specs=in_specs, out_specs=out_specs, check_vma=False)
        return mapped(observed, kernels, band_kernel, masks)

    return whole
```

```python
import functools

import jax
import jax.numpy as jnp
from jax import lax
from jax.experimental import pallas as pl
from jax.experimental.pallas import tpu as pltpu
from jax.sharding import PartitionSpec as P

TILE = 128
BAND = 8
ITERS = 3
TAPS = 5
NEAR, FAR = 8, 4
MARGIN = 2 * BAND
PAD = BAND
STEPS = (((6, 46), (8, 40)), ((10, 42), (12, 36)), ((14, 38), (16, 32)))
SIDES = (0, 1, 3, 4)


SMOOTHING = 1024.0
DECAY_RATE = 0.9


def padded_2(cells, sides, width):
    for axis, dim in sides:
        count = lax.axis_size(axis)
        ends = count - 1
        head = lax.slice_in_dim(cells, 0, width, axis=dim)
        tail = lax.slice_in_dim(cells, cells.shape[dim] - width, cells.shape[dim], axis=dim)
        cells = jnp.concatenate(
            [
                lax.ppermute(tail, axis, [(i, (i + 1) % count) for i in range(ends)]),
                cells,
                lax.ppermute(head, axis, [((i + 1) % count, i) for i in range(ends)]),
            ],
            axis=dim,
        )
    return cells


def tap_rows(tap_table, band_kernel, first_row, row_count, height):
    row_ids = jnp.clip(first_row + jnp.arange(row_count), 0, height - 1)
    row_bands = row_ids // BAND
    band_slots = jnp.arange(band_kernel.shape[0])
    kernel_ids = jnp.sum(
        jnp.where(row_bands[:, None] == band_slots[None, :], band_kernel[None, :], 0), axis=1
    )
    kernel_slots = jnp.arange(tap_table.shape[0])
    picked = jnp.where(
        kernel_ids[:, None, None] == kernel_slots[None, :, None], tap_table[None, :, :], 0.0
    )
    return jnp.sum(picked, axis=1)


def blur_rows(padded, row_taps, row_count):
    summed = row_taps[:, 0][None, :, None] * padded[:, 0:row_count]
    for offset in range(1, 5):
        summed = (
            summed + row_taps[:, offset][None, :, None] * padded[:, offset : offset + row_count]
        )
    return summed


def back_rows(padded_quotient, outer_taps, row_count):
    summed = outer_taps[4 : 4 + row_count, 0][None, :, None] * padded_quotient[:, 4 : 4 + row_count]
    for offset in range(1, 5):
        start = 4 - offset
        summed = (
            summed
            + outer_taps[start : start + row_count, offset][None, :, None]
            * padded_quotient[:, start : start + row_count]
        )
    return summed


def temporal(series_block):
    frame_total, item_count, columns = series_block.shape
    values = series_block.astype(jnp.float32).reshape(frame_total, item_count * columns)
    frame_ids = jnp.arange(frame_total)
    at_ends = (frame_ids == 0) | (frame_ids == frame_total - 1)
    middle = (1.0 + SMOOTHING * jnp.where(at_ends, 1.0, 2.0)).astype(jnp.float32)
    sub_diag = jnp.where(frame_ids == 0, 0.0, -SMOOTHING).astype(jnp.float32)
    super_diag = jnp.where(frame_ids == frame_total - 1, 0.0, -SMOOTHING).astype(jnp.float32)
    baseline = lax.linalg.tridiagonal_solve(sub_diag, middle, super_diag, values)
    detrended = values - baseline
    earlier = jnp.concatenate(
        [jnp.zeros((1, values.shape[1]), jnp.float32), detrended[:-1]], axis=0
    )
    result = (detrended - DECAY_RATE * earlier).astype(jnp.bfloat16)
    return result.reshape(frame_total, item_count, columns)


def local(observed, kernels, band_kernel, masks):
    frames_dev, rows_dev, row_pixels = observed.shape
    height = rows_dev * lax.axis_size("row")
    tap_table = kernels / jnp.sum(kernels, axis=1, keepdims=True)
    first_row = lax.axis_index("row") * rows_dev
    own_taps = tap_rows(tap_table, band_kernel, first_row, rows_dev, height)
    outer_taps = tap_rows(tap_table, band_kernel, first_row - 2, rows_dev + 4, height)
    current = observed
    for iteration in range(ITERS):
        padded = padded_2(current, (("row", 1),), 2)
        blurred = blur_rows(padded, own_taps, rows_dev)
        quotient = observed / blurred
        padded_quotient = padded_2(quotient, (("row", 1),), 2)
        current = current * back_rows(padded_quotient, outer_taps, rows_dev)
    estimate = current.astype(jnp.bfloat16)
    spikes = temporal(lax.all_to_all(estimate, "frame", split_axis=2, concat_axis=0, tiled=True))
    frames_all, _, columns = spikes.shape
    tile_count = columns // TILE
    tile_sums = jnp.sum(
        spikes.reshape(frames_all, rows_dev * tile_count, TILE).astype(jnp.float32), axis=2
    )
    weights = masks.astype(jnp.float32).reshape(masks.shape[0], rows_dev * tile_count)
    local_sums = lax.dot_general(
        weights, tile_sums, (((1,), (1,)), ((), ())), precision=lax.Precision.HIGHEST
    )
    counts = jnp.sum(weights, axis=1)
    trace_sums, totals = (
        lax.psum_scatter(local_sums, ("frame", "row"), scatter_dimension=0, tiled=True),
        lax.psum_scatter(counts, ("frame", "row"), scatter_dimension=0, tiled=True),
    )
    traces = trace_sums / (TILE * totals[:, None])
    return (spikes, traces)


def halo_kernel(observed_ref, inner_ref, outer_ref, own_ref):
    even = lax.axis_index("row") % 2 == 0
    frames = observed_ref.shape[0]
    own_ref[...] = observed_ref[...]
    for frame in range(frames):
        near = frame * NEAR
        far = frames * NEAR + frame * FAR
        bottom, top = observed_ref[frame, -NEAR:, :], observed_ref[frame, :NEAR, :]
        inner_ref[near : near + NEAR, :] = jnp.where(even, bottom, top)
        outer_ref[near : near + NEAR, :] = jnp.where(even, top, bottom)
        bottom, top = observed_ref[frame, -NEAR - FAR : -NEAR, :], observed_ref[frame, NEAR : NEAR + FAR, :]
        inner_ref[far : far + FAR, :] = jnp.where(even, bottom, top)
        outer_ref[far : far + FAR, :] = jnp.where(even, top, bottom)


def taps_kernel(band_ref, kernels_ref, taps_ref, back_ref, pad_ref, *, height, rows_dev):
    span = rows_dev + 2 * MARGIN
    first_row = lax.axis_index("row") * rows_dev - MARGIN
    row_ids = lax.broadcasted_iota(jnp.int32, (BAND, TILE), 0)
    pad_ref[...] = jnp.zeros_like(pad_ref)
    for band in range(span // BAND):
        row = first_row + band * BAND
        inside = (row >= 0) & (row < height)
        kernel = band_ref[jnp.clip(row, 0, height - 1) // BAND]
        centre = jnp.full((BAND, TILE), kernels_ref[kernel, TAPS // 2], jnp.float32)
        start = band * BAND
        for slot, tap in enumerate(SIDES):
            weight = jnp.full((BAND, TILE), kernels_ref[kernel, tap], jnp.float32) / centre
            target = row_ids + (row + tap - TAPS // 2)
            weight = jnp.where(inside & (target >= 0) & (target < height), weight, 0.0)
            taps_ref[slot, start : start + BAND, :] = weight
            pad_ref[slot, BAND + start : 2 * BAND + start, :] = weight
    for slot, tap in enumerate(SIDES):
        start = BAND + TAPS // 2 - tap
        back_ref[slot] = pad_ref[slot, start : start + span, :]


def feet_kernel(masks_ref, feet_ref, *, n_frame, n_row):
    flat = jnp.concatenate([masks_ref[row].astype(jnp.float32) for row in range(masks_ref.shape[0])], axis=0)
    positions = flat.shape[0]
    both = jnp.concatenate([flat, flat], axis=0).T
    share = both.shape[0] // (n_frame * n_row)
    left = lax.broadcasted_iota(jnp.int32, (share, TILE), 1) < positions
    half = n_frame * n_row // 2
    starts = [(block * n_row + row) * share for row in range(n_row) for block in range(n_frame)]
    for place in range(half):
        first, second = starts[place], starts[place + half]
        halves = jnp.where(left, both[first : first + share], both[second : second + share])
        feet_ref[place * share : (place + 1) * share, :] = halves.astype(jnp.bfloat16)


def gather_kernel(*refs):
    pieces, feet_ref = refs[:-1], refs[-1]
    place = lax.axis_index("frame")
    half = feet_ref.shape[0] // 2
    left = lax.broadcasted_iota(jnp.int32, (half, TILE), 1) < TILE // 2
    for step, piece in enumerate(pieces):
        columns = pl.ds(pl.multiple_of((place ^ step) * TILE, TILE), TILE)
        feet = piece[...].astype(jnp.float32)
        feet_ref[:half, columns] = jnp.where(left, feet, 0.0).astype(jnp.bfloat16)
        feet_ref[half:, columns] = jnp.where(left, 0.0, feet).astype(jnp.bfloat16)


def restore_kernel(
    taps_ref, back_ref, feet_ref, own_ref, inner_ref, outer_ref, out_ref, sums_ref, image_ref, current_ref, quotient_ref
):
    n_frame = out_ref.shape[0]
    frames, rows_dev, width = own_ref.shape
    tiles_dev = width // (n_frame * TILE)
    positions = rows_dev * tiles_dev
    for ref in (image_ref, current_ref, quotient_ref):
        ref[...] = jnp.ones_like(ref)
    row = lax.axis_index("row")
    even = row % 2 == 0
    above = jnp.where(row == 0, 1.0, 0.0)
    below = jnp.where(row == lax.axis_size("row") - 1, 1.0, 0.0)

    def columns_step(step, carry):
        columns = pl.ds(pl.multiple_of(step * TILE, TILE), TILE)
        for frame in range(frames):
            near, far = frame * NEAR, frames * NEAR + frame * FAR
            start, stop = PAD + MARGIN, PAD + MARGIN + rows_dev
            inner, outer = inner_ref[near : near + NEAR, columns], outer_ref[near : near + NEAR, columns]
            image_ref[frame, start - NEAR : start, :] = jnp.where(even, outer, inner) + above
            image_ref[frame, stop : stop + NEAR, :] = jnp.where(even, inner, outer) + below
            inner, outer = inner_ref[far : far + FAR, columns], outer_ref[far : far + FAR, columns]
            image_ref[frame, start - NEAR - FAR : start - NEAR, :] = jnp.where(even, outer, inner) + above
            image_ref[frame, stop + NEAR : stop + NEAR + FAR, :] = jnp.where(even, inner, outer) + below
            image_ref[frame, start:stop, :] = own_ref[frame, :, columns]
        source_ref = image_ref
        for (first, last), (back_first, back_last) in STEPS:
            for row in range(first, last, BAND):
                weights = [taps_ref[slot, row : row + BAND, :] for slot in range(len(SIDES))]
                for frame in range(frames):
                    rows = slice(PAD + row, PAD + row + BAND)
                    blurred = source_ref[frame, rows, :]
                    for weight, tap in zip(weights, SIDES):
                        start = PAD + row + tap - TAPS // 2
                        blurred = blurred + weight * source_ref[frame, start : start + BAND, :]
                    quotient_ref[frame, rows, :] = image_ref[frame, rows, :] / blurred
            for row in range(back_first, back_last, BAND):
                weights = [back_ref[slot, row : row + BAND, :] for slot in range(len(SIDES))]
                for frame in range(frames):
                    rows = slice(PAD + row, PAD + row + BAND)
                    spread = quotient_ref[frame, rows, :]
                    for weight, tap in zip(weights, SIDES):
                        start = PAD + row - tap + TAPS // 2
                        spread = spread + weight * quotient_ref[frame, start : start + BAND, :]
                    current_ref[frame, rows, :] = source_ref[frame, rows, :] * spread
            source_ref = current_ref
        first = pl.multiple_of(lax.rem(step, tiles_dev) * rows_dev, rows_dev)
        for frame in range(frames):
            estimate = current_ref[frame, PAD + MARGIN : PAD + MARGIN + rows_dev, :].astype(jnp.bfloat16)
            start = pl.multiple_of(first + frame * positions, rows_dev)
            out_ref[step // tiles_dev, pl.ds(start, rows_dev), :] = estimate
        return carry

    lax.fori_loop(0, n_frame * tiles_dev, columns_step, 0)
    lane_tiles = lax.broadcasted_iota(jnp.int32, (TILE, TILE), 1) % tiles_dev
    gathered = jnp.zeros((frames * n_frame * rows_dev, TILE), jnp.float32)
    for tile in range(tiles_dev):
        pieces = []
        for frame in range(frames):
            start = frame * positions + tile * rows_dev
            pieces += [out_ref[block, start : start + rows_dev, :] for block in range(n_frame)]
        picked = jnp.where(lane_tiles == tile, 1.0, 0.0).astype(jnp.bfloat16)
        gathered = gathered + jnp.dot(jnp.concatenate(pieces, axis=0), picked, preferred_element_type=jnp.float32)
    lanes = lax.broadcasted_iota(jnp.int32, (rows_dev, TILE), 1)
    here = lanes % positions // tiles_dev == lax.broadcasted_iota(jnp.int32, (rows_dev, TILE), 0)
    series = []
    for frame in range(frames):
        sums = []
        for block in range(n_frame):
            start = (frame * n_frame + block) * rows_dev
            sums.append(jnp.sum(jnp.where(here, gathered[start : start + rows_dev], 0.0), axis=0, keepdims=True))
        series.append(jnp.concatenate(sums, axis=1))
    series = jnp.concatenate(series, axis=0)
    parts = []
    for _ in range(3):
        part = series.astype(jnp.bfloat16).astype(jnp.float32)
        series = series - part
        parts.append(part)
    parts.append(jnp.ones((4, n_frame * TILE), jnp.float32))
    totals = lax.dot_general(
        jnp.concatenate(parts, axis=0).astype(jnp.bfloat16),
        feet_ref[...],
        (((1,), (1,)), ((), ())),
        preferred_element_type=jnp.float32,
    )
    sums = totals[:frames] + totals[frames : 2 * frames] + totals[2 * frames : 3 * frames]
    sums = jnp.concatenate([sums, totals[3 * frames :]], axis=0)
    share = sums.shape[1] // sums_ref.shape[0]
    sums_ref[...] = jnp.zeros_like(sums_ref)
    for row in range(sums_ref.shape[0]):
        sums_ref[row, :, :share] = sums[:, row * share : (row + 1) * share]


def deconvolved(series):
    total = len(series)
    factors = []
    for step in range(total):
        middle = 1.0 + SMOOTHING * (1.0 if step in (0, total - 1) else 2.0)
        if step:
            middle -= SMOOTHING * SMOOTHING * factors[-1]
        factors.append(1.0 / middle)
    forward = [series[0] * factors[0]]
    for step in range(1, total):
        forward.append((series[step] + SMOOTHING * forward[step - 1]) * factors[step])
    baseline = [None] * total
    baseline[total - 1] = forward[total - 1]
    for step in range(total - 2, -1, -1):
        baseline[step] = forward[step] + (SMOOTHING * factors[step]) * baseline[step + 1]
    result, earlier = [], None
    for step in range(total):
        detrended = series[step] - baseline[step]
        result.append(detrended if earlier is None else detrended - DECAY_RATE * earlier)
        earlier = detrended
    return result


def temporal_kernel(*refs, frames):
    pieces, (spikes_ref, in_ref) = refs[:-2], refs[-2:]
    place = lax.axis_index("frame")
    for step, piece in enumerate(pieces):
        in_ref[place ^ step] = piece[...]
    total, rows_dev, columns = spikes_ref.shape
    positions = in_ref.shape[1] // frames
    for tile in range(columns // TILE):
        series = []
        for t in range(total):
            start = t % frames * positions + tile * rows_dev
            series.append(in_ref[t // frames, start : start + rows_dev, :].astype(jnp.float32))
        for t, spikes in enumerate(deconvolved(series)):
            spikes_ref[t, :, tile * TILE : (tile + 1) * TILE] = spikes.astype(spikes_ref.dtype)


def add_kernel(*refs):
    total = refs[0][...]
    for piece in refs[1:-1]:
        total = total + piece[...]
    refs[-1][...] = total


def means_kernel(*refs, frames):
    pieces, (traces_ref, sums_ref) = refs[:-2], refs[-2:]
    place = lax.axis_index("frame")
    for step, piece in enumerate(pieces):
        sums_ref[place ^ step] = piece[...]
    share, total = traces_ref.shape
    series = deconvolved([sums_ref[t // frames, t % frames : t % frames + 1, :] for t in range(total)])
    means = jnp.concatenate(series, axis=0) / (TILE * sums_ref[0, frames : frames + 1, :])
    means = pltpu.roll(means, lax.rem(TILE - place * share, TILE), 1)
    traces_ref[...] = means.T[:share]


def swapped(parts, axis):
    count, place = lax.axis_size(axis), lax.axis_index(axis)
    arrived = [lax.dynamic_index_in_dim(parts, place, 0, keepdims=False, allow_negative_indices=False)]
    for step in range(1, count):
        part = lax.dynamic_index_in_dim(parts, place ^ step, 0, keepdims=False, allow_negative_indices=False)
        arrived.append(lax.ppermute(part, axis, [(i, i ^ step) for i in range(count)]))
    return arrived


def spread_out(part, axis):
    count = lax.axis_size(axis)
    return [part] + [lax.ppermute(part, axis, [(i, i ^ step) for i in range(count)]) for step in range(1, count)]


def in_turn(*arrays):
    done = []
    for array in arrays:
        done = list(lax.optimization_barrier((*done, array)))
    return done


def by_halo(observed, kernels, band_kernel, masks):
    n_frame, n_row = lax.axis_size("frame"), lax.axis_size("row")
    frames, rows_dev, width = observed.shape
    components, _, tiles_dev = masks.shape
    positions = rows_dev * tiles_dev
    share = components // (n_frame * n_row)
    span = rows_dev + 2 * MARGIN
    smem, vmem = pl.BlockSpec(memory_space=pltpu.SMEM), pl.BlockSpec(memory_space=pltpu.VMEM)

    def call(kernel, name, in_specs, out_shape, scratch=(), cost=1000):
        many = isinstance(out_shape, tuple)
        return pl.pallas_call(
            kernel,
            name=name,
            out_shape=out_shape,
            in_specs=in_specs,
            out_specs=(vmem,) * len(out_shape) if many else vmem,
            scratch_shapes=scratch,
            compiler_params=pltpu.CompilerParams(vmem_limit_bytes=16 << 20),
            cost_estimate=pl.CostEstimate(flops=cost, bytes_accessed=cost, transcendentals=0),
        )

    def array(*shape, dtype=jnp.float32):
        return jax.ShapeDtypeStruct(shape, dtype)

    packed = array(frames * (NEAR + FAR), width)
    inner, outer, own = call(halo_kernel, "halo", [vmem], (packed, packed, array(*observed.shape)))(observed)
    swaps = [
        [pair for i in range(first, n_row - 1, 2) for pair in ((i, i + 1), (i + 1, i))] for first in (0, 1)
    ]
    inner, outer = (lax.ppermute(rows.astype(jnp.float16), "row", swap) for rows, swap in zip((inner, outer), swaps))
    outer, inner = in_turn(outer, inner)
    taps, back = call(
        functools.partial(taps_kernel, height=rows_dev * n_row, rows_dev=rows_dev),
        "taps",
        [smem, smem],
        (array(len(SIDES), span, TILE),) * 2,
        [pltpu.VMEM((len(SIDES), span + 2 * PAD, TILE), jnp.float32)],
    )(band_kernel, kernels)
    feet = call(
        functools.partial(feet_kernel, n_frame=n_frame, n_row=n_row),
        "feet",
        [vmem],
        array(components // 2, TILE, dtype=jnp.bfloat16),
    )(masks.transpose(1, 2, 0))
    feet = call(
        gather_kernel, "gather", [vmem] * n_frame, array(components, n_frame * TILE, dtype=jnp.bfloat16)
    )(*spread_out(feet, "frame"))
    blocks, sums = call(
        restore_kernel,
        "restore",
        [vmem] * 6,
        (
            array(n_frame, frames * positions, TILE, dtype=jnp.bfloat16),
            array(n_row, 2 * frames, TILE),
        ),
        [pltpu.VMEM((frames, span + 2 * PAD, TILE), jnp.float32)] * 3,
    )(taps, back, feet, own, inner.astype(jnp.float32), outer.astype(jnp.float32))
    shares = swapped(sums, "row")
    pieces = swapped(blocks, "frame")
    sums = call(add_kernel, "add", [vmem] * n_row, array(2 * frames, TILE))(*in_turn(*shares[::-1]))
    spikes = call(
        functools.partial(temporal_kernel, frames=frames),
        "temporal",
        [vmem] * n_frame,
        array(n_frame * frames, rows_dev, tiles_dev * TILE, dtype=jnp.bfloat16),
        [pltpu.VMEM((n_frame, frames * positions, TILE), jnp.bfloat16)],
    )(*pieces)
    spikes, *sums = lax.optimization_barrier((spikes, *spread_out(sums, "frame")))
    traces = call(
        functools.partial(means_kernel, frames=frames),
        "means",
        [vmem] * n_frame,
        array(share, n_frame * frames),
        [pltpu.VMEM((n_frame, 2 * frames, TILE), jnp.float32)],
    )(*sums)
    return (spikes, traces)


def fits(mesh, observed, masks):
    frames_dev = observed.shape[0] // mesh.shape["frame"]
    rows_dev = masks.shape[1] // (mesh.shape["groups"] * mesh.shape["row"])
    tiles_dev = masks.shape[2] // mesh.shape["frame"]
    places = mesh.shape["frame"] * mesh.shape["row"]
    return (
        frames_dev == mesh.shape["frame"] == mesh.shape["row"] == 4
        and 2 * rows_dev * tiles_dev == TILE
        and rows_dev == 16
        and masks.shape[0] // places == 16
    )


def solution(mesh):
    in_specs = (
        P("frame", ("groups", "row"), None),
        P(),
        P("groups"),
        P(None, ("groups", "row"), "frame"),
    )
    out_specs = (P(None, ("groups", "row"), "frame"), P(("groups", "frame", "row"), None))

    def whole(observed, kernels, band_kernel, masks):
        body = by_halo if fits(mesh, observed, masks) else local
        mapped = jax.shard_map(body, mesh=mesh, in_specs=in_specs, out_specs=out_specs, check_vma=False)
        return mapped(observed, kernels, band_kernel, masks)

    return whole
```

```python
import functools

import jax
import jax.numpy as jnp
from jax import lax
from jax.experimental import pallas as pl
from jax.experimental.pallas import tpu as pltpu
from jax.sharding import PartitionSpec as P

TILE = 128
BAND = 8
ITERS = 3
TAPS = 5
NEAR, FAR = 8, 4
MARGIN = 2 * BAND
PAD = BAND
STEPS = (((6, 46), (8, 40)), ((10, 42), (12, 36)), ((14, 38), (16, 32)))
SIDES = (0, 1, 3, 4)


SMOOTHING = 1024.0
DECAY_RATE = 0.9


def padded_2(cells, sides, width):
    for axis, dim in sides:
        count = lax.axis_size(axis)
        ends = count - 1
        head = lax.slice_in_dim(cells, 0, width, axis=dim)
        tail = lax.slice_in_dim(cells, cells.shape[dim] - width, cells.shape[dim], axis=dim)
        cells = jnp.concatenate(
            [
                lax.ppermute(tail, axis, [(i, (i + 1) % count) for i in range(ends)]),
                cells,
                lax.ppermute(head, axis, [((i + 1) % count, i) for i in range(ends)]),
            ],
            axis=dim,
        )
    return cells


def tap_rows(tap_table, band_kernel, first_row, row_count, height):
    row_ids = jnp.clip(first_row + jnp.arange(row_count), 0, height - 1)
    row_bands = row_ids // BAND
    band_slots = jnp.arange(band_kernel.shape[0])
    kernel_ids = jnp.sum(
        jnp.where(row_bands[:, None] == band_slots[None, :], band_kernel[None, :], 0), axis=1
    )
    kernel_slots = jnp.arange(tap_table.shape[0])
    picked = jnp.where(
        kernel_ids[:, None, None] == kernel_slots[None, :, None], tap_table[None, :, :], 0.0
    )
    return jnp.sum(picked, axis=1)


def blur_rows(padded, row_taps, row_count):
    summed = row_taps[:, 0][None, :, None] * padded[:, 0:row_count]
    for offset in range(1, 5):
        summed = (
            summed + row_taps[:, offset][None, :, None] * padded[:, offset : offset + row_count]
        )
    return summed


def back_rows(padded_quotient, outer_taps, row_count):
    summed = outer_taps[4 : 4 + row_count, 0][None, :, None] * padded_quotient[:, 4 : 4 + row_count]
    for offset in range(1, 5):
        start = 4 - offset
        summed = (
            summed
            + outer_taps[start : start + row_count, offset][None, :, None]
            * padded_quotient[:, start : start + row_count]
        )
    return summed


def temporal(series_block):
    frame_total, item_count, columns = series_block.shape
    values = series_block.astype(jnp.float32).reshape(frame_total, item_count * columns)
    frame_ids = jnp.arange(frame_total)
    at_ends = (frame_ids == 0) | (frame_ids == frame_total - 1)
    middle = (1.0 + SMOOTHING * jnp.where(at_ends, 1.0, 2.0)).astype(jnp.float32)
    sub_diag = jnp.where(frame_ids == 0, 0.0, -SMOOTHING).astype(jnp.float32)
    super_diag = jnp.where(frame_ids == frame_total - 1, 0.0, -SMOOTHING).astype(jnp.float32)
    baseline = lax.linalg.tridiagonal_solve(sub_diag, middle, super_diag, values)
    detrended = values - baseline
    earlier = jnp.concatenate(
        [jnp.zeros((1, values.shape[1]), jnp.float32), detrended[:-1]], axis=0
    )
    result = (detrended - DECAY_RATE * earlier).astype(jnp.bfloat16)
    return result.reshape(frame_total, item_count, columns)


def local(observed, kernels, band_kernel, masks):
    frames_dev, rows_dev, row_pixels = observed.shape
    height = rows_dev * lax.axis_size("row")
    tap_table = kernels / jnp.sum(kernels, axis=1, keepdims=True)
    first_row = lax.axis_index("row") * rows_dev
    own_taps = tap_rows(tap_table, band_kernel, first_row, rows_dev, height)
    outer_taps = tap_rows(tap_table, band_kernel, first_row - 2, rows_dev + 4, height)
    current = observed
    for iteration in range(ITERS):
        padded = padded_2(current, (("row", 1),), 2)
        blurred = blur_rows(padded, own_taps, rows_dev)
        quotient = observed / blurred
        padded_quotient = padded_2(quotient, (("row", 1),), 2)
        current = current * back_rows(padded_quotient, outer_taps, rows_dev)
    estimate = current.astype(jnp.bfloat16)
    spikes = temporal(lax.all_to_all(estimate, "frame", split_axis=2, concat_axis=0, tiled=True))
    frames_all, _, columns = spikes.shape
    tile_count = columns // TILE
    tile_sums = jnp.sum(
        spikes.reshape(frames_all, rows_dev * tile_count, TILE).astype(jnp.float32), axis=2
    )
    weights = masks.astype(jnp.float32).reshape(masks.shape[0], rows_dev * tile_count)
    local_sums = lax.dot_general(
        weights, tile_sums, (((1,), (1,)), ((), ())), precision=lax.Precision.HIGHEST
    )
    counts = jnp.sum(weights, axis=1)
    trace_sums, totals = (
        lax.psum_scatter(local_sums, ("frame", "row"), scatter_dimension=0, tiled=True),
        lax.psum_scatter(counts, ("frame", "row"), scatter_dimension=0, tiled=True),
    )
    traces = trace_sums / (TILE * totals[:, None])
    return (spikes, traces)


def halo_kernel(observed_ref, inner_ref, outer_ref, own_ref):
    even = lax.axis_index("row") % 2 == 0
    frames = observed_ref.shape[0]
    own_ref[...] = observed_ref[...]
    for frame in range(frames):
        near = frame * NEAR
        far = frames * NEAR + frame * FAR
        bottom, top = observed_ref[frame, -NEAR:, :], observed_ref[frame, :NEAR, :]
        inner_ref[near : near + NEAR, :] = jnp.where(even, bottom, top)
        outer_ref[near : near + NEAR, :] = jnp.where(even, top, bottom)
        bottom, top = observed_ref[frame, -NEAR - FAR : -NEAR, :], observed_ref[frame, NEAR : NEAR + FAR, :]
        inner_ref[far : far + FAR, :] = jnp.where(even, bottom, top)
        outer_ref[far : far + FAR, :] = jnp.where(even, top, bottom)


def taps_kernel(band_ref, kernels_ref, taps_ref, back_ref, pad_ref, *, height, rows_dev):
    span = rows_dev + 2 * MARGIN
    first_row = lax.axis_index("row") * rows_dev - MARGIN
    row_ids = lax.broadcasted_iota(jnp.int32, (BAND, TILE), 0)
    pad_ref[...] = jnp.zeros_like(pad_ref)
    for band in range(span // BAND):
        row = first_row + band * BAND
        inside = (row >= 0) & (row < height)
        kernel = band_ref[jnp.clip(row, 0, height - 1) // BAND]
        centre = jnp.full((BAND, TILE), kernels_ref[kernel, TAPS // 2], jnp.float32)
        start = band * BAND
        for slot, tap in enumerate(SIDES):
            weight = jnp.full((BAND, TILE), kernels_ref[kernel, tap], jnp.float32) / centre
            target = row_ids + (row + tap - TAPS // 2)
            weight = jnp.where(inside & (target >= 0) & (target < height), weight, 0.0)
            taps_ref[slot, start : start + BAND, :] = weight
            pad_ref[slot, BAND + start : 2 * BAND + start, :] = weight
    for slot, tap in enumerate(SIDES):
        start = BAND + TAPS // 2 - tap
        back_ref[slot] = pad_ref[slot, start : start + span, :]


def feet_kernel(masks_ref, feet_ref):
    rows_dev = masks_ref.shape[0]
    flat = jnp.concatenate([masks_ref[row].astype(jnp.float32) for row in range(rows_dev)], axis=0)
    positions = flat.shape[0]
    both = jnp.concatenate([flat, flat], axis=0).T
    half = feet_ref.shape[1]
    left = lax.broadcasted_iota(jnp.int32, (half, TILE), 1) < positions
    for block in range(feet_ref.shape[0]):
        start = 2 * block * half
        halves = jnp.where(left, both[start : start + half], both[start + half : start + 2 * half])
        feet_ref[block] = halves.astype(jnp.bfloat16)


def restore_kernel(
    taps_ref, back_ref, feet_ref, own_ref, inner_ref, outer_ref, out_ref, side_ref, image_ref, current_ref, quotient_ref
):
    n_frame = out_ref.shape[0]
    frames, rows_dev, width = own_ref.shape
    tiles_dev = width // (n_frame * TILE)
    positions = rows_dev * tiles_dev
    for ref in (image_ref, current_ref, quotient_ref):
        ref[...] = jnp.ones_like(ref)
    row = lax.axis_index("row")
    even = row % 2 == 0
    above = jnp.where(row == 0, 1.0, 0.0)
    below = jnp.where(row == lax.axis_size("row") - 1, 1.0, 0.0)

    def columns_step(step, carry):
        columns = pl.ds(pl.multiple_of(step * TILE, TILE), TILE)
        for frame in range(frames):
            near, far = frame * NEAR, frames * NEAR + frame * FAR
            start, stop = PAD + MARGIN, PAD + MARGIN + rows_dev
            inner, outer = inner_ref[near : near + NEAR, columns], outer_ref[near : near + NEAR, columns]
            image_ref[frame, start - NEAR : start, :] = jnp.where(even, outer, inner) + above
            image_ref[frame, stop : stop + NEAR, :] = jnp.where(even, inner, outer) + below
            inner, outer = inner_ref[far : far + FAR, columns], outer_ref[far : far + FAR, columns]
            image_ref[frame, start - NEAR - FAR : start - NEAR, :] = jnp.where(even, outer, inner) + above
            image_ref[frame, stop + NEAR : stop + NEAR + FAR, :] = jnp.where(even, inner, outer) + below
            image_ref[frame, start:stop, :] = own_ref[frame, :, columns]
        source_ref = image_ref
        for (first, last), (back_first, back_last) in STEPS:
            for row in range(first, last, BAND):
                weights = [taps_ref[slot, row : row + BAND, :] for slot in range(len(SIDES))]
                for frame in range(frames):
                    rows = slice(PAD + row, PAD + row + BAND)
                    blurred = source_ref[frame, rows, :]
                    for weight, tap in zip(weights, SIDES):
                        start = PAD + row + tap - TAPS // 2
                        blurred = blurred + weight * source_ref[frame, start : start + BAND, :]
                    quotient_ref[frame, rows, :] = image_ref[frame, rows, :] / blurred
            for row in range(back_first, back_last, BAND):
                weights = [back_ref[slot, row : row + BAND, :] for slot in range(len(SIDES))]
                for frame in range(frames):
                    rows = slice(PAD + row, PAD + row + BAND)
                    spread = quotient_ref[frame, rows, :]
                    for weight, tap in zip(weights, SIDES):
                        start = PAD + row - tap + TAPS // 2
                        spread = spread + weight * quotient_ref[frame, start : start + BAND, :]
                    current_ref[frame, rows, :] = source_ref[frame, rows, :] * spread
            source_ref = current_ref
        first = pl.multiple_of(lax.rem(step, tiles_dev) * rows_dev, rows_dev)
        for frame in range(frames):
            estimate = current_ref[frame, PAD + MARGIN : PAD + MARGIN + rows_dev, :].astype(jnp.bfloat16)
            start = pl.multiple_of(first + frame * positions, rows_dev)
            out_ref[step // tiles_dev, pl.ds(start, rows_dev), :] = estimate
        return carry

    lax.fori_loop(0, n_frame * tiles_dev, columns_step, 0)
    lane_tiles = lax.broadcasted_iota(jnp.int32, (TILE, TILE), 1) % tiles_dev
    gathered = jnp.zeros((frames * n_frame * rows_dev, TILE), jnp.float32)
    for tile in range(tiles_dev):
        pieces = []
        for frame in range(frames):
            start = frame * positions + tile * rows_dev
            pieces += [out_ref[block, start : start + rows_dev, :] for block in range(n_frame)]
        picked = jnp.where(lane_tiles == tile, 1.0, 0.0).astype(jnp.bfloat16)
        gathered = gathered + jnp.dot(jnp.concatenate(pieces, axis=0), picked, preferred_element_type=jnp.float32)
    lanes = lax.broadcasted_iota(jnp.int32, (rows_dev, TILE), 1)
    here = lanes % positions // tiles_dev == lax.broadcasted_iota(jnp.int32, (rows_dev, TILE), 0)
    sums = []
    for place in range(frames * n_frame):
        part = jnp.where(here, gathered[place * rows_dev : (place + 1) * rows_dev], 0.0)
        sums.append(jnp.sum(part, axis=0, keepdims=True))
    sums = jnp.concatenate(sums, axis=0)
    high = sums.astype(jnp.bfloat16).astype(jnp.float32)
    split = jnp.where(lax.broadcasted_iota(jnp.int32, sums.shape, 1) < positions, high, sums - high).astype(jnp.bfloat16)
    for block in range(n_frame):
        side_ref[block, : split.shape[0], :] = split
        side_ref[block, split.shape[0] :, :] = feet_ref[block]


def deconvolved(series):
    total = len(series)
    factors = []
    for step in range(total):
        middle = 1.0 + SMOOTHING * (1.0 if step in (0, total - 1) else 2.0)
        if step:
            middle -= SMOOTHING * SMOOTHING * factors[-1]
        factors.append(1.0 / middle)
    forward = [series[0] * factors[0]]
    for step in range(1, total):
        forward.append((series[step] + SMOOTHING * forward[step - 1]) * factors[step])
    baseline = [None] * total
    baseline[total - 1] = forward[total - 1]
    for step in range(total - 2, -1, -1):
        baseline[step] = forward[step] + (SMOOTHING * factors[step]) * baseline[step + 1]
    result, earlier = [], None
    for step in range(total):
        detrended = series[step] - baseline[step]
        result.append(detrended if earlier is None else detrended - DECAY_RATE * earlier)
        earlier = detrended
    return result


def partial_kernel(*refs, positions):
    pieces, (out_ref, sums_ref, feet_ref) = refs[:-3], refs[-3:]
    n_frame = len(pieces)
    place = lax.axis_index("frame")
    rows = sums_ref.shape[0] // n_frame
    half = feet_ref.shape[1]
    for step, piece in enumerate(pieces):
        sums_ref[pl.ds(pl.multiple_of((place ^ step) * rows, rows), rows), :] = piece[:rows, :].astype(jnp.float32)
        feet_ref[place ^ step] = piece[rows:, :].astype(jnp.float32)
    series = [sums_ref[t * n_frame : (t + 1) * n_frame, :] for t in range(rows)]
    for t, sums in enumerate(deconvolved(series)):
        sums_ref[t * n_frame : (t + 1) * n_frame, :] = sums + pltpu.roll(sums, TILE // 2, 1)
    left = lax.broadcasted_iota(jnp.int32, (half, TILE), 1) < positions
    weights, sums = [], []
    extra = jnp.where(lax.broadcasted_iota(jnp.int32, (8, TILE), 0) == 0, 1.0, 0.0)
    for block in range(n_frame):
        feet = feet_ref[block]
        weights.append(jnp.concatenate([jnp.where(left, feet, 0.0), jnp.where(left, 0.0, feet)], axis=0))
        sums.append(jnp.concatenate([sums_ref[pl.ds(block, rows, stride=n_frame), :], extra], axis=0))
    totals = lax.dot_general(
        jnp.concatenate(weights, axis=1),
        jnp.concatenate(sums, axis=1),
        (((1,), (1,)), ((), ())),
        precision=lax.Precision.HIGHEST,
        preferred_element_type=jnp.float32,
    )
    share = out_ref.shape[1]
    out_ref[...] = jnp.zeros_like(out_ref)
    for row in range(out_ref.shape[0]):
        out_ref[row, :, : rows + 8] = totals[row * share : (row + 1) * share]


def temporal_kernel(*refs, frames):
    pieces, (spikes_ref, in_ref) = refs[:-2], refs[-2:]
    place = lax.axis_index("frame")
    for step, piece in enumerate(pieces):
        in_ref[place ^ step] = piece[...]
    total, rows_dev, columns = spikes_ref.shape
    positions = in_ref.shape[1] // frames
    for tile in range(columns // TILE):
        series = []
        for t in range(total):
            start = t % frames * positions + tile * rows_dev
            series.append(in_ref[t // frames, start : start + rows_dev, :].astype(jnp.float32))
        for t, spikes in enumerate(deconvolved(series)):
            spikes_ref[t, :, tile * TILE : (tile + 1) * TILE] = spikes.astype(spikes_ref.dtype)


def means_kernel(*refs):
    pieces, traces_ref = refs[:-1], refs[-1]
    frames = traces_ref.shape[1]
    total = pieces[0][...]
    for piece in pieces[1:]:
        total = total + piece[...]
    traces_ref[...] = total[:, :frames] / (TILE * total[:, frames : frames + 1])


def swapped(parts, axis):
    count, place = lax.axis_size(axis), lax.axis_index(axis)
    arrived = [lax.dynamic_index_in_dim(parts, place, 0, keepdims=False, allow_negative_indices=False)]
    for step in range(1, count):
        part = lax.dynamic_index_in_dim(parts, place ^ step, 0, keepdims=False, allow_negative_indices=False)
        arrived.append(lax.ppermute(part, axis, [(i, i ^ step) for i in range(count)]))
    return arrived


def in_turn(*arrays):
    done = []
    for array in arrays:
        done = list(lax.optimization_barrier((*done, array)))
    return done


def by_halo(observed, kernels, band_kernel, masks):
    n_frame, n_row = lax.axis_size("frame"), lax.axis_size("row")
    frames, rows_dev, width = observed.shape
    components, _, tiles_dev = masks.shape
    positions = rows_dev * tiles_dev
    share = components // (n_frame * n_row)
    span = rows_dev + 2 * MARGIN
    smem, vmem = pl.BlockSpec(memory_space=pltpu.SMEM), pl.BlockSpec(memory_space=pltpu.VMEM)

    def call(kernel, name, in_specs, out_shape, scratch=(), cost=1000):
        many = isinstance(out_shape, tuple)
        return pl.pallas_call(
            kernel,
            name=name,
            out_shape=out_shape,
            in_specs=in_specs,
            out_specs=(vmem,) * len(out_shape) if many else vmem,
            scratch_shapes=scratch,
            compiler_params=pltpu.CompilerParams(vmem_limit_bytes=16 << 20),
            cost_estimate=pl.CostEstimate(flops=cost, bytes_accessed=cost, transcendentals=0),
        )

    def array(*shape, dtype=jnp.float32):
        return jax.ShapeDtypeStruct(shape, dtype)

    packed = array(frames * (NEAR + FAR), width)
    inner, outer, own = call(halo_kernel, "halo", [vmem], (packed, packed, array(*observed.shape)))(observed)
    swaps = [
        [pair for i in range(first, n_row - 1, 2) for pair in ((i, i + 1), (i + 1, i))] for first in (0, 1)
    ]
    inner, outer = (lax.ppermute(rows.astype(jnp.float16), "row", swap) for rows, swap in zip((inner, outer), swaps))
    outer, inner = in_turn(outer, inner)
    taps, back = call(
        functools.partial(taps_kernel, height=rows_dev * n_row, rows_dev=rows_dev),
        "taps",
        [smem, smem],
        (array(len(SIDES), span, TILE),) * 2,
        [pltpu.VMEM((len(SIDES), span + 2 * PAD, TILE), jnp.float32)],
    )(band_kernel, kernels)
    feet = call(feet_kernel, "feet", [vmem], array(n_frame, n_row * share // 2, TILE, dtype=jnp.bfloat16))(
        masks.transpose(1, 2, 0)
    )
    side_rows = frames * n_frame + n_row * share // 2
    blocks, sides = call(
        restore_kernel,
        "restore",
        [vmem] * 6,
        (
            array(n_frame, frames * positions, TILE, dtype=jnp.bfloat16),
            array(n_frame, side_rows, TILE, dtype=jnp.bfloat16),
        ),
        [pltpu.VMEM((frames, span + 2 * PAD, TILE), jnp.float32)] * 3,
    )(taps, back, feet, own, inner.astype(jnp.float32), outer.astype(jnp.float32))
    sides = swapped(sides, "frame")
    pieces = swapped(blocks, "frame")
    partial = call(
        functools.partial(partial_kernel, positions=positions),
        "partial",
        [vmem] * n_frame,
        array(n_row, share, TILE),
        [
            pltpu.VMEM((n_frame * frames * n_frame, TILE), jnp.float32),
            pltpu.VMEM((n_frame, n_row * share // 2, TILE), jnp.float32),
        ],
    )(*sides)
    shares = swapped(partial, "row")
    spikes = call(
        functools.partial(temporal_kernel, frames=frames),
        "temporal",
        [vmem] * n_frame,
        array(n_frame * frames, rows_dev, tiles_dev * TILE, dtype=jnp.bfloat16),
        [pltpu.VMEM((n_frame, frames * positions, TILE), jnp.bfloat16)],
    )(*pieces)
    spikes, *shares = in_turn(spikes, *shares[::-1])
    traces = call(means_kernel, "means", [vmem] * n_row, array(share, n_frame * frames))(*shares)
    return (spikes, traces)


def fits(mesh, observed, masks):
    frames_dev = observed.shape[0] // mesh.shape["frame"]
    rows_dev = masks.shape[1] // (mesh.shape["groups"] * mesh.shape["row"])
    tiles_dev = masks.shape[2] // mesh.shape["frame"]
    places = mesh.shape["frame"] * mesh.shape["row"]
    return (
        frames_dev == mesh.shape["frame"] == mesh.shape["row"] == 4
        and 2 * rows_dev * tiles_dev == TILE
        and rows_dev == 16
        and masks.shape[0] // places == 16
    )


def solution(mesh):
    in_specs = (
        P("frame", ("groups", "row"), None),
        P(),
        P("groups"),
        P(None, ("groups", "row"), "frame"),
    )
    out_specs = (P(None, ("groups", "row"), "frame"), P(("groups", "frame", "row"), None))

    def whole(observed, kernels, band_kernel, masks):
        body = by_halo if fits(mesh, observed, masks) else local
        mapped = jax.shard_map(body, mesh=mesh, in_specs=in_specs, out_specs=out_specs, check_vma=False)
        return mapped(observed, kernels, band_kernel, masks)

    return whole
```

```python
import functools

import jax
import jax.numpy as jnp
from jax import lax
from jax.experimental import pallas as pl
from jax.experimental.pallas import tpu as pltpu
from jax.sharding import PartitionSpec as P

TILE = 128
BAND = 8
ITERS = 3
TAPS = 5
NEAR, FAR = 8, 4
MARGIN = 2 * BAND
PAD = BAND
STEPS = (((6, 46), (8, 40)), ((10, 42), (12, 36)), ((14, 38), (16, 32)))
SIDES = (0, 1, 3, 4)


SMOOTHING = 1024.0
DECAY_RATE = 0.9


def padded_2(cells, sides, width):
    for axis, dim in sides:
        count = lax.axis_size(axis)
        ends = count - 1
        head = lax.slice_in_dim(cells, 0, width, axis=dim)
        tail = lax.slice_in_dim(cells, cells.shape[dim] - width, cells.shape[dim], axis=dim)
        cells = jnp.concatenate(
            [
                lax.ppermute(tail, axis, [(i, (i + 1) % count) for i in range(ends)]),
                cells,
                lax.ppermute(head, axis, [((i + 1) % count, i) for i in range(ends)]),
            ],
            axis=dim,
        )
    return cells


def tap_rows(tap_table, band_kernel, first_row, row_count, height):
    row_ids = jnp.clip(first_row + jnp.arange(row_count), 0, height - 1)
    row_bands = row_ids // BAND
    band_slots = jnp.arange(band_kernel.shape[0])
    kernel_ids = jnp.sum(
        jnp.where(row_bands[:, None] == band_slots[None, :], band_kernel[None, :], 0), axis=1
    )
    kernel_slots = jnp.arange(tap_table.shape[0])
    picked = jnp.where(
        kernel_ids[:, None, None] == kernel_slots[None, :, None], tap_table[None, :, :], 0.0
    )
    return jnp.sum(picked, axis=1)


def blur_rows(padded, row_taps, row_count):
    summed = row_taps[:, 0][None, :, None] * padded[:, 0:row_count]
    for offset in range(1, 5):
        summed = (
            summed + row_taps[:, offset][None, :, None] * padded[:, offset : offset + row_count]
        )
    return summed


def back_rows(padded_quotient, outer_taps, row_count):
    summed = outer_taps[4 : 4 + row_count, 0][None, :, None] * padded_quotient[:, 4 : 4 + row_count]
    for offset in range(1, 5):
        start = 4 - offset
        summed = (
            summed
            + outer_taps[start : start + row_count, offset][None, :, None]
            * padded_quotient[:, start : start + row_count]
        )
    return summed


def temporal(series_block):
    frame_total, item_count, columns = series_block.shape
    values = series_block.astype(jnp.float32).reshape(frame_total, item_count * columns)
    frame_ids = jnp.arange(frame_total)
    at_ends = (frame_ids == 0) | (frame_ids == frame_total - 1)
    middle = (1.0 + SMOOTHING * jnp.where(at_ends, 1.0, 2.0)).astype(jnp.float32)
    sub_diag = jnp.where(frame_ids == 0, 0.0, -SMOOTHING).astype(jnp.float32)
    super_diag = jnp.where(frame_ids == frame_total - 1, 0.0, -SMOOTHING).astype(jnp.float32)
    baseline = lax.linalg.tridiagonal_solve(sub_diag, middle, super_diag, values)
    detrended = values - baseline
    earlier = jnp.concatenate(
        [jnp.zeros((1, values.shape[1]), jnp.float32), detrended[:-1]], axis=0
    )
    result = (detrended - DECAY_RATE * earlier).astype(jnp.bfloat16)
    return result.reshape(frame_total, item_count, columns)


def local(observed, kernels, band_kernel, masks):
    frames_dev, rows_dev, row_pixels = observed.shape
    height = rows_dev * lax.axis_size("row")
    tap_table = kernels / jnp.sum(kernels, axis=1, keepdims=True)
    first_row = lax.axis_index("row") * rows_dev
    own_taps = tap_rows(tap_table, band_kernel, first_row, rows_dev, height)
    outer_taps = tap_rows(tap_table, band_kernel, first_row - 2, rows_dev + 4, height)
    current = observed
    for iteration in range(ITERS):
        padded = padded_2(current, (("row", 1),), 2)
        blurred = blur_rows(padded, own_taps, rows_dev)
        quotient = observed / blurred
        padded_quotient = padded_2(quotient, (("row", 1),), 2)
        current = current * back_rows(padded_quotient, outer_taps, rows_dev)
    estimate = current.astype(jnp.bfloat16)
    spikes = temporal(lax.all_to_all(estimate, "frame", split_axis=2, concat_axis=0, tiled=True))
    frames_all, _, columns = spikes.shape
    tile_count = columns // TILE
    tile_sums = jnp.sum(
        spikes.reshape(frames_all, rows_dev * tile_count, TILE).astype(jnp.float32), axis=2
    )
    weights = masks.astype(jnp.float32).reshape(masks.shape[0], rows_dev * tile_count)
    local_sums = lax.dot_general(
        weights, tile_sums, (((1,), (1,)), ((), ())), precision=lax.Precision.HIGHEST
    )
    counts = jnp.sum(weights, axis=1)
    trace_sums, totals = (
        lax.psum_scatter(local_sums, ("frame", "row"), scatter_dimension=0, tiled=True),
        lax.psum_scatter(counts, ("frame", "row"), scatter_dimension=0, tiled=True),
    )
    traces = trace_sums / (TILE * totals[:, None])
    return (spikes, traces)


def halo_kernel(observed_ref, inner_ref, outer_ref, own_ref):
    even = lax.axis_index("row") % 2 == 0
    frames = observed_ref.shape[0]
    own_ref[...] = observed_ref[...]
    for frame in range(frames):
        near = frame * NEAR
        far = frames * NEAR + frame * FAR
        bottom, top = observed_ref[frame, -NEAR:, :], observed_ref[frame, :NEAR, :]
        inner_ref[near : near + NEAR, :] = jnp.where(even, bottom, top)
        outer_ref[near : near + NEAR, :] = jnp.where(even, top, bottom)
        bottom, top = observed_ref[frame, -NEAR - FAR : -NEAR, :], observed_ref[frame, NEAR : NEAR + FAR, :]
        inner_ref[far : far + FAR, :] = jnp.where(even, bottom, top)
        outer_ref[far : far + FAR, :] = jnp.where(even, top, bottom)


def taps_kernel(band_ref, kernels_ref, taps_ref, back_ref, pad_ref, *, height, rows_dev):
    span = rows_dev + 2 * MARGIN
    first_row = lax.axis_index("row") * rows_dev - MARGIN
    row_ids = lax.broadcasted_iota(jnp.int32, (BAND, TILE), 0)
    pad_ref[...] = jnp.zeros_like(pad_ref)
    for band in range(span // BAND):
        row = first_row + band * BAND
        inside = (row >= 0) & (row < height)
        kernel = band_ref[jnp.clip(row, 0, height - 1) // BAND]
        centre = jnp.full((BAND, TILE), kernels_ref[kernel, TAPS // 2], jnp.float32)
        start = band * BAND
        for slot, tap in enumerate(SIDES):
            weight = jnp.full((BAND, TILE), kernels_ref[kernel, tap], jnp.float32) / centre
            target = row_ids + (row + tap - TAPS // 2)
            weight = jnp.where(inside & (target >= 0) & (target < height), weight, 0.0)
            taps_ref[slot, start : start + BAND, :] = weight
            pad_ref[slot, BAND + start : 2 * BAND + start, :] = weight
    for slot, tap in enumerate(SIDES):
        start = BAND + TAPS // 2 - tap
        back_ref[slot] = pad_ref[slot, start : start + span, :]


def feet_kernel(masks_ref, feet_ref):
    rows_dev = masks_ref.shape[0]
    flat = jnp.concatenate([masks_ref[row].astype(jnp.float32) for row in range(rows_dev)], axis=0)
    positions = flat.shape[0]
    both = jnp.concatenate([flat, flat], axis=0).T
    half = feet_ref.shape[1]
    left = lax.broadcasted_iota(jnp.int32, (half, TILE), 1) < positions
    for block in range(feet_ref.shape[0]):
        start = 2 * block * half
        halves = jnp.where(left, both[start : start + half], both[start + half : start + 2 * half])
        feet_ref[block] = halves.astype(jnp.bfloat16)


def restore_kernel(
    taps_ref, back_ref, feet_ref, own_ref, top_ref, bottom_ref, out_ref, side_ref, image_ref, current_ref, quotient_ref
):
    n_frame = out_ref.shape[0]
    frames, rows_dev, width = own_ref.shape
    tiles_dev = width // (n_frame * TILE)
    positions = rows_dev * tiles_dev
    for ref in (image_ref, current_ref, quotient_ref):
        ref[...] = jnp.ones_like(ref)

    def columns_step(step, carry):
        columns = pl.ds(pl.multiple_of(step * TILE, TILE), TILE)
        for frame in range(frames):
            near, far = frame * NEAR, frames * NEAR + frame * FAR
            start, stop = PAD + MARGIN, PAD + MARGIN + rows_dev
            image_ref[frame, start - NEAR - FAR : start - NEAR, :] = top_ref[far : far + FAR, columns]
            image_ref[frame, start - NEAR : start, :] = top_ref[near : near + NEAR, columns]
            image_ref[frame, stop : stop + NEAR, :] = bottom_ref[near : near + NEAR, columns]
            image_ref[frame, stop + NEAR : stop + NEAR + FAR, :] = bottom_ref[far : far + FAR, columns]
            image_ref[frame, start:stop, :] = own_ref[frame, :, columns]
        source_ref = image_ref
        for (first, last), (back_first, back_last) in STEPS:
            for row in range(first, last, BAND):
                weights = [taps_ref[slot, row : row + BAND, :] for slot in range(len(SIDES))]
                for frame in range(frames):
                    rows = slice(PAD + row, PAD + row + BAND)
                    blurred = source_ref[frame, rows, :]
                    for weight, tap in zip(weights, SIDES):
                        start = PAD + row + tap - TAPS // 2
                        blurred = blurred + weight * source_ref[frame, start : start + BAND, :]
                    quotient_ref[frame, rows, :] = image_ref[frame, rows, :] / blurred
            for row in range(back_first, back_last, BAND):
                weights = [back_ref[slot, row : row + BAND, :] for slot in range(len(SIDES))]
                for frame in range(frames):
                    rows = slice(PAD + row, PAD + row + BAND)
                    spread = quotient_ref[frame, rows, :]
                    for weight, tap in zip(weights, SIDES):
                        start = PAD + row - tap + TAPS // 2
                        spread = spread + weight * quotient_ref[frame, start : start + BAND, :]
                    current_ref[frame, rows, :] = source_ref[frame, rows, :] * spread
            source_ref = current_ref
        first = pl.multiple_of(lax.rem(step, tiles_dev) * rows_dev, rows_dev)
        for frame in range(frames):
            estimate = current_ref[frame, PAD + MARGIN : PAD + MARGIN + rows_dev, :].astype(jnp.bfloat16)
            start = pl.multiple_of(first + frame * positions, rows_dev)
            out_ref[step // tiles_dev, pl.ds(start, rows_dev), :] = estimate
        return carry

    lax.fori_loop(0, n_frame * tiles_dev, columns_step, 0)
    lane_tiles = lax.broadcasted_iota(jnp.int32, (TILE, TILE), 1) % tiles_dev
    gathered = jnp.zeros((frames * n_frame * rows_dev, TILE), jnp.float32)
    for tile in range(tiles_dev):
        pieces = []
        for frame in range(frames):
            start = frame * positions + tile * rows_dev
            pieces += [out_ref[block, start : start + rows_dev, :] for block in range(n_frame)]
        picked = jnp.where(lane_tiles == tile, 1.0, 0.0).astype(jnp.bfloat16)
        gathered = gathered + jnp.dot(jnp.concatenate(pieces, axis=0), picked, preferred_element_type=jnp.float32)
    lanes = lax.broadcasted_iota(jnp.int32, (rows_dev, TILE), 1)
    here = lanes % positions // tiles_dev == lax.broadcasted_iota(jnp.int32, (rows_dev, TILE), 0)
    sums = []
    for place in range(frames * n_frame):
        part = jnp.where(here, gathered[place * rows_dev : (place + 1) * rows_dev], 0.0)
        sums.append(jnp.sum(part, axis=0, keepdims=True))
    sums = jnp.concatenate(sums, axis=0)
    high = sums.astype(jnp.bfloat16).astype(jnp.float32)
    split = jnp.where(lax.broadcasted_iota(jnp.int32, sums.shape, 1) < positions, high, sums - high).astype(jnp.bfloat16)
    for block in range(n_frame):
        side_ref[block, : split.shape[0], :] = split
        side_ref[block, split.shape[0] :, :] = feet_ref[block]


def deconvolved(series):
    total = len(series)
    factors = []
    for step in range(total):
        middle = 1.0 + SMOOTHING * (1.0 if step in (0, total - 1) else 2.0)
        if step:
            middle -= SMOOTHING * SMOOTHING * factors[-1]
        factors.append(1.0 / middle)
    forward = [series[0] * factors[0]]
    for step in range(1, total):
        forward.append((series[step] + SMOOTHING * forward[step - 1]) * factors[step])
    baseline = [None] * total
    baseline[total - 1] = forward[total - 1]
    for step in range(total - 2, -1, -1):
        baseline[step] = forward[step] + (SMOOTHING * factors[step]) * baseline[step + 1]
    result, earlier = [], None
    for step in range(total):
        detrended = series[step] - baseline[step]
        result.append(detrended if earlier is None else detrended - DECAY_RATE * earlier)
        earlier = detrended
    return result


def partial_kernel(*refs, positions):
    pieces, (out_ref, sums_ref, feet_ref) = refs[:-3], refs[-3:]
    n_frame = len(pieces)
    place = lax.axis_index("frame")
    rows = sums_ref.shape[0] // n_frame
    half = feet_ref.shape[1]
    for step, piece in enumerate(pieces[::-1]):
        sums_ref[pl.ds(pl.multiple_of((place ^ step) * rows, rows), rows), :] = piece[:rows, :].astype(jnp.float32)
        feet_ref[place ^ step] = piece[rows:, :].astype(jnp.float32)
    series = [sums_ref[t * n_frame : (t + 1) * n_frame, :] for t in range(rows)]
    for t, sums in enumerate(deconvolved(series)):
        sums_ref[t * n_frame : (t + 1) * n_frame, :] = sums + pltpu.roll(sums, TILE // 2, 1)
    left = lax.broadcasted_iota(jnp.int32, (half, TILE), 1) < positions
    weights, sums = [], []
    extra = jnp.where(lax.broadcasted_iota(jnp.int32, (8, TILE), 0) == 0, 1.0, 0.0)
    for block in range(n_frame):
        feet = feet_ref[block]
        weights.append(jnp.concatenate([jnp.where(left, feet, 0.0), jnp.where(left, 0.0, feet)], axis=0))
        sums.append(jnp.concatenate([sums_ref[pl.ds(block, rows, stride=n_frame), :], extra], axis=0))
    totals = lax.dot_general(
        jnp.concatenate(weights, axis=1),
        jnp.concatenate(sums, axis=1),
        (((1,), (1,)), ((), ())),
        precision=lax.Precision.HIGHEST,
        preferred_element_type=jnp.float32,
    )
    share = out_ref.shape[1]
    out_ref[...] = jnp.zeros_like(out_ref)
    for row in range(out_ref.shape[0]):
        out_ref[row, :, : rows + 8] = totals[row * share : (row + 1) * share]


def temporal_kernel(*refs, frames):
    pieces, (spikes_ref, in_ref) = refs[:-2], refs[-2:]
    place = lax.axis_index("frame")
    for step, piece in enumerate(pieces[::-1]):
        in_ref[place ^ step] = piece[...]
    total, rows_dev, columns = spikes_ref.shape
    positions = in_ref.shape[1] // frames
    for tile in range(columns // TILE):
        series = []
        for t in range(total):
            start = t % frames * positions + tile * rows_dev
            series.append(in_ref[t // frames, start : start + rows_dev, :].astype(jnp.float32))
        for t, spikes in enumerate(deconvolved(series)):
            spikes_ref[t, :, tile * TILE : (tile + 1) * TILE] = spikes.astype(spikes_ref.dtype)


def means_kernel(*refs):
    pieces, traces_ref = refs[:-1], refs[-1]
    frames = traces_ref.shape[1]
    total = pieces[0][...]
    for piece in pieces[1:]:
        total = total + piece[...]
    traces_ref[...] = total[:, :frames] / (TILE * total[:, frames : frames + 1])


def swapped(parts, axis):
    count, place = lax.axis_size(axis), lax.axis_index(axis)
    arrived = [lax.dynamic_index_in_dim(parts, place, 0, keepdims=False, allow_negative_indices=False)]
    for step in range(1, count):
        part = lax.dynamic_index_in_dim(parts, place ^ step, 0, keepdims=False, allow_negative_indices=False)
        arrived.append(lax.ppermute(part, axis, [(i, i ^ step) for i in range(count)]))
    return arrived


def in_turn(*arrays):
    done = []
    for array in arrays:
        done = list(lax.optimization_barrier((*done, array)))
    return done


def by_halo(observed, kernels, band_kernel, masks):
    n_frame, n_row = lax.axis_size("frame"), lax.axis_size("row")
    frames, rows_dev, width = observed.shape
    components, _, tiles_dev = masks.shape
    positions = rows_dev * tiles_dev
    share = components // (n_frame * n_row)
    span = rows_dev + 2 * MARGIN
    smem, vmem = pl.BlockSpec(memory_space=pltpu.SMEM), pl.BlockSpec(memory_space=pltpu.VMEM)

    def call(kernel, name, in_specs, out_shape, scratch=(), cost=1000):
        many = isinstance(out_shape, tuple)
        return pl.pallas_call(
            kernel,
            name=name,
            out_shape=out_shape,
            in_specs=in_specs,
            out_specs=(vmem,) * len(out_shape) if many else vmem,
            scratch_shapes=scratch,
            compiler_params=pltpu.CompilerParams(vmem_limit_bytes=16 << 20),
            cost_estimate=pl.CostEstimate(flops=cost, bytes_accessed=cost, transcendentals=0),
        )

    def array(*shape, dtype=jnp.float32):
        return jax.ShapeDtypeStruct(shape, dtype)

    packed = array(frames * (NEAR + FAR), width)
    inner, outer, own = call(halo_kernel, "halo", [vmem], (packed, packed, array(*observed.shape)))(observed)
    swaps = [
        [pair for i in range(first, n_row - 1, 2) for pair in ((i, i + 1), (i + 1, i))] for first in (0, 1)
    ]
    inner, outer = (lax.ppermute(rows.astype(jnp.float16), "row", swap) for rows, swap in zip((inner, outer), swaps))
    outer, inner = in_turn(outer, inner)
    taps, back = call(
        functools.partial(taps_kernel, height=rows_dev * n_row, rows_dev=rows_dev),
        "taps",
        [smem, smem],
        (array(len(SIDES), span, TILE),) * 2,
        [pltpu.VMEM((len(SIDES), span + 2 * PAD, TILE), jnp.float32)],
    )(band_kernel, kernels)
    feet = call(feet_kernel, "feet", [vmem], array(n_frame, n_row * share // 2, TILE, dtype=jnp.bfloat16))(
        masks.transpose(1, 2, 0)
    )
    row = lax.axis_index("row")
    even = row % 2 == 0
    alone = (row == 0) | (row == n_row - 1)
    inner, outer = inner.astype(jnp.float32), jnp.where(alone, 1.0, outer.astype(jnp.float32))
    top, bottom = jnp.where(even, outer, inner), jnp.where(even, inner, outer)
    side_rows = frames * n_frame + n_row * share // 2
    blocks, sides = call(
        restore_kernel,
        "restore",
        [vmem] * 6,
        (
            array(n_frame, frames * positions, TILE, dtype=jnp.bfloat16),
            array(n_frame, side_rows, TILE, dtype=jnp.bfloat16),
        ),
        [pltpu.VMEM((frames, span + 2 * PAD, TILE), jnp.float32)] * 3,
    )(taps, back, feet, own, top, bottom)
    sides = swapped(sides, "frame")
    pieces = swapped(blocks, "frame")
    partial = call(
        functools.partial(partial_kernel, positions=positions),
        "partial",
        [vmem] * n_frame,
        array(n_row, share, TILE),
        [
            pltpu.VMEM((n_frame * frames * n_frame, TILE), jnp.float32),
            pltpu.VMEM((n_frame, n_row * share // 2, TILE), jnp.float32),
        ],
    )(*sides[::-1])
    shares = swapped(partial, "row")
    spikes = call(
        functools.partial(temporal_kernel, frames=frames),
        "temporal",
        [vmem] * n_frame,
        array(n_frame * frames, rows_dev, tiles_dev * TILE, dtype=jnp.bfloat16),
        [pltpu.VMEM((n_frame, frames * positions, TILE), jnp.bfloat16)],
    )(*pieces[::-1])
    spikes, *shares = in_turn(spikes, *shares[::-1])
    traces = call(means_kernel, "means", [vmem] * n_row, array(share, n_frame * frames))(*shares)
    return (spikes, traces)


def fits(mesh, observed, masks):
    frames_dev = observed.shape[0] // mesh.shape["frame"]
    rows_dev = masks.shape[1] // (mesh.shape["groups"] * mesh.shape["row"])
    tiles_dev = masks.shape[2] // mesh.shape["frame"]
    places = mesh.shape["frame"] * mesh.shape["row"]
    return (
        frames_dev == mesh.shape["frame"] == mesh.shape["row"] == 4
        and 2 * rows_dev * tiles_dev == TILE
        and rows_dev == 16
        and masks.shape[0] // places == 16
    )


def solution(mesh):
    in_specs = (
        P("frame", ("groups", "row"), None),
        P(),
        P("groups"),
        P(None, ("groups", "row"), "frame"),
    )
    out_specs = (P(None, ("groups", "row"), "frame"), P(("groups", "frame", "row"), None))

    def whole(observed, kernels, band_kernel, masks):
        body = by_halo if fits(mesh, observed, masks) else local
        mapped = jax.shard_map(body, mesh=mesh, in_specs=in_specs, out_specs=out_specs, check_vma=False)
        return mapped(observed, kernels, band_kernel, masks)

    return whole
```

```python
import functools

import jax
import jax.numpy as jnp
from jax import lax
from jax.experimental import pallas as pl
from jax.experimental.pallas import tpu as pltpu
from jax.sharding import PartitionSpec as P

TILE = 128
BAND = 8
ITERS = 3
TAPS = 5
NEAR, FAR = 8, 4
MARGIN = 2 * BAND
PAD = BAND
STEPS = (((6, 46), (8, 40)), ((10, 42), (12, 36)), ((14, 38), (16, 32)))
SIDES = (0, 1, 3, 4)


SMOOTHING = 1024.0
DECAY_RATE = 0.9


def padded_2(cells, sides, width):
    for axis, dim in sides:
        count = lax.axis_size(axis)
        ends = count - 1
        head = lax.slice_in_dim(cells, 0, width, axis=dim)
        tail = lax.slice_in_dim(cells, cells.shape[dim] - width, cells.shape[dim], axis=dim)
        cells = jnp.concatenate(
            [
                lax.ppermute(tail, axis, [(i, (i + 1) % count) for i in range(ends)]),
                cells,
                lax.ppermute(head, axis, [((i + 1) % count, i) for i in range(ends)]),
            ],
            axis=dim,
        )
    return cells


def tap_rows(tap_table, band_kernel, first_row, row_count, height):
    row_ids = jnp.clip(first_row + jnp.arange(row_count), 0, height - 1)
    row_bands = row_ids // BAND
    band_slots = jnp.arange(band_kernel.shape[0])
    kernel_ids = jnp.sum(
        jnp.where(row_bands[:, None] == band_slots[None, :], band_kernel[None, :], 0), axis=1
    )
    kernel_slots = jnp.arange(tap_table.shape[0])
    picked = jnp.where(
        kernel_ids[:, None, None] == kernel_slots[None, :, None], tap_table[None, :, :], 0.0
    )
    return jnp.sum(picked, axis=1)


def blur_rows(padded, row_taps, row_count):
    summed = row_taps[:, 0][None, :, None] * padded[:, 0:row_count]
    for offset in range(1, 5):
        summed = (
            summed + row_taps[:, offset][None, :, None] * padded[:, offset : offset + row_count]
        )
    return summed


def back_rows(padded_quotient, outer_taps, row_count):
    summed = outer_taps[4 : 4 + row_count, 0][None, :, None] * padded_quotient[:, 4 : 4 + row_count]
    for offset in range(1, 5):
        start = 4 - offset
        summed = (
            summed
            + outer_taps[start : start + row_count, offset][None, :, None]
            * padded_quotient[:, start : start + row_count]
        )
    return summed


def temporal(series_block):
    frame_total, item_count, columns = series_block.shape
    values = series_block.astype(jnp.float32).reshape(frame_total, item_count * columns)
    frame_ids = jnp.arange(frame_total)
    at_ends = (frame_ids == 0) | (frame_ids == frame_total - 1)
    middle = (1.0 + SMOOTHING * jnp.where(at_ends, 1.0, 2.0)).astype(jnp.float32)
    sub_diag = jnp.where(frame_ids == 0, 0.0, -SMOOTHING).astype(jnp.float32)
    super_diag = jnp.where(frame_ids == frame_total - 1, 0.0, -SMOOTHING).astype(jnp.float32)
    baseline = lax.linalg.tridiagonal_solve(sub_diag, middle, super_diag, values)
    detrended = values - baseline
    earlier = jnp.concatenate(
        [jnp.zeros((1, values.shape[1]), jnp.float32), detrended[:-1]], axis=0
    )
    result = (detrended - DECAY_RATE * earlier).astype(jnp.bfloat16)
    return result.reshape(frame_total, item_count, columns)


def local(observed, kernels, band_kernel, masks):
    frames_dev, rows_dev, row_pixels = observed.shape
    height = rows_dev * lax.axis_size("row")
    tap_table = kernels / jnp.sum(kernels, axis=1, keepdims=True)
    first_row = lax.axis_index("row") * rows_dev
    own_taps = tap_rows(tap_table, band_kernel, first_row, rows_dev, height)
    outer_taps = tap_rows(tap_table, band_kernel, first_row - 2, rows_dev + 4, height)
    current = observed
    for iteration in range(ITERS):
        padded = padded_2(current, (("row", 1),), 2)
        blurred = blur_rows(padded, own_taps, rows_dev)
        quotient = observed / blurred
        padded_quotient = padded_2(quotient, (("row", 1),), 2)
        current = current * back_rows(padded_quotient, outer_taps, rows_dev)
    estimate = current.astype(jnp.bfloat16)
    spikes = temporal(lax.all_to_all(estimate, "frame", split_axis=2, concat_axis=0, tiled=True))
    frames_all, _, columns = spikes.shape
    tile_count = columns // TILE
    tile_sums = jnp.sum(
        spikes.reshape(frames_all, rows_dev * tile_count, TILE).astype(jnp.float32), axis=2
    )
    weights = masks.astype(jnp.float32).reshape(masks.shape[0], rows_dev * tile_count)
    local_sums = lax.dot_general(
        weights, tile_sums, (((1,), (1,)), ((), ())), precision=lax.Precision.HIGHEST
    )
    counts = jnp.sum(weights, axis=1)
    trace_sums, totals = (
        lax.psum_scatter(local_sums, ("frame", "row"), scatter_dimension=0, tiled=True),
        lax.psum_scatter(counts, ("frame", "row"), scatter_dimension=0, tiled=True),
    )
    traces = trace_sums / (TILE * totals[:, None])
    return (spikes, traces)


def halo_kernel(observed_ref, inner_ref, outer_ref, own_ref, arrived):
    even = lax.axis_index("row") % 2 == 0
    frames = own_ref.shape[0]
    copies = [
        pltpu.make_async_copy(observed_ref.at[frame], own_ref.at[frame], arrived.at[frame]) for frame in range(frames)
    ]
    for copy in copies:
        copy.start()
    for frame, copy in enumerate(copies):
        copy.wait()
        near = frame * NEAR
        far = frames * NEAR + frame * FAR
        bottom, top = own_ref[frame, -NEAR:, :], own_ref[frame, :NEAR, :]
        inner_ref[near : near + NEAR, :] = jnp.where(even, bottom, top)
        outer_ref[near : near + NEAR, :] = jnp.where(even, top, bottom)
        bottom, top = own_ref[frame, -NEAR - FAR : -NEAR, :], own_ref[frame, NEAR : NEAR + FAR, :]
        inner_ref[far : far + FAR, :] = jnp.where(even, bottom, top)
        outer_ref[far : far + FAR, :] = jnp.where(even, top, bottom)


def taps_kernel(band_ref, kernels_ref, taps_ref, back_ref, pad_ref, *, height, rows_dev):
    span = rows_dev + 2 * MARGIN
    first_row = lax.axis_index("row") * rows_dev - MARGIN
    row_ids = lax.broadcasted_iota(jnp.int32, (BAND, TILE), 0)
    pad_ref[...] = jnp.zeros_like(pad_ref)
    for band in range(span // BAND):
        row = first_row + band * BAND
        inside = (row >= 0) & (row < height)
        kernel = band_ref[jnp.clip(row, 0, height - 1) // BAND]
        centre = jnp.full((BAND, TILE), kernels_ref[kernel, TAPS // 2], jnp.float32)
        start = band * BAND
        for slot, tap in enumerate(SIDES):
            weight = jnp.full((BAND, TILE), kernels_ref[kernel, tap], jnp.float32) / centre
            target = row_ids + (row + tap - TAPS // 2)
            weight = jnp.where(inside & (target >= 0) & (target < height), weight, 0.0)
            taps_ref[slot, start : start + BAND, :] = weight
            pad_ref[slot, BAND + start : 2 * BAND + start, :] = weight
    for slot, tap in enumerate(SIDES):
        start = BAND + TAPS // 2 - tap
        back_ref[slot] = pad_ref[slot, start : start + span, :]


def feet_kernel(masks_ref, feet_ref):
    rows_dev = masks_ref.shape[0]
    flat = jnp.concatenate([masks_ref[row].astype(jnp.float32) for row in range(rows_dev)], axis=0)
    positions = flat.shape[0]
    both = jnp.concatenate([flat, flat], axis=0).T
    half = feet_ref.shape[1]
    left = lax.broadcasted_iota(jnp.int32, (half, TILE), 1) < positions
    for block in range(feet_ref.shape[0]):
        start = 2 * block * half
        halves = jnp.where(left, both[start : start + half], both[start + half : start + 2 * half])
        feet_ref[block] = halves.astype(jnp.bfloat16)


def restore_kernel(
    taps_ref, back_ref, feet_ref, own_ref, top_ref, bottom_ref, out_ref, side_ref, image_ref, current_ref, quotient_ref
):
    n_frame = out_ref.shape[0]
    frames, rows_dev, width = own_ref.shape
    tiles_dev = width // (n_frame * TILE)
    positions = rows_dev * tiles_dev
    for ref in (image_ref, current_ref, quotient_ref):
        ref[...] = jnp.ones_like(ref)

    def columns_step(step, carry):
        columns = pl.ds(pl.multiple_of(step * TILE, TILE), TILE)
        for frame in range(frames):
            near, far = frame * NEAR, frames * NEAR + frame * FAR
            start, stop = PAD + MARGIN, PAD + MARGIN + rows_dev
            image_ref[frame, start - NEAR - FAR : start - NEAR, :] = top_ref[far : far + FAR, columns]
            image_ref[frame, start - NEAR : start, :] = top_ref[near : near + NEAR, columns]
            image_ref[frame, stop : stop + NEAR, :] = bottom_ref[near : near + NEAR, columns]
            image_ref[frame, stop + NEAR : stop + NEAR + FAR, :] = bottom_ref[far : far + FAR, columns]
            image_ref[frame, start:stop, :] = own_ref[frame, :, columns]
        source_ref = image_ref
        for (first, last), (back_first, back_last) in STEPS:
            for row in range(first, last, BAND):
                weights = [taps_ref[slot, row : row + BAND, :] for slot in range(len(SIDES))]
                for frame in range(frames):
                    rows = slice(PAD + row, PAD + row + BAND)
                    blurred = source_ref[frame, rows, :]
                    for weight, tap in zip(weights, SIDES):
                        start = PAD + row + tap - TAPS // 2
                        blurred = blurred + weight * source_ref[frame, start : start + BAND, :]
                    quotient_ref[frame, rows, :] = image_ref[frame, rows, :] / blurred
            for row in range(back_first, back_last, BAND):
                weights = [back_ref[slot, row : row + BAND, :] for slot in range(len(SIDES))]
                for frame in range(frames):
                    rows = slice(PAD + row, PAD + row + BAND)
                    spread = quotient_ref[frame, rows, :]
                    for weight, tap in zip(weights, SIDES):
                        start = PAD + row - tap + TAPS // 2
                        spread = spread + weight * quotient_ref[frame, start : start + BAND, :]
                    current_ref[frame, rows, :] = source_ref[frame, rows, :] * spread
            source_ref = current_ref
        first = pl.multiple_of(lax.rem(step, tiles_dev) * rows_dev, rows_dev)
        for frame in range(frames):
            estimate = current_ref[frame, PAD + MARGIN : PAD + MARGIN + rows_dev, :].astype(jnp.bfloat16)
            start = pl.multiple_of(first + frame * positions, rows_dev)
            out_ref[step // tiles_dev, pl.ds(start, rows_dev), :] = estimate
        return carry

    lax.fori_loop(0, n_frame * tiles_dev, columns_step, 0)
    lane_tiles = lax.broadcasted_iota(jnp.int32, (TILE, TILE), 1) % tiles_dev
    gathered = jnp.zeros((frames * n_frame * rows_dev, TILE), jnp.float32)
    for tile in range(tiles_dev):
        pieces = []
        for frame in range(frames):
            start = frame * positions + tile * rows_dev
            pieces += [out_ref[block, start : start + rows_dev, :] for block in range(n_frame)]
        picked = jnp.where(lane_tiles == tile, 1.0, 0.0).astype(jnp.bfloat16)
        gathered = gathered + jnp.dot(jnp.concatenate(pieces, axis=0), picked, preferred_element_type=jnp.float32)
    lanes = lax.broadcasted_iota(jnp.int32, (rows_dev, TILE), 1)
    here = lanes % positions // tiles_dev == lax.broadcasted_iota(jnp.int32, (rows_dev, TILE), 0)
    sums = []
    for place in range(frames * n_frame):
        part = jnp.where(here, gathered[place * rows_dev : (place + 1) * rows_dev], 0.0)
        sums.append(jnp.sum(part, axis=0, keepdims=True))
    sums = jnp.concatenate(sums, axis=0)
    high = sums.astype(jnp.bfloat16).astype(jnp.float32)
    split = jnp.where(lax.broadcasted_iota(jnp.int32, sums.shape, 1) < positions, high, sums - high).astype(jnp.bfloat16)
    for block in range(n_frame):
        side_ref[block, : split.shape[0], :] = split
        side_ref[block, split.shape[0] :, :] = feet_ref[block]


def deconvolved(series):
    total = len(series)
    factors = []
    for step in range(total):
        middle = 1.0 + SMOOTHING * (1.0 if step in (0, total - 1) else 2.0)
        if step:
            middle -= SMOOTHING * SMOOTHING * factors[-1]
        factors.append(1.0 / middle)
    forward = [series[0] * factors[0]]
    for step in range(1, total):
        forward.append((series[step] + SMOOTHING * forward[step - 1]) * factors[step])
    baseline = [None] * total
    baseline[total - 1] = forward[total - 1]
    for step in range(total - 2, -1, -1):
        baseline[step] = forward[step] + (SMOOTHING * factors[step]) * baseline[step + 1]
    result, earlier = [], None
    for step in range(total):
        detrended = series[step] - baseline[step]
        result.append(detrended if earlier is None else detrended - DECAY_RATE * earlier)
        earlier = detrended
    return result


def partial_kernel(*refs, positions):
    pieces, (out_ref, sums_ref, feet_ref) = refs[:-3], refs[-3:]
    n_frame = len(pieces)
    place = lax.axis_index("frame")
    rows = sums_ref.shape[0] // n_frame
    half = feet_ref.shape[1]
    for step, piece in enumerate(pieces[::-1]):
        sums_ref[pl.ds(pl.multiple_of((place ^ step) * rows, rows), rows), :] = piece[:rows, :].astype(jnp.float32)
        feet_ref[place ^ step] = piece[rows:, :].astype(jnp.float32)
    series = [sums_ref[t * n_frame : (t + 1) * n_frame, :] for t in range(rows)]
    for t, sums in enumerate(deconvolved(series)):
        sums_ref[t * n_frame : (t + 1) * n_frame, :] = sums + pltpu.roll(sums, TILE // 2, 1)
    left = lax.broadcasted_iota(jnp.int32, (half, TILE), 1) < positions
    weights, sums = [], []
    extra = jnp.where(lax.broadcasted_iota(jnp.int32, (8, TILE), 0) == 0, 1.0, 0.0)
    for block in range(n_frame):
        feet = feet_ref[block]
        weights.append(jnp.concatenate([jnp.where(left, feet, 0.0), jnp.where(left, 0.0, feet)], axis=0))
        sums.append(jnp.concatenate([sums_ref[pl.ds(block, rows, stride=n_frame), :], extra], axis=0))
    totals = lax.dot_general(
        jnp.concatenate(weights, axis=1),
        jnp.concatenate(sums, axis=1),
        (((1,), (1,)), ((), ())),
        precision=lax.Precision.HIGHEST,
        preferred_element_type=jnp.float32,
    )
    share = out_ref.shape[1]
    out_ref[...] = jnp.zeros_like(out_ref)
    for row in range(out_ref.shape[0]):
        out_ref[row, :, : rows + 8] = totals[row * share : (row + 1) * share]


def temporal_kernel(*refs, frames):
    pieces, (spikes_ref, in_ref) = refs[:-2], refs[-2:]
    place = lax.axis_index("frame")
    for step, piece in enumerate(pieces[::-1]):
        in_ref[place ^ step] = piece[...]
    total, rows_dev, columns = spikes_ref.shape
    positions = in_ref.shape[1] // frames
    for tile in range(columns // TILE):
        series = []
        for t in range(total):
            start = t % frames * positions + tile * rows_dev
            series.append(in_ref[t // frames, start : start + rows_dev, :].astype(jnp.float32))
        for t, spikes in enumerate(deconvolved(series)):
            spikes_ref[t, :, tile * TILE : (tile + 1) * TILE] = spikes.astype(spikes_ref.dtype)


def means_kernel(*refs):
    pieces, traces_ref = refs[:-1], refs[-1]
    frames = traces_ref.shape[1]
    total = pieces[0][...]
    for piece in pieces[1:]:
        total = total + piece[...]
    traces_ref[...] = total[:, :frames] / (TILE * total[:, frames : frames + 1])


def swapped(parts, axis):
    count, place = lax.axis_size(axis), lax.axis_index(axis)
    arrived = [lax.dynamic_index_in_dim(parts, place, 0, keepdims=False, allow_negative_indices=False)]
    for step in range(1, count):
        part = lax.dynamic_index_in_dim(parts, place ^ step, 0, keepdims=False, allow_negative_indices=False)
        arrived.append(lax.ppermute(part, axis, [(i, i ^ step) for i in range(count)]))
    return arrived


def in_turn(*arrays):
    done = []
    for array in arrays:
        done = list(lax.optimization_barrier((*done, array)))
    return done


def by_halo(observed, kernels, band_kernel, masks):
    n_frame, n_row = lax.axis_size("frame"), lax.axis_size("row")
    frames, rows_dev, width = observed.shape
    components, _, tiles_dev = masks.shape
    positions = rows_dev * tiles_dev
    share = components // (n_frame * n_row)
    span = rows_dev + 2 * MARGIN
    smem, vmem = pl.BlockSpec(memory_space=pltpu.SMEM), pl.BlockSpec(memory_space=pltpu.VMEM)

    def call(kernel, name, in_specs, out_shape, scratch=(), cost=1000):
        many = isinstance(out_shape, tuple)
        return pl.pallas_call(
            kernel,
            name=name,
            out_shape=out_shape,
            in_specs=in_specs,
            out_specs=(vmem,) * len(out_shape) if many else vmem,
            scratch_shapes=scratch,
            compiler_params=pltpu.CompilerParams(vmem_limit_bytes=16 << 20),
            cost_estimate=pl.CostEstimate(flops=cost, bytes_accessed=cost, transcendentals=0),
        )

    def array(*shape, dtype=jnp.float32):
        return jax.ShapeDtypeStruct(shape, dtype)

    packed = array(frames * (NEAR + FAR), width)
    inner, outer, own = call(
        halo_kernel,
        "halo",
        [pl.BlockSpec(memory_space=pltpu.HBM)],
        (packed, packed, array(*observed.shape)),
        [pltpu.SemaphoreType.DMA((frames,))],
    )(pltpu.with_memory_space_constraint(observed, pltpu.HBM))
    swaps = [
        [pair for i in range(first, n_row - 1, 2) for pair in ((i, i + 1), (i + 1, i))] for first in (0, 1)
    ]
    inner, outer = (lax.ppermute(rows.astype(jnp.float16), "row", swap) for rows, swap in zip((inner, outer), swaps))
    outer, inner = in_turn(outer, inner)
    taps, back = call(
        functools.partial(taps_kernel, height=rows_dev * n_row, rows_dev=rows_dev),
        "taps",
        [smem, smem],
        (array(len(SIDES), span, TILE),) * 2,
        [pltpu.VMEM((len(SIDES), span + 2 * PAD, TILE), jnp.float32)],
    )(band_kernel, kernels)
    feet = call(feet_kernel, "feet", [vmem], array(n_frame, n_row * share // 2, TILE, dtype=jnp.bfloat16))(
        masks.transpose(1, 2, 0)
    )
    row = lax.axis_index("row")
    even = row % 2 == 0
    alone = (row == 0) | (row == n_row - 1)
    inner, outer = inner.astype(jnp.float32), jnp.where(alone, 1.0, outer.astype(jnp.float32))
    top, bottom = jnp.where(even, outer, inner), jnp.where(even, inner, outer)
    side_rows = frames * n_frame + n_row * share // 2
    blocks, sides = call(
        restore_kernel,
        "restore",
        [vmem] * 6,
        (
            array(n_frame, frames * positions, TILE, dtype=jnp.bfloat16),
            array(n_frame, side_rows, TILE, dtype=jnp.bfloat16),
        ),
        [pltpu.VMEM((frames, span + 2 * PAD, TILE), jnp.float32)] * 3,
    )(taps, back, feet, own, top, bottom)
    sides = swapped(sides, "frame")
    pieces = swapped(blocks, "frame")
    partial = call(
        functools.partial(partial_kernel, positions=positions),
        "partial",
        [vmem] * n_frame,
        array(n_row, share, TILE),
        [
            pltpu.VMEM((n_frame * frames * n_frame, TILE), jnp.float32),
            pltpu.VMEM((n_frame, n_row * share // 2, TILE), jnp.float32),
        ],
    )(*sides[::-1])
    shares = swapped(partial, "row")
    spikes = call(
        functools.partial(temporal_kernel, frames=frames),
        "temporal",
        [vmem] * n_frame,
        array(n_frame * frames, rows_dev, tiles_dev * TILE, dtype=jnp.bfloat16),
        [pltpu.VMEM((n_frame, frames * positions, TILE), jnp.bfloat16)],
    )(*pieces[::-1])
    spikes, *shares = in_turn(spikes, *shares[::-1])
    traces = call(means_kernel, "means", [vmem] * n_row, array(share, n_frame * frames))(*shares)
    return (spikes, traces)


def fits(mesh, observed, masks):
    frames_dev = observed.shape[0] // mesh.shape["frame"]
    rows_dev = masks.shape[1] // (mesh.shape["groups"] * mesh.shape["row"])
    tiles_dev = masks.shape[2] // mesh.shape["frame"]
    places = mesh.shape["frame"] * mesh.shape["row"]
    return (
        frames_dev == mesh.shape["frame"] == mesh.shape["row"] == 4
        and 2 * rows_dev * tiles_dev == TILE
        and rows_dev == 16
        and masks.shape[0] // places == 16
    )


def solution(mesh):
    in_specs = (
        P("frame", ("groups", "row"), None),
        P(),
        P("groups"),
        P(None, ("groups", "row"), "frame"),
    )
    out_specs = (P(None, ("groups", "row"), "frame"), P(("groups", "frame", "row"), None))

    def whole(observed, kernels, band_kernel, masks):
        body = by_halo if fits(mesh, observed, masks) else local
        mapped = jax.shard_map(body, mesh=mesh, in_specs=in_specs, out_specs=out_specs, check_vma=False)
        return mapped(observed, kernels, band_kernel, masks)

    return whole
```

```python
import functools

import jax
import jax.numpy as jnp
from jax import lax
from jax.experimental import pallas as pl
from jax.experimental.pallas import tpu as pltpu
from jax.sharding import PartitionSpec as P

TILE = 128
BAND = 8
ITERS = 3
TAPS = 5
NEAR, FAR = 8, 4
MARGIN = 2 * BAND
PAD = BAND
STEPS = (((6, 46), (8, 40)), ((10, 42), (12, 36)), ((14, 38), (16, 32)))
SIDES = (0, 1, 3, 4)


SMOOTHING = 1024.0
DECAY_RATE = 0.9


def padded_2(cells, sides, width):
    for axis, dim in sides:
        count = lax.axis_size(axis)
        ends = count - 1
        head = lax.slice_in_dim(cells, 0, width, axis=dim)
        tail = lax.slice_in_dim(cells, cells.shape[dim] - width, cells.shape[dim], axis=dim)
        cells = jnp.concatenate(
            [
                lax.ppermute(tail, axis, [(i, (i + 1) % count) for i in range(ends)]),
                cells,
                lax.ppermute(head, axis, [((i + 1) % count, i) for i in range(ends)]),
            ],
            axis=dim,
        )
    return cells


def tap_rows(tap_table, band_kernel, first_row, row_count, height):
    row_ids = jnp.clip(first_row + jnp.arange(row_count), 0, height - 1)
    row_bands = row_ids // BAND
    band_slots = jnp.arange(band_kernel.shape[0])
    kernel_ids = jnp.sum(
        jnp.where(row_bands[:, None] == band_slots[None, :], band_kernel[None, :], 0), axis=1
    )
    kernel_slots = jnp.arange(tap_table.shape[0])
    picked = jnp.where(
        kernel_ids[:, None, None] == kernel_slots[None, :, None], tap_table[None, :, :], 0.0
    )
    return jnp.sum(picked, axis=1)


def blur_rows(padded, row_taps, row_count):
    summed = row_taps[:, 0][None, :, None] * padded[:, 0:row_count]
    for offset in range(1, 5):
        summed = (
            summed + row_taps[:, offset][None, :, None] * padded[:, offset : offset + row_count]
        )
    return summed


def back_rows(padded_quotient, outer_taps, row_count):
    summed = outer_taps[4 : 4 + row_count, 0][None, :, None] * padded_quotient[:, 4 : 4 + row_count]
    for offset in range(1, 5):
        start = 4 - offset
        summed = (
            summed
            + outer_taps[start : start + row_count, offset][None, :, None]
            * padded_quotient[:, start : start + row_count]
        )
    return summed


def temporal(series_block):
    frame_total, item_count, columns = series_block.shape
    values = series_block.astype(jnp.float32).reshape(frame_total, item_count * columns)
    frame_ids = jnp.arange(frame_total)
    at_ends = (frame_ids == 0) | (frame_ids == frame_total - 1)
    middle = (1.0 + SMOOTHING * jnp.where(at_ends, 1.0, 2.0)).astype(jnp.float32)
    sub_diag = jnp.where(frame_ids == 0, 0.0, -SMOOTHING).astype(jnp.float32)
    super_diag = jnp.where(frame_ids == frame_total - 1, 0.0, -SMOOTHING).astype(jnp.float32)
    baseline = lax.linalg.tridiagonal_solve(sub_diag, middle, super_diag, values)
    detrended = values - baseline
    earlier = jnp.concatenate(
        [jnp.zeros((1, values.shape[1]), jnp.float32), detrended[:-1]], axis=0
    )
    result = (detrended - DECAY_RATE * earlier).astype(jnp.bfloat16)
    return result.reshape(frame_total, item_count, columns)


def local(observed, kernels, band_kernel, masks):
    frames_dev, rows_dev, row_pixels = observed.shape
    height = rows_dev * lax.axis_size("row")
    tap_table = kernels / jnp.sum(kernels, axis=1, keepdims=True)
    first_row = lax.axis_index("row") * rows_dev
    own_taps = tap_rows(tap_table, band_kernel, first_row, rows_dev, height)
    outer_taps = tap_rows(tap_table, band_kernel, first_row - 2, rows_dev + 4, height)
    current = observed
    for iteration in range(ITERS):
        padded = padded_2(current, (("row", 1),), 2)
        blurred = blur_rows(padded, own_taps, rows_dev)
        quotient = observed / blurred
        padded_quotient = padded_2(quotient, (("row", 1),), 2)
        current = current * back_rows(padded_quotient, outer_taps, rows_dev)
    estimate = current.astype(jnp.bfloat16)
    spikes = temporal(lax.all_to_all(estimate, "frame", split_axis=2, concat_axis=0, tiled=True))
    frames_all, _, columns = spikes.shape
    tile_count = columns // TILE
    tile_sums = jnp.sum(
        spikes.reshape(frames_all, rows_dev * tile_count, TILE).astype(jnp.float32), axis=2
    )
    weights = masks.astype(jnp.float32).reshape(masks.shape[0], rows_dev * tile_count)
    local_sums = lax.dot_general(
        weights, tile_sums, (((1,), (1,)), ((), ())), precision=lax.Precision.HIGHEST
    )
    counts = jnp.sum(weights, axis=1)
    trace_sums, totals = (
        lax.psum_scatter(local_sums, ("frame", "row"), scatter_dimension=0, tiled=True),
        lax.psum_scatter(counts, ("frame", "row"), scatter_dimension=0, tiled=True),
    )
    traces = trace_sums / (TILE * totals[:, None])
    return (spikes, traces)


def halo_kernel(observed_ref, inner_ref, outer_ref, own_ref):
    even = lax.axis_index("row") % 2 == 0
    frames = observed_ref.shape[0]
    own_ref[...] = observed_ref[...]
    for frame in range(frames):
        near = frame * NEAR
        far = frames * NEAR + frame * FAR
        bottom, top = observed_ref[frame, -NEAR:, :], observed_ref[frame, :NEAR, :]
        inner_ref[near : near + NEAR, :] = jnp.where(even, bottom, top)
        outer_ref[near : near + NEAR, :] = jnp.where(even, top, bottom)
        bottom, top = observed_ref[frame, -NEAR - FAR : -NEAR, :], observed_ref[frame, NEAR : NEAR + FAR, :]
        inner_ref[far : far + FAR, :] = jnp.where(even, bottom, top)
        outer_ref[far : far + FAR, :] = jnp.where(even, top, bottom)


def taps_kernel(band_ref, kernels_ref, taps_ref, back_ref, pad_ref, *, height, rows_dev):
    span = rows_dev + 2 * MARGIN
    first_row = lax.axis_index("row") * rows_dev - MARGIN
    row_ids = lax.broadcasted_iota(jnp.int32, (BAND, TILE), 0)
    pad_ref[...] = jnp.zeros_like(pad_ref)
    for band in range(span // BAND):
        row = first_row + band * BAND
        inside = (row >= 0) & (row < height)
        kernel = band_ref[jnp.clip(row, 0, height - 1) // BAND]
        centre = jnp.full((BAND, TILE), kernels_ref[kernel, TAPS // 2], jnp.float32)
        start = band * BAND
        for slot, tap in enumerate(SIDES):
            weight = jnp.full((BAND, TILE), kernels_ref[kernel, tap], jnp.float32) / centre
            target = row_ids + (row + tap - TAPS // 2)
            weight = jnp.where(inside & (target >= 0) & (target < height), weight, 0.0)
            taps_ref[slot, start : start + BAND, :] = weight
            pad_ref[slot, BAND + start : 2 * BAND + start, :] = weight
    for slot, tap in enumerate(SIDES):
        start = BAND + TAPS // 2 - tap
        back_ref[slot] = pad_ref[slot, start : start + span, :]


def feet_kernel(masks_ref, feet_ref):
    rows_dev = masks_ref.shape[0]
    flat = jnp.concatenate([masks_ref[row].astype(jnp.float32) for row in range(rows_dev)], axis=0)
    positions = flat.shape[0]
    both = jnp.concatenate([flat, flat], axis=0).T
    half = feet_ref.shape[1]
    left = lax.broadcasted_iota(jnp.int32, (half, TILE), 1) < positions
    for block in range(feet_ref.shape[0]):
        start = 2 * block * half
        halves = jnp.where(left, both[start : start + half], both[start + half : start + 2 * half])
        feet_ref[block] = halves.astype(jnp.bfloat16)


def restore_kernel(
    taps_ref, back_ref, feet_ref, own_ref, top_ref, bottom_ref, out_ref, side_ref, image_ref, current_ref, quotient_ref
):
    n_frame = out_ref.shape[0]
    frames, rows_dev, width = own_ref.shape
    tiles_dev = width // (n_frame * TILE)
    positions = rows_dev * tiles_dev
    for ref in (image_ref, current_ref, quotient_ref):
        ref[...] = jnp.ones_like(ref)

    def columns_step(step, carry):
        columns = pl.ds(pl.multiple_of(step * TILE, TILE), TILE)
        for frame in range(frames):
            near, far = frame * NEAR, frames * NEAR + frame * FAR
            start, stop = PAD + MARGIN, PAD + MARGIN + rows_dev
            image_ref[frame, start - NEAR - FAR : start - NEAR, :] = top_ref[far : far + FAR, columns]
            image_ref[frame, start - NEAR : start, :] = top_ref[near : near + NEAR, columns]
            image_ref[frame, stop : stop + NEAR, :] = bottom_ref[near : near + NEAR, columns]
            image_ref[frame, stop + NEAR : stop + NEAR + FAR, :] = bottom_ref[far : far + FAR, columns]
            image_ref[frame, start:stop, :] = own_ref[frame, :, columns]
        source_ref = image_ref
        for (first, last), (back_first, back_last) in STEPS:
            for row in range(first, last, BAND):
                weights = [taps_ref[slot, row : row + BAND, :] for slot in range(len(SIDES))]
                for frame in range(frames):
                    rows = slice(PAD + row, PAD + row + BAND)
                    terms = []
                    for weight, tap in zip(weights, SIDES):
                        start = PAD + row + tap - TAPS // 2
                        terms.append(weight * source_ref[frame, start : start + BAND, :])
                    blurred = source_ref[frame, rows, :] + ((terms[0] + terms[1]) + (terms[2] + terms[3]))
                    quotient_ref[frame, rows, :] = image_ref[frame, rows, :] / blurred
            for row in range(back_first, back_last, BAND):
                weights = [back_ref[slot, row : row + BAND, :] for slot in range(len(SIDES))]
                for frame in range(frames):
                    rows = slice(PAD + row, PAD + row + BAND)
                    terms = []
                    for weight, tap in zip(weights, SIDES):
                        start = PAD + row - tap + TAPS // 2
                        terms.append(weight * quotient_ref[frame, start : start + BAND, :])
                    spread = quotient_ref[frame, rows, :] + ((terms[0] + terms[1]) + (terms[2] + terms[3]))
                    current_ref[frame, rows, :] = source_ref[frame, rows, :] * spread
            source_ref = current_ref
        first = pl.multiple_of(lax.rem(step, tiles_dev) * rows_dev, rows_dev)
        for frame in range(frames):
            estimate = current_ref[frame, PAD + MARGIN : PAD + MARGIN + rows_dev, :].astype(jnp.bfloat16)
            start = pl.multiple_of(first + frame * positions, rows_dev)
            out_ref[step // tiles_dev, pl.ds(start, rows_dev), :] = estimate
        return carry

    lax.fori_loop(0, n_frame * tiles_dev, columns_step, 0, unroll=2)
    lane_tiles = lax.broadcasted_iota(jnp.int32, (TILE, TILE), 1) % tiles_dev
    gathered = jnp.zeros((frames * n_frame * rows_dev, TILE), jnp.float32)
    for tile in range(tiles_dev):
        pieces = []
        for frame in range(frames):
            start = frame * positions + tile * rows_dev
            pieces += [out_ref[block, start : start + rows_dev, :] for block in range(n_frame)]
        picked = jnp.where(lane_tiles == tile, 1.0, 0.0).astype(jnp.bfloat16)
        gathered = gathered + jnp.dot(jnp.concatenate(pieces, axis=0), picked, preferred_element_type=jnp.float32)
    lanes = lax.broadcasted_iota(jnp.int32, (rows_dev, TILE), 1)
    here = lanes % positions // tiles_dev == lax.broadcasted_iota(jnp.int32, (rows_dev, TILE), 0)
    sums = []
    for place in range(frames * n_frame):
        part = jnp.where(here, gathered[place * rows_dev : (place + 1) * rows_dev], 0.0)
        sums.append(jnp.sum(part, axis=0, keepdims=True))
    sums = jnp.concatenate(sums, axis=0)
    high = sums.astype(jnp.bfloat16).astype(jnp.float32)
    split = jnp.where(lax.broadcasted_iota(jnp.int32, sums.shape, 1) < positions, high, sums - high).astype(jnp.bfloat16)
    for block in range(n_frame):
        side_ref[block, : split.shape[0], :] = split
        side_ref[block, split.shape[0] :, :] = feet_ref[block]


def deconvolved(series):
    total = len(series)
    factors = []
    for step in range(total):
        middle = 1.0 + SMOOTHING * (1.0 if step in (0, total - 1) else 2.0)
        if step:
            middle -= SMOOTHING * SMOOTHING * factors[-1]
        factors.append(1.0 / middle)
    forward = [series[0] * factors[0]]
    for step in range(1, total):
        forward.append((series[step] + SMOOTHING * forward[step - 1]) * factors[step])
    baseline = [None] * total
    baseline[total - 1] = forward[total - 1]
    for step in range(total - 2, -1, -1):
        baseline[step] = forward[step] + (SMOOTHING * factors[step]) * baseline[step + 1]
    result, earlier = [], None
    for step in range(total):
        detrended = series[step] - baseline[step]
        result.append(detrended if earlier is None else detrended - DECAY_RATE * earlier)
        earlier = detrended
    return result


def partial_kernel(*refs, positions):
    pieces, (out_ref, sums_ref, feet_ref) = refs[:-3], refs[-3:]
    n_frame = len(pieces)
    place = lax.axis_index("frame")
    rows = sums_ref.shape[0] // n_frame
    half = feet_ref.shape[1]
    for step, piece in enumerate(pieces[::-1]):
        sums_ref[pl.ds(pl.multiple_of((place ^ step) * rows, rows), rows), :] = piece[:rows, :].astype(jnp.float32)
        feet_ref[place ^ step] = piece[rows:, :].astype(jnp.float32)
    series = [sums_ref[t * n_frame : (t + 1) * n_frame, :] for t in range(rows)]
    for t, sums in enumerate(deconvolved(series)):
        sums_ref[t * n_frame : (t + 1) * n_frame, :] = sums + pltpu.roll(sums, TILE // 2, 1)
    left = lax.broadcasted_iota(jnp.int32, (half, TILE), 1) < positions
    weights, sums = [], []
    extra = jnp.where(lax.broadcasted_iota(jnp.int32, (8, TILE), 0) == 0, 1.0, 0.0)
    for block in range(n_frame):
        feet = feet_ref[block]
        weights.append(jnp.concatenate([jnp.where(left, feet, 0.0), jnp.where(left, 0.0, feet)], axis=0))
        sums.append(jnp.concatenate([sums_ref[pl.ds(block, rows, stride=n_frame), :], extra], axis=0))
    totals = lax.dot_general(
        jnp.concatenate(weights, axis=1),
        jnp.concatenate(sums, axis=1),
        (((1,), (1,)), ((), ())),
        precision=lax.Precision.HIGHEST,
        preferred_element_type=jnp.float32,
    )
    share = out_ref.shape[1]
    out_ref[...] = jnp.zeros_like(out_ref)
    for row in range(out_ref.shape[0]):
        out_ref[row, :, : rows + 8] = totals[row * share : (row + 1) * share]


def temporal_kernel(*refs, frames):
    pieces, (spikes_ref, in_ref) = refs[:-2], refs[-2:]
    place = lax.axis_index("frame")
    for step, piece in enumerate(pieces[::-1]):
        in_ref[place ^ step] = piece[...]
    total, rows_dev, columns = spikes_ref.shape
    positions = in_ref.shape[1] // frames
    for tile in range(columns // TILE):
        series = []
        for t in range(total):
            start = t % frames * positions + tile * rows_dev
            series.append(in_ref[t // frames, start : start + rows_dev, :].astype(jnp.float32))
        for t, spikes in enumerate(deconvolved(series)):
            spikes_ref[t, :, tile * TILE : (tile + 1) * TILE] = spikes.astype(spikes_ref.dtype)


def means_kernel(*refs):
    pieces, traces_ref = refs[:-1], refs[-1]
    frames = traces_ref.shape[1]
    total = pieces[0][...]
    for piece in pieces[1:]:
        total = total + piece[...]
    traces_ref[...] = total[:, :frames] / (TILE * total[:, frames : frames + 1])


def swapped(parts, axis):
    count, place = lax.axis_size(axis), lax.axis_index(axis)
    arrived = [lax.dynamic_index_in_dim(parts, place, 0, keepdims=False, allow_negative_indices=False)]
    for step in range(1, count):
        part = lax.dynamic_index_in_dim(parts, place ^ step, 0, keepdims=False, allow_negative_indices=False)
        arrived.append(lax.ppermute(part, axis, [(i, i ^ step) for i in range(count)]))
    return arrived


def in_turn(*arrays):
    done = []
    for array in arrays:
        done = list(lax.optimization_barrier((*done, array)))
    return done


def by_halo(observed, kernels, band_kernel, masks):
    n_frame, n_row = lax.axis_size("frame"), lax.axis_size("row")
    frames, rows_dev, width = observed.shape
    components, _, tiles_dev = masks.shape
    positions = rows_dev * tiles_dev
    share = components // (n_frame * n_row)
    span = rows_dev + 2 * MARGIN
    smem, vmem = pl.BlockSpec(memory_space=pltpu.SMEM), pl.BlockSpec(memory_space=pltpu.VMEM)

    def call(kernel, name, in_specs, out_shape, scratch=(), cost=1000):
        many = isinstance(out_shape, tuple)
        return pl.pallas_call(
            kernel,
            name=name,
            out_shape=out_shape,
            in_specs=in_specs,
            out_specs=(vmem,) * len(out_shape) if many else vmem,
            scratch_shapes=scratch,
            compiler_params=pltpu.CompilerParams(vmem_limit_bytes=16 << 20),
            cost_estimate=pl.CostEstimate(flops=cost, bytes_accessed=cost, transcendentals=0),
        )

    def array(*shape, dtype=jnp.float32):
        return jax.ShapeDtypeStruct(shape, dtype)

    packed = array(frames * (NEAR + FAR), width)
    inner, outer, own = call(halo_kernel, "halo", [vmem], (packed, packed, array(*observed.shape)))(observed)
    inner_swap = [(i, i ^ 1) for i in range(n_row)]
    outer_swap = []
    for f in range(n_frame):
        for i in range(n_row):
            there = (f ^ 1, i) if i in (0, n_row - 1) else (f, (i - 1 ^ 1) + 1)
            outer_swap.append((f * n_row + i, there[0] * n_row + there[1]))
    outer = lax.ppermute(outer.astype(jnp.float16), ("frame", "row"), outer_swap)
    inner = lax.ppermute(inner.astype(jnp.float16), "row", inner_swap)
    outer, inner = in_turn(outer, inner)
    taps, back = call(
        functools.partial(taps_kernel, height=rows_dev * n_row, rows_dev=rows_dev),
        "taps",
        [smem, smem],
        (array(len(SIDES), span, TILE),) * 2,
        [pltpu.VMEM((len(SIDES), span + 2 * PAD, TILE), jnp.float32)],
    )(band_kernel, kernels)
    feet = call(feet_kernel, "feet", [vmem], array(n_frame, n_row * share // 2, TILE, dtype=jnp.bfloat16))(
        masks.transpose(1, 2, 0)
    )
    row = lax.axis_index("row")
    even = row % 2 == 0
    alone = (row == 0) | (row == n_row - 1)
    inner, outer = inner.astype(jnp.float32), jnp.where(alone, 1.0, outer.astype(jnp.float32))
    top, bottom = jnp.where(even, outer, inner), jnp.where(even, inner, outer)
    side_rows = frames * n_frame + n_row * share // 2
    blocks, sides = call(
        restore_kernel,
        "restore",
        [vmem] * 6,
        (
            array(n_frame, frames * positions, TILE, dtype=jnp.bfloat16),
            array(n_frame, side_rows, TILE, dtype=jnp.bfloat16),
        ),
        [pltpu.VMEM((frames, span + 2 * PAD, TILE), jnp.float32)] * 3,
    )(taps, back, feet, own, top, bottom)
    sides = swapped(sides, "frame")
    pieces = swapped(blocks, "frame")
    partial = call(
        functools.partial(partial_kernel, positions=positions),
        "partial",
        [vmem] * n_frame,
        array(n_row, share, TILE),
        [
            pltpu.VMEM((n_frame * frames * n_frame, TILE), jnp.float32),
            pltpu.VMEM((n_frame, n_row * share // 2, TILE), jnp.float32),
        ],
    )(*sides[::-1])
    shares = swapped(partial, "row")
    spikes = call(
        functools.partial(temporal_kernel, frames=frames),
        "temporal",
        [vmem] * n_frame,
        array(n_frame * frames, rows_dev, tiles_dev * TILE, dtype=jnp.bfloat16),
        [pltpu.VMEM((n_frame, frames * positions, TILE), jnp.bfloat16)],
    )(*pieces[::-1])
    spikes, *shares = in_turn(spikes, *shares[::-1])
    traces = call(means_kernel, "means", [vmem] * n_row, array(share, n_frame * frames))(*shares)
    return (spikes, traces)


def fits(mesh, observed, masks):
    frames_dev = observed.shape[0] // mesh.shape["frame"]
    rows_dev = masks.shape[1] // (mesh.shape["groups"] * mesh.shape["row"])
    tiles_dev = masks.shape[2] // mesh.shape["frame"]
    places = mesh.shape["frame"] * mesh.shape["row"]
    return (
        frames_dev == mesh.shape["frame"] == mesh.shape["row"] == 4
        and 2 * rows_dev * tiles_dev == TILE
        and rows_dev == 16
        and masks.shape[0] // places == 16
    )


def solution(mesh):
    in_specs = (
        P("frame", ("groups", "row"), None),
        P(),
        P("groups"),
        P(None, ("groups", "row"), "frame"),
    )
    out_specs = (P(None, ("groups", "row"), "frame"), P(("groups", "frame", "row"), None))

    def whole(observed, kernels, band_kernel, masks):
        body = by_halo if fits(mesh, observed, masks) else local
        mapped = jax.shard_map(body, mesh=mesh, in_specs=in_specs, out_specs=out_specs, check_vma=False)
        return mapped(observed, kernels, band_kernel, masks)

    return whole
```

```python
import functools

import jax
import jax.numpy as jnp
from jax import lax
from jax.experimental import pallas as pl
from jax.experimental.pallas import tpu as pltpu
from jax.sharding import PartitionSpec as P

TILE = 128
BAND = 8
ITERS = 3
TAPS = 5
NEAR, FAR = 8, 4
MARGIN = 2 * BAND
PAD = BAND
STEPS = (((6, 46), (8, 40)), ((10, 42), (12, 36)), ((14, 38), (16, 32)))
SIDES = (0, 1, 3, 4)


SMOOTHING = 1024.0
DECAY_RATE = 0.9


def padded_2(cells, sides, width):
    for axis, dim in sides:
        count = lax.axis_size(axis)
        ends = count - 1
        head = lax.slice_in_dim(cells, 0, width, axis=dim)
        tail = lax.slice_in_dim(cells, cells.shape[dim] - width, cells.shape[dim], axis=dim)
        cells = jnp.concatenate(
            [
                lax.ppermute(tail, axis, [(i, (i + 1) % count) for i in range(ends)]),
                cells,
                lax.ppermute(head, axis, [((i + 1) % count, i) for i in range(ends)]),
            ],
            axis=dim,
        )
    return cells


def tap_rows(tap_table, band_kernel, first_row, row_count, height):
    row_ids = jnp.clip(first_row + jnp.arange(row_count), 0, height - 1)
    row_bands = row_ids // BAND
    band_slots = jnp.arange(band_kernel.shape[0])
    kernel_ids = jnp.sum(
        jnp.where(row_bands[:, None] == band_slots[None, :], band_kernel[None, :], 0), axis=1
    )
    kernel_slots = jnp.arange(tap_table.shape[0])
    picked = jnp.where(
        kernel_ids[:, None, None] == kernel_slots[None, :, None], tap_table[None, :, :], 0.0
    )
    return jnp.sum(picked, axis=1)


def blur_rows(padded, row_taps, row_count):
    summed = row_taps[:, 0][None, :, None] * padded[:, 0:row_count]
    for offset in range(1, 5):
        summed = (
            summed + row_taps[:, offset][None, :, None] * padded[:, offset : offset + row_count]
        )
    return summed


def back_rows(padded_quotient, outer_taps, row_count):
    summed = outer_taps[4 : 4 + row_count, 0][None, :, None] * padded_quotient[:, 4 : 4 + row_count]
    for offset in range(1, 5):
        start = 4 - offset
        summed = (
            summed
            + outer_taps[start : start + row_count, offset][None, :, None]
            * padded_quotient[:, start : start + row_count]
        )
    return summed


def temporal(series_block):
    frame_total, item_count, columns = series_block.shape
    values = series_block.astype(jnp.float32).reshape(frame_total, item_count * columns)
    frame_ids = jnp.arange(frame_total)
    at_ends = (frame_ids == 0) | (frame_ids == frame_total - 1)
    middle = (1.0 + SMOOTHING * jnp.where(at_ends, 1.0, 2.0)).astype(jnp.float32)
    sub_diag = jnp.where(frame_ids == 0, 0.0, -SMOOTHING).astype(jnp.float32)
    super_diag = jnp.where(frame_ids == frame_total - 1, 0.0, -SMOOTHING).astype(jnp.float32)
    baseline = lax.linalg.tridiagonal_solve(sub_diag, middle, super_diag, values)
    detrended = values - baseline
    earlier = jnp.concatenate(
        [jnp.zeros((1, values.shape[1]), jnp.float32), detrended[:-1]], axis=0
    )
    result = (detrended - DECAY_RATE * earlier).astype(jnp.bfloat16)
    return result.reshape(frame_total, item_count, columns)


def local(observed, kernels, band_kernel, masks):
    frames_dev, rows_dev, row_pixels = observed.shape
    height = rows_dev * lax.axis_size("row")
    tap_table = kernels / jnp.sum(kernels, axis=1, keepdims=True)
    first_row = lax.axis_index("row") * rows_dev
    own_taps = tap_rows(tap_table, band_kernel, first_row, rows_dev, height)
    outer_taps = tap_rows(tap_table, band_kernel, first_row - 2, rows_dev + 4, height)
    current = observed
    for iteration in range(ITERS):
        padded = padded_2(current, (("row", 1),), 2)
        blurred = blur_rows(padded, own_taps, rows_dev)
        quotient = observed / blurred
        padded_quotient = padded_2(quotient, (("row", 1),), 2)
        current = current * back_rows(padded_quotient, outer_taps, rows_dev)
    estimate = current.astype(jnp.bfloat16)
    spikes = temporal(lax.all_to_all(estimate, "frame", split_axis=2, concat_axis=0, tiled=True))
    frames_all, _, columns = spikes.shape
    tile_count = columns // TILE
    tile_sums = jnp.sum(
        spikes.reshape(frames_all, rows_dev * tile_count, TILE).astype(jnp.float32), axis=2
    )
    weights = masks.astype(jnp.float32).reshape(masks.shape[0], rows_dev * tile_count)
    local_sums = lax.dot_general(
        weights, tile_sums, (((1,), (1,)), ((), ())), precision=lax.Precision.HIGHEST
    )
    counts = jnp.sum(weights, axis=1)
    trace_sums, totals = (
        lax.psum_scatter(local_sums, ("frame", "row"), scatter_dimension=0, tiled=True),
        lax.psum_scatter(counts, ("frame", "row"), scatter_dimension=0, tiled=True),
    )
    traces = trace_sums / (TILE * totals[:, None])
    return (spikes, traces)


def halo_kernel(observed_ref, inner_ref, outer_ref, own_ref):
    even = lax.axis_index("row") % 2 == 0
    frames = observed_ref.shape[0]
    own_ref[...] = observed_ref[...]
    for frame in range(frames):
        near = frame * NEAR
        far = frames * NEAR + frame * FAR
        bottom, top = observed_ref[frame, -NEAR:, :], observed_ref[frame, :NEAR, :]
        inner_ref[near : near + NEAR, :] = jnp.where(even, bottom, top)
        outer_ref[near : near + NEAR, :] = jnp.where(even, top, bottom)
        bottom, top = observed_ref[frame, -NEAR - FAR : -NEAR, :], observed_ref[frame, NEAR : NEAR + FAR, :]
        inner_ref[far : far + FAR, :] = jnp.where(even, bottom, top)
        outer_ref[far : far + FAR, :] = jnp.where(even, top, bottom)


def taps_kernel(band_ref, kernels_ref, taps_ref, back_ref, pad_ref, *, height, rows_dev):
    span = rows_dev + 2 * MARGIN
    first_row = lax.axis_index("row") * rows_dev - MARGIN
    row_ids = lax.broadcasted_iota(jnp.int32, (BAND, TILE), 0)
    pad_ref[...] = jnp.zeros_like(pad_ref)
    for band in range(span // BAND):
        row = first_row + band * BAND
        inside = (row >= 0) & (row < height)
        kernel = band_ref[jnp.clip(row, 0, height - 1) // BAND]
        centre = jnp.full((BAND, TILE), kernels_ref[kernel, TAPS // 2], jnp.float32)
        start = band * BAND
        for slot, tap in enumerate(SIDES):
            weight = jnp.full((BAND, TILE), kernels_ref[kernel, tap], jnp.float32) / centre
            target = row_ids + (row + tap - TAPS // 2)
            weight = jnp.where(inside & (target >= 0) & (target < height), weight, 0.0)
            taps_ref[slot, start : start + BAND, :] = weight
            pad_ref[slot, BAND + start : 2 * BAND + start, :] = weight
    for slot, tap in enumerate(SIDES):
        start = BAND + TAPS // 2 - tap
        back_ref[slot] = pad_ref[slot, start : start + span, :]


def feet_kernel(masks_ref, feet_ref):
    rows_dev = masks_ref.shape[0]
    flat = jnp.concatenate([masks_ref[row].astype(jnp.float32) for row in range(rows_dev)], axis=0)
    positions = flat.shape[0]
    both = jnp.concatenate([flat, flat], axis=0).T
    half = feet_ref.shape[1]
    left = lax.broadcasted_iota(jnp.int32, (half, TILE), 1) < positions
    for block in range(feet_ref.shape[0]):
        start = 2 * block * half
        halves = jnp.where(left, both[start : start + half], both[start + half : start + 2 * half])
        feet_ref[block] = halves.astype(jnp.bfloat16)


def restore_kernel(
    taps_ref, back_ref, feet_ref, own_ref, top_ref, bottom_ref, out_ref, side_ref, image_ref, current_ref, quotient_ref
):
    n_frame = out_ref.shape[0]
    frames, rows_dev, width = own_ref.shape
    tiles_dev = width // (n_frame * TILE)
    positions = rows_dev * tiles_dev
    for ref in (image_ref, current_ref, quotient_ref):
        ref[...] = jnp.ones_like(ref)

    def columns_step(step, carry):
        columns = pl.ds(pl.multiple_of(step * TILE, TILE), TILE)
        for frame in range(frames):
            near, far = frame * NEAR, frames * NEAR + frame * FAR
            start, stop = PAD + MARGIN, PAD + MARGIN + rows_dev
            image_ref[frame, start - NEAR - FAR : start - NEAR, :] = top_ref[far : far + FAR, columns]
            image_ref[frame, start - NEAR : start, :] = top_ref[near : near + NEAR, columns]
            image_ref[frame, stop : stop + NEAR, :] = bottom_ref[near : near + NEAR, columns]
            image_ref[frame, stop + NEAR : stop + NEAR + FAR, :] = bottom_ref[far : far + FAR, columns]
            image_ref[frame, start:stop, :] = own_ref[frame, :, columns]
        source_ref = image_ref
        for (first, last), (back_first, back_last) in STEPS:
            for row in range(first, last, BAND):
                weights = [taps_ref[slot, row : row + BAND, :] for slot in range(len(SIDES))]
                for frame in range(frames):
                    rows = slice(PAD + row, PAD + row + BAND)
                    terms = []
                    for weight, tap in zip(weights, SIDES):
                        start = PAD + row + tap - TAPS // 2
                        terms.append(weight * source_ref[frame, start : start + BAND, :])
                    blurred = source_ref[frame, rows, :] + ((terms[0] + terms[1]) + (terms[2] + terms[3]))
                    quotient_ref[frame, rows, :] = image_ref[frame, rows, :] / blurred
            for row in range(back_first, back_last, BAND):
                weights = [back_ref[slot, row : row + BAND, :] for slot in range(len(SIDES))]
                for frame in range(frames):
                    rows = slice(PAD + row, PAD + row + BAND)
                    terms = []
                    for weight, tap in zip(weights, SIDES):
                        start = PAD + row - tap + TAPS // 2
                        terms.append(weight * quotient_ref[frame, start : start + BAND, :])
                    spread = quotient_ref[frame, rows, :] + ((terms[0] + terms[1]) + (terms[2] + terms[3]))
                    current_ref[frame, rows, :] = source_ref[frame, rows, :] * spread
            source_ref = current_ref
        first = pl.multiple_of(lax.rem(step, tiles_dev) * rows_dev, rows_dev)
        for frame in range(frames):
            estimate = current_ref[frame, PAD + MARGIN : PAD + MARGIN + rows_dev, :].astype(jnp.bfloat16)
            start = pl.multiple_of(first + frame * positions, rows_dev)
            out_ref[step // tiles_dev, pl.ds(start, rows_dev), :] = estimate
        return carry

    lax.fori_loop(0, n_frame * tiles_dev, columns_step, 0, unroll=2)
    lane_tiles = lax.broadcasted_iota(jnp.int32, (TILE, TILE), 1) % tiles_dev
    gathered = jnp.zeros((frames * n_frame * rows_dev, TILE), jnp.float32)
    for tile in range(tiles_dev):
        pieces = []
        for frame in range(frames):
            start = frame * positions + tile * rows_dev
            pieces += [out_ref[block, start : start + rows_dev, :] for block in range(n_frame)]
        picked = jnp.where(lane_tiles == tile, 1.0, 0.0).astype(jnp.bfloat16)
        gathered = gathered + jnp.dot(jnp.concatenate(pieces, axis=0), picked, preferred_element_type=jnp.float32)
    lanes = lax.broadcasted_iota(jnp.int32, (rows_dev, TILE), 1)
    here = lanes % positions // tiles_dev == lax.broadcasted_iota(jnp.int32, (rows_dev, TILE), 0)
    sums = []
    for place in range(frames * n_frame):
        part = jnp.where(here, gathered[place * rows_dev : (place + 1) * rows_dev], 0.0)
        sums.append(jnp.sum(part, axis=0, keepdims=True))
    sums = jnp.concatenate(sums, axis=0)
    high = sums.astype(jnp.bfloat16).astype(jnp.float32)
    split = jnp.where(lax.broadcasted_iota(jnp.int32, sums.shape, 1) < positions, high, sums - high).astype(jnp.bfloat16)
    for block in range(n_frame):
        side_ref[block, : split.shape[0], :] = split
        side_ref[block, split.shape[0] :, :] = feet_ref[block]


def deconvolved(series):
    total = len(series)
    factors = []
    for step in range(total):
        middle = 1.0 + SMOOTHING * (1.0 if step in (0, total - 1) else 2.0)
        if step:
            middle -= SMOOTHING * SMOOTHING * factors[-1]
        factors.append(1.0 / middle)
    forward = [series[0] * factors[0]]
    for step in range(1, total):
        forward.append((series[step] + SMOOTHING * forward[step - 1]) * factors[step])
    baseline = [None] * total
    baseline[total - 1] = forward[total - 1]
    for step in range(total - 2, -1, -1):
        baseline[step] = forward[step] + (SMOOTHING * factors[step]) * baseline[step + 1]
    result, earlier = [], None
    for step in range(total):
        detrended = series[step] - baseline[step]
        result.append(detrended if earlier is None else detrended - DECAY_RATE * earlier)
        earlier = detrended
    return result


def partial_kernel(*refs, positions):
    pieces, (out_ref, sums_ref, feet_ref) = refs[:-3], refs[-3:]
    n_frame = len(pieces)
    place = lax.axis_index("frame")
    rows = sums_ref.shape[0] // n_frame
    half = feet_ref.shape[1]
    for step, piece in enumerate(pieces[::-1]):
        sums_ref[pl.ds(pl.multiple_of((place ^ step) * rows, rows), rows), :] = piece[:rows, :].astype(jnp.float32)
        feet_ref[place ^ step] = piece[rows:, :].astype(jnp.float32)
    series = [sums_ref[t * n_frame : (t + 1) * n_frame, :] for t in range(rows)]
    for t, sums in enumerate(deconvolved(series)):
        sums_ref[t * n_frame : (t + 1) * n_frame, :] = sums + pltpu.roll(sums, TILE // 2, 1)
    left = lax.broadcasted_iota(jnp.int32, (half, TILE), 1) < positions
    weights, sums = [], []
    extra = jnp.where(lax.broadcasted_iota(jnp.int32, (8, TILE), 0) == 0, 1.0, 0.0)
    for block in range(n_frame):
        feet = feet_ref[block]
        weights.append(jnp.concatenate([jnp.where(left, feet, 0.0), jnp.where(left, 0.0, feet)], axis=0))
        sums.append(jnp.concatenate([sums_ref[pl.ds(block, rows, stride=n_frame), :], extra], axis=0))
    totals = lax.dot_general(
        jnp.concatenate(weights, axis=1),
        jnp.concatenate(sums, axis=1),
        (((1,), (1,)), ((), ())),
        precision=lax.Precision.HIGHEST,
        preferred_element_type=jnp.float32,
    )
    share = out_ref.shape[1]
    out_ref[...] = jnp.zeros_like(out_ref)
    for row in range(out_ref.shape[0]):
        out_ref[row, :, : rows + 8] = totals[row * share : (row + 1) * share]


def temporal_kernel(*refs, frames):
    pieces, (spikes_ref, in_ref) = refs[:-2], refs[-2:]
    place = lax.axis_index("frame")
    for step, piece in enumerate(pieces[::-1]):
        in_ref[place ^ step] = piece[...]
    total, rows_dev, columns = spikes_ref.shape
    positions = in_ref.shape[1] // frames
    for tile in range(columns // TILE):
        series = []
        for t in range(total):
            start = t % frames * positions + tile * rows_dev
            series.append(in_ref[t // frames, start : start + rows_dev, :].astype(jnp.float32))
        for t, spikes in enumerate(deconvolved(series)):
            spikes_ref[t, :, tile * TILE : (tile + 1) * TILE] = spikes.astype(spikes_ref.dtype)


def means_kernel(*refs):
    pieces, traces_ref = refs[:-1], refs[-1]
    frames = traces_ref.shape[1]
    total = pieces[0][...]
    for piece in pieces[1:]:
        total = total + piece[...]
    traces_ref[...] = total[:, :frames] / (TILE * total[:, frames : frames + 1])


def swapped(parts, axis):
    count, place = lax.axis_size(axis), lax.axis_index(axis)
    arrived = [lax.dynamic_index_in_dim(parts, place, 0, keepdims=False, allow_negative_indices=False)]
    for step in range(1, count):
        part = lax.dynamic_index_in_dim(parts, place ^ step, 0, keepdims=False, allow_negative_indices=False)
        arrived.append(lax.ppermute(part, axis, [(i, i ^ step) for i in range(count)]))
    return arrived


def in_turn(*arrays):
    done = []
    for array in arrays:
        done = list(lax.optimization_barrier((*done, array)))
    return done


def by_halo(observed, kernels, band_kernel, masks):
    n_frame, n_row = lax.axis_size("frame"), lax.axis_size("row")
    frames, rows_dev, width = observed.shape
    components, _, tiles_dev = masks.shape
    positions = rows_dev * tiles_dev
    share = components // (n_frame * n_row)
    span = rows_dev + 2 * MARGIN
    smem, vmem = pl.BlockSpec(memory_space=pltpu.SMEM), pl.BlockSpec(memory_space=pltpu.VMEM)

    def call(kernel, name, in_specs, out_shape, scratch=(), cost=1000):
        many = isinstance(out_shape, tuple)
        return pl.pallas_call(
            kernel,
            name=name,
            out_shape=out_shape,
            in_specs=in_specs,
            out_specs=(vmem,) * len(out_shape) if many else vmem,
            scratch_shapes=scratch,
            compiler_params=pltpu.CompilerParams(vmem_limit_bytes=16 << 20),
            cost_estimate=pl.CostEstimate(flops=cost, bytes_accessed=cost, transcendentals=0),
        )

    def array(*shape, dtype=jnp.float32):
        return jax.ShapeDtypeStruct(shape, dtype)

    packed = array(frames * (NEAR + FAR), width)
    inner, outer, own = call(halo_kernel, "halo", [vmem], (packed, packed, array(*observed.shape)))(observed)
    inner_swap = [(i, i ^ 1) for i in range(n_row)]
    outer_swap = []
    for f in range(n_frame):
        for i in range(n_row):
            there = (f ^ 1, i) if i in (0, n_row - 1) else (f, (i - 1 ^ 1) + 1)
            outer_swap.append((f * n_row + i, there[0] * n_row + there[1]))
    inner = lax.ppermute(inner.astype(jnp.float16), "row", inner_swap)
    outer = lax.ppermute(outer.astype(jnp.float16), ("frame", "row"), outer_swap)
    inner, outer = in_turn(inner, outer)
    taps, back = call(
        functools.partial(taps_kernel, height=rows_dev * n_row, rows_dev=rows_dev),
        "taps",
        [smem, smem],
        (array(len(SIDES), span, TILE),) * 2,
        [pltpu.VMEM((len(SIDES), span + 2 * PAD, TILE), jnp.float32)],
    )(band_kernel, kernels)
    feet = call(feet_kernel, "feet", [vmem], array(n_frame, n_row * share // 2, TILE, dtype=jnp.bfloat16))(
        masks.transpose(1, 2, 0)
    )
    row = lax.axis_index("row")
    even = row % 2 == 0
    alone = (row == 0) | (row == n_row - 1)
    inner, outer = inner.astype(jnp.float32), jnp.where(alone, 1.0, outer.astype(jnp.float32))
    top, bottom = jnp.where(even, outer, inner), jnp.where(even, inner, outer)
    side_rows = frames * n_frame + n_row * share // 2
    blocks, sides = call(
        restore_kernel,
        "restore",
        [vmem] * 6,
        (
            array(n_frame, frames * positions, TILE, dtype=jnp.bfloat16),
            array(n_frame, side_rows, TILE, dtype=jnp.bfloat16),
        ),
        [pltpu.VMEM((frames, span + 2 * PAD, TILE), jnp.float32)] * 3,
    )(taps, back, feet, own, top, bottom)
    sides = swapped(sides, "frame")
    pieces = swapped(blocks, "frame")
    partial = call(
        functools.partial(partial_kernel, positions=positions),
        "partial",
        [vmem] * n_frame,
        array(n_row, share, TILE),
        [
            pltpu.VMEM((n_frame * frames * n_frame, TILE), jnp.float32),
            pltpu.VMEM((n_frame, n_row * share // 2, TILE), jnp.float32),
        ],
    )(*sides[::-1])
    shares = swapped(partial, "row")
    spikes = call(
        functools.partial(temporal_kernel, frames=frames),
        "temporal",
        [vmem] * n_frame,
        array(n_frame * frames, rows_dev, tiles_dev * TILE, dtype=jnp.bfloat16),
        [pltpu.VMEM((n_frame, frames * positions, TILE), jnp.bfloat16)],
    )(*pieces[::-1])
    spikes, *shares = in_turn(spikes, *shares[::-1])
    traces = call(means_kernel, "means", [vmem] * n_row, array(share, n_frame * frames))(*shares)
    return (spikes, traces)


def fits(mesh, observed, masks):
    frames_dev = observed.shape[0] // mesh.shape["frame"]
    rows_dev = masks.shape[1] // (mesh.shape["groups"] * mesh.shape["row"])
    tiles_dev = masks.shape[2] // mesh.shape["frame"]
    places = mesh.shape["frame"] * mesh.shape["row"]
    return (
        frames_dev == mesh.shape["frame"] == mesh.shape["row"] == 4
        and 2 * rows_dev * tiles_dev == TILE
        and rows_dev == 16
        and masks.shape[0] // places == 16
    )


def solution(mesh):
    in_specs = (
        P("frame", ("groups", "row"), None),
        P(),
        P("groups"),
        P(None, ("groups", "row"), "frame"),
    )
    out_specs = (P(None, ("groups", "row"), "frame"), P(("groups", "frame", "row"), None))

    def whole(observed, kernels, band_kernel, masks):
        body = by_halo if fits(mesh, observed, masks) else local
        mapped = jax.shard_map(body, mesh=mesh, in_specs=in_specs, out_specs=out_specs, check_vma=False)
        return mapped(observed, kernels, band_kernel, masks)

    return whole
```

```python
import functools

import jax
import jax.numpy as jnp
from jax import lax
from jax.experimental import pallas as pl
from jax.experimental.pallas import tpu as pltpu
from jax.sharding import PartitionSpec as P

TILE = 128
BAND = 8
ITERS = 3
TAPS = 5
NEAR, FAR = 8, 4
MARGIN = 2 * BAND
PAD = BAND
STEPS = (((6, 46), (8, 40)), ((10, 42), (12, 36)), ((14, 38), (16, 32)))
SIDES = (0, 1, 3, 4)


SMOOTHING = 1024.0
DECAY_RATE = 0.9


def padded_2(cells, sides, width):
    for axis, dim in sides:
        count = lax.axis_size(axis)
        ends = count - 1
        head = lax.slice_in_dim(cells, 0, width, axis=dim)
        tail = lax.slice_in_dim(cells, cells.shape[dim] - width, cells.shape[dim], axis=dim)
        cells = jnp.concatenate(
            [
                lax.ppermute(tail, axis, [(i, (i + 1) % count) for i in range(ends)]),
                cells,
                lax.ppermute(head, axis, [((i + 1) % count, i) for i in range(ends)]),
            ],
            axis=dim,
        )
    return cells


def tap_rows(tap_table, band_kernel, first_row, row_count, height):
    row_ids = jnp.clip(first_row + jnp.arange(row_count), 0, height - 1)
    row_bands = row_ids // BAND
    band_slots = jnp.arange(band_kernel.shape[0])
    kernel_ids = jnp.sum(
        jnp.where(row_bands[:, None] == band_slots[None, :], band_kernel[None, :], 0), axis=1
    )
    kernel_slots = jnp.arange(tap_table.shape[0])
    picked = jnp.where(
        kernel_ids[:, None, None] == kernel_slots[None, :, None], tap_table[None, :, :], 0.0
    )
    return jnp.sum(picked, axis=1)


def blur_rows(padded, row_taps, row_count):
    summed = row_taps[:, 0][None, :, None] * padded[:, 0:row_count]
    for offset in range(1, 5):
        summed = (
            summed + row_taps[:, offset][None, :, None] * padded[:, offset : offset + row_count]
        )
    return summed


def back_rows(padded_quotient, outer_taps, row_count):
    summed = outer_taps[4 : 4 + row_count, 0][None, :, None] * padded_quotient[:, 4 : 4 + row_count]
    for offset in range(1, 5):
        start = 4 - offset
        summed = (
            summed
            + outer_taps[start : start + row_count, offset][None, :, None]
            * padded_quotient[:, start : start + row_count]
        )
    return summed


def temporal(series_block):
    frame_total, item_count, columns = series_block.shape
    values = series_block.astype(jnp.float32).reshape(frame_total, item_count * columns)
    frame_ids = jnp.arange(frame_total)
    at_ends = (frame_ids == 0) | (frame_ids == frame_total - 1)
    middle = (1.0 + SMOOTHING * jnp.where(at_ends, 1.0, 2.0)).astype(jnp.float32)
    sub_diag = jnp.where(frame_ids == 0, 0.0, -SMOOTHING).astype(jnp.float32)
    super_diag = jnp.where(frame_ids == frame_total - 1, 0.0, -SMOOTHING).astype(jnp.float32)
    baseline = lax.linalg.tridiagonal_solve(sub_diag, middle, super_diag, values)
    detrended = values - baseline
    earlier = jnp.concatenate(
        [jnp.zeros((1, values.shape[1]), jnp.float32), detrended[:-1]], axis=0
    )
    result = (detrended - DECAY_RATE * earlier).astype(jnp.bfloat16)
    return result.reshape(frame_total, item_count, columns)


def local(observed, kernels, band_kernel, masks):
    frames_dev, rows_dev, row_pixels = observed.shape
    height = rows_dev * lax.axis_size("row")
    tap_table = kernels / jnp.sum(kernels, axis=1, keepdims=True)
    first_row = lax.axis_index("row") * rows_dev
    own_taps = tap_rows(tap_table, band_kernel, first_row, rows_dev, height)
    outer_taps = tap_rows(tap_table, band_kernel, first_row - 2, rows_dev + 4, height)
    current = observed
    for iteration in range(ITERS):
        padded = padded_2(current, (("row", 1),), 2)
        blurred = blur_rows(padded, own_taps, rows_dev)
        quotient = observed / blurred
        padded_quotient = padded_2(quotient, (("row", 1),), 2)
        current = current * back_rows(padded_quotient, outer_taps, rows_dev)
    estimate = current.astype(jnp.bfloat16)
    spikes = temporal(lax.all_to_all(estimate, "frame", split_axis=2, concat_axis=0, tiled=True))
    frames_all, _, columns = spikes.shape
    tile_count = columns // TILE
    tile_sums = jnp.sum(
        spikes.reshape(frames_all, rows_dev * tile_count, TILE).astype(jnp.float32), axis=2
    )
    weights = masks.astype(jnp.float32).reshape(masks.shape[0], rows_dev * tile_count)
    local_sums = lax.dot_general(
        weights, tile_sums, (((1,), (1,)), ((), ())), precision=lax.Precision.HIGHEST
    )
    counts = jnp.sum(weights, axis=1)
    trace_sums, totals = (
        lax.psum_scatter(local_sums, ("frame", "row"), scatter_dimension=0, tiled=True),
        lax.psum_scatter(counts, ("frame", "row"), scatter_dimension=0, tiled=True),
    )
    traces = trace_sums / (TILE * totals[:, None])
    return (spikes, traces)


def halo_kernel(observed_ref, inner_ref, outer_ref, own_ref):
    even = lax.axis_index("row") % 2 == 0
    frames = observed_ref.shape[0]
    own_ref[...] = observed_ref[...]
    for frame in range(frames):
        near = frame * NEAR
        far = frames * NEAR + frame * FAR
        bottom, top = observed_ref[frame, -NEAR:, :], observed_ref[frame, :NEAR, :]
        inner_ref[near : near + NEAR, :] = jnp.where(even, bottom, top)
        outer_ref[near : near + NEAR, :] = jnp.where(even, top, bottom)
        bottom, top = observed_ref[frame, -NEAR - FAR : -NEAR, :], observed_ref[frame, NEAR : NEAR + FAR, :]
        inner_ref[far : far + FAR, :] = jnp.where(even, bottom, top)
        outer_ref[far : far + FAR, :] = jnp.where(even, top, bottom)


def taps_kernel(band_ref, kernels_ref, taps_ref, back_ref, pad_ref, *, height, rows_dev):
    span = rows_dev + 2 * MARGIN
    first_row = lax.axis_index("row") * rows_dev - MARGIN
    row_ids = lax.broadcasted_iota(jnp.int32, (BAND, TILE), 0)
    pad_ref[...] = jnp.zeros_like(pad_ref)
    for band in range(span // BAND):
        row = first_row + band * BAND
        inside = (row >= 0) & (row < height)
        kernel = band_ref[jnp.clip(row, 0, height - 1) // BAND]
        centre = jnp.full((BAND, TILE), kernels_ref[kernel, TAPS // 2], jnp.float32)
        start = band * BAND
        for slot, tap in enumerate(SIDES):
            weight = jnp.full((BAND, TILE), kernels_ref[kernel, tap], jnp.float32) / centre
            target = row_ids + (row + tap - TAPS // 2)
            weight = jnp.where(inside & (target >= 0) & (target < height), weight, 0.0)
            taps_ref[slot, start : start + BAND, :] = weight
            pad_ref[slot, BAND + start : 2 * BAND + start, :] = weight
    for slot, tap in enumerate(SIDES):
        start = BAND + TAPS // 2 - tap
        back_ref[slot] = pad_ref[slot, start : start + span, :]


def feet_kernel(masks_ref, feet_ref):
    rows_dev = masks_ref.shape[0]
    flat = jnp.concatenate([masks_ref[row].astype(jnp.float32) for row in range(rows_dev)], axis=0)
    positions = flat.shape[0]
    both = jnp.concatenate([flat, flat], axis=0).T
    half = feet_ref.shape[1]
    left = lax.broadcasted_iota(jnp.int32, (half, TILE), 1) < positions
    for block in range(feet_ref.shape[0]):
        start = 2 * block * half
        halves = jnp.where(left, both[start : start + half], both[start + half : start + 2 * half])
        feet_ref[block] = halves.astype(jnp.bfloat16)


def restore_kernel(
    taps_ref, back_ref, feet_ref, own_ref, top_ref, bottom_ref, out_ref, side_ref, image_ref, current_ref, quotient_ref
):
    n_frame = out_ref.shape[0]
    frames, rows_dev, width = own_ref.shape
    tiles_dev = width // (n_frame * TILE)
    positions = rows_dev * tiles_dev
    for ref in (image_ref, current_ref, quotient_ref):
        ref[...] = jnp.ones_like(ref)

    def columns_step(step, carry):
        columns = pl.ds(pl.multiple_of(step * TILE, TILE), TILE)
        for frame in range(frames):
            near, far = frame * NEAR, frames * NEAR + frame * FAR
            start, stop = PAD + MARGIN, PAD + MARGIN + rows_dev
            image_ref[frame, start - NEAR - FAR : start - NEAR, :] = top_ref[far : far + FAR, columns]
            image_ref[frame, start - NEAR : start, :] = top_ref[near : near + NEAR, columns]
            image_ref[frame, stop : stop + NEAR, :] = bottom_ref[near : near + NEAR, columns]
            image_ref[frame, stop + NEAR : stop + NEAR + FAR, :] = bottom_ref[far : far + FAR, columns]
            image_ref[frame, start:stop, :] = own_ref[frame, :, columns]
        source_ref = image_ref
        for (first, last), (back_first, back_last) in STEPS:
            for row in range(first, last, BAND):
                weights = [taps_ref[slot, row : row + BAND, :] for slot in range(len(SIDES))]
                for frame in range(frames):
                    rows = slice(PAD + row, PAD + row + BAND)
                    terms = []
                    for weight, tap in zip(weights, SIDES):
                        start = PAD + row + tap - TAPS // 2
                        terms.append(weight * source_ref[frame, start : start + BAND, :])
                    blurred = source_ref[frame, rows, :] + ((terms[0] + terms[1]) + (terms[2] + terms[3]))
                    quotient_ref[frame, rows, :] = image_ref[frame, rows, :] / blurred
            for row in range(back_first, back_last, BAND):
                weights = [back_ref[slot, row : row + BAND, :] for slot in range(len(SIDES))]
                for frame in range(frames):
                    rows = slice(PAD + row, PAD + row + BAND)
                    terms = []
                    for weight, tap in zip(weights, SIDES):
                        start = PAD + row - tap + TAPS // 2
                        terms.append(weight * quotient_ref[frame, start : start + BAND, :])
                    spread = quotient_ref[frame, rows, :] + ((terms[0] + terms[1]) + (terms[2] + terms[3]))
                    current_ref[frame, rows, :] = source_ref[frame, rows, :] * spread
            source_ref = current_ref
        first = pl.multiple_of(lax.rem(step, tiles_dev) * rows_dev, rows_dev)
        for frame in range(frames):
            estimate = current_ref[frame, PAD + MARGIN : PAD + MARGIN + rows_dev, :].astype(jnp.bfloat16)
            start = pl.multiple_of(first + frame * positions, rows_dev)
            out_ref[step // tiles_dev, pl.ds(start, rows_dev), :] = estimate
        return carry

    lax.fori_loop(0, n_frame * tiles_dev, columns_step, 0, unroll=2)
    lane_tiles = lax.broadcasted_iota(jnp.int32, (TILE, TILE), 1) % tiles_dev
    gathered = jnp.zeros((frames * n_frame * rows_dev, TILE), jnp.float32)
    for tile in range(tiles_dev):
        pieces = []
        for frame in range(frames):
            start = frame * positions + tile * rows_dev
            pieces += [out_ref[block, start : start + rows_dev, :] for block in range(n_frame)]
        picked = jnp.where(lane_tiles == tile, 1.0, 0.0).astype(jnp.bfloat16)
        gathered = gathered + jnp.dot(jnp.concatenate(pieces, axis=0), picked, preferred_element_type=jnp.float32)
    lanes = lax.broadcasted_iota(jnp.int32, (rows_dev, TILE), 1)
    here = lanes % positions // tiles_dev == lax.broadcasted_iota(jnp.int32, (rows_dev, TILE), 0)
    sums = []
    for place in range(frames * n_frame):
        part = jnp.where(here, gathered[place * rows_dev : (place + 1) * rows_dev], 0.0)
        sums.append(jnp.sum(part, axis=0, keepdims=True))
    sums = jnp.concatenate(sums, axis=0)
    high = sums.astype(jnp.bfloat16).astype(jnp.float32)
    split = jnp.where(lax.broadcasted_iota(jnp.int32, sums.shape, 1) < positions, high, sums - high).astype(jnp.bfloat16)
    for block in range(n_frame):
        side_ref[block, : split.shape[0], :] = split
        side_ref[block, split.shape[0] :, :] = feet_ref[block]


def deconvolved(series):
    total = len(series)
    factors = []
    for step in range(total):
        middle = 1.0 + SMOOTHING * (1.0 if step in (0, total - 1) else 2.0)
        if step:
            middle -= SMOOTHING * SMOOTHING * factors[-1]
        factors.append(1.0 / middle)
    forward = [series[0] * factors[0]]
    for step in range(1, total):
        forward.append((series[step] + SMOOTHING * forward[step - 1]) * factors[step])
    baseline = [None] * total
    baseline[total - 1] = forward[total - 1]
    for step in range(total - 2, -1, -1):
        baseline[step] = forward[step] + (SMOOTHING * factors[step]) * baseline[step + 1]
    result, earlier = [], None
    for step in range(total):
        detrended = series[step] - baseline[step]
        result.append(detrended if earlier is None else detrended - DECAY_RATE * earlier)
        earlier = detrended
    return result


def partial_kernel(*refs, positions):
    pieces, (out_ref, sums_ref, feet_ref) = refs[:-3], refs[-3:]
    n_frame = len(pieces)
    place = lax.axis_index("frame")
    rows = sums_ref.shape[0] // n_frame
    half = feet_ref.shape[1]
    for step, piece in enumerate(pieces[::-1]):
        sums_ref[pl.ds(pl.multiple_of((place ^ step) * rows, rows), rows), :] = piece[:rows, :].astype(jnp.float32)
        feet_ref[place ^ step] = piece[rows:, :].astype(jnp.float32)
    series = [sums_ref[t * n_frame : (t + 1) * n_frame, :] for t in range(rows)]
    for t, sums in enumerate(deconvolved(series)):
        sums_ref[t * n_frame : (t + 1) * n_frame, :] = sums + pltpu.roll(sums, TILE // 2, 1)
    left = lax.broadcasted_iota(jnp.int32, (half, TILE), 1) < positions
    weights, sums = [], []
    extra = jnp.where(lax.broadcasted_iota(jnp.int32, (8, TILE), 0) == 0, 1.0, 0.0)
    for block in range(n_frame):
        feet = feet_ref[block]
        weights.append(jnp.concatenate([jnp.where(left, feet, 0.0), jnp.where(left, 0.0, feet)], axis=0))
        sums.append(jnp.concatenate([sums_ref[pl.ds(block, rows, stride=n_frame), :], extra], axis=0))
    totals = lax.dot_general(
        jnp.concatenate(weights, axis=1),
        jnp.concatenate(sums, axis=1),
        (((1,), (1,)), ((), ())),
        precision=lax.Precision.HIGHEST,
        preferred_element_type=jnp.float32,
    )
    share = out_ref.shape[2]
    out_ref[...] = jnp.zeros_like(out_ref)
    for row in range(2 * out_ref.shape[1]):
        out_ref[row % 2, row // 2, :, : rows + 8] = totals[row * share : (row + 1) * share]


def temporal_kernel(*refs, frames):
    pieces, (spikes_ref, in_ref) = refs[:-2], refs[-2:]
    place = lax.axis_index("frame")
    for step, piece in enumerate(pieces[::-1]):
        in_ref[place ^ step] = piece[...]
    total, rows_dev, columns = spikes_ref.shape
    positions = in_ref.shape[1] // frames
    for tile in range(columns // TILE):
        series = []
        for t in range(total):
            start = t % frames * positions + tile * rows_dev
            series.append(in_ref[t // frames, start : start + rows_dev, :].astype(jnp.float32))
        for t, spikes in enumerate(deconvolved(series)):
            spikes_ref[t, :, tile * TILE : (tile + 1) * TILE] = spikes.astype(spikes_ref.dtype)


def add_kernel(first_ref, second_ref, out_ref):
    out_ref[...] = first_ref[...] + second_ref[...]


def means_kernel(*refs):
    pieces, traces_ref = refs[:-1], refs[-1]
    frames = traces_ref.shape[1]
    total = pieces[0][...]
    for piece in pieces[1:]:
        total = total + piece[...]
    traces_ref[...] = total[:, :frames] / (TILE * total[:, frames : frames + 1])


def swapped(parts, axis):
    count, place = lax.axis_size(axis), lax.axis_index(axis)
    arrived = [lax.dynamic_index_in_dim(parts, place, 0, keepdims=False, allow_negative_indices=False)]
    for step in range(1, count):
        part = lax.dynamic_index_in_dim(parts, place ^ step, 0, keepdims=False, allow_negative_indices=False)
        arrived.append(lax.ppermute(part, axis, [(i, i ^ step) for i in range(count)]))
    return arrived


def swapped_one(parts, axis, mine, step):
    own, there = (
        lax.dynamic_index_in_dim(parts, index, 0, keepdims=False, allow_negative_indices=False) for index in (mine, mine ^ 1)
    )
    return own, lax.ppermute(there, axis, [(i, i ^ step) for i in range(lax.axis_size(axis))])


def in_turn(*arrays):
    done = []
    for array in arrays:
        done = list(lax.optimization_barrier((*done, array)))
    return done


def by_halo(observed, kernels, band_kernel, masks):
    n_frame, n_row = lax.axis_size("frame"), lax.axis_size("row")
    frames, rows_dev, width = observed.shape
    components, _, tiles_dev = masks.shape
    positions = rows_dev * tiles_dev
    share = components // (n_frame * n_row)
    span = rows_dev + 2 * MARGIN
    smem, vmem = pl.BlockSpec(memory_space=pltpu.SMEM), pl.BlockSpec(memory_space=pltpu.VMEM)

    def call(kernel, name, in_specs, out_shape, scratch=(), cost=1000):
        many = isinstance(out_shape, tuple)
        return pl.pallas_call(
            kernel,
            name=name,
            out_shape=out_shape,
            in_specs=in_specs,
            out_specs=(vmem,) * len(out_shape) if many else vmem,
            scratch_shapes=scratch,
            compiler_params=pltpu.CompilerParams(vmem_limit_bytes=16 << 20),
            cost_estimate=pl.CostEstimate(flops=cost, bytes_accessed=cost, transcendentals=0),
        )

    def array(*shape, dtype=jnp.float32):
        return jax.ShapeDtypeStruct(shape, dtype)

    packed = array(frames * (NEAR + FAR), width)
    inner, outer, own = call(halo_kernel, "halo", [vmem], (packed, packed, array(*observed.shape)))(observed)
    inner_swap = [(i, i ^ 1) for i in range(n_row)]
    outer_swap = []
    for f in range(n_frame):
        for i in range(n_row):
            there = (f ^ 1, i) if i in (0, n_row - 1) else (f, (i - 1 ^ 1) + 1)
            outer_swap.append((f * n_row + i, there[0] * n_row + there[1]))
    inner = lax.ppermute(inner.astype(jnp.float16), "row", inner_swap)
    outer = lax.ppermute(outer.astype(jnp.float16), ("frame", "row"), outer_swap)
    inner, outer = in_turn(inner, outer)
    taps, back = call(
        functools.partial(taps_kernel, height=rows_dev * n_row, rows_dev=rows_dev),
        "taps",
        [smem, smem],
        (array(len(SIDES), span, TILE),) * 2,
        [pltpu.VMEM((len(SIDES), span + 2 * PAD, TILE), jnp.float32)],
    )(band_kernel, kernels)
    feet = call(feet_kernel, "feet", [vmem], array(n_frame, n_row * share // 2, TILE, dtype=jnp.bfloat16))(
        masks.transpose(1, 2, 0)
    )
    row = lax.axis_index("row")
    even = row % 2 == 0
    alone = (row == 0) | (row == n_row - 1)
    inner, outer = inner.astype(jnp.float32), jnp.where(alone, 1.0, outer.astype(jnp.float32))
    top, bottom = jnp.where(even, outer, inner), jnp.where(even, inner, outer)
    side_rows = frames * n_frame + n_row * share // 2
    blocks, sides = call(
        restore_kernel,
        "restore",
        [vmem] * 6,
        (
            array(n_frame, frames * positions, TILE, dtype=jnp.bfloat16),
            array(n_frame, side_rows, TILE, dtype=jnp.bfloat16),
        ),
        [pltpu.VMEM((frames, span + 2 * PAD, TILE), jnp.float32)] * 3,
    )(taps, back, feet, own, top, bottom)
    sides = swapped(sides, "frame")
    pieces = swapped(blocks, "frame")
    partial = call(
        functools.partial(partial_kernel, positions=positions),
        "partial",
        [vmem] * n_frame,
        array(2, n_row // 2, share, TILE),
        [
            pltpu.VMEM((n_frame * frames * n_frame, TILE), jnp.float32),
            pltpu.VMEM((n_frame, n_row * share // 2, TILE), jnp.float32),
        ],
    )(*sides[::-1])
    pairs = call(add_kernel, "add", [vmem] * 2, array(n_row // 2, share, TILE))(*swapped_one(partial, "row", row % 2, 1))
    shares = swapped_one(pairs, "row", row // 2, 2)
    spikes = call(
        functools.partial(temporal_kernel, frames=frames),
        "temporal",
        [vmem] * n_frame,
        array(n_frame * frames, rows_dev, tiles_dev * TILE, dtype=jnp.bfloat16),
        [pltpu.VMEM((n_frame, frames * positions, TILE), jnp.bfloat16)],
    )(*pieces[::-1])
    spikes, *shares = in_turn(spikes, *shares)
    traces = call(means_kernel, "means", [vmem] * 2, array(share, n_frame * frames))(*shares)
    return (spikes, traces)


def fits(mesh, observed, masks):
    frames_dev = observed.shape[0] // mesh.shape["frame"]
    rows_dev = masks.shape[1] // (mesh.shape["groups"] * mesh.shape["row"])
    tiles_dev = masks.shape[2] // mesh.shape["frame"]
    places = mesh.shape["frame"] * mesh.shape["row"]
    return (
        frames_dev == mesh.shape["frame"] == mesh.shape["row"] == 4
        and 2 * rows_dev * tiles_dev == TILE
        and rows_dev == 16
        and masks.shape[0] // places == 16
    )


def solution(mesh):
    in_specs = (
        P("frame", ("groups", "row"), None),
        P(),
        P("groups"),
        P(None, ("groups", "row"), "frame"),
    )
    out_specs = (P(None, ("groups", "row"), "frame"), P(("groups", "frame", "row"), None))

    def whole(observed, kernels, band_kernel, masks):
        body = by_halo if fits(mesh, observed, masks) else local
        mapped = jax.shard_map(body, mesh=mesh, in_specs=in_specs, out_specs=out_specs, check_vma=False)
        return mapped(observed, kernels, band_kernel, masks)

    return whole
```

```python
import functools

import jax
import jax.numpy as jnp
from jax import lax
from jax.experimental import pallas as pl
from jax.experimental.pallas import tpu as pltpu
from jax.sharding import PartitionSpec as P

TILE = 128
BAND = 8
ITERS = 3
TAPS = 5
NEAR, FAR = 8, 4
MARGIN = 2 * BAND
PAD = BAND
STEPS = (((6, 46), (8, 40)), ((10, 42), (12, 36)), ((14, 38), (16, 32)))
SIDES = (0, 1, 3, 4)


SMOOTHING = 1024.0
DECAY_RATE = 0.9


def padded_2(cells, sides, width):
    for axis, dim in sides:
        count = lax.axis_size(axis)
        ends = count - 1
        head = lax.slice_in_dim(cells, 0, width, axis=dim)
        tail = lax.slice_in_dim(cells, cells.shape[dim] - width, cells.shape[dim], axis=dim)
        cells = jnp.concatenate(
            [
                lax.ppermute(tail, axis, [(i, (i + 1) % count) for i in range(ends)]),
                cells,
                lax.ppermute(head, axis, [((i + 1) % count, i) for i in range(ends)]),
            ],
            axis=dim,
        )
    return cells


def tap_rows(tap_table, band_kernel, first_row, row_count, height):
    row_ids = jnp.clip(first_row + jnp.arange(row_count), 0, height - 1)
    row_bands = row_ids // BAND
    band_slots = jnp.arange(band_kernel.shape[0])
    kernel_ids = jnp.sum(
        jnp.where(row_bands[:, None] == band_slots[None, :], band_kernel[None, :], 0), axis=1
    )
    kernel_slots = jnp.arange(tap_table.shape[0])
    picked = jnp.where(
        kernel_ids[:, None, None] == kernel_slots[None, :, None], tap_table[None, :, :], 0.0
    )
    return jnp.sum(picked, axis=1)


def blur_rows(padded, row_taps, row_count):
    summed = row_taps[:, 0][None, :, None] * padded[:, 0:row_count]
    for offset in range(1, 5):
        summed = (
            summed + row_taps[:, offset][None, :, None] * padded[:, offset : offset + row_count]
        )
    return summed


def back_rows(padded_quotient, outer_taps, row_count):
    summed = outer_taps[4 : 4 + row_count, 0][None, :, None] * padded_quotient[:, 4 : 4 + row_count]
    for offset in range(1, 5):
        start = 4 - offset
        summed = (
            summed
            + outer_taps[start : start + row_count, offset][None, :, None]
            * padded_quotient[:, start : start + row_count]
        )
    return summed


def temporal(series_block):
    frame_total, item_count, columns = series_block.shape
    values = series_block.astype(jnp.float32).reshape(frame_total, item_count * columns)
    frame_ids = jnp.arange(frame_total)
    at_ends = (frame_ids == 0) | (frame_ids == frame_total - 1)
    middle = (1.0 + SMOOTHING * jnp.where(at_ends, 1.0, 2.0)).astype(jnp.float32)
    sub_diag = jnp.where(frame_ids == 0, 0.0, -SMOOTHING).astype(jnp.float32)
    super_diag = jnp.where(frame_ids == frame_total - 1, 0.0, -SMOOTHING).astype(jnp.float32)
    baseline = lax.linalg.tridiagonal_solve(sub_diag, middle, super_diag, values)
    detrended = values - baseline
    earlier = jnp.concatenate(
        [jnp.zeros((1, values.shape[1]), jnp.float32), detrended[:-1]], axis=0
    )
    result = (detrended - DECAY_RATE * earlier).astype(jnp.bfloat16)
    return result.reshape(frame_total, item_count, columns)


def local(observed, kernels, band_kernel, masks):
    frames_dev, rows_dev, row_pixels = observed.shape
    height = rows_dev * lax.axis_size("row")
    tap_table = kernels / jnp.sum(kernels, axis=1, keepdims=True)
    first_row = lax.axis_index("row") * rows_dev
    own_taps = tap_rows(tap_table, band_kernel, first_row, rows_dev, height)
    outer_taps = tap_rows(tap_table, band_kernel, first_row - 2, rows_dev + 4, height)
    current = observed
    for iteration in range(ITERS):
        padded = padded_2(current, (("row", 1),), 2)
        blurred = blur_rows(padded, own_taps, rows_dev)
        quotient = observed / blurred
        padded_quotient = padded_2(quotient, (("row", 1),), 2)
        current = current * back_rows(padded_quotient, outer_taps, rows_dev)
    estimate = current.astype(jnp.bfloat16)
    spikes = temporal(lax.all_to_all(estimate, "frame", split_axis=2, concat_axis=0, tiled=True))
    frames_all, _, columns = spikes.shape
    tile_count = columns // TILE
    tile_sums = jnp.sum(
        spikes.reshape(frames_all, rows_dev * tile_count, TILE).astype(jnp.float32), axis=2
    )
    weights = masks.astype(jnp.float32).reshape(masks.shape[0], rows_dev * tile_count)
    local_sums = lax.dot_general(
        weights, tile_sums, (((1,), (1,)), ((), ())), precision=lax.Precision.HIGHEST
    )
    counts = jnp.sum(weights, axis=1)
    trace_sums, totals = (
        lax.psum_scatter(local_sums, ("frame", "row"), scatter_dimension=0, tiled=True),
        lax.psum_scatter(counts, ("frame", "row"), scatter_dimension=0, tiled=True),
    )
    traces = trace_sums / (TILE * totals[:, None])
    return (spikes, traces)


def halo_kernel(observed_ref, inner_ref, outer_ref, own_ref):
    even = lax.axis_index("row") % 2 == 0
    frames = observed_ref.shape[0]
    own_ref[...] = observed_ref[...]
    for frame in range(frames):
        near = frame * NEAR
        far = frames * NEAR + frame * FAR
        bottom, top = observed_ref[frame, -NEAR:, :], observed_ref[frame, :NEAR, :]
        inner_ref[near : near + NEAR, :] = jnp.where(even, bottom, top)
        outer_ref[near : near + NEAR, :] = jnp.where(even, top, bottom)
        bottom, top = observed_ref[frame, -NEAR - FAR : -NEAR, :], observed_ref[frame, NEAR : NEAR + FAR, :]
        inner_ref[far : far + FAR, :] = jnp.where(even, bottom, top)
        outer_ref[far : far + FAR, :] = jnp.where(even, top, bottom)


def taps_kernel(band_ref, kernels_ref, taps_ref, back_ref, pad_ref, *, height, rows_dev):
    span = rows_dev + 2 * MARGIN
    first_row = lax.axis_index("row") * rows_dev - MARGIN
    row_ids = lax.broadcasted_iota(jnp.int32, (BAND, TILE), 0)
    pad_ref[...] = jnp.zeros_like(pad_ref)
    for band in range(span // BAND):
        row = first_row + band * BAND
        inside = (row >= 0) & (row < height)
        kernel = band_ref[jnp.clip(row, 0, height - 1) // BAND]
        centre = jnp.full((BAND, TILE), kernels_ref[kernel, TAPS // 2], jnp.float32)
        start = band * BAND
        for slot, tap in enumerate(SIDES):
            weight = jnp.full((BAND, TILE), kernels_ref[kernel, tap], jnp.float32) / centre
            target = row_ids + (row + tap - TAPS // 2)
            weight = jnp.where(inside & (target >= 0) & (target < height), weight, 0.0)
            taps_ref[slot, start : start + BAND, :] = weight
            pad_ref[slot, BAND + start : 2 * BAND + start, :] = weight
    for slot, tap in enumerate(SIDES):
        start = BAND + TAPS // 2 - tap
        back_ref[slot] = pad_ref[slot, start : start + span, :]


def feet_kernel(masks_ref, feet_ref):
    rows_dev = masks_ref.shape[0]
    flat = jnp.concatenate([masks_ref[row].astype(jnp.float32) for row in range(rows_dev)], axis=0)
    positions = flat.shape[0]
    both = jnp.concatenate([flat, flat], axis=0).T
    half = feet_ref.shape[1]
    left = lax.broadcasted_iota(jnp.int32, (half, TILE), 1) < positions
    for block in range(feet_ref.shape[0]):
        start = 2 * block * half
        halves = jnp.where(left, both[start : start + half], both[start + half : start + 2 * half])
        feet_ref[block] = halves.astype(jnp.bfloat16)


def restore_kernel(
    taps_ref, back_ref, feet_ref, own_ref, top_ref, bottom_ref, out_ref, side_ref, image_ref, current_ref, quotient_ref
):
    n_frame = out_ref.shape[0]
    frames, rows_dev, width = own_ref.shape
    tiles_dev = width // (n_frame * TILE)
    positions = rows_dev * tiles_dev
    for ref in (image_ref, current_ref, quotient_ref):
        ref[...] = jnp.ones_like(ref)

    def columns_step(step, carry):
        columns = pl.ds(pl.multiple_of(step * TILE, TILE), TILE)
        for frame in range(frames):
            near, far = frame * NEAR, frames * NEAR + frame * FAR
            start, stop = PAD + MARGIN, PAD + MARGIN + rows_dev
            image_ref[frame, start - NEAR - FAR : start - NEAR, :] = top_ref[far : far + FAR, columns]
            image_ref[frame, start - NEAR : start, :] = top_ref[near : near + NEAR, columns]
            image_ref[frame, stop : stop + NEAR, :] = bottom_ref[near : near + NEAR, columns]
            image_ref[frame, stop + NEAR : stop + NEAR + FAR, :] = bottom_ref[far : far + FAR, columns]
            image_ref[frame, start:stop, :] = own_ref[frame, :, columns]
        source_ref = image_ref
        for (first, last), (back_first, back_last) in STEPS:
            for row in range(first, last, BAND):
                weights = [taps_ref[slot, row : row + BAND, :] for slot in range(len(SIDES))]
                for frame in range(frames):
                    rows = slice(PAD + row, PAD + row + BAND)
                    terms = []
                    for weight, tap in zip(weights, SIDES):
                        start = PAD + row + tap - TAPS // 2
                        terms.append(weight * source_ref[frame, start : start + BAND, :])
                    blurred = source_ref[frame, rows, :] + ((terms[0] + terms[1]) + (terms[2] + terms[3]))
                    quotient_ref[frame, rows, :] = image_ref[frame, rows, :] / blurred
            for row in range(back_first, back_last, BAND):
                weights = [back_ref[slot, row : row + BAND, :] for slot in range(len(SIDES))]
                for frame in range(frames):
                    rows = slice(PAD + row, PAD + row + BAND)
                    terms = []
                    for weight, tap in zip(weights, SIDES):
                        start = PAD + row - tap + TAPS // 2
                        terms.append(weight * quotient_ref[frame, start : start + BAND, :])
                    spread = quotient_ref[frame, rows, :] + ((terms[0] + terms[1]) + (terms[2] + terms[3]))
                    current_ref[frame, rows, :] = source_ref[frame, rows, :] * spread
            source_ref = current_ref
        first = pl.multiple_of(lax.rem(step, tiles_dev) * rows_dev, rows_dev)
        for frame in range(frames):
            estimate = current_ref[frame, PAD + MARGIN : PAD + MARGIN + rows_dev, :].astype(jnp.bfloat16)
            start = pl.multiple_of(first + frame * positions, rows_dev)
            out_ref[step // tiles_dev, pl.ds(start, rows_dev), :] = estimate
        return carry

    lax.fori_loop(0, n_frame * tiles_dev, columns_step, 0, unroll=2)
    lane_tiles = lax.broadcasted_iota(jnp.int32, (TILE, TILE), 1) % tiles_dev
    gathered = jnp.zeros((frames * n_frame * rows_dev, TILE), jnp.float32)
    for tile in range(tiles_dev):
        pieces = []
        for frame in range(frames):
            start = frame * positions + tile * rows_dev
            pieces += [out_ref[block, start : start + rows_dev, :] for block in range(n_frame)]
        picked = jnp.where(lane_tiles == tile, 1.0, 0.0).astype(jnp.bfloat16)
        gathered = gathered + jnp.dot(jnp.concatenate(pieces, axis=0), picked, preferred_element_type=jnp.float32)
    lanes = lax.broadcasted_iota(jnp.int32, (rows_dev, TILE), 1)
    here = lanes % positions // tiles_dev == lax.broadcasted_iota(jnp.int32, (rows_dev, TILE), 0)
    sums = []
    for place in range(frames * n_frame):
        part = jnp.where(here, gathered[place * rows_dev : (place + 1) * rows_dev], 0.0)
        sums.append(jnp.sum(part, axis=0, keepdims=True))
    sums = jnp.concatenate(sums, axis=0)
    high = sums.astype(jnp.bfloat16).astype(jnp.float32)
    split = jnp.where(lax.broadcasted_iota(jnp.int32, sums.shape, 1) < positions, high, sums - high).astype(jnp.bfloat16)
    for block in range(n_frame):
        side_ref[block, : split.shape[0], :] = split
        side_ref[block, split.shape[0] :, :] = feet_ref[block]


def deconvolved(series):
    total = len(series)
    factors = []
    for step in range(total):
        middle = 1.0 + SMOOTHING * (1.0 if step in (0, total - 1) else 2.0)
        if step:
            middle -= SMOOTHING * SMOOTHING * factors[-1]
        factors.append(1.0 / middle)
    scaled = [cells * factor for cells, factor in zip(series, factors)]
    forward = [scaled[0]]
    for step in range(1, total):
        forward.append(scaled[step] + (SMOOTHING * factors[step]) * forward[step - 1])
    baseline = [None] * total
    baseline[total - 1] = forward[total - 1]
    for step in range(total - 2, -1, -1):
        baseline[step] = forward[step] + (SMOOTHING * factors[step]) * baseline[step + 1]
    result, earlier = [], None
    for step in range(total):
        detrended = series[step] - baseline[step]
        result.append(detrended if earlier is None else detrended - DECAY_RATE * earlier)
        earlier = detrended
    return result


def partial_kernel(*refs, positions):
    pieces, (out_ref, sums_ref, feet_ref) = refs[:-3], refs[-3:]
    n_frame = len(pieces)
    place = lax.axis_index("frame")
    rows = sums_ref.shape[0] // n_frame
    half = feet_ref.shape[1]
    for step, piece in enumerate(pieces[::-1]):
        sums_ref[pl.ds(pl.multiple_of((place ^ step) * rows, rows), rows), :] = piece[:rows, :].astype(jnp.float32)
        feet_ref[place ^ step] = piece[rows:, :].astype(jnp.float32)
    series = [sums_ref[t * n_frame : (t + 1) * n_frame, :] for t in range(rows)]
    for t, sums in enumerate(deconvolved(series)):
        sums_ref[t * n_frame : (t + 1) * n_frame, :] = sums + pltpu.roll(sums, TILE // 2, 1)
    left = lax.broadcasted_iota(jnp.int32, (half, TILE), 1) < positions
    weights, sums = [], []
    extra = jnp.where(lax.broadcasted_iota(jnp.int32, (8, TILE), 0) == 0, 1.0, 0.0)
    for block in range(n_frame):
        feet = feet_ref[block]
        weights.append(jnp.concatenate([jnp.where(left, feet, 0.0), jnp.where(left, 0.0, feet)], axis=0))
        sums.append(jnp.concatenate([sums_ref[pl.ds(block, rows, stride=n_frame), :], extra], axis=0))
    sums = jnp.concatenate(sums, axis=1)
    parts = []
    for _ in range(3):
        parts.append(sums.astype(jnp.bfloat16))
        sums = sums - parts[-1].astype(jnp.float32)
    totals = lax.dot_general(
        jnp.concatenate(weights * 3, axis=1).astype(jnp.bfloat16),
        jnp.concatenate(parts, axis=1),
        (((1,), (1,)), ((), ())),
        preferred_element_type=jnp.float32,
    )
    share = out_ref.shape[1]
    out_ref[...] = jnp.zeros_like(out_ref)
    for row in range(out_ref.shape[0]):
        out_ref[row, :, : rows + 8] = totals[row * share : (row + 1) * share]


def temporal_kernel(*refs, frames):
    pieces, (spikes_ref, in_ref) = refs[:-2], refs[-2:]
    place = lax.axis_index("frame")
    for step, piece in enumerate(pieces[::-1]):
        in_ref[place ^ step] = piece[...]
    total, rows_dev, columns = spikes_ref.shape
    positions = in_ref.shape[1] // frames
    for tile in range(columns // TILE):
        series = []
        for t in range(total):
            start = t % frames * positions + tile * rows_dev
            series.append(in_ref[t // frames, start : start + rows_dev, :].astype(jnp.float32))
        for t, spikes in enumerate(deconvolved(series)):
            spikes_ref[t, :, tile * TILE : (tile + 1) * TILE] = spikes.astype(spikes_ref.dtype)


def means_kernel(*refs):
    pieces, traces_ref = refs[:-1], refs[-1]
    frames = traces_ref.shape[1]
    total = pieces[0][...]
    for piece in pieces[1:]:
        total = total + piece[...]
    traces_ref[...] = total[:, :frames] / (TILE * total[:, frames : frames + 1])


def swapped(parts, axis):
    count, place = lax.axis_size(axis), lax.axis_index(axis)
    arrived = [lax.dynamic_index_in_dim(parts, place, 0, keepdims=False, allow_negative_indices=False)]
    for step in range(1, count):
        part = lax.dynamic_index_in_dim(parts, place ^ step, 0, keepdims=False, allow_negative_indices=False)
        arrived.append(lax.ppermute(part, axis, [(i, i ^ step) for i in range(count)]))
    return arrived


def in_turn(*arrays):
    done = []
    for array in arrays:
        done = list(lax.optimization_barrier((*done, array)))
    return done


def by_halo(observed, kernels, band_kernel, masks):
    n_frame, n_row = lax.axis_size("frame"), lax.axis_size("row")
    frames, rows_dev, width = observed.shape
    components, _, tiles_dev = masks.shape
    positions = rows_dev * tiles_dev
    share = components // (n_frame * n_row)
    span = rows_dev + 2 * MARGIN
    smem, vmem = pl.BlockSpec(memory_space=pltpu.SMEM), pl.BlockSpec(memory_space=pltpu.VMEM)

    def call(kernel, name, in_specs, out_shape, scratch=(), cost=1000):
        many = isinstance(out_shape, tuple)
        return pl.pallas_call(
            kernel,
            name=name,
            out_shape=out_shape,
            in_specs=in_specs,
            out_specs=(vmem,) * len(out_shape) if many else vmem,
            scratch_shapes=scratch,
            compiler_params=pltpu.CompilerParams(vmem_limit_bytes=16 << 20),
            cost_estimate=pl.CostEstimate(flops=cost, bytes_accessed=cost, transcendentals=0),
        )

    def array(*shape, dtype=jnp.float32):
        return jax.ShapeDtypeStruct(shape, dtype)

    packed = array(frames * (NEAR + FAR), width)
    inner, outer, own = call(halo_kernel, "halo", [vmem], (packed, packed, array(*observed.shape)))(observed)
    inner_swap = [(i, i ^ 1) for i in range(n_row)]
    outer_swap = []
    for f in range(n_frame):
        for i in range(n_row):
            there = (f ^ 1, i) if i in (0, n_row - 1) else (f, (i - 1 ^ 1) + 1)
            outer_swap.append((f * n_row + i, there[0] * n_row + there[1]))
    inner = lax.ppermute(inner.astype(jnp.float16), "row", inner_swap)
    outer = lax.ppermute(outer.astype(jnp.float16), ("frame", "row"), outer_swap)
    inner, outer = in_turn(inner, outer)
    taps, back = call(
        functools.partial(taps_kernel, height=rows_dev * n_row, rows_dev=rows_dev),
        "taps",
        [smem, smem],
        (array(len(SIDES), span, TILE),) * 2,
        [pltpu.VMEM((len(SIDES), span + 2 * PAD, TILE), jnp.float32)],
    )(band_kernel, kernels)
    feet = call(feet_kernel, "feet", [vmem], array(n_frame, n_row * share // 2, TILE, dtype=jnp.bfloat16))(
        masks.transpose(1, 2, 0)
    )
    row = lax.axis_index("row")
    even = row % 2 == 0
    alone = (row == 0) | (row == n_row - 1)
    inner, outer = inner.astype(jnp.float32), jnp.where(alone, 1.0, outer.astype(jnp.float32))
    top, bottom = jnp.where(even, outer, inner), jnp.where(even, inner, outer)
    side_rows = frames * n_frame + n_row * share // 2
    blocks, sides = call(
        restore_kernel,
        "restore",
        [vmem] * 6,
        (
            array(n_frame, frames * positions, TILE, dtype=jnp.bfloat16),
            array(n_frame, side_rows, TILE, dtype=jnp.bfloat16),
        ),
        [pltpu.VMEM((frames, span + 2 * PAD, TILE), jnp.float32)] * 3,
    )(taps, back, feet, own, top, bottom)
    sides = swapped(sides, "frame")
    pieces = swapped(blocks, "frame")
    partial = call(
        functools.partial(partial_kernel, positions=positions),
        "partial",
        [vmem] * n_frame,
        array(n_row, share, TILE),
        [
            pltpu.VMEM((n_frame * frames * n_frame, TILE), jnp.float32),
            pltpu.VMEM((n_frame, n_row * share // 2, TILE), jnp.float32),
        ],
    )(*sides[::-1])
    shares = swapped(partial, "row")
    spikes = call(
        functools.partial(temporal_kernel, frames=frames),
        "temporal",
        [vmem] * n_frame,
        array(n_frame * frames, rows_dev, tiles_dev * TILE, dtype=jnp.bfloat16),
        [pltpu.VMEM((n_frame, frames * positions, TILE), jnp.bfloat16)],
    )(*pieces[::-1])
    spikes, *shares = in_turn(spikes, *shares[::-1])
    traces = call(means_kernel, "means", [vmem] * n_row, array(share, n_frame * frames))(*shares)
    return (spikes, traces)


def fits(mesh, observed, masks):
    frames_dev = observed.shape[0] // mesh.shape["frame"]
    rows_dev = masks.shape[1] // (mesh.shape["groups"] * mesh.shape["row"])
    tiles_dev = masks.shape[2] // mesh.shape["frame"]
    places = mesh.shape["frame"] * mesh.shape["row"]
    return (
        frames_dev == mesh.shape["frame"] == mesh.shape["row"] == 4
        and 2 * rows_dev * tiles_dev == TILE
        and rows_dev == 16
        and masks.shape[0] // places == 16
    )


def solution(mesh):
    in_specs = (
        P("frame", ("groups", "row"), None),
        P(),
        P("groups"),
        P(None, ("groups", "row"), "frame"),
    )
    out_specs = (P(None, ("groups", "row"), "frame"), P(("groups", "frame", "row"), None))

    def whole(observed, kernels, band_kernel, masks):
        body = by_halo if fits(mesh, observed, masks) else local
        mapped = jax.shard_map(body, mesh=mesh, in_specs=in_specs, out_specs=out_specs, check_vma=False)
        return mapped(observed, kernels, band_kernel, masks)

    return whole
```

```python
import functools

import jax
import jax.numpy as jnp
from jax import lax
from jax.experimental import pallas as pl
from jax.experimental.pallas import tpu as pltpu
from jax.sharding import PartitionSpec as P

TILE = 128
BAND = 8
ITERS = 3
TAPS = 5
NEAR, FAR = 8, 4
MARGIN = 2 * BAND
PAD = BAND
STEPS = (((6, 46), (8, 40)), ((10, 42), (12, 36)), ((14, 38), (16, 32)))
SIDES = (0, 1, 3, 4)


SMOOTHING = 1024.0
DECAY_RATE = 0.9


def padded_2(cells, sides, width):
    for axis, dim in sides:
        count = lax.axis_size(axis)
        ends = count - 1
        head = lax.slice_in_dim(cells, 0, width, axis=dim)
        tail = lax.slice_in_dim(cells, cells.shape[dim] - width, cells.shape[dim], axis=dim)
        cells = jnp.concatenate(
            [
                lax.ppermute(tail, axis, [(i, (i + 1) % count) for i in range(ends)]),
                cells,
                lax.ppermute(head, axis, [((i + 1) % count, i) for i in range(ends)]),
            ],
            axis=dim,
        )
    return cells


def tap_rows(tap_table, band_kernel, first_row, row_count, height):
    row_ids = jnp.clip(first_row + jnp.arange(row_count), 0, height - 1)
    row_bands = row_ids // BAND
    band_slots = jnp.arange(band_kernel.shape[0])
    kernel_ids = jnp.sum(
        jnp.where(row_bands[:, None] == band_slots[None, :], band_kernel[None, :], 0), axis=1
    )
    kernel_slots = jnp.arange(tap_table.shape[0])
    picked = jnp.where(
        kernel_ids[:, None, None] == kernel_slots[None, :, None], tap_table[None, :, :], 0.0
    )
    return jnp.sum(picked, axis=1)


def blur_rows(padded, row_taps, row_count):
    summed = row_taps[:, 0][None, :, None] * padded[:, 0:row_count]
    for offset in range(1, 5):
        summed = (
            summed + row_taps[:, offset][None, :, None] * padded[:, offset : offset + row_count]
        )
    return summed


def back_rows(padded_quotient, outer_taps, row_count):
    summed = outer_taps[4 : 4 + row_count, 0][None, :, None] * padded_quotient[:, 4 : 4 + row_count]
    for offset in range(1, 5):
        start = 4 - offset
        summed = (
            summed
            + outer_taps[start : start + row_count, offset][None, :, None]
            * padded_quotient[:, start : start + row_count]
        )
    return summed


def temporal(series_block):
    frame_total, item_count, columns = series_block.shape
    values = series_block.astype(jnp.float32).reshape(frame_total, item_count * columns)
    frame_ids = jnp.arange(frame_total)
    at_ends = (frame_ids == 0) | (frame_ids == frame_total - 1)
    middle = (1.0 + SMOOTHING * jnp.where(at_ends, 1.0, 2.0)).astype(jnp.float32)
    sub_diag = jnp.where(frame_ids == 0, 0.0, -SMOOTHING).astype(jnp.float32)
    super_diag = jnp.where(frame_ids == frame_total - 1, 0.0, -SMOOTHING).astype(jnp.float32)
    baseline = lax.linalg.tridiagonal_solve(sub_diag, middle, super_diag, values)
    detrended = values - baseline
    earlier = jnp.concatenate(
        [jnp.zeros((1, values.shape[1]), jnp.float32), detrended[:-1]], axis=0
    )
    result = (detrended - DECAY_RATE * earlier).astype(jnp.bfloat16)
    return result.reshape(frame_total, item_count, columns)


def local(observed, kernels, band_kernel, masks):
    frames_dev, rows_dev, row_pixels = observed.shape
    height = rows_dev * lax.axis_size("row")
    tap_table = kernels / jnp.sum(kernels, axis=1, keepdims=True)
    first_row = lax.axis_index("row") * rows_dev
    own_taps = tap_rows(tap_table, band_kernel, first_row, rows_dev, height)
    outer_taps = tap_rows(tap_table, band_kernel, first_row - 2, rows_dev + 4, height)
    current = observed
    for iteration in range(ITERS):
        padded = padded_2(current, (("row", 1),), 2)
        blurred = blur_rows(padded, own_taps, rows_dev)
        quotient = observed / blurred
        padded_quotient = padded_2(quotient, (("row", 1),), 2)
        current = current * back_rows(padded_quotient, outer_taps, rows_dev)
    estimate = current.astype(jnp.bfloat16)
    spikes = temporal(lax.all_to_all(estimate, "frame", split_axis=2, concat_axis=0, tiled=True))
    frames_all, _, columns = spikes.shape
    tile_count = columns // TILE
    tile_sums = jnp.sum(
        spikes.reshape(frames_all, rows_dev * tile_count, TILE).astype(jnp.float32), axis=2
    )
    weights = masks.astype(jnp.float32).reshape(masks.shape[0], rows_dev * tile_count)
    local_sums = lax.dot_general(
        weights, tile_sums, (((1,), (1,)), ((), ())), precision=lax.Precision.HIGHEST
    )
    counts = jnp.sum(weights, axis=1)
    trace_sums, totals = (
        lax.psum_scatter(local_sums, ("frame", "row"), scatter_dimension=0, tiled=True),
        lax.psum_scatter(counts, ("frame", "row"), scatter_dimension=0, tiled=True),
    )
    traces = trace_sums / (TILE * totals[:, None])
    return (spikes, traces)


def halo_kernel(observed_ref, inner_ref, outer_ref, own_ref):
    even = lax.axis_index("row") % 2 == 0
    frames = observed_ref.shape[0]
    own_ref[...] = observed_ref[...]
    for frame in range(frames):
        near = frame * NEAR
        far = frames * NEAR + frame * FAR
        bottom, top = observed_ref[frame, -NEAR:, :], observed_ref[frame, :NEAR, :]
        inner_ref[near : near + NEAR, :] = jnp.where(even, bottom, top)
        outer_ref[near : near + NEAR, :] = jnp.where(even, top, bottom)
        bottom, top = observed_ref[frame, -NEAR - FAR : -NEAR, :], observed_ref[frame, NEAR : NEAR + FAR, :]
        inner_ref[far : far + FAR, :] = jnp.where(even, bottom, top)
        outer_ref[far : far + FAR, :] = jnp.where(even, top, bottom)


def taps_kernel(band_ref, kernels_ref, taps_ref, back_ref, pad_ref, *, height, rows_dev):
    span = rows_dev + 2 * MARGIN
    first_row = lax.axis_index("row") * rows_dev - MARGIN
    row_ids = lax.broadcasted_iota(jnp.int32, (BAND, TILE), 0)
    pad_ref[...] = jnp.zeros_like(pad_ref)
    for band in range(span // BAND):
        row = first_row + band * BAND
        inside = (row >= 0) & (row < height)
        kernel = band_ref[jnp.clip(row, 0, height - 1) // BAND]
        centre = jnp.full((BAND, TILE), kernels_ref[kernel, TAPS // 2], jnp.float32)
        start = band * BAND
        for slot, tap in enumerate(SIDES):
            weight = jnp.full((BAND, TILE), kernels_ref[kernel, tap], jnp.float32) / centre
            target = row_ids + (row + tap - TAPS // 2)
            weight = jnp.where(inside & (target >= 0) & (target < height), weight, 0.0)
            taps_ref[slot, start : start + BAND, :] = weight
            pad_ref[slot, BAND + start : 2 * BAND + start, :] = weight
    for slot, tap in enumerate(SIDES):
        start = BAND + TAPS // 2 - tap
        back_ref[slot] = pad_ref[slot, start : start + span, :]


def feet_kernel(masks_ref, feet_ref):
    rows_dev = masks_ref.shape[0]
    flat = jnp.concatenate([masks_ref[row].astype(jnp.float32) for row in range(rows_dev)], axis=0)
    positions = flat.shape[0]
    both = jnp.concatenate([flat, flat], axis=0).T
    half = feet_ref.shape[1]
    left = lax.broadcasted_iota(jnp.int32, (half, TILE), 1) < positions
    for block in range(feet_ref.shape[0]):
        start = 2 * block * half
        halves = jnp.where(left, both[start : start + half], both[start + half : start + 2 * half])
        feet_ref[block] = halves.astype(jnp.bfloat16)


def restore_kernel(
    taps_ref, back_ref, feet_ref, own_ref, top_ref, bottom_ref, out_ref, side_ref, image_ref, current_ref, quotient_ref
):
    n_frame = out_ref.shape[0]
    frames, rows_dev, width = own_ref.shape
    tiles_dev = width // (n_frame * TILE)
    positions = rows_dev * tiles_dev
    for ref in (image_ref, current_ref, quotient_ref):
        ref[...] = jnp.ones_like(ref)

    def columns_step(step, carry):
        columns = pl.ds(pl.multiple_of(step * TILE, TILE), TILE)
        for frame in range(frames):
            near, far = frame * NEAR, frames * NEAR + frame * FAR
            start, stop = PAD + MARGIN, PAD + MARGIN + rows_dev
            image_ref[frame, start - NEAR - FAR : start - NEAR, :] = top_ref[far : far + FAR, columns]
            image_ref[frame, start - NEAR : start, :] = top_ref[near : near + NEAR, columns]
            image_ref[frame, stop : stop + NEAR, :] = bottom_ref[near : near + NEAR, columns]
            image_ref[frame, stop + NEAR : stop + NEAR + FAR, :] = bottom_ref[far : far + FAR, columns]
            image_ref[frame, start:stop, :] = own_ref[frame, :, columns]
        source_ref = image_ref
        for (first, last), (back_first, back_last) in STEPS:
            for row in range(first, last, BAND):
                weights = [taps_ref[slot, row : row + BAND, :] for slot in range(len(SIDES))]
                for frame in range(frames):
                    rows = slice(PAD + row, PAD + row + BAND)
                    terms = []
                    for weight, tap in zip(weights, SIDES):
                        start = PAD + row + tap - TAPS // 2
                        terms.append(weight * source_ref[frame, start : start + BAND, :])
                    blurred = source_ref[frame, rows, :] + ((terms[0] + terms[1]) + (terms[2] + terms[3]))
                    quotient_ref[frame, rows, :] = image_ref[frame, rows, :] / blurred
            for row in range(back_first, back_last, BAND):
                weights = [back_ref[slot, row : row + BAND, :] for slot in range(len(SIDES))]
                for frame in range(frames):
                    rows = slice(PAD + row, PAD + row + BAND)
                    terms = []
                    for weight, tap in zip(weights, SIDES):
                        start = PAD + row - tap + TAPS // 2
                        terms.append(weight * quotient_ref[frame, start : start + BAND, :])
                    spread = quotient_ref[frame, rows, :] + ((terms[0] + terms[1]) + (terms[2] + terms[3]))
                    current_ref[frame, rows, :] = source_ref[frame, rows, :] * spread
            source_ref = current_ref
        first = pl.multiple_of(lax.rem(step, tiles_dev) * rows_dev, rows_dev)
        for frame in range(frames):
            estimate = current_ref[frame, PAD + MARGIN : PAD + MARGIN + rows_dev, :].astype(jnp.bfloat16)
            start = pl.multiple_of(first + frame * positions, rows_dev)
            out_ref[step // tiles_dev, pl.ds(start, rows_dev), :] = estimate
        return carry

    lax.fori_loop(0, n_frame * tiles_dev, columns_step, 0, unroll=2)
    lane_tiles = lax.broadcasted_iota(jnp.int32, (TILE, TILE), 1) % tiles_dev
    gathered = jnp.zeros((frames * n_frame * rows_dev, TILE), jnp.float32)
    for tile in range(tiles_dev):
        pieces = []
        for frame in range(frames):
            start = frame * positions + tile * rows_dev
            pieces += [out_ref[block, start : start + rows_dev, :] for block in range(n_frame)]
        picked = jnp.where(lane_tiles == tile, 1.0, 0.0).astype(jnp.bfloat16)
        gathered = gathered + jnp.dot(jnp.concatenate(pieces, axis=0), picked, preferred_element_type=jnp.float32)
    lanes = lax.broadcasted_iota(jnp.int32, (rows_dev, TILE), 1)
    here = lanes % positions // tiles_dev == lax.broadcasted_iota(jnp.int32, (rows_dev, TILE), 0)
    sums = []
    for place in range(frames * n_frame):
        part = jnp.where(here, gathered[place * rows_dev : (place + 1) * rows_dev], 0.0)
        sums.append(jnp.sum(part, axis=0, keepdims=True))
    sums = jnp.concatenate(sums, axis=0)
    high = sums.astype(jnp.bfloat16).astype(jnp.float32)
    split = jnp.where(lax.broadcasted_iota(jnp.int32, sums.shape, 1) < positions, high, sums - high).astype(jnp.bfloat16)
    for block in range(n_frame):
        side_ref[block, : split.shape[0], :] = split
        side_ref[block, split.shape[0] :, :] = feet_ref[block]


def deconvolved(series):
    total = len(series)
    factors = []
    for step in range(total):
        middle = 1.0 + SMOOTHING * (1.0 if step in (0, total - 1) else 2.0)
        if step:
            middle -= SMOOTHING * SMOOTHING * factors[-1]
        factors.append(1.0 / middle)
    scaled = [cells * factor for cells, factor in zip(series, factors)]
    forward = [scaled[0]]
    for step in range(1, total):
        forward.append(scaled[step] + (SMOOTHING * factors[step]) * forward[step - 1])
    baseline = [None] * total
    baseline[total - 1] = forward[total - 1]
    for step in range(total - 2, -1, -1):
        baseline[step] = forward[step] + (SMOOTHING * factors[step]) * baseline[step + 1]
    result, earlier = [], None
    for step in range(total):
        detrended = series[step] - baseline[step]
        result.append(detrended if earlier is None else detrended - DECAY_RATE * earlier)
        earlier = detrended
    return result


def partial_kernel(*refs, positions):
    pieces, (out_ref, sums_ref, feet_ref) = refs[:-3], refs[-3:]
    n_frame = len(pieces)
    place = lax.axis_index("frame")
    rows = sums_ref.shape[0] // n_frame
    half = feet_ref.shape[1]
    for step, piece in enumerate(pieces[::-1]):
        sums_ref[pl.ds(pl.multiple_of((place ^ step) * rows, rows), rows), :] = piece[:rows, :].astype(jnp.float32)
        feet_ref[place ^ step] = piece[rows:, :].astype(jnp.float32)
    series = [sums_ref[t * n_frame : (t + 1) * n_frame, :] for t in range(rows)]
    for t, sums in enumerate(deconvolved(series)):
        sums_ref[t * n_frame : (t + 1) * n_frame, :] = sums + pltpu.roll(sums, TILE // 2, 1)
    left = lax.broadcasted_iota(jnp.int32, (half, TILE), 1) < positions
    weights, sums = [], []
    extra = jnp.where(lax.broadcasted_iota(jnp.int32, (8, TILE), 0) == 0, 1.0, 0.0)
    for block in range(n_frame):
        feet = feet_ref[block]
        weights.append(jnp.concatenate([jnp.where(left, feet, 0.0), jnp.where(left, 0.0, feet)], axis=0))
        sums.append(jnp.concatenate([sums_ref[pl.ds(block, rows, stride=n_frame), :], extra], axis=0))
    sums = jnp.concatenate(sums, axis=1)
    parts = []
    for _ in range(3):
        parts.append(sums.astype(jnp.bfloat16))
        sums = sums - parts[-1].astype(jnp.float32)
    totals = lax.dot_general(
        jnp.concatenate(weights * 3, axis=1).astype(jnp.bfloat16),
        jnp.concatenate(parts, axis=1),
        (((1,), (1,)), ((), ())),
        preferred_element_type=jnp.float32,
    )
    share = out_ref.shape[2]
    out_ref[...] = jnp.zeros_like(out_ref)
    for row in range(2 * out_ref.shape[1]):
        out_ref[row % 2, row // 2, :, : rows + 8] = totals[row * share : (row + 1) * share]


def temporal_kernel(*refs, frames):
    pieces, (spikes_ref, in_ref) = refs[:-2], refs[-2:]
    place = lax.axis_index("frame")
    for step, piece in enumerate(pieces[::-1]):
        in_ref[place ^ step] = piece[...]
    total, rows_dev, columns = spikes_ref.shape
    positions = in_ref.shape[1] // frames
    for tile in range(columns // TILE):
        series = []
        for t in range(total):
            start = t % frames * positions + tile * rows_dev
            series.append(in_ref[t // frames, start : start + rows_dev, :].astype(jnp.float32))
        for t, spikes in enumerate(deconvolved(series)):
            spikes_ref[t, :, tile * TILE : (tile + 1) * TILE] = spikes.astype(spikes_ref.dtype)


def add_kernel(first_ref, second_ref, out_ref):
    out_ref[...] = first_ref[...] + second_ref[...]


def means_kernel(*refs):
    pieces, traces_ref = refs[:-1], refs[-1]
    frames = traces_ref.shape[1]
    total = pieces[0][...]
    for piece in pieces[1:]:
        total = total + piece[...]
    traces_ref[...] = total[:, :frames] / (TILE * total[:, frames : frames + 1])


def swapped(parts, axis):
    count, place = lax.axis_size(axis), lax.axis_index(axis)
    arrived = [lax.dynamic_index_in_dim(parts, place, 0, keepdims=False, allow_negative_indices=False)]
    for step in range(1, count):
        part = lax.dynamic_index_in_dim(parts, place ^ step, 0, keepdims=False, allow_negative_indices=False)
        arrived.append(lax.ppermute(part, axis, [(i, i ^ step) for i in range(count)]))
    return arrived


def swapped_one(parts, axis, mine, step):
    own, there = (
        lax.dynamic_index_in_dim(parts, index, 0, keepdims=False, allow_negative_indices=False) for index in (mine, mine ^ 1)
    )
    return own, lax.ppermute(there, axis, [(i, i ^ step) for i in range(lax.axis_size(axis))])


def in_turn(*arrays):
    done = []
    for array in arrays:
        done = list(lax.optimization_barrier((*done, array)))
    return done


def by_halo(observed, kernels, band_kernel, masks):
    n_frame, n_row = lax.axis_size("frame"), lax.axis_size("row")
    frames, rows_dev, width = observed.shape
    components, _, tiles_dev = masks.shape
    positions = rows_dev * tiles_dev
    share = components // (n_frame * n_row)
    span = rows_dev + 2 * MARGIN
    smem, vmem = pl.BlockSpec(memory_space=pltpu.SMEM), pl.BlockSpec(memory_space=pltpu.VMEM)

    def call(kernel, name, in_specs, out_shape, scratch=(), cost=1000):
        many = isinstance(out_shape, tuple)
        return pl.pallas_call(
            kernel,
            name=name,
            out_shape=out_shape,
            in_specs=in_specs,
            out_specs=(vmem,) * len(out_shape) if many else vmem,
            scratch_shapes=scratch,
            compiler_params=pltpu.CompilerParams(vmem_limit_bytes=16 << 20),
            cost_estimate=pl.CostEstimate(flops=cost, bytes_accessed=cost, transcendentals=0),
        )

    def array(*shape, dtype=jnp.float32):
        return jax.ShapeDtypeStruct(shape, dtype)

    packed = array(frames * (NEAR + FAR), width)
    inner, outer, own = call(halo_kernel, "halo", [vmem], (packed, packed, array(*observed.shape)))(observed)
    inner_swap = [(i, i ^ 1) for i in range(n_row)]
    outer_swap = []
    for f in range(n_frame):
        for i in range(n_row):
            there = (f ^ 1, i) if i in (0, n_row - 1) else (f, (i - 1 ^ 1) + 1)
            outer_swap.append((f * n_row + i, there[0] * n_row + there[1]))
    inner = lax.ppermute(inner.astype(jnp.float16), "row", inner_swap)
    outer = lax.ppermute(outer.astype(jnp.float16), ("frame", "row"), outer_swap)
    inner, outer = in_turn(inner, outer)
    taps, back = call(
        functools.partial(taps_kernel, height=rows_dev * n_row, rows_dev=rows_dev),
        "taps",
        [smem, smem],
        (array(len(SIDES), span, TILE),) * 2,
        [pltpu.VMEM((len(SIDES), span + 2 * PAD, TILE), jnp.float32)],
    )(band_kernel, kernels)
    feet = call(feet_kernel, "feet", [vmem], array(n_frame, n_row * share // 2, TILE, dtype=jnp.bfloat16))(
        masks.transpose(1, 2, 0)
    )
    row = lax.axis_index("row")
    even = row % 2 == 0
    alone = (row == 0) | (row == n_row - 1)
    inner, outer = inner.astype(jnp.float32), jnp.where(alone, 1.0, outer.astype(jnp.float32))
    top, bottom = jnp.where(even, outer, inner), jnp.where(even, inner, outer)
    side_rows = frames * n_frame + n_row * share // 2
    blocks, sides = call(
        restore_kernel,
        "restore",
        [vmem] * 6,
        (
            array(n_frame, frames * positions, TILE, dtype=jnp.bfloat16),
            array(n_frame, side_rows, TILE, dtype=jnp.bfloat16),
        ),
        [pltpu.VMEM((frames, span + 2 * PAD, TILE), jnp.float32)] * 3,
    )(taps, back, feet, own, top, bottom)
    sides = swapped(sides, "frame")
    pieces = swapped(blocks, "frame")
    partial = call(
        functools.partial(partial_kernel, positions=positions),
        "partial",
        [vmem] * n_frame,
        array(2, n_row // 2, share, TILE),
        [
            pltpu.VMEM((n_frame * frames * n_frame, TILE), jnp.float32),
            pltpu.VMEM((n_frame, n_row * share // 2, TILE), jnp.float32),
        ],
    )(*sides[::-1])
    own, there = swapped_one(partial, "row", row % 2, 1)
    *pieces, there = lax.optimization_barrier((*pieces[::-1], there))
    pairs = call(add_kernel, "add", [vmem] * 2, array(n_row // 2, share, TILE))(own, there)
    shares = swapped_one(pairs, "row", row // 2, 2)
    spikes = call(
        functools.partial(temporal_kernel, frames=frames),
        "temporal",
        [vmem] * n_frame,
        array(n_frame * frames, rows_dev, tiles_dev * TILE, dtype=jnp.bfloat16),
        [pltpu.VMEM((n_frame, frames * positions, TILE), jnp.bfloat16)],
    )(*pieces)
    spikes, *shares = in_turn(spikes, *shares)
    traces = call(means_kernel, "means", [vmem] * 2, array(share, n_frame * frames))(*shares)
    return (spikes, traces)


def fits(mesh, observed, masks):
    frames_dev = observed.shape[0] // mesh.shape["frame"]
    rows_dev = masks.shape[1] // (mesh.shape["groups"] * mesh.shape["row"])
    tiles_dev = masks.shape[2] // mesh.shape["frame"]
    places = mesh.shape["frame"] * mesh.shape["row"]
    return (
        frames_dev == mesh.shape["frame"] == mesh.shape["row"] == 4
        and 2 * rows_dev * tiles_dev == TILE
        and rows_dev == 16
        and masks.shape[0] // places == 16
    )


def solution(mesh):
    in_specs = (
        P("frame", ("groups", "row"), None),
        P(),
        P("groups"),
        P(None, ("groups", "row"), "frame"),
    )
    out_specs = (P(None, ("groups", "row"), "frame"), P(("groups", "frame", "row"), None))

    def whole(observed, kernels, band_kernel, masks):
        body = by_halo if fits(mesh, observed, masks) else local
        mapped = jax.shard_map(body, mesh=mesh, in_specs=in_specs, out_specs=out_specs, check_vma=False)
        return mapped(observed, kernels, band_kernel, masks)

    return whole
```

```python
import functools

import jax
import jax.numpy as jnp
from jax import lax
from jax.experimental import pallas as pl
from jax.experimental.pallas import tpu as pltpu
from jax.sharding import PartitionSpec as P

TILE = 128
BAND = 8
ITERS = 3
TAPS = 5
NEAR, FAR = 8, 4
MARGIN = 2 * BAND
PAD = BAND
STEPS = (((6, 46), (8, 40)), ((10, 42), (12, 36)), ((14, 38), (16, 32)))
SIDES = (0, 1, 3, 4)


SMOOTHING = 1024.0
DECAY_RATE = 0.9


def padded_2(cells, sides, width):
    for axis, dim in sides:
        count = lax.axis_size(axis)
        ends = count - 1
        head = lax.slice_in_dim(cells, 0, width, axis=dim)
        tail = lax.slice_in_dim(cells, cells.shape[dim] - width, cells.shape[dim], axis=dim)
        cells = jnp.concatenate(
            [
                lax.ppermute(tail, axis, [(i, (i + 1) % count) for i in range(ends)]),
                cells,
                lax.ppermute(head, axis, [((i + 1) % count, i) for i in range(ends)]),
            ],
            axis=dim,
        )
    return cells


def tap_rows(tap_table, band_kernel, first_row, row_count, height):
    row_ids = jnp.clip(first_row + jnp.arange(row_count), 0, height - 1)
    row_bands = row_ids // BAND
    band_slots = jnp.arange(band_kernel.shape[0])
    kernel_ids = jnp.sum(
        jnp.where(row_bands[:, None] == band_slots[None, :], band_kernel[None, :], 0), axis=1
    )
    kernel_slots = jnp.arange(tap_table.shape[0])
    picked = jnp.where(
        kernel_ids[:, None, None] == kernel_slots[None, :, None], tap_table[None, :, :], 0.0
    )
    return jnp.sum(picked, axis=1)


def blur_rows(padded, row_taps, row_count):
    summed = row_taps[:, 0][None, :, None] * padded[:, 0:row_count]
    for offset in range(1, 5):
        summed = (
            summed + row_taps[:, offset][None, :, None] * padded[:, offset : offset + row_count]
        )
    return summed


def back_rows(padded_quotient, outer_taps, row_count):
    summed = outer_taps[4 : 4 + row_count, 0][None, :, None] * padded_quotient[:, 4 : 4 + row_count]
    for offset in range(1, 5):
        start = 4 - offset
        summed = (
            summed
            + outer_taps[start : start + row_count, offset][None, :, None]
            * padded_quotient[:, start : start + row_count]
        )
    return summed


def temporal(series_block):
    frame_total, item_count, columns = series_block.shape
    values = series_block.astype(jnp.float32).reshape(frame_total, item_count * columns)
    frame_ids = jnp.arange(frame_total)
    at_ends = (frame_ids == 0) | (frame_ids == frame_total - 1)
    middle = (1.0 + SMOOTHING * jnp.where(at_ends, 1.0, 2.0)).astype(jnp.float32)
    sub_diag = jnp.where(frame_ids == 0, 0.0, -SMOOTHING).astype(jnp.float32)
    super_diag = jnp.where(frame_ids == frame_total - 1, 0.0, -SMOOTHING).astype(jnp.float32)
    baseline = lax.linalg.tridiagonal_solve(sub_diag, middle, super_diag, values)
    detrended = values - baseline
    earlier = jnp.concatenate(
        [jnp.zeros((1, values.shape[1]), jnp.float32), detrended[:-1]], axis=0
    )
    result = (detrended - DECAY_RATE * earlier).astype(jnp.bfloat16)
    return result.reshape(frame_total, item_count, columns)


def local(observed, kernels, band_kernel, masks):
    frames_dev, rows_dev, row_pixels = observed.shape
    height = rows_dev * lax.axis_size("row")
    tap_table = kernels / jnp.sum(kernels, axis=1, keepdims=True)
    first_row = lax.axis_index("row") * rows_dev
    own_taps = tap_rows(tap_table, band_kernel, first_row, rows_dev, height)
    outer_taps = tap_rows(tap_table, band_kernel, first_row - 2, rows_dev + 4, height)
    current = observed
    for iteration in range(ITERS):
        padded = padded_2(current, (("row", 1),), 2)
        blurred = blur_rows(padded, own_taps, rows_dev)
        quotient = observed / blurred
        padded_quotient = padded_2(quotient, (("row", 1),), 2)
        current = current * back_rows(padded_quotient, outer_taps, rows_dev)
    estimate = current.astype(jnp.bfloat16)
    spikes = temporal(lax.all_to_all(estimate, "frame", split_axis=2, concat_axis=0, tiled=True))
    frames_all, _, columns = spikes.shape
    tile_count = columns // TILE
    tile_sums = jnp.sum(
        spikes.reshape(frames_all, rows_dev * tile_count, TILE).astype(jnp.float32), axis=2
    )
    weights = masks.astype(jnp.float32).reshape(masks.shape[0], rows_dev * tile_count)
    local_sums = lax.dot_general(
        weights, tile_sums, (((1,), (1,)), ((), ())), precision=lax.Precision.HIGHEST
    )
    counts = jnp.sum(weights, axis=1)
    trace_sums, totals = (
        lax.psum_scatter(local_sums, ("frame", "row"), scatter_dimension=0, tiled=True),
        lax.psum_scatter(counts, ("frame", "row"), scatter_dimension=0, tiled=True),
    )
    traces = trace_sums / (TILE * totals[:, None])
    return (spikes, traces)


def halo_kernel(observed_ref, inner_ref, outer_ref, own_ref):
    even = lax.axis_index("row") % 2 == 0
    frames = observed_ref.shape[0]
    own_ref[...] = observed_ref[...]
    for frame in range(frames):
        near = frame * NEAR
        far = frames * NEAR + frame * FAR
        bottom, top = observed_ref[frame, -NEAR:, :], observed_ref[frame, :NEAR, :]
        inner_ref[near : near + NEAR, :] = jnp.where(even, bottom, top)
        outer_ref[near : near + NEAR, :] = jnp.where(even, top, bottom)
        bottom, top = observed_ref[frame, -NEAR - FAR : -NEAR, :], observed_ref[frame, NEAR : NEAR + FAR, :]
        inner_ref[far : far + FAR, :] = jnp.where(even, bottom, top)
        outer_ref[far : far + FAR, :] = jnp.where(even, top, bottom)


def taps_kernel(band_ref, kernels_ref, taps_ref, back_ref, pad_ref, *, height, rows_dev):
    span = rows_dev + 2 * MARGIN
    first_row = lax.axis_index("row") * rows_dev - MARGIN
    row_ids = lax.broadcasted_iota(jnp.int32, (BAND, TILE), 0)
    pad_ref[...] = jnp.zeros_like(pad_ref)
    for band in range(span // BAND):
        row = first_row + band * BAND
        inside = (row >= 0) & (row < height)
        kernel = band_ref[jnp.clip(row, 0, height - 1) // BAND]
        centre = jnp.full((BAND, TILE), kernels_ref[kernel, TAPS // 2], jnp.float32)
        start = band * BAND
        for slot, tap in enumerate(SIDES):
            weight = jnp.full((BAND, TILE), kernels_ref[kernel, tap], jnp.float32) / centre
            target = row_ids + (row + tap - TAPS // 2)
            weight = jnp.where(inside & (target >= 0) & (target < height), weight, 0.0)
            taps_ref[slot, start : start + BAND, :] = weight
            pad_ref[slot, BAND + start : 2 * BAND + start, :] = weight
    for slot, tap in enumerate(SIDES):
        start = BAND + TAPS // 2 - tap
        back_ref[slot] = pad_ref[slot, start : start + span, :]


def feet_kernel(masks_ref, feet_ref):
    rows_dev = masks_ref.shape[0]
    flat = jnp.concatenate([masks_ref[row].astype(jnp.float32) for row in range(rows_dev)], axis=0)
    positions = flat.shape[0]
    both = jnp.concatenate([flat, flat], axis=0).T
    half = feet_ref.shape[1]
    left = lax.broadcasted_iota(jnp.int32, (half, TILE), 1) < positions
    for block in range(feet_ref.shape[0]):
        start = 2 * block * half
        halves = jnp.where(left, both[start : start + half], both[start + half : start + 2 * half])
        feet_ref[block] = halves.astype(jnp.bfloat16)


def restore_kernel(
    taps_ref, back_ref, feet_ref, own_ref, top_ref, bottom_ref, out_ref, side_ref, image_ref, current_ref, quotient_ref
):
    n_frame = out_ref.shape[0]
    frames, rows_dev, width = own_ref.shape
    tiles_dev = width // (n_frame * TILE)
    positions = rows_dev * tiles_dev
    for ref in (image_ref, current_ref, quotient_ref):
        ref[...] = jnp.ones_like(ref)

    def columns_step(step, carry):
        columns = pl.ds(pl.multiple_of(step * TILE, TILE), TILE)
        for frame in range(frames):
            near, far = frame * NEAR, frames * NEAR + frame * FAR
            start, stop = PAD + MARGIN, PAD + MARGIN + rows_dev
            image_ref[frame, start - NEAR - FAR : start - NEAR, :] = top_ref[far : far + FAR, columns]
            image_ref[frame, start - NEAR : start, :] = top_ref[near : near + NEAR, columns]
            image_ref[frame, stop : stop + NEAR, :] = bottom_ref[near : near + NEAR, columns]
            image_ref[frame, stop + NEAR : stop + NEAR + FAR, :] = bottom_ref[far : far + FAR, columns]
            image_ref[frame, start:stop, :] = own_ref[frame, :, columns]
        source_ref = image_ref
        for (first, last), (back_first, back_last) in STEPS:
            for row in range(first, last, BAND):
                weights = [taps_ref[slot, row : row + BAND, :] for slot in range(len(SIDES))]
                for frame in range(frames):
                    rows = slice(PAD + row, PAD + row + BAND)
                    terms = []
                    for weight, tap in zip(weights, SIDES):
                        start = PAD + row + tap - TAPS // 2
                        terms.append(weight * source_ref[frame, start : start + BAND, :])
                    blurred = source_ref[frame, rows, :] + ((terms[0] + terms[1]) + (terms[2] + terms[3]))
                    quotient_ref[frame, rows, :] = image_ref[frame, rows, :] / blurred
            for row in range(back_first, back_last, BAND):
                weights = [back_ref[slot, row : row + BAND, :] for slot in range(len(SIDES))]
                for frame in range(frames):
                    rows = slice(PAD + row, PAD + row + BAND)
                    terms = []
                    for weight, tap in zip(weights, SIDES):
                        start = PAD + row - tap + TAPS // 2
                        terms.append(weight * quotient_ref[frame, start : start + BAND, :])
                    spread = quotient_ref[frame, rows, :] + ((terms[0] + terms[1]) + (terms[2] + terms[3]))
                    current_ref[frame, rows, :] = source_ref[frame, rows, :] * spread
            source_ref = current_ref
        first = pl.multiple_of(lax.rem(step, tiles_dev) * rows_dev, rows_dev)
        for frame in range(frames):
            estimate = current_ref[frame, PAD + MARGIN : PAD + MARGIN + rows_dev, :].astype(jnp.bfloat16)
            start = pl.multiple_of(first + frame * positions, rows_dev)
            out_ref[step // tiles_dev, pl.ds(start, rows_dev), :] = estimate
        return carry

    lax.fori_loop(0, n_frame * tiles_dev, columns_step, 0, unroll=2)
    lane_tiles = lax.broadcasted_iota(jnp.int32, (TILE, TILE), 1) % tiles_dev
    gathered = jnp.zeros((frames * n_frame * rows_dev, TILE), jnp.float32)
    for tile in range(tiles_dev):
        pieces = []
        for frame in range(frames):
            start = frame * positions + tile * rows_dev
            pieces += [out_ref[block, start : start + rows_dev, :] for block in range(n_frame)]
        picked = jnp.where(lane_tiles == tile, 1.0, 0.0).astype(jnp.bfloat16)
        gathered = gathered + jnp.dot(jnp.concatenate(pieces, axis=0), picked, preferred_element_type=jnp.float32)
    lanes = lax.broadcasted_iota(jnp.int32, (rows_dev, TILE), 1)
    here = lanes % positions // tiles_dev == lax.broadcasted_iota(jnp.int32, (rows_dev, TILE), 0)
    sums = []
    for place in range(frames * n_frame):
        part = jnp.where(here, gathered[place * rows_dev : (place + 1) * rows_dev], 0.0)
        sums.append(jnp.sum(part, axis=0, keepdims=True))
    sums = jnp.concatenate(sums, axis=0)
    high = sums.astype(jnp.bfloat16).astype(jnp.float32)
    split = jnp.where(lax.broadcasted_iota(jnp.int32, sums.shape, 1) < positions, high, sums - high).astype(jnp.bfloat16)
    for block in range(n_frame):
        side_ref[block, : split.shape[0], :] = split
        side_ref[block, split.shape[0] :, :] = feet_ref[block]


def deconvolved(series):
    total = len(series)
    factors = []
    for step in range(total):
        middle = 1.0 + SMOOTHING * (1.0 if step in (0, total - 1) else 2.0)
        if step:
            middle -= SMOOTHING * SMOOTHING * factors[-1]
        factors.append(1.0 / middle)
    scaled = [cells * factor for cells, factor in zip(series, factors)]
    forward = [scaled[0]]
    for step in range(1, total):
        forward.append(scaled[step] + (SMOOTHING * factors[step]) * forward[step - 1])
    baseline = [None] * total
    baseline[total - 1] = forward[total - 1]
    for step in range(total - 2, -1, -1):
        baseline[step] = forward[step] + (SMOOTHING * factors[step]) * baseline[step + 1]
    result, earlier = [], None
    for step in range(total):
        detrended = series[step] - baseline[step]
        result.append(detrended if earlier is None else detrended - DECAY_RATE * earlier)
        earlier = detrended
    return result


def partial_kernel(*refs, positions):
    pieces, (out_ref, sums_ref, feet_ref) = refs[:-3], refs[-3:]
    n_frame = len(pieces)
    place = lax.axis_index("frame")
    rows = sums_ref.shape[0] // n_frame
    half = feet_ref.shape[1]
    for step, piece in enumerate(pieces[::-1]):
        sums_ref[pl.ds(pl.multiple_of((place ^ step) * rows, rows), rows), :] = piece[:rows, :].astype(jnp.float32)
        feet_ref[place ^ step] = piece[rows:, :].astype(jnp.float32)
    series = [sums_ref[t * n_frame : (t + 1) * n_frame, :] for t in range(rows)]
    for t, sums in enumerate(deconvolved(series)):
        sums_ref[t * n_frame : (t + 1) * n_frame, :] = sums + pltpu.roll(sums, TILE // 2, 1)
    left = lax.broadcasted_iota(jnp.int32, (half, TILE), 1) < positions
    weights, sums = [], []
    extra = jnp.where(lax.broadcasted_iota(jnp.int32, (8, TILE), 0) == 0, 1.0, 0.0)
    for block in range(n_frame):
        feet = feet_ref[block]
        weights.append(jnp.concatenate([jnp.where(left, feet, 0.0), jnp.where(left, 0.0, feet)], axis=0))
        sums.append(jnp.concatenate([sums_ref[pl.ds(block, rows, stride=n_frame), :], extra], axis=0))
    sums = jnp.concatenate(sums, axis=1)
    parts = []
    for _ in range(3):
        parts.append(sums.astype(jnp.bfloat16))
        sums = sums - parts[-1].astype(jnp.float32)
    totals = lax.dot_general(
        jnp.concatenate(weights * 3, axis=1).astype(jnp.bfloat16),
        jnp.concatenate(parts, axis=1),
        (((1,), (1,)), ((), ())),
        preferred_element_type=jnp.float32,
    )
    share = out_ref.shape[1]
    out_ref[...] = jnp.zeros_like(out_ref)
    for row in range(out_ref.shape[0]):
        out_ref[row, :, : rows + 8] = totals[row * share : (row + 1) * share]


def temporal_kernel(*refs, frames):
    pieces, (spikes_ref, in_ref) = refs[:-2], refs[-2:]
    place = lax.axis_index("frame")
    for step, piece in enumerate(pieces[::-1]):
        in_ref[place ^ step] = piece[...]
    total, rows_dev, columns = spikes_ref.shape
    positions = in_ref.shape[1] // frames
    for tile in range(columns // TILE):
        series = []
        for t in range(total):
            start = t % frames * positions + tile * rows_dev
            series.append(in_ref[t // frames, start : start + rows_dev, :].astype(jnp.float32))
        for t, spikes in enumerate(deconvolved(series)):
            spikes_ref[t, :, tile * TILE : (tile + 1) * TILE] = spikes.astype(spikes_ref.dtype)


def means_kernel(*refs):
    pieces, traces_ref = refs[:-1], refs[-1]
    frames = traces_ref.shape[1]
    total = pieces[0][...]
    for piece in pieces[1:]:
        total = total + piece[...]
    traces_ref[...] = total[:, :frames] / (TILE * total[:, frames : frames + 1])


def swapped(parts, axis):
    count, place = lax.axis_size(axis), lax.axis_index(axis)
    arrived = [lax.dynamic_index_in_dim(parts, place, 0, keepdims=False, allow_negative_indices=False)]
    for step in range(1, count):
        part = lax.dynamic_index_in_dim(parts, place ^ step, 0, keepdims=False, allow_negative_indices=False)
        arrived.append(lax.ppermute(part, axis, [(i, i ^ step) for i in range(count)]))
    return arrived


def in_turn(*arrays):
    done = []
    for array in arrays:
        done = list(lax.optimization_barrier((*done, array)))
    return done


def by_halo(observed, kernels, band_kernel, masks):
    n_frame, n_row = lax.axis_size("frame"), lax.axis_size("row")
    frames, rows_dev, width = observed.shape
    components, _, tiles_dev = masks.shape
    positions = rows_dev * tiles_dev
    share = components // (n_frame * n_row)
    span = rows_dev + 2 * MARGIN
    smem, vmem = pl.BlockSpec(memory_space=pltpu.SMEM), pl.BlockSpec(memory_space=pltpu.VMEM)

    def call(kernel, name, in_specs, out_shape, scratch=(), cost=1000):
        many = isinstance(out_shape, tuple)
        return pl.pallas_call(
            kernel,
            name=name,
            out_shape=out_shape,
            in_specs=in_specs,
            out_specs=(vmem,) * len(out_shape) if many else vmem,
            scratch_shapes=scratch,
            compiler_params=pltpu.CompilerParams(vmem_limit_bytes=16 << 20),
            cost_estimate=pl.CostEstimate(flops=cost, bytes_accessed=cost, transcendentals=0),
        )

    def array(*shape, dtype=jnp.float32):
        return jax.ShapeDtypeStruct(shape, dtype)

    packed = array(frames * (NEAR + FAR), width)
    inner, outer, own = call(halo_kernel, "halo", [vmem], (packed, packed, array(*observed.shape)))(observed)
    inner_swap = [(i, i ^ 1) for i in range(n_row)]
    outer_swap = []
    for f in range(n_frame):
        for i in range(n_row):
            there = (f ^ 1, i) if i in (0, n_row - 1) else (f, (i - 1 ^ 1) + 1)
            outer_swap.append((f * n_row + i, there[0] * n_row + there[1]))
    inner = inner.astype(jnp.float16)
    inner, band_kernel = lax.optimization_barrier((inner, band_kernel))
    inner = lax.ppermute(inner, "row", inner_swap)
    taps, back = call(
        functools.partial(taps_kernel, height=rows_dev * n_row, rows_dev=rows_dev),
        "taps",
        [smem, smem],
        (array(len(SIDES), span, TILE),) * 2,
        [pltpu.VMEM((len(SIDES), span + 2 * PAD, TILE), jnp.float32)],
    )(band_kernel, kernels)
    outer, taps = lax.optimization_barrier((outer, taps))
    outer = lax.ppermute(outer.astype(jnp.float16), ("frame", "row"), outer_swap)
    inner, outer = in_turn(inner, outer)
    feet = call(feet_kernel, "feet", [vmem], array(n_frame, n_row * share // 2, TILE, dtype=jnp.bfloat16))(
        masks.transpose(1, 2, 0)
    )
    row = lax.axis_index("row")
    even = row % 2 == 0
    alone = (row == 0) | (row == n_row - 1)
    inner, outer = inner.astype(jnp.float32), jnp.where(alone, 1.0, outer.astype(jnp.float32))
    top, bottom = jnp.where(even, outer, inner), jnp.where(even, inner, outer)
    side_rows = frames * n_frame + n_row * share // 2
    blocks, sides = call(
        restore_kernel,
        "restore",
        [vmem] * 6,
        (
            array(n_frame, frames * positions, TILE, dtype=jnp.bfloat16),
            array(n_frame, side_rows, TILE, dtype=jnp.bfloat16),
        ),
        [pltpu.VMEM((frames, span + 2 * PAD, TILE), jnp.float32)] * 3,
    )(taps, back, feet, own, top, bottom)
    sides = swapped(sides, "frame")
    pieces = swapped(blocks, "frame")
    partial = call(
        functools.partial(partial_kernel, positions=positions),
        "partial",
        [vmem] * n_frame,
        array(n_row, share, TILE),
        [
            pltpu.VMEM((n_frame * frames * n_frame, TILE), jnp.float32),
            pltpu.VMEM((n_frame, n_row * share // 2, TILE), jnp.float32),
        ],
    )(*sides[::-1])
    shares = swapped(partial, "row")
    spikes = call(
        functools.partial(temporal_kernel, frames=frames),
        "temporal",
        [vmem] * n_frame,
        array(n_frame * frames, rows_dev, tiles_dev * TILE, dtype=jnp.bfloat16),
        [pltpu.VMEM((n_frame, frames * positions, TILE), jnp.bfloat16)],
    )(*pieces[::-1])
    spikes, *shares = in_turn(spikes, *shares[::-1])
    traces = call(means_kernel, "means", [vmem] * n_row, array(share, n_frame * frames))(*shares)
    return (spikes, traces)


def fits(mesh, observed, masks):
    frames_dev = observed.shape[0] // mesh.shape["frame"]
    rows_dev = masks.shape[1] // (mesh.shape["groups"] * mesh.shape["row"])
    tiles_dev = masks.shape[2] // mesh.shape["frame"]
    places = mesh.shape["frame"] * mesh.shape["row"]
    return (
        frames_dev == mesh.shape["frame"] == mesh.shape["row"] == 4
        and 2 * rows_dev * tiles_dev == TILE
        and rows_dev == 16
        and masks.shape[0] // places == 16
    )


def solution(mesh):
    in_specs = (
        P("frame", ("groups", "row"), None),
        P(),
        P("groups"),
        P(None, ("groups", "row"), "frame"),
    )
    out_specs = (P(None, ("groups", "row"), "frame"), P(("groups", "frame", "row"), None))

    def whole(observed, kernels, band_kernel, masks):
        body = by_halo if fits(mesh, observed, masks) else local
        mapped = jax.shard_map(body, mesh=mesh, in_specs=in_specs, out_specs=out_specs, check_vma=False)
        return mapped(observed, kernels, band_kernel, masks)

    return whole
```

```python
import functools

import jax
import jax.numpy as jnp
from jax import lax
from jax.experimental import pallas as pl
from jax.experimental.pallas import tpu as pltpu
from jax.sharding import PartitionSpec as P

TILE = 128
BAND = 8
ITERS = 3
TAPS = 5
NEAR, FAR = 8, 4
MARGIN = 2 * BAND
PAD = BAND
STEPS = (((6, 46), (8, 40)), ((10, 42), (12, 36)), ((14, 38), (16, 32)))
SIDES = (0, 1, 3, 4)


SMOOTHING = 1024.0
DECAY_RATE = 0.9


def padded_2(cells, sides, width):
    for axis, dim in sides:
        count = lax.axis_size(axis)
        ends = count - 1
        head = lax.slice_in_dim(cells, 0, width, axis=dim)
        tail = lax.slice_in_dim(cells, cells.shape[dim] - width, cells.shape[dim], axis=dim)
        cells = jnp.concatenate(
            [
                lax.ppermute(tail, axis, [(i, (i + 1) % count) for i in range(ends)]),
                cells,
                lax.ppermute(head, axis, [((i + 1) % count, i) for i in range(ends)]),
            ],
            axis=dim,
        )
    return cells


def tap_rows(tap_table, band_kernel, first_row, row_count, height):
    row_ids = jnp.clip(first_row + jnp.arange(row_count), 0, height - 1)
    row_bands = row_ids // BAND
    band_slots = jnp.arange(band_kernel.shape[0])
    kernel_ids = jnp.sum(
        jnp.where(row_bands[:, None] == band_slots[None, :], band_kernel[None, :], 0), axis=1
    )
    kernel_slots = jnp.arange(tap_table.shape[0])
    picked = jnp.where(
        kernel_ids[:, None, None] == kernel_slots[None, :, None], tap_table[None, :, :], 0.0
    )
    return jnp.sum(picked, axis=1)


def blur_rows(padded, row_taps, row_count):
    summed = row_taps[:, 0][None, :, None] * padded[:, 0:row_count]
    for offset in range(1, 5):
        summed = (
            summed + row_taps[:, offset][None, :, None] * padded[:, offset : offset + row_count]
        )
    return summed


def back_rows(padded_quotient, outer_taps, row_count):
    summed = outer_taps[4 : 4 + row_count, 0][None, :, None] * padded_quotient[:, 4 : 4 + row_count]
    for offset in range(1, 5):
        start = 4 - offset
        summed = (
            summed
            + outer_taps[start : start + row_count, offset][None, :, None]
            * padded_quotient[:, start : start + row_count]
        )
    return summed


def temporal(series_block):
    frame_total, item_count, columns = series_block.shape
    values = series_block.astype(jnp.float32).reshape(frame_total, item_count * columns)
    frame_ids = jnp.arange(frame_total)
    at_ends = (frame_ids == 0) | (frame_ids == frame_total - 1)
    middle = (1.0 + SMOOTHING * jnp.where(at_ends, 1.0, 2.0)).astype(jnp.float32)
    sub_diag = jnp.where(frame_ids == 0, 0.0, -SMOOTHING).astype(jnp.float32)
    super_diag = jnp.where(frame_ids == frame_total - 1, 0.0, -SMOOTHING).astype(jnp.float32)
    baseline = lax.linalg.tridiagonal_solve(sub_diag, middle, super_diag, values)
    detrended = values - baseline
    earlier = jnp.concatenate(
        [jnp.zeros((1, values.shape[1]), jnp.float32), detrended[:-1]], axis=0
    )
    result = (detrended - DECAY_RATE * earlier).astype(jnp.bfloat16)
    return result.reshape(frame_total, item_count, columns)


def local(observed, kernels, band_kernel, masks):
    frames_dev, rows_dev, row_pixels = observed.shape
    height = rows_dev * lax.axis_size("row")
    tap_table = kernels / jnp.sum(kernels, axis=1, keepdims=True)
    first_row = lax.axis_index("row") * rows_dev
    own_taps = tap_rows(tap_table, band_kernel, first_row, rows_dev, height)
    outer_taps = tap_rows(tap_table, band_kernel, first_row - 2, rows_dev + 4, height)
    current = observed
    for iteration in range(ITERS):
        padded = padded_2(current, (("row", 1),), 2)
        blurred = blur_rows(padded, own_taps, rows_dev)
        quotient = observed / blurred
        padded_quotient = padded_2(quotient, (("row", 1),), 2)
        current = current * back_rows(padded_quotient, outer_taps, rows_dev)
    estimate = current.astype(jnp.bfloat16)
    spikes = temporal(lax.all_to_all(estimate, "frame", split_axis=2, concat_axis=0, tiled=True))
    frames_all, _, columns = spikes.shape
    tile_count = columns // TILE
    tile_sums = jnp.sum(
        spikes.reshape(frames_all, rows_dev * tile_count, TILE).astype(jnp.float32), axis=2
    )
    weights = masks.astype(jnp.float32).reshape(masks.shape[0], rows_dev * tile_count)
    local_sums = lax.dot_general(
        weights, tile_sums, (((1,), (1,)), ((), ())), precision=lax.Precision.HIGHEST
    )
    counts = jnp.sum(weights, axis=1)
    trace_sums, totals = (
        lax.psum_scatter(local_sums, ("frame", "row"), scatter_dimension=0, tiled=True),
        lax.psum_scatter(counts, ("frame", "row"), scatter_dimension=0, tiled=True),
    )
    traces = trace_sums / (TILE * totals[:, None])
    return (spikes, traces)


def halo_kernel(observed_ref, inner_ref, outer_ref, own_ref):
    even = lax.axis_index("row") % 2 == 0
    frames = observed_ref.shape[0]
    own_ref[...] = observed_ref[...]
    for frame in range(frames):
        near = frame * NEAR
        far = frames * NEAR + frame * FAR
        bottom, top = observed_ref[frame, -NEAR:, :], observed_ref[frame, :NEAR, :]
        inner_ref[near : near + NEAR, :] = jnp.where(even, bottom, top)
        outer_ref[near : near + NEAR, :] = jnp.where(even, top, bottom)
        bottom, top = observed_ref[frame, -NEAR - FAR : -NEAR, :], observed_ref[frame, NEAR : NEAR + FAR, :]
        inner_ref[far : far + FAR, :] = jnp.where(even, bottom, top)
        outer_ref[far : far + FAR, :] = jnp.where(even, top, bottom)


def taps_kernel(band_ref, kernels_ref, taps_ref, back_ref, pad_ref, *, height, rows_dev):
    span = rows_dev + 2 * MARGIN
    first_row = lax.axis_index("row") * rows_dev - MARGIN
    row_ids = lax.broadcasted_iota(jnp.int32, (BAND, TILE), 0)
    pad_ref[...] = jnp.zeros_like(pad_ref)
    for band in range(span // BAND):
        row = first_row + band * BAND
        inside = (row >= 0) & (row < height)
        kernel = band_ref[jnp.clip(row, 0, height - 1) // BAND]
        centre = jnp.full((BAND, TILE), kernels_ref[kernel, TAPS // 2], jnp.float32)
        start = band * BAND
        for slot, tap in enumerate(SIDES):
            weight = jnp.full((BAND, TILE), kernels_ref[kernel, tap], jnp.float32) / centre
            target = row_ids + (row + tap - TAPS // 2)
            weight = jnp.where(inside & (target >= 0) & (target < height), weight, 0.0)
            taps_ref[slot, start : start + BAND, :] = weight
            pad_ref[slot, BAND + start : 2 * BAND + start, :] = weight
    for slot, tap in enumerate(SIDES):
        start = BAND + TAPS // 2 - tap
        back_ref[slot] = pad_ref[slot, start : start + span, :]


def feet_kernel(masks_ref, feet_ref):
    rows_dev = masks_ref.shape[0]
    flat = jnp.concatenate([masks_ref[row].astype(jnp.float32) for row in range(rows_dev)], axis=0)
    positions = flat.shape[0]
    both = jnp.concatenate([flat, flat], axis=0).T
    half = feet_ref.shape[1]
    left = lax.broadcasted_iota(jnp.int32, (half, TILE), 1) < positions
    for block in range(feet_ref.shape[0]):
        start = 2 * block * half
        halves = jnp.where(left, both[start : start + half], both[start + half : start + 2 * half])
        feet_ref[block] = halves.astype(jnp.bfloat16)


def weights_kernel(*refs):
    pieces, weights_ref = refs[:-1], refs[-1]
    place = lax.axis_index("frame")
    half = weights_ref.shape[0] // 2
    left = lax.broadcasted_iota(jnp.int32, (half, TILE), 1) < TILE // 2
    for step, piece in enumerate(pieces):
        columns = pl.ds(pl.multiple_of((place ^ step) * TILE, TILE), TILE)
        feet = piece[...].astype(jnp.float32)
        weights_ref[:half, columns] = jnp.where(left, feet, 0.0).astype(jnp.bfloat16)
        weights_ref[half:, columns] = jnp.where(left, 0.0, feet).astype(jnp.bfloat16)


def restore_kernel(
    taps_ref, back_ref, own_ref, top_ref, bottom_ref, out_ref, side_ref, image_ref, current_ref, quotient_ref
):
    n_frame = out_ref.shape[0]
    frames, rows_dev, width = own_ref.shape
    tiles_dev = width // (n_frame * TILE)
    positions = rows_dev * tiles_dev
    for ref in (image_ref, current_ref, quotient_ref):
        ref[...] = jnp.ones_like(ref)

    def columns_step(step, carry):
        columns = pl.ds(pl.multiple_of(step * TILE, TILE), TILE)
        for frame in range(frames):
            near, far = frame * NEAR, frames * NEAR + frame * FAR
            start, stop = PAD + MARGIN, PAD + MARGIN + rows_dev
            image_ref[frame, start - NEAR - FAR : start - NEAR, :] = top_ref[far : far + FAR, columns]
            image_ref[frame, start - NEAR : start, :] = top_ref[near : near + NEAR, columns]
            image_ref[frame, stop : stop + NEAR, :] = bottom_ref[near : near + NEAR, columns]
            image_ref[frame, stop + NEAR : stop + NEAR + FAR, :] = bottom_ref[far : far + FAR, columns]
            image_ref[frame, start:stop, :] = own_ref[frame, :, columns]
        source_ref = image_ref
        for (first, last), (back_first, back_last) in STEPS:
            for row in range(first, last, BAND):
                weights = [taps_ref[slot, row : row + BAND, :] for slot in range(len(SIDES))]
                for frame in range(frames):
                    rows = slice(PAD + row, PAD + row + BAND)
                    terms = []
                    for weight, tap in zip(weights, SIDES):
                        start = PAD + row + tap - TAPS // 2
                        terms.append(weight * source_ref[frame, start : start + BAND, :])
                    blurred = source_ref[frame, rows, :] + ((terms[0] + terms[1]) + (terms[2] + terms[3]))
                    quotient_ref[frame, rows, :] = image_ref[frame, rows, :] / blurred
            for row in range(back_first, back_last, BAND):
                weights = [back_ref[slot, row : row + BAND, :] for slot in range(len(SIDES))]
                for frame in range(frames):
                    rows = slice(PAD + row, PAD + row + BAND)
                    terms = []
                    for weight, tap in zip(weights, SIDES):
                        start = PAD + row - tap + TAPS // 2
                        terms.append(weight * quotient_ref[frame, start : start + BAND, :])
                    spread = quotient_ref[frame, rows, :] + ((terms[0] + terms[1]) + (terms[2] + terms[3]))
                    current_ref[frame, rows, :] = source_ref[frame, rows, :] * spread
            source_ref = current_ref
        first = pl.multiple_of(lax.rem(step, tiles_dev) * rows_dev, rows_dev)
        for frame in range(frames):
            estimate = current_ref[frame, PAD + MARGIN : PAD + MARGIN + rows_dev, :].astype(jnp.bfloat16)
            start = pl.multiple_of(first + frame * positions, rows_dev)
            out_ref[step // tiles_dev, pl.ds(start, rows_dev), :] = estimate
        return carry

    lax.fori_loop(0, n_frame * tiles_dev, columns_step, 0, unroll=2)
    lane_tiles = lax.broadcasted_iota(jnp.int32, (TILE, TILE), 1) % tiles_dev
    gathered = jnp.zeros((frames * n_frame * rows_dev, TILE), jnp.float32)
    for tile in range(tiles_dev):
        pieces = []
        for frame in range(frames):
            start = frame * positions + tile * rows_dev
            pieces += [out_ref[block, start : start + rows_dev, :] for block in range(n_frame)]
        picked = jnp.where(lane_tiles == tile, 1.0, 0.0).astype(jnp.bfloat16)
        gathered = gathered + jnp.dot(jnp.concatenate(pieces, axis=0), picked, preferred_element_type=jnp.float32)
    lanes = lax.broadcasted_iota(jnp.int32, (rows_dev, TILE), 1)
    here = lanes % positions // tiles_dev == lax.broadcasted_iota(jnp.int32, (rows_dev, TILE), 0)
    sums = []
    for place in range(frames * n_frame):
        part = jnp.where(here, gathered[place * rows_dev : (place + 1) * rows_dev], 0.0)
        sums.append(jnp.sum(part, axis=0, keepdims=True))
    sums = jnp.concatenate(sums, axis=0)
    high = sums.astype(jnp.bfloat16).astype(jnp.float32)
    split = jnp.where(lax.broadcasted_iota(jnp.int32, sums.shape, 1) < positions, high, sums - high).astype(jnp.bfloat16)
    side_ref[...] = split


def deconvolved(series):
    total = len(series)
    factors = []
    for step in range(total):
        middle = 1.0 + SMOOTHING * (1.0 if step in (0, total - 1) else 2.0)
        if step:
            middle -= SMOOTHING * SMOOTHING * factors[-1]
        factors.append(1.0 / middle)
    scaled = [cells * factor for cells, factor in zip(series, factors)]
    forward = [scaled[0]]
    for step in range(1, total):
        forward.append(scaled[step] + (SMOOTHING * factors[step]) * forward[step - 1])
    baseline = [None] * total
    baseline[total - 1] = forward[total - 1]
    for step in range(total - 2, -1, -1):
        baseline[step] = forward[step] + (SMOOTHING * factors[step]) * baseline[step + 1]
    result, earlier = [], None
    for step in range(total):
        detrended = series[step] - baseline[step]
        result.append(detrended if earlier is None else detrended - DECAY_RATE * earlier)
        earlier = detrended
    return result


def partial_kernel(weights_ref, *refs):
    pieces, (out_ref, sums_ref) = refs[:-2], refs[-2:]
    n_frame = len(pieces)
    place = lax.axis_index("frame")
    rows = sums_ref.shape[0] // n_frame
    for step, piece in enumerate(pieces[::-1]):
        sums_ref[pl.ds(pl.multiple_of((place ^ step) * rows, rows), rows), :] = piece[...].astype(jnp.float32)
    series = [sums_ref[t * n_frame : (t + 1) * n_frame, :] for t in range(rows)]
    for t, sums in enumerate(deconvolved(series)):
        sums_ref[t * n_frame : (t + 1) * n_frame, :] = sums + pltpu.roll(sums, TILE // 2, 1)
    extra = jnp.where(lax.broadcasted_iota(jnp.int32, (8, TILE), 0) == 0, 1.0, 0.0)
    sums = [
        jnp.concatenate([sums_ref[pl.ds(block, rows, stride=n_frame), :], extra], axis=0) for block in range(n_frame)
    ]
    sums = jnp.concatenate(sums, axis=1)
    parts = []
    for _ in range(3):
        parts.append(sums.astype(jnp.bfloat16))
        sums = sums - parts[-1].astype(jnp.float32)
    totals = lax.dot_general(
        jnp.concatenate([weights_ref[...]] * 3, axis=1),
        jnp.concatenate(parts, axis=1),
        (((1,), (1,)), ((), ())),
        preferred_element_type=jnp.float32,
    )
    share = out_ref.shape[1]
    out_ref[...] = jnp.zeros_like(out_ref)
    for row in range(out_ref.shape[0]):
        out_ref[row, :, : rows + 8] = totals[row * share : (row + 1) * share]


def temporal_kernel(*refs, frames):
    pieces, (spikes_ref, in_ref) = refs[:-2], refs[-2:]
    place = lax.axis_index("frame")
    for step, piece in enumerate(pieces[::-1]):
        in_ref[place ^ step] = piece[...]
    total, rows_dev, columns = spikes_ref.shape
    positions = in_ref.shape[1] // frames
    for tile in range(columns // TILE):
        series = []
        for t in range(total):
            start = t % frames * positions + tile * rows_dev
            series.append(in_ref[t // frames, start : start + rows_dev, :].astype(jnp.float32))
        for t, spikes in enumerate(deconvolved(series)):
            spikes_ref[t, :, tile * TILE : (tile + 1) * TILE] = spikes.astype(spikes_ref.dtype)


def means_kernel(*refs):
    pieces, traces_ref = refs[:-1], refs[-1]
    frames = traces_ref.shape[1]
    total = pieces[0][...]
    for piece in pieces[1:]:
        total = total + piece[...]
    traces_ref[...] = total[:, :frames] / (TILE * total[:, frames : frames + 1])


def swapped(parts, axis):
    count, place = lax.axis_size(axis), lax.axis_index(axis)
    arrived = [lax.dynamic_index_in_dim(parts, place, 0, keepdims=False, allow_negative_indices=False)]
    for step in range(1, count):
        part = lax.dynamic_index_in_dim(parts, place ^ step, 0, keepdims=False, allow_negative_indices=False)
        arrived.append(lax.ppermute(part, axis, [(i, i ^ step) for i in range(count)]))
    return arrived


def spread_out(part, axis):
    count = lax.axis_size(axis)
    return [part] + [lax.ppermute(part, axis, [(i, i ^ step) for i in range(count)]) for step in range(1, count)]


def in_turn(*arrays):
    done = []
    for array in arrays:
        done = list(lax.optimization_barrier((*done, array)))
    return done


def by_halo(observed, kernels, band_kernel, masks):
    n_frame, n_row = lax.axis_size("frame"), lax.axis_size("row")
    frames, rows_dev, width = observed.shape
    components, _, tiles_dev = masks.shape
    positions = rows_dev * tiles_dev
    share = components // (n_frame * n_row)
    span = rows_dev + 2 * MARGIN
    smem, vmem = pl.BlockSpec(memory_space=pltpu.SMEM), pl.BlockSpec(memory_space=pltpu.VMEM)

    def call(kernel, name, in_specs, out_shape, scratch=(), cost=1000):
        many = isinstance(out_shape, tuple)
        return pl.pallas_call(
            kernel,
            name=name,
            out_shape=out_shape,
            in_specs=in_specs,
            out_specs=(vmem,) * len(out_shape) if many else vmem,
            scratch_shapes=scratch,
            compiler_params=pltpu.CompilerParams(vmem_limit_bytes=16 << 20),
            cost_estimate=pl.CostEstimate(flops=cost, bytes_accessed=cost, transcendentals=0),
        )

    def array(*shape, dtype=jnp.float32):
        return jax.ShapeDtypeStruct(shape, dtype)

    packed = array(frames * (NEAR + FAR), width)
    inner, outer, own = call(halo_kernel, "halo", [vmem], (packed, packed, array(*observed.shape)))(observed)
    inner_swap = [(i, i ^ 1) for i in range(n_row)]
    outer_swap = []
    for f in range(n_frame):
        for i in range(n_row):
            there = (f ^ 1, i) if i in (0, n_row - 1) else (f, (i - 1 ^ 1) + 1)
            outer_swap.append((f * n_row + i, there[0] * n_row + there[1]))
    inner = lax.ppermute(inner.astype(jnp.float16), "row", inner_swap)
    outer = lax.ppermute(outer.astype(jnp.float16), ("frame", "row"), outer_swap)
    inner, outer = in_turn(inner, outer)
    taps, back = call(
        functools.partial(taps_kernel, height=rows_dev * n_row, rows_dev=rows_dev),
        "taps",
        [smem, smem],
        (array(len(SIDES), span, TILE),) * 2,
        [pltpu.VMEM((len(SIDES), span + 2 * PAD, TILE), jnp.float32)],
    )(band_kernel, kernels)
    feet = call(feet_kernel, "feet", [vmem], array(n_frame, n_row * share // 2, TILE, dtype=jnp.bfloat16))(
        masks.transpose(1, 2, 0)
    )
    row = lax.axis_index("row")
    even = row % 2 == 0
    alone = (row == 0) | (row == n_row - 1)
    inner, outer = inner.astype(jnp.float32), jnp.where(alone, 1.0, outer.astype(jnp.float32))
    top, bottom = jnp.where(even, outer, inner), jnp.where(even, inner, outer)
    weights = call(weights_kernel, "weights", [vmem] * n_frame, array(n_row * share, n_frame * TILE, dtype=jnp.bfloat16))(
        *swapped(feet, "frame")
    )
    taps, weights = lax.optimization_barrier((taps, weights))
    blocks, sides = call(
        restore_kernel,
        "restore",
        [vmem] * 5,
        (
            array(n_frame, frames * positions, TILE, dtype=jnp.bfloat16),
            array(frames * n_frame, TILE, dtype=jnp.bfloat16),
        ),
        [pltpu.VMEM((frames, span + 2 * PAD, TILE), jnp.float32)] * 3,
    )(taps, back, own, top, bottom)
    own_sums, *sides = spread_out(sides, "frame")
    sides[1], sides[2], sides[0] = in_turn(sides[1], sides[2], sides[0])
    pieces = swapped(blocks, "frame")
    partial = call(
        partial_kernel,
        "partial",
        [vmem] * (n_frame + 1),
        array(n_row, share, TILE),
        [pltpu.VMEM((n_frame * frames * n_frame, TILE), jnp.float32)],
    )(weights, *sides[::-1], own_sums)
    shares = swapped(partial, "row")
    spikes = call(
        functools.partial(temporal_kernel, frames=frames),
        "temporal",
        [vmem] * n_frame,
        array(n_frame * frames, rows_dev, tiles_dev * TILE, dtype=jnp.bfloat16),
        [pltpu.VMEM((n_frame, frames * positions, TILE), jnp.bfloat16)],
    )(*pieces[::-1])
    spikes, *shares = in_turn(spikes, *shares[::-1])
    traces = call(means_kernel, "means", [vmem] * n_row, array(share, n_frame * frames))(*shares)
    return (spikes, traces)


def fits(mesh, observed, masks):
    frames_dev = observed.shape[0] // mesh.shape["frame"]
    rows_dev = masks.shape[1] // (mesh.shape["groups"] * mesh.shape["row"])
    tiles_dev = masks.shape[2] // mesh.shape["frame"]
    places = mesh.shape["frame"] * mesh.shape["row"]
    return (
        frames_dev == mesh.shape["frame"] == mesh.shape["row"] == 4
        and 2 * rows_dev * tiles_dev == TILE
        and rows_dev == 16
        and masks.shape[0] // places == 16
    )


def solution(mesh):
    in_specs = (
        P("frame", ("groups", "row"), None),
        P(),
        P("groups"),
        P(None, ("groups", "row"), "frame"),
    )
    out_specs = (P(None, ("groups", "row"), "frame"), P(("groups", "frame", "row"), None))

    def whole(observed, kernels, band_kernel, masks):
        body = by_halo if fits(mesh, observed, masks) else local
        mapped = jax.shard_map(body, mesh=mesh, in_specs=in_specs, out_specs=out_specs, check_vma=False)
        return mapped(observed, kernels, band_kernel, masks)

    return whole
```

```python
import functools

import jax
import jax.numpy as jnp
from jax import lax
from jax.experimental import pallas as pl
from jax.experimental.pallas import tpu as pltpu
from jax.sharding import PartitionSpec as P

TILE = 128
BAND = 8
ITERS = 3
TAPS = 5
NEAR, FAR = 8, 4
MARGIN = 2 * BAND
PAD = BAND
STEPS = (((6, 46), (8, 40)), ((10, 42), (12, 36)), ((14, 38), (16, 32)))
SIDES = (0, 1, 3, 4)


SMOOTHING = 1024.0
DECAY_RATE = 0.9


def padded_2(cells, sides, width):
    for axis, dim in sides:
        count = lax.axis_size(axis)
        ends = count - 1
        head = lax.slice_in_dim(cells, 0, width, axis=dim)
        tail = lax.slice_in_dim(cells, cells.shape[dim] - width, cells.shape[dim], axis=dim)
        cells = jnp.concatenate(
            [
                lax.ppermute(tail, axis, [(i, (i + 1) % count) for i in range(ends)]),
                cells,
                lax.ppermute(head, axis, [((i + 1) % count, i) for i in range(ends)]),
            ],
            axis=dim,
        )
    return cells


def tap_rows(tap_table, band_kernel, first_row, row_count, height):
    row_ids = jnp.clip(first_row + jnp.arange(row_count), 0, height - 1)
    row_bands = row_ids // BAND
    band_slots = jnp.arange(band_kernel.shape[0])
    kernel_ids = jnp.sum(
        jnp.where(row_bands[:, None] == band_slots[None, :], band_kernel[None, :], 0), axis=1
    )
    kernel_slots = jnp.arange(tap_table.shape[0])
    picked = jnp.where(
        kernel_ids[:, None, None] == kernel_slots[None, :, None], tap_table[None, :, :], 0.0
    )
    return jnp.sum(picked, axis=1)


def blur_rows(padded, row_taps, row_count):
    summed = row_taps[:, 0][None, :, None] * padded[:, 0:row_count]
    for offset in range(1, 5):
        summed = (
            summed + row_taps[:, offset][None, :, None] * padded[:, offset : offset + row_count]
        )
    return summed


def back_rows(padded_quotient, outer_taps, row_count):
    summed = outer_taps[4 : 4 + row_count, 0][None, :, None] * padded_quotient[:, 4 : 4 + row_count]
    for offset in range(1, 5):
        start = 4 - offset
        summed = (
            summed
            + outer_taps[start : start + row_count, offset][None, :, None]
            * padded_quotient[:, start : start + row_count]
        )
    return summed


def temporal(series_block):
    frame_total, item_count, columns = series_block.shape
    values = series_block.astype(jnp.float32).reshape(frame_total, item_count * columns)
    frame_ids = jnp.arange(frame_total)
    at_ends = (frame_ids == 0) | (frame_ids == frame_total - 1)
    middle = (1.0 + SMOOTHING * jnp.where(at_ends, 1.0, 2.0)).astype(jnp.float32)
    sub_diag = jnp.where(frame_ids == 0, 0.0, -SMOOTHING).astype(jnp.float32)
    super_diag = jnp.where(frame_ids == frame_total - 1, 0.0, -SMOOTHING).astype(jnp.float32)
    baseline = lax.linalg.tridiagonal_solve(sub_diag, middle, super_diag, values)
    detrended = values - baseline
    earlier = jnp.concatenate(
        [jnp.zeros((1, values.shape[1]), jnp.float32), detrended[:-1]], axis=0
    )
    result = (detrended - DECAY_RATE * earlier).astype(jnp.bfloat16)
    return result.reshape(frame_total, item_count, columns)


def local(observed, kernels, band_kernel, masks):
    frames_dev, rows_dev, row_pixels = observed.shape
    height = rows_dev * lax.axis_size("row")
    tap_table = kernels / jnp.sum(kernels, axis=1, keepdims=True)
    first_row = lax.axis_index("row") * rows_dev
    own_taps = tap_rows(tap_table, band_kernel, first_row, rows_dev, height)
    outer_taps = tap_rows(tap_table, band_kernel, first_row - 2, rows_dev + 4, height)
    current = observed
    for iteration in range(ITERS):
        padded = padded_2(current, (("row", 1),), 2)
        blurred = blur_rows(padded, own_taps, rows_dev)
        quotient = observed / blurred
        padded_quotient = padded_2(quotient, (("row", 1),), 2)
        current = current * back_rows(padded_quotient, outer_taps, rows_dev)
    estimate = current.astype(jnp.bfloat16)
    spikes = temporal(lax.all_to_all(estimate, "frame", split_axis=2, concat_axis=0, tiled=True))
    frames_all, _, columns = spikes.shape
    tile_count = columns // TILE
    tile_sums = jnp.sum(
        spikes.reshape(frames_all, rows_dev * tile_count, TILE).astype(jnp.float32), axis=2
    )
    weights = masks.astype(jnp.float32).reshape(masks.shape[0], rows_dev * tile_count)
    local_sums = lax.dot_general(
        weights, tile_sums, (((1,), (1,)), ((), ())), precision=lax.Precision.HIGHEST
    )
    counts = jnp.sum(weights, axis=1)
    trace_sums, totals = (
        lax.psum_scatter(local_sums, ("frame", "row"), scatter_dimension=0, tiled=True),
        lax.psum_scatter(counts, ("frame", "row"), scatter_dimension=0, tiled=True),
    )
    traces = trace_sums / (TILE * totals[:, None])
    return (spikes, traces)


def pack(observed_ref, out_ref, low):
    frames = observed_ref.shape[0]
    for frame in range(frames):
        near = frame * NEAR
        far = frames * NEAR + frame * FAR
        bottom, top = observed_ref[frame, -NEAR:, :], observed_ref[frame, :NEAR, :]
        out_ref[near : near + NEAR, :] = jnp.where(low, bottom, top)
        bottom, top = observed_ref[frame, -NEAR - FAR : -NEAR, :], observed_ref[frame, NEAR : NEAR + FAR, :]
        out_ref[far : far + FAR, :] = jnp.where(low, bottom, top)


def inner_kernel(observed_ref, inner_ref, own_ref):
    pack(observed_ref, inner_ref, lax.axis_index("row") % 2 == 0)
    own_ref[...] = observed_ref[...]


def outer_kernel(own_ref, outer_ref):
    pack(own_ref, outer_ref, lax.axis_index("row") % 2 == 1)


def taps_kernel(band_ref, kernels_ref, taps_ref, back_ref, pad_ref, *, height, rows_dev):
    span = rows_dev + 2 * MARGIN
    first_row = lax.axis_index("row") * rows_dev - MARGIN
    row_ids = lax.broadcasted_iota(jnp.int32, (BAND, TILE), 0)
    pad_ref[...] = jnp.zeros_like(pad_ref)
    for band in range(span // BAND):
        row = first_row + band * BAND
        inside = (row >= 0) & (row < height)
        kernel = band_ref[jnp.clip(row, 0, height - 1) // BAND]
        centre = jnp.full((BAND, TILE), kernels_ref[kernel, TAPS // 2], jnp.float32)
        start = band * BAND
        for slot, tap in enumerate(SIDES):
            weight = jnp.full((BAND, TILE), kernels_ref[kernel, tap], jnp.float32) / centre
            target = row_ids + (row + tap - TAPS // 2)
            weight = jnp.where(inside & (target >= 0) & (target < height), weight, 0.0)
            taps_ref[slot, start : start + BAND, :] = weight
            pad_ref[slot, BAND + start : 2 * BAND + start, :] = weight
    for slot, tap in enumerate(SIDES):
        start = BAND + TAPS // 2 - tap
        back_ref[slot] = pad_ref[slot, start : start + span, :]


def feet_kernel(masks_ref, feet_ref):
    rows_dev = masks_ref.shape[0]
    flat = jnp.concatenate([masks_ref[row].astype(jnp.float32) for row in range(rows_dev)], axis=0)
    positions = flat.shape[0]
    both = jnp.concatenate([flat, flat], axis=0).T
    half = feet_ref.shape[1]
    left = lax.broadcasted_iota(jnp.int32, (half, TILE), 1) < positions
    for block in range(feet_ref.shape[0]):
        start = 2 * block * half
        halves = jnp.where(left, both[start : start + half], both[start + half : start + 2 * half])
        feet_ref[block] = halves.astype(jnp.bfloat16)


def restore_kernel(
    taps_ref, back_ref, feet_ref, own_ref, top_ref, bottom_ref, out_ref, side_ref, image_ref, current_ref, quotient_ref
):
    n_frame = out_ref.shape[0]
    frames, rows_dev, width = own_ref.shape
    tiles_dev = width // (n_frame * TILE)
    positions = rows_dev * tiles_dev
    for ref in (image_ref, current_ref, quotient_ref):
        ref[...] = jnp.ones_like(ref)

    def columns_step(step, carry):
        columns = pl.ds(pl.multiple_of(step * TILE, TILE), TILE)
        for frame in range(frames):
            near, far = frame * NEAR, frames * NEAR + frame * FAR
            start, stop = PAD + MARGIN, PAD + MARGIN + rows_dev
            image_ref[frame, start - NEAR - FAR : start - NEAR, :] = top_ref[far : far + FAR, columns]
            image_ref[frame, start - NEAR : start, :] = top_ref[near : near + NEAR, columns]
            image_ref[frame, stop : stop + NEAR, :] = bottom_ref[near : near + NEAR, columns]
            image_ref[frame, stop + NEAR : stop + NEAR + FAR, :] = bottom_ref[far : far + FAR, columns]
            image_ref[frame, start:stop, :] = own_ref[frame, :, columns]
        source_ref = image_ref
        for (first, last), (back_first, back_last) in STEPS:
            for row in range(first, last, BAND):
                weights = [taps_ref[slot, row : row + BAND, :] for slot in range(len(SIDES))]
                for frame in range(frames):
                    rows = slice(PAD + row, PAD + row + BAND)
                    terms = []
                    for weight, tap in zip(weights, SIDES):
                        start = PAD + row + tap - TAPS // 2
                        terms.append(weight * source_ref[frame, start : start + BAND, :])
                    blurred = source_ref[frame, rows, :] + ((terms[0] + terms[1]) + (terms[2] + terms[3]))
                    quotient_ref[frame, rows, :] = image_ref[frame, rows, :] / blurred
            for row in range(back_first, back_last, BAND):
                weights = [back_ref[slot, row : row + BAND, :] for slot in range(len(SIDES))]
                for frame in range(frames):
                    rows = slice(PAD + row, PAD + row + BAND)
                    terms = []
                    for weight, tap in zip(weights, SIDES):
                        start = PAD + row - tap + TAPS // 2
                        terms.append(weight * quotient_ref[frame, start : start + BAND, :])
                    spread = quotient_ref[frame, rows, :] + ((terms[0] + terms[1]) + (terms[2] + terms[3]))
                    current_ref[frame, rows, :] = source_ref[frame, rows, :] * spread
            source_ref = current_ref
        first = pl.multiple_of(lax.rem(step, tiles_dev) * rows_dev, rows_dev)
        for frame in range(frames):
            estimate = current_ref[frame, PAD + MARGIN : PAD + MARGIN + rows_dev, :].astype(jnp.bfloat16)
            start = pl.multiple_of(first + frame * positions, rows_dev)
            out_ref[step // tiles_dev, pl.ds(start, rows_dev), :] = estimate
        return carry

    lax.fori_loop(0, n_frame * tiles_dev, columns_step, 0, unroll=2)
    lane_tiles = lax.broadcasted_iota(jnp.int32, (TILE, TILE), 1) % tiles_dev
    gathered = jnp.zeros((frames * n_frame * rows_dev, TILE), jnp.float32)
    for tile in range(tiles_dev):
        pieces = []
        for frame in range(frames):
            start = frame * positions + tile * rows_dev
            pieces += [out_ref[block, start : start + rows_dev, :] for block in range(n_frame)]
        picked = jnp.where(lane_tiles == tile, 1.0, 0.0).astype(jnp.bfloat16)
        gathered = gathered + jnp.dot(jnp.concatenate(pieces, axis=0), picked, preferred_element_type=jnp.float32)
    lanes = lax.broadcasted_iota(jnp.int32, (rows_dev, TILE), 1)
    here = lanes % positions // tiles_dev == lax.broadcasted_iota(jnp.int32, (rows_dev, TILE), 0)
    sums = []
    for place in range(frames * n_frame):
        part = jnp.where(here, gathered[place * rows_dev : (place + 1) * rows_dev], 0.0)
        sums.append(jnp.sum(part, axis=0, keepdims=True))
    sums = jnp.concatenate(sums, axis=0)
    high = sums.astype(jnp.bfloat16).astype(jnp.float32)
    split = jnp.where(lax.broadcasted_iota(jnp.int32, sums.shape, 1) < positions, high, sums - high).astype(jnp.bfloat16)
    for block in range(n_frame):
        side_ref[block, : split.shape[0], :] = split
        side_ref[block, split.shape[0] :, :] = feet_ref[block]


def deconvolved(series):
    total = len(series)
    factors = []
    for step in range(total):
        middle = 1.0 + SMOOTHING * (1.0 if step in (0, total - 1) else 2.0)
        if step:
            middle -= SMOOTHING * SMOOTHING * factors[-1]
        factors.append(1.0 / middle)
    scaled = [cells * factor for cells, factor in zip(series, factors)]
    forward = [scaled[0]]
    for step in range(1, total):
        forward.append(scaled[step] + (SMOOTHING * factors[step]) * forward[step - 1])
    baseline = [None] * total
    baseline[total - 1] = forward[total - 1]
    for step in range(total - 2, -1, -1):
        baseline[step] = forward[step] + (SMOOTHING * factors[step]) * baseline[step + 1]
    result, earlier = [], None
    for step in range(total):
        detrended = series[step] - baseline[step]
        result.append(detrended if earlier is None else detrended - DECAY_RATE * earlier)
        earlier = detrended
    return result


def partial_kernel(*refs, positions):
    pieces, (out_ref, sums_ref, feet_ref) = refs[:-3], refs[-3:]
    n_frame = len(pieces)
    place = lax.axis_index("frame")
    rows = sums_ref.shape[0] // n_frame
    half = feet_ref.shape[1]
    for step, piece in enumerate(pieces[::-1]):
        sums_ref[pl.ds(pl.multiple_of((place ^ step) * rows, rows), rows), :] = piece[:rows, :].astype(jnp.float32)
        feet_ref[place ^ step] = piece[rows:, :].astype(jnp.float32)
    series = [sums_ref[t * n_frame : (t + 1) * n_frame, :] for t in range(rows)]
    for t, sums in enumerate(deconvolved(series)):
        sums_ref[t * n_frame : (t + 1) * n_frame, :] = sums + pltpu.roll(sums, TILE // 2, 1)
    left = lax.broadcasted_iota(jnp.int32, (half, TILE), 1) < positions
    weights, sums = [], []
    extra = jnp.where(lax.broadcasted_iota(jnp.int32, (8, TILE), 0) == 0, 1.0, 0.0)
    for block in range(n_frame):
        feet = feet_ref[block]
        weights.append(jnp.concatenate([jnp.where(left, feet, 0.0), jnp.where(left, 0.0, feet)], axis=0))
        sums.append(jnp.concatenate([sums_ref[pl.ds(block, rows, stride=n_frame), :], extra], axis=0))
    sums = jnp.concatenate(sums, axis=1)
    parts = []
    for _ in range(2):
        parts.append(sums.astype(jnp.bfloat16))
        sums = sums - parts[-1].astype(jnp.float32)
    totals = lax.dot_general(
        jnp.concatenate(weights * 2, axis=1).astype(jnp.bfloat16),
        jnp.concatenate(parts, axis=1),
        (((1,), (1,)), ((), ())),
        preferred_element_type=jnp.float32,
    )
    share = out_ref.shape[1]
    out_ref[...] = jnp.zeros_like(out_ref)
    for row in range(out_ref.shape[0]):
        out_ref[row, :, : rows + 8] = totals[row * share : (row + 1) * share]


def temporal_kernel(*refs, frames):
    pieces, (spikes_ref, in_ref) = refs[:-2], refs[-2:]
    place = lax.axis_index("frame")
    for step, piece in enumerate(pieces[::-1]):
        in_ref[place ^ step] = piece[...]
    total, rows_dev, columns = spikes_ref.shape
    positions = in_ref.shape[1] // frames
    for tile in range(columns // TILE):
        series = []
        for t in range(total):
            start = t % frames * positions + tile * rows_dev
            series.append(in_ref[t // frames, start : start + rows_dev, :].astype(jnp.float32))
        for t, spikes in enumerate(deconvolved(series)):
            spikes_ref[t, :, tile * TILE : (tile + 1) * TILE] = spikes.astype(spikes_ref.dtype)


def means_kernel(*refs):
    pieces, traces_ref = refs[:-1], refs[-1]
    frames = traces_ref.shape[1]
    total = pieces[0][...]
    for piece in pieces[1:]:
        total = total + piece[...]
    traces_ref[...] = total[:, :frames] / (TILE * total[:, frames : frames + 1])


def swapped(parts, axis):
    count, place = lax.axis_size(axis), lax.axis_index(axis)
    arrived = [lax.dynamic_index_in_dim(parts, place, 0, keepdims=False, allow_negative_indices=False)]
    for step in range(1, count):
        part = lax.dynamic_index_in_dim(parts, place ^ step, 0, keepdims=False, allow_negative_indices=False)
        arrived.append(lax.ppermute(part, axis, [(i, i ^ step) for i in range(count)]))
    return arrived


def in_turn(*arrays):
    done = []
    for array in arrays:
        done = list(lax.optimization_barrier((*done, array)))
    return done


def by_halo(observed, kernels, band_kernel, masks):
    n_frame, n_row = lax.axis_size("frame"), lax.axis_size("row")
    frames, rows_dev, width = observed.shape
    components, _, tiles_dev = masks.shape
    positions = rows_dev * tiles_dev
    share = components // (n_frame * n_row)
    span = rows_dev + 2 * MARGIN
    smem, vmem = pl.BlockSpec(memory_space=pltpu.SMEM), pl.BlockSpec(memory_space=pltpu.VMEM)

    def call(kernel, name, in_specs, out_shape, scratch=(), cost=1000):
        many = isinstance(out_shape, tuple)
        return pl.pallas_call(
            kernel,
            name=name,
            out_shape=out_shape,
            in_specs=in_specs,
            out_specs=(vmem,) * len(out_shape) if many else vmem,
            scratch_shapes=scratch,
            compiler_params=pltpu.CompilerParams(vmem_limit_bytes=16 << 20),
            cost_estimate=pl.CostEstimate(flops=cost, bytes_accessed=cost, transcendentals=0),
        )

    def array(*shape, dtype=jnp.float32):
        return jax.ShapeDtypeStruct(shape, dtype)

    packed = array(frames * (NEAR + FAR), width)
    inner, own = call(inner_kernel, "halo", [vmem], (packed, array(*observed.shape)))(observed)
    inner_swap = [(i, i ^ 1) for i in range(n_row)]
    outer_swap = []
    for f in range(n_frame):
        for i in range(n_row):
            there = (f ^ 1, i) if i in (0, n_row - 1) else (f, (i - 1 ^ 1) + 1)
            outer_swap.append((f * n_row + i, there[0] * n_row + there[1]))
    inner = inner.astype(jnp.float16)
    own, inner = lax.optimization_barrier((own, inner))
    inner = lax.ppermute(inner, "row", inner_swap)
    outer = call(outer_kernel, "outer", [vmem], packed)(own)
    outer = lax.ppermute(outer.astype(jnp.float16), ("frame", "row"), outer_swap)
    inner, outer = in_turn(inner, outer)
    taps, back = call(
        functools.partial(taps_kernel, height=rows_dev * n_row, rows_dev=rows_dev),
        "taps",
        [smem, smem],
        (array(len(SIDES), span, TILE),) * 2,
        [pltpu.VMEM((len(SIDES), span + 2 * PAD, TILE), jnp.float32)],
    )(band_kernel, kernels)
    feet = call(feet_kernel, "feet", [vmem], array(n_frame, n_row * share // 2, TILE, dtype=jnp.bfloat16))(
        masks.transpose(1, 2, 0)
    )
    row = lax.axis_index("row")
    even = row % 2 == 0
    alone = (row == 0) | (row == n_row - 1)
    inner, outer = inner.astype(jnp.float32), jnp.where(alone, 1.0, outer.astype(jnp.float32))
    top, bottom = jnp.where(even, outer, inner), jnp.where(even, inner, outer)
    side_rows = frames * n_frame + n_row * share // 2
    blocks, sides = call(
        restore_kernel,
        "restore",
        [vmem] * 6,
        (
            array(n_frame, frames * positions, TILE, dtype=jnp.bfloat16),
            array(n_frame, side_rows, TILE, dtype=jnp.bfloat16),
        ),
        [pltpu.VMEM((frames, span + 2 * PAD, TILE), jnp.float32)] * 3,
    )(taps, back, feet, own, top, bottom)
    sides = swapped(sides, "frame")
    pieces = swapped(blocks, "frame")
    partial = call(
        functools.partial(partial_kernel, positions=positions),
        "partial",
        [vmem] * n_frame,
        array(n_row, share, TILE),
        [
            pltpu.VMEM((n_frame * frames * n_frame, TILE), jnp.float32),
            pltpu.VMEM((n_frame, n_row * share // 2, TILE), jnp.float32),
        ],
    )(*sides[::-1])
    shares = swapped(partial, "row")
    spikes = call(
        functools.partial(temporal_kernel, frames=frames),
        "temporal",
        [vmem] * n_frame,
        array(n_frame * frames, rows_dev, tiles_dev * TILE, dtype=jnp.bfloat16),
        [pltpu.VMEM((n_frame, frames * positions, TILE), jnp.bfloat16)],
    )(*pieces[::-1])
    spikes, *shares = in_turn(spikes, *shares[::-1])
    traces = call(means_kernel, "means", [vmem] * n_row, array(share, n_frame * frames))(*shares)
    return (spikes, traces)


def fits(mesh, observed, masks):
    frames_dev = observed.shape[0] // mesh.shape["frame"]
    rows_dev = masks.shape[1] // (mesh.shape["groups"] * mesh.shape["row"])
    tiles_dev = masks.shape[2] // mesh.shape["frame"]
    places = mesh.shape["frame"] * mesh.shape["row"]
    return (
        frames_dev == mesh.shape["frame"] == mesh.shape["row"] == 4
        and 2 * rows_dev * tiles_dev == TILE
        and rows_dev == 16
        and masks.shape[0] // places == 16
    )


def solution(mesh):
    in_specs = (
        P("frame", ("groups", "row"), None),
        P(),
        P("groups"),
        P(None, ("groups", "row"), "frame"),
    )
    out_specs = (P(None, ("groups", "row"), "frame"), P(("groups", "frame", "row"), None))

    def whole(observed, kernels, band_kernel, masks):
        body = by_halo if fits(mesh, observed, masks) else local
        mapped = jax.shard_map(body, mesh=mesh, in_specs=in_specs, out_specs=out_specs, check_vma=False)
        return mapped(observed, kernels, band_kernel, masks)

    return whole
```

```python
import functools

import jax
import jax.numpy as jnp
from jax import lax
from jax.experimental import pallas as pl
from jax.experimental.pallas import tpu as pltpu
from jax.sharding import PartitionSpec as P

TILE = 128
BAND = 8
ITERS = 3
TAPS = 5
NEAR, FAR = 8, 4
MARGIN = 2 * BAND
PAD = BAND
STEPS = (((6, 46), (8, 40)), ((10, 42), (12, 36)), ((14, 38), (16, 32)))
SIDES = (0, 1, 3, 4)


SMOOTHING = 1024.0
DECAY_RATE = 0.9


def padded_2(cells, sides, width):
    for axis, dim in sides:
        count = lax.axis_size(axis)
        ends = count - 1
        head = lax.slice_in_dim(cells, 0, width, axis=dim)
        tail = lax.slice_in_dim(cells, cells.shape[dim] - width, cells.shape[dim], axis=dim)
        cells = jnp.concatenate(
            [
                lax.ppermute(tail, axis, [(i, (i + 1) % count) for i in range(ends)]),
                cells,
                lax.ppermute(head, axis, [((i + 1) % count, i) for i in range(ends)]),
            ],
            axis=dim,
        )
    return cells


def tap_rows(tap_table, band_kernel, first_row, row_count, height):
    row_ids = jnp.clip(first_row + jnp.arange(row_count), 0, height - 1)
    row_bands = row_ids // BAND
    band_slots = jnp.arange(band_kernel.shape[0])
    kernel_ids = jnp.sum(
        jnp.where(row_bands[:, None] == band_slots[None, :], band_kernel[None, :], 0), axis=1
    )
    kernel_slots = jnp.arange(tap_table.shape[0])
    picked = jnp.where(
        kernel_ids[:, None, None] == kernel_slots[None, :, None], tap_table[None, :, :], 0.0
    )
    return jnp.sum(picked, axis=1)


def blur_rows(padded, row_taps, row_count):
    summed = row_taps[:, 0][None, :, None] * padded[:, 0:row_count]
    for offset in range(1, 5):
        summed = (
            summed + row_taps[:, offset][None, :, None] * padded[:, offset : offset + row_count]
        )
    return summed


def back_rows(padded_quotient, outer_taps, row_count):
    summed = outer_taps[4 : 4 + row_count, 0][None, :, None] * padded_quotient[:, 4 : 4 + row_count]
    for offset in range(1, 5):
        start = 4 - offset
        summed = (
            summed
            + outer_taps[start : start + row_count, offset][None, :, None]
            * padded_quotient[:, start : start + row_count]
        )
    return summed


def temporal(series_block):
    frame_total, item_count, columns = series_block.shape
    values = series_block.astype(jnp.float32).reshape(frame_total, item_count * columns)
    frame_ids = jnp.arange(frame_total)
    at_ends = (frame_ids == 0) | (frame_ids == frame_total - 1)
    middle = (1.0 + SMOOTHING * jnp.where(at_ends, 1.0, 2.0)).astype(jnp.float32)
    sub_diag = jnp.where(frame_ids == 0, 0.0, -SMOOTHING).astype(jnp.float32)
    super_diag = jnp.where(frame_ids == frame_total - 1, 0.0, -SMOOTHING).astype(jnp.float32)
    baseline = lax.linalg.tridiagonal_solve(sub_diag, middle, super_diag, values)
    detrended = values - baseline
    earlier = jnp.concatenate(
        [jnp.zeros((1, values.shape[1]), jnp.float32), detrended[:-1]], axis=0
    )
    result = (detrended - DECAY_RATE * earlier).astype(jnp.bfloat16)
    return result.reshape(frame_total, item_count, columns)


def local(observed, kernels, band_kernel, masks):
    frames_dev, rows_dev, row_pixels = observed.shape
    height = rows_dev * lax.axis_size("row")
    tap_table = kernels / jnp.sum(kernels, axis=1, keepdims=True)
    first_row = lax.axis_index("row") * rows_dev
    own_taps = tap_rows(tap_table, band_kernel, first_row, rows_dev, height)
    outer_taps = tap_rows(tap_table, band_kernel, first_row - 2, rows_dev + 4, height)
    current = observed
    for iteration in range(ITERS):
        padded = padded_2(current, (("row", 1),), 2)
        blurred = blur_rows(padded, own_taps, rows_dev)
        quotient = observed / blurred
        padded_quotient = padded_2(quotient, (("row", 1),), 2)
        current = current * back_rows(padded_quotient, outer_taps, rows_dev)
    estimate = current.astype(jnp.bfloat16)
    spikes = temporal(lax.all_to_all(estimate, "frame", split_axis=2, concat_axis=0, tiled=True))
    frames_all, _, columns = spikes.shape
    tile_count = columns // TILE
    tile_sums = jnp.sum(
        spikes.reshape(frames_all, rows_dev * tile_count, TILE).astype(jnp.float32), axis=2
    )
    weights = masks.astype(jnp.float32).reshape(masks.shape[0], rows_dev * tile_count)
    local_sums = lax.dot_general(
        weights, tile_sums, (((1,), (1,)), ((), ())), precision=lax.Precision.HIGHEST
    )
    counts = jnp.sum(weights, axis=1)
    trace_sums, totals = (
        lax.psum_scatter(local_sums, ("frame", "row"), scatter_dimension=0, tiled=True),
        lax.psum_scatter(counts, ("frame", "row"), scatter_dimension=0, tiled=True),
    )
    traces = trace_sums / (TILE * totals[:, None])
    return (spikes, traces)


def halo_kernel(observed_ref, inner_ref, outer_ref, own_ref):
    even = lax.axis_index("row") % 2 == 0
    frames = observed_ref.shape[0]
    own_ref[...] = observed_ref[...]
    for frame in range(frames):
        near = frame * NEAR
        far = frames * NEAR + frame * FAR
        bottom, top = observed_ref[frame, -NEAR:, :], observed_ref[frame, :NEAR, :]
        inner_ref[near : near + NEAR, :] = jnp.where(even, bottom, top)
        outer_ref[near : near + NEAR, :] = jnp.where(even, top, bottom)
        bottom, top = observed_ref[frame, -NEAR - FAR : -NEAR, :], observed_ref[frame, NEAR : NEAR + FAR, :]
        inner_ref[far : far + FAR, :] = jnp.where(even, bottom, top)
        outer_ref[far : far + FAR, :] = jnp.where(even, top, bottom)


def taps_kernel(band_ref, kernels_ref, taps_ref, back_ref, pad_ref, *, height, rows_dev):
    span = rows_dev + 2 * MARGIN
    first_row = lax.axis_index("row") * rows_dev - MARGIN
    row_ids = lax.broadcasted_iota(jnp.int32, (BAND, TILE), 0)
    pad_ref[...] = jnp.zeros_like(pad_ref)
    for band in range(span // BAND):
        row = first_row + band * BAND
        inside = (row >= 0) & (row < height)
        kernel = band_ref[jnp.clip(row, 0, height - 1) // BAND]
        centre = jnp.full((BAND, TILE), kernels_ref[kernel, TAPS // 2], jnp.float32)
        start = band * BAND
        for slot, tap in enumerate(SIDES):
            weight = jnp.full((BAND, TILE), kernels_ref[kernel, tap], jnp.float32) / centre
            target = row_ids + (row + tap - TAPS // 2)
            weight = jnp.where(inside & (target >= 0) & (target < height), weight, 0.0)
            taps_ref[slot, start : start + BAND, :] = weight
            pad_ref[slot, BAND + start : 2 * BAND + start, :] = weight
    for slot, tap in enumerate(SIDES):
        start = BAND + TAPS // 2 - tap
        back_ref[slot] = pad_ref[slot, start : start + span, :]


def feet_kernel(masks_ref, feet_ref):
    rows_dev = masks_ref.shape[0]
    flat = jnp.concatenate([masks_ref[row].astype(jnp.float32) for row in range(rows_dev)], axis=0)
    positions = flat.shape[0]
    both = jnp.concatenate([flat, flat], axis=0).T
    half = feet_ref.shape[1]
    left = lax.broadcasted_iota(jnp.int32, (half, TILE), 1) < positions
    for block in range(feet_ref.shape[0]):
        start = 2 * block * half
        halves = jnp.where(left, both[start : start + half], both[start + half : start + 2 * half])
        feet_ref[block] = halves.astype(jnp.bfloat16)


def restore_kernel(
    taps_ref, back_ref, feet_ref, own_ref, top_ref, bottom_ref, out_ref, side_ref, image_ref, current_ref, quotient_ref
):
    n_frame = out_ref.shape[0]
    frames, rows_dev, width = own_ref.shape
    tiles_dev = width // (n_frame * TILE)
    positions = rows_dev * tiles_dev
    for ref in (image_ref, current_ref, quotient_ref):
        ref[...] = jnp.ones_like(ref)

    def columns_step(step, carry):
        columns = pl.ds(pl.multiple_of(step * TILE, TILE), TILE)
        for frame in range(frames):
            near, far = frame * NEAR, frames * NEAR + frame * FAR
            start, stop = PAD + MARGIN, PAD + MARGIN + rows_dev
            image_ref[frame, start - NEAR - FAR : start - NEAR, :] = top_ref[far : far + FAR, columns]
            image_ref[frame, start - NEAR : start, :] = top_ref[near : near + NEAR, columns]
            image_ref[frame, stop : stop + NEAR, :] = bottom_ref[near : near + NEAR, columns]
            image_ref[frame, stop + NEAR : stop + NEAR + FAR, :] = bottom_ref[far : far + FAR, columns]
            image_ref[frame, start:stop, :] = own_ref[frame, :, columns]
        source_ref = image_ref
        for (first, last), (back_first, back_last) in STEPS:
            for row in range(first, last, BAND):
                weights = [taps_ref[slot, row : row + BAND, :] for slot in range(len(SIDES))]
                for frame in range(frames):
                    rows = slice(PAD + row, PAD + row + BAND)
                    terms = []
                    for weight, tap in zip(weights, SIDES):
                        start = PAD + row + tap - TAPS // 2
                        terms.append(weight * source_ref[frame, start : start + BAND, :])
                    blurred = source_ref[frame, rows, :] + ((terms[0] + terms[1]) + (terms[2] + terms[3]))
                    quotient_ref[frame, rows, :] = image_ref[frame, rows, :] / blurred
            for row in range(back_first, back_last, BAND):
                weights = [back_ref[slot, row : row + BAND, :] for slot in range(len(SIDES))]
                for frame in range(frames):
                    rows = slice(PAD + row, PAD + row + BAND)
                    terms = []
                    for weight, tap in zip(weights, SIDES):
                        start = PAD + row - tap + TAPS // 2
                        terms.append(weight * quotient_ref[frame, start : start + BAND, :])
                    spread = quotient_ref[frame, rows, :] + ((terms[0] + terms[1]) + (terms[2] + terms[3]))
                    current_ref[frame, rows, :] = source_ref[frame, rows, :] * spread
            source_ref = current_ref
        first = pl.multiple_of(lax.rem(step, tiles_dev) * rows_dev, rows_dev)
        for frame in range(frames):
            estimate = current_ref[frame, PAD + MARGIN : PAD + MARGIN + rows_dev, :].astype(jnp.bfloat16)
            start = pl.multiple_of(first + frame * positions, rows_dev)
            out_ref[step // tiles_dev, pl.ds(start, rows_dev), :] = estimate
        return carry

    lax.fori_loop(0, n_frame * tiles_dev, columns_step, 0)
    lane_tiles = lax.broadcasted_iota(jnp.int32, (TILE, TILE), 1) % tiles_dev
    gathered = jnp.zeros((frames * n_frame * rows_dev, TILE), jnp.float32)
    for tile in range(tiles_dev):
        pieces = []
        for frame in range(frames):
            start = frame * positions + tile * rows_dev
            pieces += [out_ref[block, start : start + rows_dev, :] for block in range(n_frame)]
        picked = jnp.where(lane_tiles == tile, 1.0, 0.0).astype(jnp.bfloat16)
        gathered = gathered + jnp.dot(jnp.concatenate(pieces, axis=0), picked, preferred_element_type=jnp.float32)
    lanes = lax.broadcasted_iota(jnp.int32, (rows_dev, TILE), 1)
    here = lanes % positions // tiles_dev == lax.broadcasted_iota(jnp.int32, (rows_dev, TILE), 0)
    sums = []
    for place in range(frames * n_frame):
        part = jnp.where(here, gathered[place * rows_dev : (place + 1) * rows_dev], 0.0)
        sums.append(jnp.sum(part, axis=0, keepdims=True))
    sums = jnp.concatenate(sums, axis=0)
    high = sums.astype(jnp.bfloat16).astype(jnp.float32)
    split = jnp.where(lax.broadcasted_iota(jnp.int32, sums.shape, 1) < positions, high, sums - high).astype(jnp.bfloat16)
    for block in range(n_frame):
        side_ref[block, : split.shape[0], :] = split
        side_ref[block, split.shape[0] :, :] = feet_ref[block]


def deconvolved(series):
    total = len(series)
    factors = []
    for step in range(total):
        middle = 1.0 + SMOOTHING * (1.0 if step in (0, total - 1) else 2.0)
        if step:
            middle -= SMOOTHING * SMOOTHING * factors[-1]
        factors.append(1.0 / middle)
    scaled = [cells * factor for cells, factor in zip(series, factors)]
    forward = [scaled[0]]
    for step in range(1, total):
        forward.append(scaled[step] + (SMOOTHING * factors[step]) * forward[step - 1])
    baseline = [None] * total
    baseline[total - 1] = forward[total - 1]
    for step in range(total - 2, -1, -1):
        baseline[step] = forward[step] + (SMOOTHING * factors[step]) * baseline[step + 1]
    result, earlier = [], None
    for step in range(total):
        detrended = series[step] - baseline[step]
        result.append(detrended if earlier is None else detrended - DECAY_RATE * earlier)
        earlier = detrended
    return result


def partial_kernel(*refs, positions):
    pieces, (out_ref, sums_ref, feet_ref) = refs[:-3], refs[-3:]
    n_frame = len(pieces)
    place = lax.axis_index("frame")
    rows = sums_ref.shape[0] // n_frame
    half = feet_ref.shape[1]
    for step, piece in enumerate(pieces[::-1]):
        sums_ref[pl.ds(pl.multiple_of((place ^ step) * rows, rows), rows), :] = piece[:rows, :].astype(jnp.float32)
        feet_ref[place ^ step] = piece[rows:, :].astype(jnp.float32)
    series = [sums_ref[t * n_frame : (t + 1) * n_frame, :] for t in range(rows)]
    for t, sums in enumerate(deconvolved(series)):
        sums_ref[t * n_frame : (t + 1) * n_frame, :] = sums + pltpu.roll(sums, TILE // 2, 1)
    left = lax.broadcasted_iota(jnp.int32, (half, TILE), 1) < positions
    weights, sums = [], []
    extra = jnp.where(lax.broadcasted_iota(jnp.int32, (8, TILE), 0) == 0, 1.0, 0.0)
    for block in range(n_frame):
        feet = feet_ref[block]
        weights.append(jnp.concatenate([jnp.where(left, feet, 0.0), jnp.where(left, 0.0, feet)], axis=0))
        sums.append(jnp.concatenate([sums_ref[pl.ds(block, rows, stride=n_frame), :], extra], axis=0))
    sums = jnp.concatenate(sums, axis=1)
    parts = []
    for _ in range(3):
        parts.append(sums.astype(jnp.bfloat16))
        sums = sums - parts[-1].astype(jnp.float32)
    totals = lax.dot_general(
        jnp.concatenate(weights * 3, axis=1).astype(jnp.bfloat16),
        jnp.concatenate(parts, axis=1),
        (((1,), (1,)), ((), ())),
        preferred_element_type=jnp.float32,
    )
    share = out_ref.shape[1]
    out_ref[...] = jnp.zeros_like(out_ref)
    for row in range(out_ref.shape[0]):
        out_ref[row, :, : rows + 8] = totals[row * share : (row + 1) * share]


def temporal_kernel(*refs, frames):
    pieces, (spikes_ref, in_ref) = refs[:-2], refs[-2:]
    place = lax.axis_index("frame")
    for step, piece in enumerate(pieces[::-1]):
        in_ref[place ^ step] = piece[...]
    total, rows_dev, columns = spikes_ref.shape
    positions = in_ref.shape[1] // frames
    for tile in range(columns // TILE):
        series = []
        for t in range(total):
            start = t % frames * positions + tile * rows_dev
            series.append(in_ref[t // frames, start : start + rows_dev, :].astype(jnp.float32))
        for t, spikes in enumerate(deconvolved(series)):
            spikes_ref[t, :, tile * TILE : (tile + 1) * TILE] = spikes.astype(spikes_ref.dtype)


def means_kernel(*refs):
    pieces, traces_ref = refs[:-1], refs[-1]
    frames = traces_ref.shape[1]
    total = pieces[0][...]
    for piece in pieces[1:]:
        total = total + piece[...]
    traces_ref[...] = total[:, :frames] / (TILE * total[:, frames : frames + 1])


def swapped(parts, axis):
    count, place = lax.axis_size(axis), lax.axis_index(axis)
    arrived = [lax.dynamic_index_in_dim(parts, place, 0, keepdims=False, allow_negative_indices=False)]
    for step in range(1, count):
        part = lax.dynamic_index_in_dim(parts, place ^ step, 0, keepdims=False, allow_negative_indices=False)
        arrived.append(lax.ppermute(part, axis, [(i, i ^ step) for i in range(count)]))
    return arrived


def in_turn(*arrays):
    done = []
    for array in arrays:
        done = list(lax.optimization_barrier((*done, array)))
    return done


def by_halo(observed, kernels, band_kernel, masks):
    n_frame, n_row = lax.axis_size("frame"), lax.axis_size("row")
    frames, rows_dev, width = observed.shape
    components, _, tiles_dev = masks.shape
    positions = rows_dev * tiles_dev
    share = components // (n_frame * n_row)
    span = rows_dev + 2 * MARGIN
    smem, vmem = pl.BlockSpec(memory_space=pltpu.SMEM), pl.BlockSpec(memory_space=pltpu.VMEM)

    def call(kernel, name, in_specs, out_shape, scratch=(), cost=1000):
        many = isinstance(out_shape, tuple)
        return pl.pallas_call(
            kernel,
            name=name,
            out_shape=out_shape,
            in_specs=in_specs,
            out_specs=(vmem,) * len(out_shape) if many else vmem,
            scratch_shapes=scratch,
            compiler_params=pltpu.CompilerParams(vmem_limit_bytes=16 << 20),
            cost_estimate=pl.CostEstimate(flops=cost, bytes_accessed=cost, transcendentals=0),
        )

    def array(*shape, dtype=jnp.float32):
        return jax.ShapeDtypeStruct(shape, dtype)

    packed = array(frames * (NEAR + FAR), width)
    inner, outer, own = call(halo_kernel, "halo", [vmem], (packed, packed, array(*observed.shape)))(observed)
    inner_swap = [(i, i ^ 1) for i in range(n_row)]
    outer_swap = []
    for f in range(n_frame):
        for i in range(n_row):
            there = (f ^ 1, i) if i in (0, n_row - 1) else (f, (i - 1 ^ 1) + 1)
            outer_swap.append((f * n_row + i, there[0] * n_row + there[1]))
    inner = lax.ppermute(inner.astype(jnp.float16), "row", inner_swap)
    outer = lax.ppermute(outer.astype(jnp.float16), ("frame", "row"), outer_swap)
    inner, outer = in_turn(inner, outer)
    taps, back = call(
        functools.partial(taps_kernel, height=rows_dev * n_row, rows_dev=rows_dev),
        "taps",
        [smem, smem],
        (array(len(SIDES), span, TILE),) * 2,
        [pltpu.VMEM((len(SIDES), span + 2 * PAD, TILE), jnp.float32)],
    )(band_kernel, kernels)
    feet = call(feet_kernel, "feet", [vmem], array(n_frame, n_row * share // 2, TILE, dtype=jnp.bfloat16))(
        masks.transpose(1, 2, 0)
    )
    row = lax.axis_index("row")
    even = row % 2 == 0
    alone = (row == 0) | (row == n_row - 1)
    inner, outer = inner.astype(jnp.float32), jnp.where(alone, 1.0, outer.astype(jnp.float32))
    top, bottom = jnp.where(even, outer, inner), jnp.where(even, inner, outer)
    side_rows = frames * n_frame + n_row * share // 2
    blocks, sides = call(
        restore_kernel,
        "restore",
        [vmem] * 6,
        (
            array(n_frame, frames * positions, TILE, dtype=jnp.bfloat16),
            array(n_frame, side_rows, TILE, dtype=jnp.bfloat16),
        ),
        [pltpu.VMEM((frames, span + 2 * PAD, TILE), jnp.float32)] * 3,
    )(taps, back, feet, own, top, bottom)
    sides = swapped(sides, "frame")
    pieces = swapped(blocks, "frame")
    partial = call(
        functools.partial(partial_kernel, positions=positions),
        "partial",
        [vmem] * n_frame,
        array(n_row, share, TILE),
        [
            pltpu.VMEM((n_frame * frames * n_frame, TILE), jnp.float32),
            pltpu.VMEM((n_frame, n_row * share // 2, TILE), jnp.float32),
        ],
    )(*sides[::-1])
    shares = swapped(partial, "row")
    spikes = call(
        functools.partial(temporal_kernel, frames=frames),
        "temporal",
        [vmem] * n_frame,
        array(n_frame * frames, rows_dev, tiles_dev * TILE, dtype=jnp.bfloat16),
        [pltpu.VMEM((n_frame, frames * positions, TILE), jnp.bfloat16)],
    )(*pieces[::-1])
    spikes, *shares = in_turn(spikes, *shares[::-1])
    traces = call(means_kernel, "means", [vmem] * n_row, array(share, n_frame * frames))(*shares)
    return (spikes, traces)


def fits(mesh, observed, masks):
    frames_dev = observed.shape[0] // mesh.shape["frame"]
    rows_dev = masks.shape[1] // (mesh.shape["groups"] * mesh.shape["row"])
    tiles_dev = masks.shape[2] // mesh.shape["frame"]
    places = mesh.shape["frame"] * mesh.shape["row"]
    return (
        frames_dev == mesh.shape["frame"] == mesh.shape["row"] == 4
        and 2 * rows_dev * tiles_dev == TILE
        and rows_dev == 16
        and masks.shape[0] // places == 16
    )


def solution(mesh):
    in_specs = (
        P("frame", ("groups", "row"), None),
        P(),
        P("groups"),
        P(None, ("groups", "row"), "frame"),
    )
    out_specs = (P(None, ("groups", "row"), "frame"), P(("groups", "frame", "row"), None))

    def whole(observed, kernels, band_kernel, masks):
        body = by_halo if fits(mesh, observed, masks) else local
        mapped = jax.shard_map(body, mesh=mesh, in_specs=in_specs, out_specs=out_specs, check_vma=False)
        return mapped(observed, kernels, band_kernel, masks)

    return whole
```
